32 devices in a mesh: strip: 4 (over x, core), sub: 8 (over z, y).
Axes of the slice: x: 2, y: 2, z: 4, core: 2. Of those that a mesh axis runs over, the one named last changes fastest.
Arguments:
- node_latents: bfloat16 [8192, 128], P(('strip', 'sub')), may hold values from -6 to 6
- edge_latents: bfloat16 [131072, 128], P(('strip', 'sub')), may hold values from -6 to 6
- senders: int32 [131072], P(('strip', 'sub')), may hold values from 0 to 8191, as said below
- receivers: int32 [131072], P(('strip', 'sub')), may hold values from 0 to 255
- edge_count: int32 [32], P(('strip', 'sub')), may hold values from 1024 to 4096, as said below
- w_edge_in: bfloat16 [384, 128], replicated, may hold values from -0.3125 to 0.3125
- w_edge_out: bfloat16 [128, 128], replicated, may hold values from -0.5 to 0.5
- w_node_in: bfloat16 [256, 128], replicated, may hold values from -0.375 to 0.375
- w_node_out: bfloat16 [128, 128], replicated, may hold values from -0.5 to 0.5
- node_cotangent: bfloat16 [8192, 128], P(('strip', 'sub')), may hold values from -6 to 6
- edge_cotangent: bfloat16 [131072, 128], P(('strip', 'sub')), may hold values from -6 to 6
Outputs:
- new_nodes: bfloat16 [8192, 128], P(('strip', 'sub'))
- new_edges: bfloat16 [131072, 128], P(('strip', 'sub'))
- node_grad: float32 [8192, 128], P(('strip', 'sub'))
- grad_edge_in: float32 [384, 128], replicated
- grad_edge_out: float32 [128, 128], replicated
- grad_node_in: float32 [256, 128], replicated
- grad_node_out: float32 [128, 128], replicated
The draws below stay inside these ranges and needn't reach their ends.
Inputs may be any that keep to these rules, and one draw needn't show every extreme that they name: `senders`: devices are numbered strip * 8 + sub-block, each holding 256 consecutive particles and 4096 consecutive edge slots. The sender of an edge held by the device at strip i and sub-block j is a particle of a device at strip i - 1, i or i + 1 and sub-block j - 1, j or j + 1 (no wrap); if that device is not the edge's own, the sender is among its first 32 particles. A device's live edges are its first edge_count slots; some device is full.
All inputs are finite; a program needn't handle non-finite values.
Results may differ from the reference program's by a relative error of at most 0.012.
Values may be sent and summed in bfloat16 or wider, within the bound.
No kernel may reach another device: no remote copies, remote signals or barrier semaphores. Data moves between devices by JAX's collectives and lax.ppermute only.
A program may use at most 64 MiB of HBM per device.

```python
import math
import jax
import jax.numpy as jnp
from jax import lax

H = 128
P_DEV = 256
BAND = 32
E_DEV = 4096
STRIPS = 4
SUBS = 8
PARTICLES = 8192
EDGES = 131072
DEVICES = 32


def draw_senders(key, part):
    key = jax.random.fold_in(key, 11)
    first, second, third, fourth, fifth = jax.random.split(key, 5)
    device = jnp.arange(EDGES, dtype=jnp.int32) // E_DEV
    strip_of = device // SUBS
    sub_of = device % SUBS
    crossing = jax.random.randint(fourth, (EDGES,), 0, 5, dtype=jnp.int32) == 0
    step_strip = jax.random.randint(first, (EDGES,), -1, 2, dtype=jnp.int32)
    step_sub = jax.random.randint(second, (EDGES,), -1, 2, dtype=jnp.int32)
    near_strip = jnp.where(crossing, jnp.clip(strip_of + step_strip, 0, STRIPS - 1), strip_of)
    near_sub = jnp.where(crossing, jnp.clip(sub_of + step_sub, 0, SUBS - 1), sub_of)
    inner = jax.random.randint(third, (EDGES,), 0, P_DEV, dtype=jnp.int32)
    border = jax.random.randint(fifth, (EDGES,), 0, BAND, dtype=jnp.int32)
    local = jnp.where(crossing, border, inner)
    return ((near_strip * SUBS + near_sub) * P_DEV + local).astype(jnp.int32)


def draw_edge_count(key, part):
    key = jax.random.fold_in(key, 23)
    first, second = jax.random.split(key)
    counts = jax.random.randint(first, (DEVICES,), E_DEV // 4, E_DEV + 1, dtype=jnp.int32)
    fullest = jax.random.randint(second, (), 0, DEVICES, dtype=jnp.int32)
    return jnp.where(jnp.arange(DEVICES, dtype=jnp.int32) == fullest, E_DEV, counts).astype(jnp.int32)


def plant(drawn, own_key, least, largest):
    place = [jax.random.randint(jax.random.fold_in(own_key, axis), (), 0, length) for axis, length in enumerate(drawn.shape)]
    main_axis = drawn.shape.index(max(drawn.shape))
    beside = place[:main_axis] + [(place[main_axis] + 1) % drawn.shape[main_axis]] + place[main_axis + 1:]
    return drawn.at[tuple(place)].set(least).at[tuple(beside)].set(largest)


def steps_of(key, dims, cuts, least, top_value):
    loudness = 1.0
    for position, parts in cuts:
        heights = jax.random.uniform(jax.random.fold_in(jax.random.fold_in(key, 6), position), (parts,), jnp.float32, least / len(cuts), top_value / len(cuts))
        loudness = loudness * jnp.repeat(jnp.exp(heights), dims[position] // parts).reshape((-1,) + (1,) * (len(dims) - 1 - position))
    return loudness


def centred(own_key, extent, deviation, reach, shards=(), kind=jnp.bfloat16):
    entries = deviation * jax.random.normal(own_key, extent, jnp.float32)
    if shards:
        entries = entries * steps_of(own_key, extent, shards, -0.22, 0.18)
    return jnp.clip(entries, -reach, reach).astype(kind)


def setup_inputs(seed: int = 0) -> dict:
    key_list = jax.random.split(jax.random.key(seed), 12)
    return {
        "node_latents": centred(key_list[0], (PARTICLES, H), 1.0, 6.0, ((0, 32),)),
        "edge_latents": centred(key_list[1], (EDGES, H), 1.0, 6.0, ((0, 32),)),
        "senders": draw_senders(jax.random.fold_in(key_list[11], 71), 0),
        "receivers": plant(jax.random.randint(key_list[3], (EDGES,), 0, P_DEV), jax.random.fold_in(key_list[3], 1), 0, P_DEV - 1).astype(jnp.int32),
        "edge_count": draw_edge_count(jax.random.fold_in(key_list[11], 71), 0),
        "w_edge_in": centred(key_list[5], (3 * H, H), (3 * H) ** -0.5, 0.3125),
        "w_edge_out": centred(key_list[6], (H, H), H ** -0.5, 0.5),
        "w_node_in": centred(key_list[7], (2 * H, H), (2 * H) ** -0.5, 0.375),
        "w_node_out": centred(key_list[8], (H, H), H ** -0.5, 0.5),
        "node_cotangent": centred(key_list[9], (PARTICLES, H), 1.0, 6.0, ((0, 32),)),
        "edge_cotangent": centred(key_list[10], (EDGES, H), 1.0, 6.0, ((0, 32),)),
    }


EPS = 1e-05

def norm_rows(values):
    centre = values - lax.optimization_barrier(jnp.mean(values, axis=1, keepdims=True))
    scale = lax.rsqrt(lax.optimization_barrier(jnp.mean(centre * centre, axis=1, keepdims=True)) + EPS)
    return (centre * scale, scale)

def norm_back(normed, scale, upstream):
    first = lax.optimization_barrier(jnp.mean(upstream, axis=1, keepdims=True))
    second = lax.optimization_barrier(jnp.mean(upstream * normed, axis=1, keepdims=True))
    return scale * (upstream - first - normed * second)

def silu_grad(values):
    sig = jax.nn.sigmoid(values)
    return sig * (1.0 + values * (1.0 - sig))

def edge_forward(send_rows, recv_rows, edges, valid, w_edge_in, w_edge_out):
    stacked = jnp.concatenate([send_rows, recv_rows, edges], axis=1)
    hidden_pre = jnp.dot(stacked, w_edge_in, preferred_element_type=jnp.float32)
    hidden = jax.nn.silu(hidden_pre).astype(jnp.bfloat16)
    outer = jnp.dot(hidden, w_edge_out, preferred_element_type=jnp.float32)
    normed, scale = norm_rows(outer)
    message = normed * valid[:, None]
    updated = (edges.astype(jnp.float32) + message).astype(jnp.bfloat16)
    return (stacked, hidden_pre, hidden, normed, scale, message, updated)

def edge_back(stacked, hidden_pre, hidden, normed, scale, valid, upstream, w_edge_in, w_edge_out):
    d_outer = norm_back(normed, scale, upstream * valid[:, None]).astype(jnp.bfloat16)
    g_out = jnp.dot(hidden.T, d_outer, preferred_element_type=jnp.float32)
    d_hidden = jnp.dot(d_outer, w_edge_out.T, preferred_element_type=jnp.float32)
    d_pre = (d_hidden * silu_grad(hidden_pre)).astype(jnp.bfloat16)
    g_in = jnp.dot(stacked.T, d_pre, preferred_element_type=jnp.float32)
    d_stacked = jnp.dot(d_pre, w_edge_in.T, preferred_element_type=jnp.float32)
    return (g_in, g_out, d_stacked)

def node_step(nodes, agg_rows, cotangent, w_node_in, w_node_out):
    joined = jnp.concatenate([nodes, agg_rows], axis=1)
    pre = jnp.dot(joined, w_node_in, preferred_element_type=jnp.float32)
    act = jax.nn.silu(pre).astype(jnp.bfloat16)
    outer = jnp.dot(act, w_node_out, preferred_element_type=jnp.float32)
    normed, scale = norm_rows(outer)
    updated = (nodes.astype(jnp.float32) + normed).astype(jnp.bfloat16)
    d_outer = norm_back(normed, scale, cotangent).astype(jnp.bfloat16)
    g_out = jnp.dot(act.T, d_outer, preferred_element_type=jnp.float32)
    d_act = jnp.dot(d_outer, w_node_out.T, preferred_element_type=jnp.float32)
    d_pre = (d_act * silu_grad(pre)).astype(jnp.bfloat16)
    g_in = jnp.dot(joined.T, d_pre, preferred_element_type=jnp.float32)
    d_joined = jnp.dot(d_pre, w_node_in.T, preferred_element_type=jnp.float32)
    return (updated, g_in, g_out, d_joined)

def reference(node_latents, edge_latents, senders, receivers, edge_count, w_edge_in, w_edge_out, w_node_in, w_node_out, node_cotangent, edge_cotangent):
    width = node_latents.shape[1]
    base = jnp.arange(DEVICES, dtype=jnp.int32)[:, None] * P_DEV
    send_blocks = senders.reshape(DEVICES, E_DEV).astype(jnp.int32)
    recv_blocks = (receivers.reshape(DEVICES, E_DEV) + base).astype(jnp.int32)
    edge_blocks = edge_latents.reshape(DEVICES, E_DEV, width)
    cot_blocks = edge_cotangent.reshape(DEVICES, E_DEV, width)
    valid_blocks = (jnp.arange(E_DEV, dtype=jnp.int32)[None, :] < edge_count[:, None]).astype(jnp.float32)

    def forward(agg, item):
        send_idx, recv_idx, edges, valid = item
        out = edge_forward(node_latents[send_idx], node_latents[recv_idx], edges, valid, w_edge_in, w_edge_out)
        return (agg.at[recv_idx].add(out[5]), out[6])
    agg, new_edges = lax.scan(forward, jnp.zeros((PARTICLES, width), jnp.float32), (send_blocks, recv_blocks, edge_blocks, valid_blocks))
    node_cot = node_cotangent.astype(jnp.float32)
    new_nodes, gn_in, gn_out, d_joined = node_step(node_latents, agg.astype(jnp.bfloat16), node_cot, w_node_in, w_node_out)
    d_agg = d_joined[:, width:]

    def backward(carry, item):
        grads, g_in, g_out = carry
        send_idx, recv_idx, edges, valid, cot = item
        out = edge_forward(node_latents[send_idx], node_latents[recv_idx], edges, valid, w_edge_in, w_edge_out)
        upstream = cot.astype(jnp.float32) + d_agg[recv_idx]
        gi, go, d_stacked = edge_back(out[0], out[1], out[2], out[3], out[4], valid, upstream, w_edge_in, w_edge_out)
        grads = grads.at[send_idx].add(d_stacked[:, :width]).at[recv_idx].add(d_stacked[:, width:2 * width])
        return ((grads, g_in + gi, g_out + go), None)
    start = (node_cot + d_joined[:, :width], jnp.zeros(w_edge_in.shape, jnp.float32), jnp.zeros(w_edge_out.shape, jnp.float32))
    (node_grad, ge_in, ge_out), unused = lax.scan(backward, start, (send_blocks, recv_blocks, edge_blocks, valid_blocks, cot_blocks))
    factor = 1.0 / math.sqrt(EDGES)
    return (new_nodes, new_edges.reshape(EDGES, width), node_grad, ge_in * factor, ge_out * factor, gn_in * factor, gn_out * factor)
```

```python
import math

import jax
import jax.numpy as jnp
from jax import lax
from jax.sharding import PartitionSpec as P

EPS = 1e-05


def padded_2(block, sides, width):
    for axis, dim in sides:
        count = lax.axis_size(axis)
        forward = [(i, i + 1) for i in range(count - 1)]
        backward = [(target, source) for source, target in forward]
        low = lax.ppermute(
            lax.slice_in_dim(block, block.shape[dim] - width, None, axis=dim), axis, forward
        )
        high = lax.ppermute(lax.slice_in_dim(block, 0, width, axis=dim), axis, backward)
        block = jnp.concatenate([low, block, high], axis=dim)
    return block


def shifted(value, axis, steps):
    count = lax.axis_size(axis)
    first, last = (max(0, -steps), min(count, count - steps))
    return lax.ppermute(value, axis, [(source, source + steps) for source in range(first, last)])


def summed_over_devices(parts):
    axes = ("strip", "sub")
    count = lax.axis_size("strip") * lax.axis_size("sub")
    width = parts[0].shape[1]
    rows = [part.shape[0] for part in parts]
    total = sum(rows)
    share = -(-total // count)
    packed = jnp.concatenate([part.astype(jnp.bfloat16) for part in parts], axis=0)
    packed = jnp.pad(packed, ((0, share * count - total), (0, 0)))
    mine = lax.all_to_all(packed.reshape(count, share, width), axes, 0, 0)
    mine = jnp.sum(mine.astype(jnp.float32), axis=0).astype(jnp.bfloat16)
    spread = jnp.broadcast_to(mine[None], (count, share, width))
    whole = lax.all_to_all(spread, axes, 0, 0).reshape(count * share, width)
    ends = [sum(rows[: i + 1]) for i in range(len(rows))]
    return [whole[end - n : end].astype(jnp.float32) for end, n in zip(ends, rows)]


def norm_rows(values):
    centre = values - jnp.mean(values, axis=1, keepdims=True)
    scale = lax.rsqrt(jnp.mean(centre * centre, axis=1, keepdims=True) + EPS)
    return (centre * scale, scale)


def norm_back(normed, scale, upstream):
    first = jnp.mean(upstream, axis=1, keepdims=True)
    second = jnp.mean(upstream * normed, axis=1, keepdims=True)
    return scale * (upstream - first - normed * second)


def silu_grad(values):
    sig = jax.nn.sigmoid(values)
    return sig * (1.0 + values * (1.0 - sig))


def pick_rows(onehot, table):
    return jnp.dot(onehot, table, preferred_element_type=jnp.float32)


def pick_exact(onehot, table):
    return jnp.dot(
        onehot.astype(jnp.float32),
        table,
        precision=lax.Precision.HIGHEST,
        preferred_element_type=jnp.float32,
    )


def sum_rows(onehot, values):
    return jnp.dot(
        onehot.astype(jnp.float32).T,
        values,
        precision=lax.Precision.HIGHEST,
        preferred_element_type=jnp.float32,
    )


def shards(
    node_latents,
    edge_latents,
    senders,
    receivers,
    edge_count,
    w_edge_in,
    w_edge_out,
    w_node_in,
    w_node_out,
    node_cotangent,
    edge_cotangent,
):
    count_p = node_latents.shape[0]
    width = node_latents.shape[1]
    count_e = edge_latents.shape[0]
    border = count_p // 8
    subs_here = lax.axis_size("sub")
    my_strip = lax.axis_index("strip")
    my_sub = lax.axis_index("sub")
    rim_rows = node_latents[:border].reshape(1, 1, border, width)
    strips_here = lax.axis_size("strip")
    rims = jnp.broadcast_to(rim_rows[0], (strips_here * subs_here, border, width))
    rims = lax.all_to_all(rims, ("strip", "sub"), 0, 0)
    rims = rims.reshape(strips_here, subs_here, border, width)
    rims = jnp.pad(rims, ((1, 1), (1, 1), (0, 0), (0, 0)))
    padded = lax.dynamic_slice(rims, (my_strip, my_sub, 0, 0), (3, 3, border, width))
    table = jnp.concatenate([node_latents, padded.reshape(9 * border, width)], axis=0)
    owner = senders // count_p
    within = senders % count_p
    is_local = owner == my_strip * subs_here + my_sub
    block = (owner // subs_here - my_strip + 1) * 3 + (owner % subs_here - my_sub + 1)
    send_index = jnp.where(
        is_local, within, count_p + block * border + jnp.minimum(within, border - 1)
    )
    valid = (jnp.arange(count_e, dtype=jnp.int32) < edge_count[0]).astype(jnp.float32)
    send_hot = (
        send_index[:, None] == jnp.arange(count_p + 9 * border, dtype=jnp.int32)[None, :]
    ).astype(jnp.bfloat16)
    recv_hot = (receivers[:, None] == jnp.arange(count_p, dtype=jnp.int32)[None, :]).astype(
        jnp.bfloat16
    )
    send_rows = pick_rows(send_hot, table).astype(jnp.bfloat16)
    recv_rows = pick_rows(recv_hot, node_latents).astype(jnp.bfloat16)
    stacked = jnp.concatenate([send_rows, recv_rows, edge_latents], axis=1)
    hidden_pre = jnp.dot(stacked, w_edge_in, preferred_element_type=jnp.float32)
    hidden = jax.nn.silu(hidden_pre).astype(jnp.bfloat16)
    outer = jnp.dot(hidden, w_edge_out, preferred_element_type=jnp.float32)
    normed, scale = norm_rows(outer)
    message = normed * valid[:, None]
    new_edges = (edge_latents.astype(jnp.float32) + message).astype(jnp.bfloat16)
    agg = sum_rows(recv_hot, message)
    joined = jnp.concatenate([node_latents, agg.astype(jnp.bfloat16)], axis=1)
    node_pre = jnp.dot(joined, w_node_in, preferred_element_type=jnp.float32)
    node_act = jax.nn.silu(node_pre).astype(jnp.bfloat16)
    node_outer = jnp.dot(node_act, w_node_out, preferred_element_type=jnp.float32)
    node_normed, node_scale = norm_rows(node_outer)
    new_nodes = (node_latents.astype(jnp.float32) + node_normed).astype(jnp.bfloat16)
    node_cot = node_cotangent.astype(jnp.float32)
    d_node_outer = norm_back(node_normed, node_scale, node_cot).astype(jnp.bfloat16)
    gn_out = jnp.dot(node_act.T, d_node_outer, preferred_element_type=jnp.float32)
    d_node_act = jnp.dot(d_node_outer, w_node_out.T, preferred_element_type=jnp.float32)
    d_node_pre = (d_node_act * silu_grad(node_pre)).astype(jnp.bfloat16)
    gn_in = jnp.dot(joined.T, d_node_pre, preferred_element_type=jnp.float32)
    d_joined = jnp.dot(d_node_pre, w_node_in.T, preferred_element_type=jnp.float32)
    upstream = edge_cotangent.astype(jnp.float32) + pick_exact(recv_hot, d_joined[:, width:])
    d_outer = norm_back(normed, scale, upstream * valid[:, None]).astype(jnp.bfloat16)
    ge_out = jnp.dot(hidden.T, d_outer, preferred_element_type=jnp.float32)
    d_hidden = jnp.dot(d_outer, w_edge_out.T, preferred_element_type=jnp.float32)
    d_pre = (d_hidden * silu_grad(hidden_pre)).astype(jnp.bfloat16)
    ge_in = jnp.dot(stacked.T, d_pre, preferred_element_type=jnp.float32)
    d_stacked = jnp.dot(d_pre, w_edge_in.T, preferred_element_type=jnp.float32)
    send_sums = sum_rows(send_hot, d_stacked[:, :width])
    owed = send_sums[count_p:].reshape(3, 3, border, width)
    local_grad = (
        node_cot
        + d_joined[:, :width]
        + sum_rows(recv_hot, d_stacked[:, width : 2 * width])
        + send_sums[:count_p]
    )
    column = (
        owed[:, 1]
        + shifted(owed[:, 0].astype(jnp.bfloat16), "sub", -1).astype(jnp.float32)
        + shifted(owed[:, 2].astype(jnp.bfloat16), "sub", 1).astype(jnp.float32)
    )
    returned = column[1] + shifted(column[0], "strip", -1) + shifted(column[2], "strip", 1)
    node_grad = local_grad.at[:border].add(returned)
    totals = summed_over_devices((ge_in, ge_out, gn_in, gn_out))
    factor = 1.0 / math.sqrt(count_e * lax.axis_size("strip") * subs_here)
    return (
        new_nodes,
        new_edges,
        node_grad,
        totals[0] * factor,
        totals[1] * factor,
        totals[2] * factor,
        totals[3] * factor,
    )


def solution(mesh):
    placed = (
        P(("strip", "sub"), None),
        P(("strip", "sub"), None),
        P(("strip", "sub")),
        P(("strip", "sub")),
        P(("strip", "sub")),
        P(),
        P(),
        P(),
        P(),
        P(("strip", "sub"), None),
        P(("strip", "sub"), None),
    )
    return jax.shard_map(
        shards,
        mesh=mesh,
        in_specs=placed,
        out_specs=(
            P(("strip", "sub"), None),
            P(("strip", "sub"), None),
            P(("strip", "sub"), None),
            P(),
            P(),
            P(),
            P(),
        ),
        check_vma=False,
    )
```

```python
import functools
import math

import jax
import jax.numpy as jnp
from jax import lax
from jax.experimental import pallas as pl
from jax.experimental.pallas import tpu as pltpu
from jax.sharding import Mesh
from jax.sharding import PartitionSpec as P

EPS = 1e-05
CHUNK = 512
PLANE = ("strip", "y")
ALL = ("strip", "z", "y")
F32 = jnp.float32
BF16 = jnp.bfloat16
VMEM = pl.BlockSpec(memory_space=pltpu.VMEM)
SMEM = pl.BlockSpec(memory_space=pltpu.SMEM)


def mm(left, right):
    return jnp.dot(left, right, preferred_element_type=F32)


def mm_nt(left, right):
    return lax.dot_general(left, right, (((1,), (1,)), ((), ())), preferred_element_type=F32)


def mm_tn(left, right):
    return lax.dot_general(left, right, (((0,), (0,)), ((), ())), preferred_element_type=F32)


def norm_rows(values):
    centre = values - jnp.mean(values, axis=1, keepdims=True)
    scale = lax.rsqrt(jnp.mean(centre * centre, axis=1, keepdims=True) + EPS)
    return (centre * scale, scale)


def norm_back(normed, scale, upstream):
    first = jnp.mean(upstream, axis=1, keepdims=True)
    second = jnp.mean(upstream * normed, axis=1, keepdims=True)
    return scale * (upstream - first - normed * second)


def silu_and_slope(values):
    sig = 0.5 + 0.5 * jnp.tanh(0.5 * values)
    act = values * sig
    return (act, sig + act * (1.0 - sig))


def call(kernel, outs, ins, scratch=()):
    return pl.pallas_call(
        kernel,
        out_shape=[jax.ShapeDtypeStruct(shape, dtype) for shape, dtype in outs],
        in_specs=[SMEM if value.ndim == 1 else VMEM for value in ins],
        out_specs=[VMEM] * len(outs),
        scratch_shapes=list(scratch),
        compiler_params=pltpu.CompilerParams(vmem_limit_bytes=48 * 2**20),
    )(*ins)


def rim_kernel(place, nodes, out):
    border = out.shape[1]
    for target in range(out.shape[0]):
        out[target] = nodes[:border]


def rim_plane_kernel(place, rims, out):
    border = rims.shape[1]
    zs = rims.shape[0]
    my_z, my_y = place[1], place[2]
    other = jnp.clip(my_z + 1 - 2 * my_y, 0, zs - 1)
    own = rims[my_z]
    beyond = rims[other]
    for target in range(out.shape[0]):
        out[target, :border] = own
        out[target, border:] = beyond


def layer_kernel(
    place,
    nodes,
    rims,
    edges,
    info,
    w_edge_in,
    w_edge_out,
    w_node_in,
    w_node_out,
    node_cot,
    edge_cot,
    new_nodes,
    new_edges,
    local_grad,
    parts,
    table,
    tables,
    recv_hot,
    recv_hot_t,
    hidden,
    slope,
    normed,
    scale,
    sums,
    ge_edge,
    ge_out,
    agg,
    packed,
):
    count_p, width = nodes.shape
    border = rims.shape[1] // 2
    chunks, _, chunk = info.shape
    slots = rims.shape[0]
    strips = slots // 2
    share = parts.shape[1] - 2 * border
    my_strip, my_y, live_count = place[0], place[2], place[3]

    table[:count_p] = nodes[...]
    spot = 0
    for d_strip in (-1, 0, 1):
        strip = jnp.clip(my_strip + d_strip, 0, strips - 1)
        for d_sub in (-1, 0, 1):
            if d_strip == 0 and d_sub == 0:
                continue
            if d_sub == 0:
                slot, part = 2 * strip + my_y, 0
            elif d_sub == 1:
                slot, part = 2 * strip + 1 - my_y, my_y
            else:
                slot, part = 2 * strip + 1 - my_y, 1 - my_y
            first = pl.multiple_of(part * border, border)
            rows = slice(count_p + spot * border, count_p + (spot + 1) * border)
            table[rows] = rims[slot, pl.ds(first, border), :]
            spot += 1
    send_rows = table.shape[0]
    tables[:send_rows] = mm(table[...], w_edge_in[:width]).astype(BF16)
    tables[send_rows : send_rows + count_p] = mm(
        nodes[...], w_edge_in[width : 2 * width]
    ).astype(BF16)
    tables[send_rows + count_p :] = w_edge_in[2 * width :]

    lane = lax.broadcasted_iota(jnp.int32, (chunk, width), 1)
    row = lax.broadcasted_iota(jnp.int32, (chunk, width), 0)

    def hot(column, blocks):
        return [(column == lane + width * k).astype(F32).astype(BF16) for k in range(blocks)]

    def hot_t(line, size):
        place_of = lax.broadcasted_iota(jnp.int32, (size, chunk), 0)
        return (place_of == line).astype(F32).astype(BF16)

    agg[...] = jnp.zeros_like(agg)

    def forward(step, carry):
        rows = pl.ds(pl.multiple_of(step * chunk, chunk), chunk)
        index = info[step]
        columns = index.T
        send = hot(columns[:, 0:1], send_rows // width)
        recv = hot(columns[:, 1:2], count_p // width)
        recv = jnp.concatenate(recv, axis=1)
        recv_hot[rows] = recv
        edge = edges[rows]
        pre = mm(jnp.concatenate(send + [recv, edge], axis=1), tables[...])
        act, slope[rows] = silu_and_slope(pre)
        act = act.astype(BF16)
        hidden[rows] = act
        unit, factor = norm_rows(mm(act, w_edge_out[...]))
        normed[rows] = unit
        scale[rows] = jnp.broadcast_to(factor, unit.shape)
        message = jnp.where(row + step * chunk < live_count, unit, 0.0)
        new_edges[rows] = (edge.astype(F32) + message).astype(BF16)
        recv_t = hot_t(index[1:2], count_p)
        recv_hot_t[step] = recv_t
        agg[...] += mm(recv_t, message.astype(BF16))
        return carry

    lax.fori_loop(0, chunks, forward, 0)

    joined = jnp.concatenate([nodes[...], agg[...].astype(BF16)], axis=1)
    node_pre = mm(joined, w_node_in[...])
    node_act, node_slope = silu_and_slope(node_pre)
    node_act = node_act.astype(BF16)
    node_unit, node_scale = norm_rows(mm(node_act, w_node_out[...]))
    new_nodes[...] = (nodes[...].astype(F32) + node_unit).astype(BF16)
    cot = node_cot[...].astype(F32)
    d_outer = norm_back(node_unit, node_scale, cot).astype(BF16)
    d_pre = (mm_nt(d_outer, w_node_out[...]) * node_slope).astype(BF16)
    d_joined = mm_nt(d_pre, w_node_in[...])
    d_agg = d_joined[:, width:].astype(BF16)
    agg[...] = cot + d_joined[:, :width]
    packed[4 * width : 6 * width] = mm_tn(joined, d_pre).astype(BF16)
    packed[6 * width : 7 * width] = mm_tn(node_act, d_outer).astype(BF16)

    sums[...] = jnp.zeros_like(sums)
    ge_edge[...] = jnp.zeros_like(ge_edge)
    ge_out[...] = jnp.zeros_like(ge_out)

    def backward(step, carry):
        rows = pl.ds(pl.multiple_of(step * chunk, chunk), chunk)
        upstream = edge_cot[rows].astype(F32) + mm(recv_hot[rows], d_agg)
        upstream = jnp.where(row + step * chunk < live_count, upstream, 0.0)
        d_out = norm_back(normed[rows], scale[rows], upstream).astype(BF16)
        ge_out[...] += mm_tn(hidden[rows], d_out)
        d_in = (mm_nt(d_out, w_edge_out[...]) * slope[rows]).astype(BF16)
        sums[:send_rows] += mm(hot_t(info[step][0:1], send_rows), d_in)
        sums[send_rows:] += mm(recv_hot_t[step], d_in)
        ge_edge[...] += mm_tn(edges[rows], d_in)
        return carry

    lax.fori_loop(0, chunks, backward, 0)

    send_sums = sums[:send_rows].astype(BF16)
    recv_sums = sums[send_rows:].astype(BF16)
    packed[:width] = mm_tn(table[...], send_sums).astype(BF16)
    packed[width : 2 * width] = mm_tn(nodes[...], recv_sums).astype(BF16)
    packed[2 * width : 3 * width] = ge_edge[...].astype(BF16)
    packed[3 * width : 4 * width] = ge_out[...].astype(BF16)
    if packed.shape[0] > 7 * width:
        packed[7 * width :] = jnp.zeros((packed.shape[0] - 7 * width, width), BF16)
    sent = mm_nt(send_sums, w_edge_in[:width])
    local_grad[...] = agg[...] + sent[:count_p] + mm_nt(recv_sums, w_edge_in[width : 2 * width])
    owed = sent[count_p:].astype(BF16)
    for slot in range(slots):
        parts[slot, :share] = packed[slot * share : (slot + 1) * share]
        parts[slot, share:] = jnp.zeros((2 * border, width), BF16)
    spot = 0
    for d_strip in (-1, 0, 1):
        strip = my_strip + d_strip
        for d_sub in (-1, 0, 1):
            if d_strip == 0 and d_sub == 0:
                continue
            if d_sub == 0:
                slot, part = 2 * strip + my_y, 0
            elif d_sub == 1:
                slot, part = 2 * strip + 1 - my_y, my_y
            else:
                slot, part = 2 * strip + 1 - my_y, 1 - my_y
            first = pl.multiple_of(share + part * border, 16)
            block = owed[spot * border : (spot + 1) * border]

            @pl.when((strip >= 0) & (strip < strips))
            def put(slot=slot, first=first, block=block):
                parts[slot, pl.ds(first, border), :] = block

            spot += 1


def plane_sum_kernel(place, came, out, mine):
    border = mine.shape[0]
    zs = out.shape[0]
    share = out.shape[1] - border
    total = came[0].astype(F32)
    for slot in range(1, came.shape[0]):
        total = total + came[slot].astype(F32)
    share_total = total[:share].astype(BF16)
    mine[...] = total[share : share + border]
    beyond = total[share + border :].astype(BF16)
    for target in range(zs):
        out[target, :share] = share_total
        out[target, share:] = jnp.zeros_like(beyond)
    target = place[1] + 1 - 2 * place[2]

    @pl.when((target >= 0) & (target < zs))
    def put():
        out[target, share:] = beyond


def line_sum_kernel(factor, place, came, mine, local_grad, out, node_grad):
    border = mine.shape[0]
    share = out.shape[1]
    total = came[0].astype(F32)
    for slot in range(1, came.shape[0]):
        total = total + came[slot].astype(F32)
    share_total = (total[:share] * factor).astype(BF16)
    for target in range(out.shape[0]):
        out[target] = share_total
    node_grad[...] = local_grad[...]
    node_grad[:border] += mine[...] + total[share:]


def spread_kernel(place, came, *outs):
    share = came.shape[1]
    start = 0
    for out in outs:
        size = out.shape[0]
        done = 0
        while done < size:
            slot, offset = divmod(start + done, share)
            step = min(size - done, share - offset)
            out[done : done + step] = came[slot, offset : offset + step].astype(F32)
            done += step
        start += size


def shards(
    node_latents,
    edge_latents,
    senders,
    receivers,
    edge_count,
    w_edge_in,
    w_edge_out,
    w_node_in,
    w_node_out,
    node_cotangent,
    edge_cotangent,
):
    count_p, width = node_latents.shape
    count_e = edge_latents.shape[0]
    border = count_p // 8
    strips, zs, ys = (lax.axis_size(axis) for axis in ALL)
    subs = zs * ys
    slots = strips * ys
    my_strip, my_z, my_y = (lax.axis_index(axis).astype(jnp.int32) for axis in ALL)
    my_sub = my_z * ys + my_y
    place = jnp.stack([my_strip, my_z, my_y, edge_count[0]])

    (rims,) = call(rim_kernel, [((zs, border, width), BF16)], [place, node_latents])
    rims = lax.all_to_all(rims, "z", 0, 0)
    (rims,) = call(rim_plane_kernel, [((slots, 2 * border, width), BF16)], [place, rims])
    rims = lax.all_to_all(rims, PLANE, 0, 0)

    owner = senders // count_p
    within = senders % count_p
    is_local = owner == my_strip * subs + my_sub
    block = (owner // subs - my_strip + 1) * 3 + (owner % subs - my_sub + 1)
    block = jnp.where(block > 4, block - 1, block)
    send_index = jnp.where(
        is_local, within, count_p + block * border + jnp.minimum(within, border - 1)
    )
    chunk = min(CHUNK, count_e)
    chunks = count_e // chunk
    info = jnp.concatenate(
        [
            send_index.reshape(chunks, 1, chunk),
            receivers.reshape(chunks, 1, chunk),
            jnp.zeros((chunks, 6, chunk), jnp.int32),
        ],
        axis=1,
    )

    total = 7 * width
    share = -(-total // (slots * 16)) * 16
    send_rows = 2 * count_p
    new_nodes, new_edges, local_grad, parts = call(
        layer_kernel,
        [
            ((count_p, width), BF16),
            ((count_e, width), BF16),
            ((count_p, width), F32),
            ((slots, share + 2 * border, width), BF16),
        ],
        [
            place,
            node_latents,
            rims,
            edge_latents,
            info,
            w_edge_in,
            w_edge_out,
            w_node_in,
            w_node_out,
            node_cotangent,
            edge_cotangent,
        ],
        [
            pltpu.VMEM((send_rows, width), BF16),
            pltpu.VMEM((send_rows + count_p + width, width), BF16),
            pltpu.VMEM((count_e, count_p), BF16),
            pltpu.VMEM((chunks, count_p, chunk), BF16),
            pltpu.VMEM((count_e, width), BF16),
            pltpu.VMEM((count_e, width), F32),
            pltpu.VMEM((count_e, width), F32),
            pltpu.VMEM((count_e, width), F32),
            pltpu.VMEM((send_rows + count_p, width), F32),
            pltpu.VMEM((width, width), F32),
            pltpu.VMEM((width, width), F32),
            pltpu.VMEM((count_p, width), F32),
            pltpu.VMEM((slots * share, width), BF16),
        ],
    )

    came = lax.all_to_all(parts, PLANE, 0, 0)
    parts, mine = call(
        plane_sum_kernel,
        [((zs, share + border, width), BF16), ((border, width), F32)],
        [place, came],
    )
    came = lax.all_to_all(parts, "z", 0, 0)
    factor = 1.0 / math.sqrt(count_e * strips * subs)
    parts, node_grad = call(
        functools.partial(line_sum_kernel, factor),
        [((slots, share, width), BF16), ((count_p, width), F32)],
        [place, came, mine, local_grad],
    )
    came = lax.all_to_all(parts, PLANE, 0, 0)
    grads = call(
        spread_kernel,
        [((rows, width), F32) for rows in (3 * width, width, 2 * width, width)],
        [place, came],
    )
    return (new_nodes, new_edges, node_grad, *grads)


def solution(mesh):
    strips, subs = mesh.devices.shape
    grid = Mesh(mesh.devices.reshape(strips, subs // 2, 2), ALL)
    rows = P(ALL, None)
    line = P(ALL)
    return jax.shard_map(
        shards,
        mesh=grid,
        in_specs=(rows, rows, line, line, line, P(), P(), P(), P(), rows, rows),
        out_specs=(rows, rows, rows, P(), P(), P(), P()),
        check_vma=False,
    )
```

```python
import functools
import math

import jax
import jax.numpy as jnp
from jax import lax
from jax.experimental import pallas as pl
from jax.experimental.pallas import tpu as pltpu
from jax.sharding import PartitionSpec as P

EPS = 1e-05
CHUNK = 512
ALL = ("strip", "sub")
F32 = jnp.float32
BF16 = jnp.bfloat16
VMEM = pl.BlockSpec(memory_space=pltpu.VMEM)
SMEM = pl.BlockSpec(memory_space=pltpu.SMEM)


def mm(left, right):
    return jnp.dot(left, right, preferred_element_type=F32)


def mm_nt(left, right):
    return lax.dot_general(left, right, (((1,), (1,)), ((), ())), preferred_element_type=F32)


def mm_tn(left, right):
    return lax.dot_general(left, right, (((0,), (0,)), ((), ())), preferred_element_type=F32)


def norm_rows(values):
    centre = values - jnp.mean(values, axis=1, keepdims=True)
    scale = lax.rsqrt(jnp.mean(centre * centre, axis=1, keepdims=True) + EPS)
    return (centre * scale, scale)


def norm_back(normed, scale, upstream):
    first = jnp.mean(upstream, axis=1, keepdims=True)
    second = jnp.mean(upstream * normed, axis=1, keepdims=True)
    return scale * (upstream - first - normed * second)


def silu_and_slope(values):
    sig = 0.5 + 0.5 * jnp.tanh(0.5 * values)
    act = values * sig
    return (act, sig + act * (1.0 - sig))


def call(kernel, outs, ins, scratch=()):
    return pl.pallas_call(
        kernel,
        out_shape=[jax.ShapeDtypeStruct(shape, dtype) for shape, dtype in outs],
        in_specs=[SMEM if value.ndim == 1 else VMEM for value in ins],
        out_specs=[VMEM] * len(outs),
        scratch_shapes=list(scratch),
        compiler_params=pltpu.CompilerParams(vmem_limit_bytes=28 * 2**20),
    )(*ins)


def rim_kernel(nodes, out):
    border = out.shape[1]
    for target in range(out.shape[0]):
        out[target] = nodes[:border]


def early_kernel(
    nodes,
    edges,
    info,
    w_edge_in,
    send_hot,
    recv_hot,
    send_hot_t,
    recv_hot_t,
    edges_t,
    pre_part,
    tables,
):
    count_p, width = nodes.shape
    chunks, _, chunk = info.shape
    send_rows = send_hot.shape[1]
    tables[:count_p] = mm(nodes[...], w_edge_in[width : 2 * width]).astype(BF16)
    tables[count_p:] = w_edge_in[2 * width :]
    lane = lax.broadcasted_iota(jnp.int32, (chunk, width), 1)

    def hot(column, blocks):
        found = [(column == lane + width * k).astype(F32).astype(BF16) for k in range(blocks)]
        return jnp.concatenate(found, axis=1)

    def hot_t(line, size):
        place_of = lax.broadcasted_iota(jnp.int32, (size, chunk), 0)
        return (place_of == line).astype(F32).astype(BF16)

    def one(step, carry):
        rows = pl.ds(pl.multiple_of(step * chunk, chunk), chunk)
        index = info[step]
        columns = index.T
        send_hot[rows] = hot(columns[:, 0:1], send_rows // width)
        recv = hot(columns[:, 1:2], count_p // width)
        recv_hot[rows] = recv
        send_hot_t[step] = hot_t(index[0:1], send_rows)
        recv_hot_t[step] = hot_t(index[1:2], count_p)
        edge = edges[rows]
        edges_t[step] = edge.T
        pre_part[rows] = mm(jnp.concatenate([recv, edge], axis=1), tables[...])
        return carry

    lax.fori_loop(0, chunks, one, 0)


def layer_kernel(
    place,
    nodes,
    rims,
    edges,
    send_hot,
    recv_hot,
    send_hot_t,
    recv_hot_t,
    edges_t,
    pre_part,
    w_edge_in,
    w_edge_out,
    w_node_in,
    w_node_out,
    node_cot,
    edge_cot,
    new_nodes,
    new_edges,
    base_grad,
    packed,
    sums_out,
    table,
    tables,
    spread,
    means,
    hidden,
    slope,
    normed,
    scale,
    sums,
    ge_edge,
    ge_out,
    agg,
):
    count_p, width = nodes.shape
    border = rims.shape[1]
    chunks, _, chunk = recv_hot_t.shape
    my_strip, my_sub, strips, subs, live_count = (place[i] for i in range(5))

    table[:count_p] = nodes[...]
    spot = 0
    for d_strip in (-1, 0, 1):
        strip = jnp.clip(my_strip + d_strip, 0, strips - 1)
        for d_sub in (-1, 0, 1):
            if d_strip == 0 and d_sub == 0:
                continue
            sub = jnp.clip(my_sub + d_sub, 0, subs - 1)
            rows = slice(count_p + spot * border, count_p + (spot + 1) * border)
            table[rows] = rims[strip * subs + sub]
            spot += 1
    send_rows = table.shape[0]
    tables[...] = mm(table[...], w_edge_in[:width]).astype(BF16)
    spread[:, :width] = w_edge_out[...]
    spread[:, width:] = jnp.broadcast_to(
        jnp.mean(w_edge_out[...].astype(F32), axis=1, keepdims=True), (width, width)
    ).astype(BF16)
    high = lax.broadcasted_iota(jnp.int32, (2 * width, 2 * width), 0) >= width
    wide = lax.broadcasted_iota(jnp.int32, (2 * width, 2 * width), 1) >= width
    means[...] = jnp.where(high == wide, 1.0 / width, 0.0).astype(BF16)

    row = lax.broadcasted_iota(jnp.int32, (chunk, width), 0)
    agg[...] = jnp.zeros_like(agg)

    def forward(step, carry):
        rows = pl.ds(pl.multiple_of(step * chunk, chunk), chunk)
        pre = pre_part[rows] + mm(send_hot[rows], tables[...])
        act, slope[rows] = silu_and_slope(pre)
        act = act.astype(BF16)
        hidden[rows] = act
        outer = mm(act, spread[...])
        centre = outer[:, :width] - outer[:, width:]
        spare = mm((centre * centre).astype(BF16), means[:width, :width])
        factor = jnp.where(row < live_count - step * chunk, lax.rsqrt(spare + EPS), 0.0)
        unit = centre * factor
        scale[rows] = factor
        normed[rows] = unit
        new_edges[rows] = (edges[rows].astype(F32) + unit).astype(BF16)
        agg[...] += mm(recv_hot_t[step], unit.astype(BF16))
        return carry

    lax.fori_loop(0, chunks, forward, 0, unroll=2)

    joined = jnp.concatenate([nodes[...], agg[...].astype(BF16)], axis=1)
    node_pre = mm(joined, w_node_in[...])
    node_act, node_slope = silu_and_slope(node_pre)
    node_act = node_act.astype(BF16)
    node_unit, node_scale = norm_rows(mm(node_act, w_node_out[...]))
    new_nodes[...] = (nodes[...].astype(F32) + node_unit).astype(BF16)
    cot = node_cot[...].astype(F32)
    d_outer = norm_back(node_unit, node_scale, cot).astype(BF16)
    d_pre = (mm_nt(d_outer, w_node_out[...]) * node_slope).astype(BF16)
    d_joined = mm_nt(d_pre, w_node_in[...])
    d_agg = d_joined[:, width:].astype(BF16)
    base_grad[...] = cot + d_joined[:, :width]
    packed[4 * width : 6 * width] = mm_tn(joined, d_pre).astype(BF16)
    packed[6 * width : 7 * width] = mm_tn(node_act, d_outer).astype(BF16)

    sums[...] = jnp.zeros_like(sums)
    ge_edge[...] = jnp.zeros_like(ge_edge)
    ge_out[...] = jnp.zeros_like(ge_out)

    def backward(step, carry):
        rows = pl.ds(pl.multiple_of(step * chunk, chunk), chunk)
        upstream = edge_cot[rows].astype(F32) + mm(recv_hot[rows], d_agg)
        unit = normed[rows]
        both = jnp.concatenate([upstream.astype(BF16), (upstream * unit).astype(BF16)], axis=1)
        both = mm(both, means[...])
        d_out = scale[rows] * (upstream - both[:, :width] - unit * both[:, width:])
        d_out = d_out.astype(BF16)
        ge_out[...] += mm_tn(hidden[rows], d_out)
        d_in = (mm_nt(d_out, w_edge_out[...]) * slope[rows]).astype(BF16)
        sums[:send_rows] += mm(send_hot_t[step], d_in)
        sums[send_rows:] += mm(recv_hot_t[step], d_in)
        ge_edge[...] += mm(edges_t[step], d_in)
        return carry

    lax.fori_loop(0, chunks, backward, 0, unroll=2)

    sums_out[...] = sums[...].astype(BF16)
    packed[:width] = mm_tn(table[...], sums_out[:send_rows]).astype(BF16)
    packed[width : 2 * width] = mm_tn(nodes[...], sums_out[send_rows:]).astype(BF16)
    packed[2 * width : 3 * width] = ge_edge[...].astype(BF16)
    packed[3 * width : 4 * width] = ge_out[...].astype(BF16)
    if packed.shape[0] > 7 * width:
        packed[7 * width :] = jnp.zeros((packed.shape[0] - 7 * width, width), BF16)


def owed_kernel(base_grad, sums, w_edge_in, local_grad, low, high, middle):
    count_p, width = base_grad.shape
    border = low.shape[1]
    send_rows = sums.shape[0] - count_p
    sent = mm_nt(sums[:send_rows], w_edge_in[:width])
    local_grad[...] = (
        base_grad[...]
        + sent[:count_p]
        + mm_nt(sums[send_rows:], w_edge_in[width : 2 * width])
    )
    block = [sent[count_p + i * border : count_p + (i + 1) * border] for i in range(8)]
    for strip, (under, over) in enumerate(((0, 2), (3, 4), (5, 7))):
        low[strip] = block[under].astype(BF16)
        high[strip] = block[over].astype(BF16)
    middle[0] = block[1]
    middle[1] = jnp.zeros_like(block[1])
    middle[2] = block[6]


def share_kernel(factor, came, out):
    total = came[0].astype(F32)
    for source in range(1, came.shape[0]):
        total = total + came[source].astype(F32)
    total = (total * factor).astype(BF16)
    for target in range(out.shape[0]):
        out[target] = total


def column_kernel(middle, low, high, down, stay, up):
    column = [middle[i] + low[i].astype(F32) + high[i].astype(F32) for i in range(3)]
    down[...] = column[0].astype(BF16)
    stay[...] = column[1]
    up[...] = column[2].astype(BF16)


def finish_kernel(came, local_grad, stay, down, up, node_grad, *outs):
    border = stay.shape[0]
    node_grad[...] = local_grad[...]
    node_grad[:border] += stay[...] + down[...].astype(F32) + up[...].astype(F32)
    start = 0
    for out in outs:
        size = out.shape[0]
        out[...] = came[start : start + size].astype(F32)
        start += size


def shifted(value, axis, steps):
    count = lax.axis_size(axis)
    first, last = (max(0, -steps), min(count, count - steps))
    return lax.ppermute(value, axis, [(source, source + steps) for source in range(first, last)])


def shards(
    node_latents,
    edge_latents,
    senders,
    receivers,
    edge_count,
    w_edge_in,
    w_edge_out,
    w_node_in,
    w_node_out,
    node_cotangent,
    edge_cotangent,
):
    count_p, width = node_latents.shape
    count_e = edge_latents.shape[0]
    border = count_p // 8
    strips, subs = (lax.axis_size(axis) for axis in ALL)
    devices = strips * subs
    my_strip, my_sub = (lax.axis_index(axis).astype(jnp.int32) for axis in ALL)
    place = jnp.stack(
        [my_strip, my_sub, jnp.int32(strips), jnp.int32(subs), edge_count[0]]
    )

    (rims,) = call(rim_kernel, [((devices, border, width), BF16)], [node_latents])
    rims = lax.all_to_all(rims, ALL, 0, 0)

    owner = senders // count_p
    within = senders % count_p
    is_local = owner == my_strip * subs + my_sub
    block = (owner // subs - my_strip + 1) * 3 + (owner % subs - my_sub + 1)
    block = jnp.where(block > 4, block - 1, block)
    send_index = jnp.where(
        is_local, within, count_p + block * border + jnp.minimum(within, border - 1)
    )
    chunk = min(CHUNK, count_e)
    chunks = count_e // chunk
    info = jnp.concatenate(
        [
            send_index.reshape(chunks, 1, chunk),
            receivers.reshape(chunks, 1, chunk),
            jnp.zeros((chunks, 6, chunk), jnp.int32),
        ],
        axis=1,
    )
    send_rows = 2 * count_p
    early = call(
        early_kernel,
        [
            ((count_e, send_rows), BF16),
            ((count_e, count_p), BF16),
            ((chunks, send_rows, chunk), BF16),
            ((chunks, count_p, chunk), BF16),
            ((chunks, width, chunk), BF16),
            ((count_e, width), F32),
        ],
        [node_latents, edge_latents, info, w_edge_in],
        [pltpu.VMEM((count_p + width, width), BF16)],
    )

    share = -(-7 * width // (devices * 16)) * 16
    new_nodes, new_edges, base_grad, packed, sums = call(
        layer_kernel,
        [
            ((count_p, width), BF16),
            ((count_e, width), BF16),
            ((count_p, width), F32),
            ((devices * share, width), BF16),
            ((send_rows + count_p, width), BF16),
        ],
        [
            place,
            node_latents,
            rims,
            edge_latents,
            *early,
            w_edge_in,
            w_edge_out,
            w_node_in,
            w_node_out,
            node_cotangent,
            edge_cotangent,
        ],
        [
            pltpu.VMEM((send_rows, width), BF16),
            pltpu.VMEM((send_rows, width), BF16),
            pltpu.VMEM((width, 2 * width), BF16),
            pltpu.VMEM((2 * width, 2 * width), BF16),
            pltpu.VMEM((count_e, width), BF16),
            pltpu.VMEM((count_e, width), F32),
            pltpu.VMEM((count_e, width), F32),
            pltpu.VMEM((count_e, width), F32),
            pltpu.VMEM((send_rows + count_p, width), F32),
            pltpu.VMEM((width, width), F32),
            pltpu.VMEM((width, width), F32),
            pltpu.VMEM((count_p, width), F32),
        ],
    )

    came = lax.all_to_all(packed.reshape(devices, share, width), ALL, 0, 0)
    local_grad, low, high, middle = call(
        owed_kernel,
        [
            ((count_p, width), F32),
            ((3, border, width), BF16),
            ((3, border, width), BF16),
            ((3, border, width), F32),
        ],
        [base_grad, sums, w_edge_in],
    )
    low = shifted(low, "sub", -1)
    high = shifted(high, "sub", 1)
    factor = 1.0 / math.sqrt(count_e * devices)
    (parts,) = call(
        functools.partial(share_kernel, factor), [((devices, share, width), BF16)], [came]
    )
    parts, low, high, middle = lax.optimization_barrier((parts, low, high, middle))
    came = lax.all_to_all(parts, ALL, 0, 0)
    down, stay, up = call(
        column_kernel,
        [((border, width), BF16), ((border, width), F32), ((border, width), BF16)],
        [middle, low, high],
    )
    down = shifted(down, "strip", -1)
    up = shifted(up, "strip", 1)
    node_grad, *grads = call(
        finish_kernel,
        [((rows, width), F32) for rows in (count_p, 3 * width, width, 2 * width, width)],
        [came.reshape(devices * share, width), local_grad, stay, down, up],
    )
    return (new_nodes, new_edges, node_grad, *grads)


def solution(mesh):
    rows = P(ALL, None)
    line = P(ALL)
    return jax.shard_map(
        shards,
        mesh=mesh,
        in_specs=(rows, rows, line, line, line, P(), P(), P(), P(), rows, rows),
        out_specs=(rows, rows, rows, P(), P(), P(), P()),
        check_vma=False,
    )
```

```python
import functools
import math

import jax
import jax.numpy as jnp
from jax import lax
from jax.experimental import pallas as pl
from jax.experimental.pallas import tpu as pltpu
from jax.sharding import Mesh
from jax.sharding import PartitionSpec as P

EPS = 1e-05
CHUNK = 1024
PLANE = ("strip", "y")
ALL = ("strip", "z", "y")
F32 = jnp.float32
BF16 = jnp.bfloat16
VMEM = pl.BlockSpec(memory_space=pltpu.VMEM)
SMEM = pl.BlockSpec(memory_space=pltpu.SMEM)
HBM = pl.BlockSpec(memory_space=pltpu.HBM)
SEM = pltpu.SemaphoreType.DMA


def mm(left, right):
    return jnp.dot(left, right, preferred_element_type=F32)


def mm_nt(left, right):
    return lax.dot_general(left, right, (((1,), (1,)), ((), ())), preferred_element_type=F32)


def mm_tn(left, right):
    return lax.dot_general(left, right, (((0,), (0,)), ((), ())), preferred_element_type=F32)


def norm_rows(values):
    centre = values - jnp.mean(values, axis=1, keepdims=True)
    scale = lax.rsqrt(jnp.mean(centre * centre, axis=1, keepdims=True) + EPS)
    return (centre * scale, scale)


def norm_back(normed, scale, upstream):
    first = jnp.mean(upstream, axis=1, keepdims=True)
    second = jnp.mean(upstream * normed, axis=1, keepdims=True)
    return scale * (upstream - first - normed * second)


def silu_and_slope(values):
    sig = 0.5 + 0.5 * jnp.tanh(0.5 * values)
    act = values * sig
    return (act, sig + act * (1.0 - sig))


def in_hbm(value):
    return pltpu.with_memory_space_constraint(value, pltpu.HBM)


def call(kernel, outs, ins, specs, scratch=(), out_specs=None, limit=24):
    out_specs = [VMEM] * len(outs) if out_specs is None else out_specs
    return pl.pallas_call(
        kernel,
        out_shape=[
            pltpu.HBM(shape, dtype) if spec is HBM else jax.ShapeDtypeStruct(shape, dtype)
            for (shape, dtype), spec in zip(outs, out_specs)
        ],
        in_specs=specs,
        out_specs=out_specs,
        scratch_shapes=list(scratch),
        compiler_params=pltpu.CompilerParams(vmem_limit_bytes=limit * 2**20),
    )(*[in_hbm(value) if spec is HBM else value for value, spec in zip(ins, specs)])


def rim_kernel(nodes, out, sems):
    border = out.shape[1]
    copies = [
        pltpu.make_async_copy(nodes.at[pl.ds(0, border)], out.at[target], sems.at[target])
        for target in range(out.shape[0])
    ]
    for copy in copies:
        copy.start()
    for copy in copies:
        copy.wait()


def early_kernel(
    nodes,
    edges,
    info,
    w_edge_in,
    send_hot,
    recv_hot,
    send_hot_t,
    recv_hot_t,
    edges_t,
    pre_part,
    tables,
):
    count_p, width = nodes.shape
    chunk = edges.shape[0]
    send_rows = send_hot.shape[1]

    @pl.when(pl.program_id(0) == 0)
    def prepare():
        tables[:count_p] = mm(nodes[...], w_edge_in[width : 2 * width]).astype(BF16)
        tables[count_p:] = w_edge_in[2 * width :]

    lane = lax.broadcasted_iota(jnp.int32, (chunk, width), 1)

    def hot(column, blocks):
        found = [(column == lane + width * k).astype(F32).astype(BF16) for k in range(blocks)]
        return jnp.concatenate(found, axis=1)

    def hot_t(line, size):
        place_of = lax.broadcasted_iota(jnp.int32, (size, chunk), 0)
        return (place_of == line).astype(F32).astype(BF16)

    index = info[0]
    columns = index.T
    edge = edges[...]
    recv = hot(columns[:, 1:2], count_p // width)
    pre_part[...] = mm(jnp.concatenate([recv, edge], axis=1), tables[...])
    recv_hot[...] = recv
    send_hot[...] = hot(columns[:, 0:1], send_rows // width)
    send_hot_t[0] = hot_t(index[0:1], send_rows)
    recv_hot_t[0] = hot_t(index[1:2], count_p)
    edges_t[0] = edge.T


def layer_kernel(
    place,
    nodes_in,
    rims_in,
    far_rims_in,
    edges_in,
    send_hot_in,
    recv_hot_in,
    send_hot_t_in,
    recv_hot_t_in,
    edges_t_in,
    pre_part_in,
    w_edge_in_in,
    w_edge_out_in,
    w_node_in_in,
    w_node_out_in,
    node_cot_in,
    edge_cot_in,
    new_nodes_out,
    new_edges_out,
    local_grad_out,
    parts,
    nodes,
    rims,
    edges,
    send_hot,
    recv_hot,
    send_hot_t,
    recv_hot_t,
    edges_t,
    pre_part,
    w_edge_in,
    w_edge_out,
    w_node_in,
    w_node_out,
    node_cot,
    edge_cot,
    new_nodes,
    new_edges,
    local_grad,
    table,
    tables,
    spread,
    means,
    hidden,
    slope,
    normed,
    scale,
    sums,
    ge_edge,
    ge_out,
    agg,
    packed,
    small_sems,
    sems,
    out_sems,
    last_sems,
):
    count_p, width = nodes.shape
    border = rims.shape[1]
    slots = parts.shape[0]
    strips = slots // 2
    chunks, _, chunk = recv_hot_t.shape
    share = parts.shape[1] - 2 * border
    my_strip, my_y, live_count = place[0], place[2], place[3]

    small = [
        pltpu.make_async_copy(source, target, small_sems.at[k])
        for k, (source, target) in enumerate(
            [
                (nodes_in, nodes),
                (rims_in, rims.at[pl.ds(0, slots)]),
                (far_rims_in, rims.at[pl.ds(slots, slots)]),
                (w_edge_in_in, w_edge_in),
                (w_edge_out_in, w_edge_out),
                (w_node_in_in, w_node_in),
                (w_node_out_in, w_node_out),
                (node_cot_in, node_cot),
            ]
        )
    ]

    def span(step):
        return pl.ds(pl.multiple_of(step * chunk, chunk), chunk)

    def fetch(step, which):
        rows = span(step)
        pairs = [
            (pre_part_in.at[rows], pre_part.at[rows]),
            (send_hot_in.at[rows], send_hot.at[rows]),
            (edges_in.at[rows], edges.at[rows]),
            (recv_hot_t_in.at[step], recv_hot_t.at[step]),
            (recv_hot_in.at[rows], recv_hot.at[rows]),
            (edge_cot_in.at[rows], edge_cot.at[rows]),
            (send_hot_t_in.at[step], send_hot_t.at[step]),
            (edges_t_in.at[step], edges_t.at[step]),
        ]
        return [
            pltpu.make_async_copy(*pairs[k], sems.at[k, step]) for k in which
        ]

    def emit(step):
        rows = span(step)
        return pltpu.make_async_copy(
            new_edges.at[rows], new_edges_out.at[rows], out_sems.at[step]
        )

    ahead, back = range(4), range(4, 8)
    for copy in small[:5] + fetch(0, ahead) + small[5:]:
        copy.start()
    for step in range(1, chunks):
        for copy in fetch(step, ahead):
            copy.start()
    for step in range(chunks):
        for copy in fetch(step, back):
            copy.start()
    for copy in small[:5]:
        copy.wait()

    table[:count_p] = nodes[...]
    spot = 0
    for d_strip in (-1, 0, 1):
        strip = jnp.clip(my_strip + d_strip, 0, strips - 1)
        for d_sub in (-1, 0, 1):
            if d_strip == 0 and d_sub == 0:
                continue
            if d_sub == 0:
                slot = 2 * strip + my_y
            elif d_sub == 1:
                slot = my_y * slots + 2 * strip + 1
            else:
                slot = (1 - my_y) * slots + 2 * strip
            rows = slice(count_p + spot * border, count_p + (spot + 1) * border)
            table[rows] = rims[slot]
            spot += 1
    send_rows = table.shape[0]
    tables[...] = mm(table[...], w_edge_in[:width]).astype(BF16)
    spread[:, :width] = w_edge_out[...]
    spread[:, width:] = jnp.broadcast_to(
        jnp.mean(w_edge_out[...].astype(F32), axis=1, keepdims=True), (width, width)
    ).astype(BF16)
    high = lax.broadcasted_iota(jnp.int32, (2 * width, 2 * width), 0) >= width
    wide = lax.broadcasted_iota(jnp.int32, (2 * width, 2 * width), 1) >= width
    means[...] = jnp.where(high == wide, 1.0 / width, 0.0).astype(BF16)

    row = lax.broadcasted_iota(jnp.int32, (chunk, width), 0)
    agg[...] = jnp.zeros_like(agg)

    def forward(step, carry):
        rows = span(step)
        for copy in fetch(step, ahead):
            copy.wait()
        begun = pre_part[rows]
        hot = send_hot[rows]
        hot_t = recv_hot_t[step]
        edge = edges[rows].astype(F32)
        so_far = agg[...]
        act, bend = silu_and_slope(begun + mm(hot, tables[...]))
        act = act.astype(BF16)
        outer = mm(act, spread[...])
        centre = outer[:, :width] - outer[:, width:]
        spare = mm((centre * centre).astype(BF16), means[:width, :width])
        factor = jnp.where(row < live_count - step * chunk, lax.rsqrt(spare + EPS), 0.0)
        unit = centre * factor
        so_far = so_far + mm(hot_t, unit.astype(BF16))
        slope[rows] = bend
        hidden[rows] = act
        scale[rows] = factor
        normed[rows] = unit
        new_edges[rows] = (edge + unit).astype(BF16)
        agg[...] = so_far
        emit(step).start()
        return carry

    lax.fori_loop(0, chunks, forward, 0)

    for copy in small[5:]:
        copy.wait()
    joined = jnp.concatenate([nodes[...], agg[...].astype(BF16)], axis=1)
    node_pre = mm(joined, w_node_in[...])
    node_act, node_slope = silu_and_slope(node_pre)
    node_act = node_act.astype(BF16)
    node_unit, node_scale = norm_rows(mm(node_act, w_node_out[...]))
    new_nodes[...] = (nodes[...].astype(F32) + node_unit).astype(BF16)
    cot = node_cot[...].astype(F32)
    d_outer = norm_back(node_unit, node_scale, cot).astype(BF16)
    d_pre = (mm_nt(d_outer, w_node_out[...]) * node_slope).astype(BF16)
    d_joined = mm_nt(d_pre, w_node_in[...])
    d_agg = d_joined[:, width:].astype(BF16)
    agg[...] = cot + d_joined[:, :width]
    packed[4 * width : 6 * width] = mm_tn(joined, d_pre).astype(BF16)
    packed[6 * width : 7 * width] = mm_tn(node_act, d_outer).astype(BF16)
    node_copy = pltpu.make_async_copy(new_nodes, new_nodes_out, last_sems.at[0])
    node_copy.start()

    sums[...] = jnp.zeros_like(sums)
    ge_edge[...] = jnp.zeros_like(ge_edge)
    ge_out[...] = jnp.zeros_like(ge_out)

    def backward(step, carry):
        rows = span(step)
        for copy in fetch(step, back):
            copy.wait()
        cot = edge_cot[rows].astype(F32)
        hot = recv_hot[rows]
        unit = normed[rows]
        factor = scale[rows]
        bend = slope[rows]
        act = hidden[rows]
        edge_t = edges_t[step]
        send_t = send_hot_t[step]
        recv_t = recv_hot_t[step]
        upstream = cot + mm(hot, d_agg)
        both = jnp.concatenate([upstream.astype(BF16), (upstream * unit).astype(BF16)], axis=1)
        both = mm(both, means[...])
        d_out = factor * (upstream - both[:, :width] - unit * both[:, width:])
        d_out = d_out.astype(BF16)
        d_in = (mm_nt(d_out, w_edge_out[...]) * bend).astype(BF16)
        ge_out[...] += mm_tn(act, d_out)
        sums[:send_rows] += mm(send_t, d_in)
        sums[send_rows:] += mm(recv_t, d_in)
        ge_edge[...] += mm(edge_t, d_in)
        return carry

    lax.fori_loop(0, chunks, backward, 0)

    send_sums = sums[:send_rows].astype(BF16)
    recv_sums = sums[send_rows:].astype(BF16)
    packed[:width] = mm_tn(table[...], send_sums).astype(BF16)
    packed[width : 2 * width] = mm_tn(nodes[...], recv_sums).astype(BF16)
    packed[2 * width : 3 * width] = ge_edge[...].astype(BF16)
    packed[3 * width : 4 * width] = ge_out[...].astype(BF16)
    if packed.shape[0] > 7 * width:
        packed[7 * width :] = jnp.zeros((packed.shape[0] - 7 * width, width), BF16)
    sent = mm_nt(send_sums, w_edge_in[:width])
    local_grad[...] = agg[...] + sent[:count_p] + mm_nt(recv_sums, w_edge_in[width : 2 * width])
    grad_copy = pltpu.make_async_copy(local_grad, local_grad_out, last_sems.at[1])
    grad_copy.start()
    owed = sent[count_p:].astype(BF16)
    for slot in range(slots):
        parts[slot, :share] = packed[slot * share : (slot + 1) * share]
        parts[slot, share:] = jnp.zeros((2 * border, width), BF16)
    spot = 0
    for d_strip in (-1, 0, 1):
        strip = my_strip + d_strip
        for d_sub in (-1, 0, 1):
            if d_strip == 0 and d_sub == 0:
                continue
            if d_sub == 0:
                slot, part = 2 * strip + my_y, 0
            elif d_sub == 1:
                slot, part = 2 * strip + 1 - my_y, my_y
            else:
                slot, part = 2 * strip + 1 - my_y, 1 - my_y
            first = pl.multiple_of(share + part * border, 16)
            block = owed[spot * border : (spot + 1) * border]

            @pl.when((strip >= 0) & (strip < strips))
            def put(slot=slot, first=first, block=block):
                parts[slot, pl.ds(first, border), :] = block

            spot += 1
    for step in range(chunks):
        emit(step).wait()
    node_copy.wait()
    grad_copy.wait()


def plane_sum_kernel(place, came, out, mine):
    border = mine.shape[0]
    zs = out.shape[0]
    share = out.shape[1] - border
    total = came[0].astype(F32)
    for slot in range(1, came.shape[0]):
        total = total + came[slot].astype(F32)
    share_total = total[:share].astype(BF16)
    mine[...] = total[share : share + border]
    beyond = total[share + border :].astype(BF16)
    for target in range(zs):
        out[target, :share] = share_total
        out[target, share:] = jnp.zeros_like(beyond)
    target = place[1] + 1 - 2 * place[2]

    @pl.when((target >= 0) & (target < zs))
    def put():
        out[target, share:] = beyond


def line_sum_kernel(factor, came, mine, out, rim_grad):
    share = out.shape[1]
    total = came[0].astype(F32)
    for slot in range(1, came.shape[0]):
        total = total + came[slot].astype(F32)
    share_total = (total[:share] * factor).astype(BF16)
    for target in range(out.shape[0]):
        out[target] = share_total
    rim_grad[...] = mine[...] + total[share:]


def finish_kernel(came, rim_grad, local_grad_in, *refs):
    outs, (local_grad, grads, in_sem, sems) = refs[:-4], refs[-4:]
    border = rim_grad.shape[0]
    slots, share, _ = came.shape
    fetch = pltpu.make_async_copy(local_grad_in, local_grad, in_sem)
    fetch.start()
    for slot in range(slots):
        grads[slot * share : (slot + 1) * share] = came[slot].astype(F32)
    copies = []
    start = 0
    for k, out in enumerate(outs[1:]):
        size = out.shape[0]
        copies.append(pltpu.make_async_copy(grads.at[pl.ds(start, size)], out, sems.at[k]))
        copies[-1].start()
        start += size
    fetch.wait()
    local_grad[:border] += rim_grad[...]
    copies.append(pltpu.make_async_copy(local_grad, outs[0], sems.at[len(outs) - 1]))
    copies[-1].start()
    for copy in copies:
        copy.wait()


def shards(
    node_latents,
    edge_latents,
    senders,
    receivers,
    edge_count,
    w_edge_in,
    w_edge_out,
    w_node_in,
    w_node_out,
    node_cotangent,
    edge_cotangent,
):
    count_p, width = node_latents.shape
    count_e = edge_latents.shape[0]
    border = count_p // 8
    strips, zs, ys = (lax.axis_size(axis) for axis in ALL)
    subs = zs * ys
    slots = strips * ys
    my_strip, my_z, my_y = (lax.axis_index(axis).astype(jnp.int32) for axis in ALL)
    my_sub = my_z * ys + my_y
    place = jnp.stack([my_strip, my_z, my_y, edge_count[0]])

    (rims,) = call(
        rim_kernel,
        [((slots, border, width), BF16)],
        [node_latents],
        [HBM],
        [SEM((slots,))],
        [HBM],
    )
    far_groups = [
        [s * subs + (2 * k + step) % subs for s in range(strips) for step in (1, 2)]
        for k in range(zs)
    ]
    near_rims = lax.all_to_all(rims, PLANE, 0, 0)
    far_rims = lax.all_to_all(rims, ALL, 0, 0, axis_index_groups=far_groups)

    owner = senders // count_p
    within = senders % count_p
    is_local = owner == my_strip * subs + my_sub
    block = (owner // subs - my_strip + 1) * 3 + (owner % subs - my_sub + 1)
    block = jnp.where(block > 4, block - 1, block)
    send_index = jnp.where(
        is_local, within, count_p + block * border + jnp.minimum(within, border - 1)
    )
    chunk = min(CHUNK, count_e)
    chunks = count_e // chunk
    info = jnp.concatenate(
        [
            send_index.reshape(chunks, 1, chunk),
            receivers.reshape(chunks, 1, chunk),
            jnp.zeros((chunks, 6, chunk), jnp.int32),
        ],
        axis=1,
    )
    send_rows = 2 * count_p

    def by_rows(*shape):
        return pl.BlockSpec(shape, lambda i: (i, 0))

    def by_chunk(*shape):
        return pl.BlockSpec((1, *shape), lambda i: (i, 0, 0))

    def whole(*shape):
        return pl.BlockSpec(shape, lambda i: (0, 0))

    early = pl.pallas_call(
        early_kernel,
        grid=(chunks,),
        out_shape=[
            pltpu.HBM(shape, dtype)
            for shape, dtype in [
                ((count_e, send_rows), BF16),
                ((count_e, count_p), BF16),
                ((chunks, send_rows, chunk), BF16),
                ((chunks, count_p, chunk), BF16),
                ((chunks, width, chunk), BF16),
                ((count_e, width), F32),
            ]
        ],
        in_specs=[
            whole(count_p, width),
            by_rows(chunk, width),
            by_chunk(8, chunk),
            whole(3 * width, width),
        ],
        out_specs=[
            by_rows(chunk, send_rows),
            by_rows(chunk, count_p),
            by_chunk(send_rows, chunk),
            by_chunk(count_p, chunk),
            by_chunk(width, chunk),
            by_rows(chunk, width),
        ],
        scratch_shapes=[pltpu.VMEM((count_p + width, width), BF16)],
        compiler_params=pltpu.CompilerParams(vmem_limit_bytes=32 * 2**20),
    )(in_hbm(node_latents), in_hbm(edge_latents), info, in_hbm(w_edge_in))

    share = -(-7 * width // (slots * 16)) * 16

    def like(value):
        return pltpu.VMEM(value.shape, value.dtype)

    new_nodes, new_edges, local_grad, parts = call(
        layer_kernel,
        [
            ((count_p, width), BF16),
            ((count_e, width), BF16),
            ((count_p, width), F32),
            ((slots, share + 2 * border, width), BF16),
        ],
        [
            place,
            node_latents,
            near_rims,
            far_rims,
            edge_latents,
            *early,
            w_edge_in,
            w_edge_out,
            w_node_in,
            w_node_out,
            node_cotangent,
            edge_cotangent,
        ],
        [SMEM] + [HBM] * 16,
        [
            like(node_latents),
            pltpu.VMEM((2 * slots, border, width), BF16),
            like(edge_latents),
            *[like(value) for value in early],
            like(w_edge_in),
            like(w_edge_out),
            like(w_node_in),
            like(w_node_out),
            like(node_cotangent),
            like(edge_cotangent),
            pltpu.VMEM((count_p, width), BF16),
            pltpu.VMEM((count_e, width), BF16),
            pltpu.VMEM((count_p, width), F32),
            pltpu.VMEM((send_rows, width), BF16),
            pltpu.VMEM((send_rows, width), BF16),
            pltpu.VMEM((width, 2 * width), BF16),
            pltpu.VMEM((2 * width, 2 * width), BF16),
            pltpu.VMEM((count_e, width), BF16),
            pltpu.VMEM((count_e, width), F32),
            pltpu.VMEM((count_e, width), F32),
            pltpu.VMEM((count_e, width), F32),
            pltpu.VMEM((send_rows + count_p, width), F32),
            pltpu.VMEM((width, width), F32),
            pltpu.VMEM((width, width), F32),
            pltpu.VMEM((count_p, width), F32),
            pltpu.VMEM((slots * share, width), BF16),
            SEM((8,)),
            SEM((8, chunks)),
            SEM((chunks,)),
            SEM((2,)),
        ],
        [HBM, HBM, HBM, VMEM],
        limit=48,
    )

    came = lax.all_to_all(parts, PLANE, 0, 0)
    parts, mine = call(
        plane_sum_kernel,
        [((zs, share + border, width), BF16), ((border, width), F32)],
        [place, came],
        [SMEM, VMEM],
    )
    came = lax.all_to_all(parts, "z", 0, 0)
    factor = 1.0 / math.sqrt(count_e * strips * subs)
    parts, rim_grad = call(
        functools.partial(line_sum_kernel, factor),
        [((slots, share, width), BF16), ((border, width), F32)],
        [came, mine],
        [VMEM, VMEM],
    )
    came = lax.all_to_all(parts, PLANE, 0, 0)
    node_grad, *grads = call(
        finish_kernel,
        [((rows, width), F32) for rows in (count_p, 3 * width, width, 2 * width, width)],
        [came, rim_grad, local_grad],
        [VMEM, VMEM, HBM],
        [
            pltpu.VMEM((count_p, width), F32),
            pltpu.VMEM((slots * share, width), F32),
            SEM,
            SEM((5,)),
        ],
        [HBM] * 5,
    )
    return (new_nodes, new_edges, node_grad, *grads)


def solution(mesh):
    strips, subs = mesh.devices.shape
    grid = Mesh(mesh.devices.reshape(strips, subs // 2, 2), ALL)
    rows = P(ALL, None)
    line = P(ALL)
    return jax.shard_map(
        shards,
        mesh=grid,
        in_specs=(rows, rows, line, line, line, P(), P(), P(), P(), rows, rows),
        out_specs=(rows, rows, rows, P(), P(), P(), P()),
        check_vma=False,
    )
```

```python
import functools
import math

import jax
import jax.numpy as jnp
from jax import lax
from jax.experimental import pallas as pl
from jax.experimental.pallas import tpu as pltpu
from jax.sharding import Mesh
from jax.sharding import PartitionSpec as P

EPS = 1e-05
CHUNK = 1024
PLANE = ("strip", "y")
ALL = ("strip", "z", "y")
F32 = jnp.float32
BF16 = jnp.bfloat16
VMEM = pl.BlockSpec(memory_space=pltpu.VMEM)
SMEM = pl.BlockSpec(memory_space=pltpu.SMEM)
HBM = pl.BlockSpec(memory_space=pltpu.HBM)
SEM = pltpu.SemaphoreType.DMA


def mm(left, right):
    return jnp.dot(left, right, preferred_element_type=F32)


def mm_nt(left, right):
    return lax.dot_general(left, right, (((1,), (1,)), ((), ())), preferred_element_type=F32)


def mm_tn(left, right):
    return lax.dot_general(left, right, (((0,), (0,)), ((), ())), preferred_element_type=F32)


def norm_rows(values):
    centre = values - jnp.mean(values, axis=1, keepdims=True)
    scale = lax.rsqrt(jnp.mean(centre * centre, axis=1, keepdims=True) + EPS)
    return (centre * scale, scale)


def norm_back(normed, scale, upstream):
    first = jnp.mean(upstream, axis=1, keepdims=True)
    second = jnp.mean(upstream * normed, axis=1, keepdims=True)
    return scale * (upstream - first - normed * second)


def silu_and_slope(values):
    sig = 0.5 + 0.5 * jnp.tanh(0.5 * values)
    act = values * sig
    return (act, sig + act * (1.0 - sig))


def in_hbm(value):
    return pltpu.with_memory_space_constraint(value, pltpu.HBM)


def call(kernel, outs, ins, specs, scratch=(), out_specs=None, limit=24):
    out_specs = [VMEM] * len(outs) if out_specs is None else out_specs
    return pl.pallas_call(
        kernel,
        out_shape=[
            pltpu.HBM(shape, dtype) if spec is HBM else jax.ShapeDtypeStruct(shape, dtype)
            for (shape, dtype), spec in zip(outs, out_specs)
        ],
        in_specs=specs,
        out_specs=out_specs,
        scratch_shapes=list(scratch),
        compiler_params=pltpu.CompilerParams(vmem_limit_bytes=limit * 2**20),
    )(*[in_hbm(value) if spec is HBM else value for value, spec in zip(ins, specs)])


def rim_kernel(nodes, out, rim, many, in_sem, out_sem):
    border = out.shape[1]
    copy = pltpu.make_async_copy(nodes.at[pl.ds(0, border)], rim, in_sem)
    copy.start()
    copy.wait()
    for target in range(out.shape[0]):
        many[target] = rim[...]
    copy = pltpu.make_async_copy(many, out, out_sem)
    copy.start()
    copy.wait()


def early_kernel(
    nodes,
    edges,
    edge_cot,
    info,
    w_edge_in,
    hot,
    hot_t,
    far,
    pre_part,
    cot_part,
    tables,
):
    count_p, width = nodes.shape
    chunk = edges.shape[0]

    @pl.when(pl.program_id(0) == 0)
    def prepare():
        tables[:count_p] = mm(nodes[...], w_edge_in[width : 2 * width]).astype(BF16)
        tables[count_p:] = w_edge_in[2 * width :]

    lane = lax.broadcasted_iota(jnp.int32, (chunk, width), 1)
    line = lax.broadcasted_iota(jnp.int32, (count_p, chunk), 0)

    def found(column):
        blocks = [
            (column == lane + width * k).astype(F32).astype(BF16)
            for k in range(count_p // width)
        ]
        return jnp.concatenate(blocks, axis=1)

    index = info[0]
    columns = index.T
    edge = edges[...]
    cot = edge_cot[...].astype(F32)
    recv = found(columns[:, 1:2])
    pre_part[...] = mm(jnp.concatenate([recv, edge], axis=1), tables[...])
    hot[:, :count_p] = found(columns[:, 0:1])
    hot[:, count_p:] = recv
    hot_t[0, :count_p] = (line == index[1:2]).astype(F32).astype(BF16)
    hot_t[0, count_p : 2 * count_p] = (line == index[0:1]).astype(F32).astype(BF16)
    hot_t[0, 2 * count_p :] = edge.T
    far[...] = jnp.broadcast_to(columns[:, 2:3], edge.shape).astype(F32).astype(BF16)
    cot_part[...] = (cot - jnp.mean(cot, axis=1, keepdims=True)).astype(BF16)


def layer_kernel(
    place,
    nodes_in,
    rims_in,
    edges_in,
    hot_in,
    hot_t_in,
    far_in,
    pre_part_in,
    cot_part_in,
    w_edge_in_in,
    w_edge_out_in,
    w_node_in_in,
    w_node_out_in,
    node_cot_in,
    new_nodes_out,
    new_edges_out,
    local_grad_out,
    parts,
    nodes,
    rims,
    edges,
    hot,
    hot_t,
    far,
    pre_part,
    cot_part,
    w_edge_in,
    w_edge_out,
    w_node_in,
    w_node_out,
    node_cot,
    new_nodes,
    new_edges,
    local_grad,
    near_rows,
    far_rows,
    tables,
    centring,
    back,
    means,
    hidden,
    slope,
    normed,
    scale,
    sums,
    ge_out,
    agg,
    packed,
    small_sems,
    sems,
    out_sems,
    last_sems,
):
    count_p, width = nodes.shape
    border = rims.shape[1]
    slots = parts.shape[0]
    strips = slots // 2
    chunks, _, chunk = hot_t.shape
    half = chunk // 2
    share = parts.shape[1] - 2 * border
    my_strip, my_y, live_count, my_sub, subs = (place[k] for k in (0, 2, 3, 4, 5))

    small = [
        pltpu.make_async_copy(source, target, small_sems.at[k])
        for k, (source, target) in enumerate(
            [
                (nodes_in, nodes),
                (rims_in, rims),
                (w_edge_in_in, w_edge_in),
                (w_edge_out_in, w_edge_out),
                (w_node_in_in, w_node_in),
                (w_node_out_in, w_node_out),
                (node_cot_in, node_cot),
            ]
        )
    ]

    def span(step):
        return pl.ds(pl.multiple_of(step * chunk, chunk), chunk)

    def pairs_of(step):
        return pl.ds(pl.multiple_of(step * half, half), half)

    def fetch(step, which):
        rows = span(step)
        first, second = pl.ds(0, count_p), pl.ds(count_p, count_p)
        rest = pl.ds(count_p, count_p + width)
        pairs = [
            (hot_in.at[rows, first], hot.at[rows, first]),
            (far_in.at[rows], far.at[rows]),
            (pre_part_in.at[rows], pre_part.at[rows]),
            (edges_in.at[rows], edges.at[rows]),
            (hot_t_in.at[step, first], hot_t.at[step, first]),
            (hot_in.at[rows, second], hot.at[rows, second]),
            (cot_part_in.at[rows], cot_part.at[rows]),
            (hot_t_in.at[step, rest], hot_t.at[step, rest]),
        ]
        return [pltpu.make_async_copy(*pairs[k], sems.at[k, step]) for k in which]

    def emit(step):
        rows = span(step)
        return pltpu.make_async_copy(
            new_edges.at[rows], new_edges_out.at[rows], out_sems.at[step]
        )

    def paired(value):
        return jnp.concatenate([value[:half], value[half:]], axis=1)

    def unpaired(value):
        return jnp.concatenate([value[:, :width], value[:, width:]], axis=0)

    def twice(block):
        zero = jnp.zeros_like(block)
        return jnp.concatenate(
            [
                jnp.concatenate([block, zero], axis=1),
                jnp.concatenate([zero, block], axis=1),
            ],
            axis=0,
        )

    ahead, behind = range(5), range(5, 8)
    for copy in small[:4] + fetch(0, ahead) + small[4:]:
        copy.start()
    for step in range(1, chunks):
        for copy in fetch(step, ahead):
            copy.start()
    for step in range(chunks):
        for copy in fetch(step, behind):
            copy.start()
    for copy in small[:4]:
        copy.wait()

    near_rows[...] = nodes[...]
    spot = 0
    for d_strip in (-1, 0, 1):
        strip = jnp.clip(my_strip + d_strip, 0, strips - 1)
        for d_sub in (-1, 0, 1):
            if d_strip == 0 and d_sub == 0:
                continue
            sub = jnp.clip(my_sub + d_sub, 0, subs - 1)
            far_rows[spot * border : (spot + 1) * border] = rims[strip * subs + sub]
            spot += 1
    tables[:, :width] = mm(near_rows[...], w_edge_in[:width]).astype(BF16)
    tables[:, width:] = mm(far_rows[...], w_edge_in[:width]).astype(BF16)
    weight = w_edge_out[...].astype(F32)
    centring[...] = twice(weight - jnp.mean(weight, axis=1, keepdims=True)).astype(BF16)
    back[...] = twice(weight).astype(BF16)
    means[...] = twice(jnp.full((width, width), 1.0 / width, F32)).astype(BF16)

    row = lax.broadcasted_iota(jnp.int32, (half, 2 * width), 0)
    lane = lax.broadcasted_iota(jnp.int32, (half, 2 * width), 1)
    edge_row = jnp.where(lane < width, row, row + half)
    agg[...] = jnp.zeros_like(agg)

    def forward(step, carry):
        rows = span(step)
        for copy in fetch(step, ahead):
            copy.wait()
        begun = pre_part[rows]
        beyond = far[rows] > 0
        picked = mm(hot[rows, :count_p], tables[...])
        edge = paired(edges[rows].astype(F32))
        recv_t = hot_t[step, :count_p]
        so_far = agg[...]
        pre = begun + jnp.where(beyond, picked[:, width:], picked[:, :width])
        act, bend = silu_and_slope(paired(pre))
        act = act.astype(BF16)
        centre = mm(act, centring[...])
        spare = mm((centre * centre).astype(BF16), means[...])
        factor = jnp.where(edge_row < live_count - step * chunk, lax.rsqrt(spare + EPS), 0.0)
        unit = centre * factor
        so_far = so_far + mm(recv_t, unpaired(unit.astype(BF16)))
        slope[pairs_of(step)] = bend
        hidden[rows] = unpaired(act)
        scale[pairs_of(step)] = factor
        normed[pairs_of(step)] = unit
        new_edges[rows] = unpaired((edge + unit).astype(BF16))
        agg[...] = so_far
        emit(step).start()
        return carry

    lax.fori_loop(0, chunks, forward, 0)

    for copy in small[4:]:
        copy.wait()
    joined = jnp.concatenate([nodes[...], agg[...].astype(BF16)], axis=1)
    node_pre = mm(joined, w_node_in[...])
    node_act, node_slope = silu_and_slope(node_pre)
    node_act = node_act.astype(BF16)
    node_unit, node_scale = norm_rows(mm(node_act, w_node_out[...]))
    new_nodes[...] = (nodes[...].astype(F32) + node_unit).astype(BF16)
    cot = node_cot[...].astype(F32)
    d_outer = norm_back(node_unit, node_scale, cot).astype(BF16)
    d_pre = (mm_nt(d_outer, w_node_out[...]) * node_slope).astype(BF16)
    d_joined = mm_nt(d_pre, w_node_in[...])
    d_agg = d_joined[:, width:]
    d_agg = (d_agg - jnp.mean(d_agg, axis=1, keepdims=True)).astype(BF16)
    agg[...] = cot + d_joined[:, :width]
    packed[4 * width : 6 * width] = mm_tn(joined, d_pre).astype(BF16)
    packed[6 * width : 7 * width] = mm_tn(node_act, d_outer).astype(BF16)
    node_copy = pltpu.make_async_copy(new_nodes, new_nodes_out, last_sems.at[0])
    node_copy.start()

    sums[...] = jnp.zeros_like(sums)
    ge_out[...] = jnp.zeros_like(ge_out)

    def backward(step, carry):
        rows = span(step)
        for copy in fetch(step, behind):
            copy.wait()
        cot = cot_part[rows].astype(F32)
        recv = hot[rows, count_p:]
        unit = normed[pairs_of(step)]
        factor = scale[pairs_of(step)]
        bend = slope[pairs_of(step)]
        act = hidden[rows]
        beyond = far[rows] > 0
        turned = hot_t[step]
        upstream = paired(cot + mm(recv, d_agg))
        along = mm((upstream * unit).astype(BF16), means[...])
        d_out = (factor * (upstream - unit * along)).astype(BF16)
        d_in = unpaired(mm_nt(d_out, back[...]) * bend)
        zero = jnp.zeros_like(d_in)
        near_far = jnp.concatenate(
            [
                jnp.where(beyond, zero, d_in).astype(BF16),
                jnp.where(beyond, d_in, zero).astype(BF16),
            ],
            axis=1,
        )
        ge_out[...] += mm_tn(act, unpaired(d_out))
        sums[...] += mm(turned, near_far)
        return carry

    lax.fori_loop(0, chunks, backward, 0)

    recv_sums = (sums[:count_p, :width] + sums[:count_p, width:]).astype(BF16)
    near_sums = sums[count_p : 2 * count_p, :width].astype(BF16)
    far_sums = sums[count_p : 2 * count_p, width:].astype(BF16)
    edge_sums = sums[2 * count_p :, :width] + sums[2 * count_p :, width:]
    packed[:width] = (mm_tn(near_rows[...], near_sums) + mm_tn(far_rows[...], far_sums)).astype(BF16)
    packed[width : 2 * width] = mm_tn(nodes[...], recv_sums).astype(BF16)
    packed[2 * width : 3 * width] = edge_sums.astype(BF16)
    packed[3 * width : 4 * width] = ge_out[...].astype(BF16)
    if packed.shape[0] > 7 * width:
        packed[7 * width :] = jnp.zeros((packed.shape[0] - 7 * width, width), BF16)
    local_grad[...] = (
        agg[...]
        + mm_nt(near_sums, w_edge_in[:width])
        + mm_nt(recv_sums, w_edge_in[width : 2 * width])
    )
    grad_copy = pltpu.make_async_copy(local_grad, local_grad_out, last_sems.at[1])
    grad_copy.start()
    owed = mm_nt(far_sums, w_edge_in[:width]).astype(BF16)
    for slot in range(slots):
        parts[slot, :share] = packed[slot * share : (slot + 1) * share]
        parts[slot, share:] = jnp.zeros((2 * border, width), BF16)
    spot = 0
    for d_strip in (-1, 0, 1):
        strip = my_strip + d_strip
        for d_sub in (-1, 0, 1):
            if d_strip == 0 and d_sub == 0:
                continue
            if d_sub == 0:
                slot, part = 2 * strip + my_y, 0
            elif d_sub == 1:
                slot, part = 2 * strip + 1 - my_y, my_y
            else:
                slot, part = 2 * strip + 1 - my_y, 1 - my_y
            first = pl.multiple_of(share + part * border, 16)
            block = owed[spot * border : (spot + 1) * border]

            @pl.when((strip >= 0) & (strip < strips))
            def put(slot=slot, first=first, block=block):
                parts[slot, pl.ds(first, border), :] = block

            spot += 1
    for step in range(chunks):
        emit(step).wait()
    node_copy.wait()
    grad_copy.wait()


def plane_sum_kernel(place, came, out, mine):
    border = mine.shape[0]
    zs = out.shape[0]
    share = out.shape[1] - border
    total = came[0].astype(F32)
    for slot in range(1, came.shape[0]):
        total = total + came[slot].astype(F32)
    share_total = total[:share].astype(BF16)
    mine[...] = total[share : share + border]
    beyond = total[share + border :].astype(BF16)
    for target in range(zs):
        out[target, :share] = share_total
        out[target, share:] = jnp.zeros_like(beyond)
    target = place[1] + 1 - 2 * place[2]

    @pl.when((target >= 0) & (target < zs))
    def put():
        out[target, share:] = beyond


def line_sum_kernel(factor, came, mine, out, rim_grad):
    share = out.shape[1]
    total = came[0].astype(F32)
    for slot in range(1, came.shape[0]):
        total = total + came[slot].astype(F32)
    share_total = (total[:share] * factor).astype(BF16)
    for target in range(out.shape[0]):
        out[target] = share_total
    rim_grad[...] = mine[...] + total[share:]


def finish_kernel(came, rim_grad, local_grad_in, *refs):
    outs, (local_grad, grads, in_sem, sems) = refs[:-4], refs[-4:]
    border = rim_grad.shape[0]
    slots, share, _ = came.shape
    fetch = pltpu.make_async_copy(local_grad_in, local_grad, in_sem)
    fetch.start()
    for slot in range(slots):
        grads[slot * share : (slot + 1) * share] = came[slot].astype(F32)
    copies = []
    start = 0
    for k, out in enumerate(outs[1:]):
        size = out.shape[0]
        copies.append(pltpu.make_async_copy(grads.at[pl.ds(start, size)], out, sems.at[k]))
        copies[-1].start()
        start += size
    fetch.wait()
    local_grad[:border] += rim_grad[...]
    copies.append(pltpu.make_async_copy(local_grad, outs[0], sems.at[len(outs) - 1]))
    copies[-1].start()
    for copy in copies:
        copy.wait()


def shards(
    node_latents,
    edge_latents,
    senders,
    receivers,
    edge_count,
    w_edge_in,
    w_edge_out,
    w_node_in,
    w_node_out,
    node_cotangent,
    edge_cotangent,
):
    count_p, width = node_latents.shape
    count_e = edge_latents.shape[0]
    border = count_p // 8
    strips, zs, ys = (lax.axis_size(axis) for axis in ALL)
    subs = zs * ys
    slots = strips * ys
    my_strip, my_z, my_y = (lax.axis_index(axis).astype(jnp.int32) for axis in ALL)
    my_sub = my_z * ys + my_y
    devices = strips * subs
    place = jnp.stack([my_strip, my_z, my_y, edge_count[0], my_sub, jnp.int32(subs)])

    (rims,) = call(
        rim_kernel,
        [((devices, border, width), BF16)],
        [node_latents],
        [HBM],
        [
            pltpu.VMEM((border, width), BF16),
            pltpu.VMEM((devices, border, width), BF16),
            SEM,
            SEM,
        ],
        [HBM],
    )
    rims = lax.all_to_all(rims, ALL, 0, 0)

    owner = senders // count_p
    within = senders % count_p
    is_local = owner == my_strip * subs + my_sub
    block = (owner // subs - my_strip + 1) * 3 + (owner % subs - my_sub + 1)
    block = jnp.where(block > 4, block - 1, block)
    send_index = jnp.where(is_local, within, block * border + jnp.minimum(within, border - 1))
    chunk = min(CHUNK, count_e)
    chunks = count_e // chunk
    info = jnp.stack(
        [
            value.reshape(chunks, chunk)
            for value in [send_index, receivers, 1 - is_local.astype(jnp.int32)]
            + [jnp.zeros_like(receivers)] * 5
        ],
        axis=1,
    )

    def by_rows(*shape):
        return pl.BlockSpec(shape, lambda i: (i, 0))

    def by_chunk(*shape):
        return pl.BlockSpec((1, *shape), lambda i: (i, 0, 0))

    def whole(*shape):
        return pl.BlockSpec(shape, lambda i: (0, 0))

    early = pl.pallas_call(
        early_kernel,
        grid=(chunks,),
        out_shape=[
            pltpu.HBM(shape, dtype)
            for shape, dtype in [
                ((count_e, 2 * count_p), BF16),
                ((chunks, 2 * count_p + width, chunk), BF16),
                ((count_e, width), BF16),
                ((count_e, width), F32),
                ((count_e, width), BF16),
            ]
        ],
        in_specs=[
            whole(count_p, width),
            by_rows(chunk, width),
            by_rows(chunk, width),
            by_chunk(8, chunk),
            whole(3 * width, width),
        ],
        out_specs=[
            by_rows(chunk, 2 * count_p),
            by_chunk(2 * count_p + width, chunk),
            by_rows(chunk, width),
            by_rows(chunk, width),
            by_rows(chunk, width),
        ],
        scratch_shapes=[pltpu.VMEM((count_p + width, width), BF16)],
        compiler_params=pltpu.CompilerParams(vmem_limit_bytes=32 * 2**20),
    )(
        in_hbm(node_latents),
        in_hbm(edge_latents),
        in_hbm(edge_cotangent),
        info,
        in_hbm(w_edge_in),
    )

    share = -(-7 * width // (slots * 16)) * 16

    def like(value):
        return pltpu.VMEM(value.shape, value.dtype)

    new_nodes, new_edges, local_grad, parts = call(
        layer_kernel,
        [
            ((count_p, width), BF16),
            ((count_e, width), BF16),
            ((count_p, width), F32),
            ((slots, share + 2 * border, width), BF16),
        ],
        [
            place,
            node_latents,
            rims,
            edge_latents,
            *early,
            w_edge_in,
            w_edge_out,
            w_node_in,
            w_node_out,
            node_cotangent,
        ],
        [SMEM] + [HBM] * 13,
        [
            like(node_latents),
            like(rims),
            like(edge_latents),
            *[like(value) for value in early],
            like(w_edge_in),
            like(w_edge_out),
            like(w_node_in),
            like(w_node_out),
            like(node_cotangent),
            pltpu.VMEM((count_p, width), BF16),
            pltpu.VMEM((count_e, width), BF16),
            pltpu.VMEM((count_p, width), F32),
            pltpu.VMEM((count_p, width), BF16),
            pltpu.VMEM((8 * border, width), BF16),
            pltpu.VMEM((count_p, 2 * width), BF16),
            pltpu.VMEM((2 * width, 2 * width), BF16),
            pltpu.VMEM((2 * width, 2 * width), BF16),
            pltpu.VMEM((2 * width, 2 * width), BF16),
            pltpu.VMEM((count_e, width), BF16),
            pltpu.VMEM((count_e // 2, 2 * width), F32),
            pltpu.VMEM((count_e // 2, 2 * width), F32),
            pltpu.VMEM((count_e // 2, 2 * width), F32),
            pltpu.VMEM((2 * count_p + width, 2 * width), F32),
            pltpu.VMEM((width, width), F32),
            pltpu.VMEM((count_p, width), F32),
            pltpu.VMEM((slots * share, width), BF16),
            SEM((7,)),
            SEM((8, chunks)),
            SEM((chunks,)),
            SEM((2,)),
        ],
        [HBM, HBM, HBM, VMEM],
        limit=48,
    )

    came = lax.all_to_all(parts, PLANE, 0, 0)
    parts, mine = call(
        plane_sum_kernel,
        [((zs, share + border, width), BF16), ((border, width), F32)],
        [place, came],
        [SMEM, VMEM],
    )
    came = lax.all_to_all(parts, "z", 0, 0)
    factor = 1.0 / math.sqrt(count_e * strips * subs)
    parts, rim_grad = call(
        functools.partial(line_sum_kernel, factor),
        [((slots, share, width), BF16), ((border, width), F32)],
        [came, mine],
        [VMEM, VMEM],
    )
    came = lax.all_to_all(parts, PLANE, 0, 0)
    node_grad, *grads = call(
        finish_kernel,
        [((rows, width), F32) for rows in (count_p, 3 * width, width, 2 * width, width)],
        [came, rim_grad, local_grad],
        [VMEM, VMEM, HBM],
        [
            pltpu.VMEM((count_p, width), F32),
            pltpu.VMEM((slots * share, width), F32),
            SEM,
            SEM((5,)),
        ],
        [HBM] * 5,
    )
    return (new_nodes, new_edges, node_grad, *grads)


def solution(mesh):
    strips, subs = mesh.devices.shape
    grid = Mesh(mesh.devices.reshape(strips, subs // 2, 2), ALL)
    rows = P(ALL, None)
    line = P(ALL)
    return jax.shard_map(
        shards,
        mesh=grid,
        in_specs=(rows, rows, line, line, line, P(), P(), P(), P(), rows, rows),
        out_specs=(rows, rows, rows, P(), P(), P(), P()),
        check_vma=False,
    )
```

```python
import functools
import math

import jax
import jax.numpy as jnp
from jax import lax
from jax.experimental import pallas as pl
from jax.experimental.pallas import tpu as pltpu
from jax.sharding import Mesh
from jax.sharding import PartitionSpec as P

EPS = 1e-05
CHUNK = 512
PLANE = ("strip", "y")
ALL = ("strip", "z", "y")
F32 = jnp.float32
BF16 = jnp.bfloat16
VMEM = pl.BlockSpec(memory_space=pltpu.VMEM)
SMEM = pl.BlockSpec(memory_space=pltpu.SMEM)
HBM = pl.BlockSpec(memory_space=pltpu.HBM)
SEM = pltpu.SemaphoreType.DMA


def mm(left, right):
    return jnp.dot(left, right, preferred_element_type=F32)


def mm_nt(left, right):
    return lax.dot_general(left, right, (((1,), (1,)), ((), ())), preferred_element_type=F32)


def mm_tn(left, right):
    return lax.dot_general(left, right, (((0,), (0,)), ((), ())), preferred_element_type=F32)


def norm_rows(values):
    centre = values - jnp.mean(values, axis=1, keepdims=True)
    scale = lax.rsqrt(jnp.mean(centre * centre, axis=1, keepdims=True) + EPS)
    return (centre * scale, scale)


def norm_back(normed, scale, upstream):
    first = jnp.mean(upstream, axis=1, keepdims=True)
    second = jnp.mean(upstream * normed, axis=1, keepdims=True)
    return scale * (upstream - first - normed * second)


def silu_and_slope(values):
    sig = 0.5 + 0.5 * jnp.tanh(0.5 * values)
    act = values * sig
    return (act, sig + act * (1.0 - sig))


def in_hbm(value):
    return pltpu.with_memory_space_constraint(value, pltpu.HBM)


def call(kernel, outs, ins, specs, scratch=(), out_specs=None, limit=24):
    out_specs = [VMEM] * len(outs) if out_specs is None else out_specs
    return pl.pallas_call(
        kernel,
        out_shape=[
            pltpu.HBM(shape, dtype) if spec is HBM else jax.ShapeDtypeStruct(shape, dtype)
            for (shape, dtype), spec in zip(outs, out_specs)
        ],
        in_specs=specs,
        out_specs=out_specs,
        scratch_shapes=list(scratch),
        compiler_params=pltpu.CompilerParams(vmem_limit_bytes=limit * 2**20),
    )(*[in_hbm(value) if spec is HBM else value for value, spec in zip(ins, specs)])


def rim_kernel(nodes, out, rim, many, in_sem, out_sem):
    border = out.shape[1]
    copy = pltpu.make_async_copy(nodes.at[pl.ds(0, border)], rim, in_sem)
    copy.start()
    copy.wait()
    for target in range(out.shape[0]):
        many[target] = rim[...]
    copy = pltpu.make_async_copy(many, out, out_sem)
    copy.start()
    copy.wait()


def early_kernel(
    nodes,
    edges,
    edge_cot,
    info,
    w_edge_in,
    hot,
    hot_t,
    far,
    pre_part,
    cot_part,
    tables,
):
    count_p, width = nodes.shape
    chunk = edges.shape[0]

    @pl.when(pl.program_id(0) == 0)
    def prepare():
        tables[:count_p] = mm(nodes[...], w_edge_in[width : 2 * width]).astype(BF16)
        tables[count_p:] = w_edge_in[2 * width :]

    lane = lax.broadcasted_iota(jnp.int32, (chunk, width), 1)
    line = lax.broadcasted_iota(jnp.int32, (count_p, chunk), 0)

    def found(column):
        blocks = [
            (column == lane + width * k).astype(F32).astype(BF16)
            for k in range(count_p // width)
        ]
        return jnp.concatenate(blocks, axis=1)

    index = info[0]
    columns = index.T
    edge = edges[...]
    cot = edge_cot[...].astype(F32)
    recv = found(columns[:, 1:2])
    pre_part[...] = mm(jnp.concatenate([recv, edge], axis=1), tables[...])
    hot[:, :count_p] = found(columns[:, 0:1])
    hot[:, count_p:] = recv
    hot_t[0, :count_p] = (line == index[1:2]).astype(F32).astype(BF16)
    hot_t[0, count_p : 2 * count_p] = (line == index[0:1]).astype(F32).astype(BF16)
    hot_t[0, 2 * count_p :] = edge.T
    far[...] = jnp.broadcast_to(columns[:, 2:3], edge.shape).astype(F32).astype(BF16)
    cot_part[...] = (cot - jnp.mean(cot, axis=1, keepdims=True)).astype(BF16)


def layer_kernel(
    edge_count,
    nodes_in,
    rims_in,
    edges_in,
    hot_in,
    hot_t_in,
    far_in,
    pre_part_in,
    cot_part_in,
    w_edge_in_in,
    w_edge_out_in,
    w_node_in_in,
    w_node_out_in,
    node_cot_in,
    new_nodes_out,
    new_edges_out,
    local_grad,
    parts,
    nodes,
    rims,
    edges,
    hot,
    hot_t,
    far,
    pre_part,
    cot_part,
    w_edge_in,
    w_edge_out,
    w_node_in,
    w_node_out,
    node_cot,
    new_nodes,
    new_edges,
    near_rows,
    far_rows,
    tables,
    centring,
    back,
    means,
    hidden,
    slope,
    normed,
    scale,
    sums,
    ge_out,
    agg,
    packed,
    act_now,
    centre_now,
    unit_now,
    out_now,
    in_now,
    last_now,
    small_sems,
    sems,
    out_sems,
    last_sem,
):
    count_p, width = nodes.shape
    border = rims.shape[1]
    slots = parts.shape[0]
    strips = slots // 2
    chunks, _, chunk = hot_t.shape
    half = chunk // 2
    share = parts.shape[1] - 2 * border
    my_strip, my_y = lax.axis_index("strip"), lax.axis_index("y")
    subs = lax.axis_size("z") * lax.axis_size("y")
    my_sub = lax.axis_index("z") * lax.axis_size("y") + my_y
    live_count = edge_count[0]

    small = [
        pltpu.make_async_copy(source, target, small_sems.at[k])
        for k, (source, target) in enumerate(
            [
                (nodes_in, nodes),
                (rims_in, rims),
                (w_edge_in_in, w_edge_in),
                (w_edge_out_in, w_edge_out),
                (w_node_in_in, w_node_in),
                (w_node_out_in, w_node_out),
                (node_cot_in, node_cot),
            ]
        )
    ]

    def span(step):
        return pl.ds(pl.multiple_of(step * chunk, chunk), chunk)

    def pairs_of(step):
        return pl.ds(pl.multiple_of(step * half, half), half)

    def fetch(step, which):
        rows = span(step)
        first, second = pl.ds(0, count_p), pl.ds(count_p, count_p)
        rest = pl.ds(count_p, count_p + width)
        pairs = [
            (hot_in.at[rows, first], hot.at[rows, first]),
            (far_in.at[rows], far.at[rows]),
            (pre_part_in.at[rows], pre_part.at[rows]),
            (edges_in.at[rows], edges.at[rows]),
            (hot_t_in.at[step, first], hot_t.at[step, first]),
            (hot_in.at[rows, second], hot.at[rows, second]),
            (cot_part_in.at[rows], cot_part.at[rows]),
            (hot_t_in.at[step, rest], hot_t.at[step, rest]),
        ]
        return [pltpu.make_async_copy(*pairs[k], sems.at[k, step]) for k in which]

    def emit(step):
        rows = span(step)
        return pltpu.make_async_copy(
            new_edges.at[rows], new_edges_out.at[rows], out_sems.at[step]
        )

    def paired(value):
        return jnp.concatenate([value[:half], value[half:]], axis=1)

    def unpaired(value):
        return jnp.concatenate([value[:, :width], value[:, width:]], axis=0)

    def twice(block):
        zero = jnp.zeros_like(block)
        return jnp.concatenate(
            [
                jnp.concatenate([block, zero], axis=1),
                jnp.concatenate([zero, block], axis=1),
            ],
            axis=0,
        )

    ahead, behind = range(5), range(5, 8)
    for copy in small[:4] + fetch(0, ahead) + small[4:]:
        copy.start()
    for step in range(1, chunks):
        for copy in fetch(step, ahead):
            copy.start()
    for step in range(chunks):
        for copy in fetch(step, behind):
            copy.start()
    for copy in small[:4]:
        copy.wait()

    near_rows[...] = nodes[...]
    spot = 0
    for d_strip in (-1, 0, 1):
        strip = jnp.clip(my_strip + d_strip, 0, strips - 1)
        for d_sub in (-1, 0, 1):
            if d_strip == 0 and d_sub == 0:
                continue
            sub = jnp.clip(my_sub + d_sub, 0, subs - 1)
            far_rows[spot * border : (spot + 1) * border] = rims[strip * subs + sub]
            spot += 1
    tables[:, :width] = mm(near_rows[...], w_edge_in[:width]).astype(BF16)
    tables[:, width:] = mm(far_rows[...], w_edge_in[:width]).astype(BF16)
    weight = w_edge_out[...].astype(F32)
    centring[...] = twice(weight - jnp.mean(weight, axis=1, keepdims=True)).astype(BF16)
    back[...] = twice(weight).astype(BF16)
    means[...] = twice(jnp.full((width, width), 1.0 / width, F32)).astype(BF16)

    row = lax.broadcasted_iota(jnp.int32, (half, 2 * width), 0)
    lane = lax.broadcasted_iota(jnp.int32, (half, 2 * width), 1)
    edge_row = jnp.where(lane < width, row, row + half)
    agg[...] = jnp.zeros_like(agg)
    for buffer in (act_now, centre_now, unit_now):
        buffer[...] = jnp.zeros_like(buffer)

    def clamped(step):
        return jnp.clip(step, 0, chunks - 1)

    def forward(step, carry):
        @pl.when(step < chunks)
        def arrive():
            for copy in fetch(step, ahead):
                copy.wait()

        agg[...] += mm(hot_t[clamped(step - 3), :count_p], unit_now[...])

        place = clamped(step - 2)
        centre = centre_now[...]
        spare = mm((centre * centre).astype(BF16), means[...])
        factor = jnp.where(edge_row < live_count - place * chunk, lax.rsqrt(spare + EPS), 0.0)
        unit = centre * factor
        scale[pairs_of(place)] = factor
        normed[pairs_of(place)] = unit
        unit_now[...] = unpaired(unit.astype(BF16))
        new_edges[span(place)] = unpaired((paired(edges[span(place)].astype(F32)) + unit).astype(BF16))

        centre_now[...] = mm(act_now[...], centring[...])

        place = clamped(step)
        rows = span(place)
        beyond = far[rows] > 0
        picked = mm(hot[rows, :count_p], tables[...])
        pre = pre_part[rows] + jnp.where(beyond, picked[:, width:], picked[:, :width])
        act, bend = silu_and_slope(paired(pre))
        act = act.astype(BF16)
        slope[pairs_of(place)] = bend
        act_now[...] = act
        hidden[rows] = unpaired(act)

        @pl.when(step >= 3)
        def leave():
            emit(step - 3).start()

        return carry

    lax.fori_loop(0, chunks + 3, forward, 0)

    for copy in small[4:]:
        copy.wait()
    joined = jnp.concatenate([nodes[...], agg[...].astype(BF16)], axis=1)
    node_pre = mm(joined, w_node_in[...])
    node_act, node_slope = silu_and_slope(node_pre)
    node_act = node_act.astype(BF16)
    node_unit, node_scale = norm_rows(mm(node_act, w_node_out[...]))
    new_nodes[...] = (nodes[...].astype(F32) + node_unit).astype(BF16)
    cot = node_cot[...].astype(F32)
    d_outer = norm_back(node_unit, node_scale, cot).astype(BF16)
    d_pre = (mm_nt(d_outer, w_node_out[...]) * node_slope).astype(BF16)
    d_joined = mm_nt(d_pre, w_node_in[...])
    d_agg = d_joined[:, width:]
    d_agg = (d_agg - jnp.mean(d_agg, axis=1, keepdims=True)).astype(BF16)
    agg[...] = cot + d_joined[:, :width]
    packed[4 * width : 6 * width] = mm_tn(joined, d_pre).astype(BF16)
    packed[6 * width : 7 * width] = mm_tn(node_act, d_outer).astype(BF16)
    node_copy = pltpu.make_async_copy(new_nodes, new_nodes_out, last_sem)
    node_copy.start()

    sums[...] = jnp.zeros_like(sums)
    ge_out[...] = jnp.zeros_like(ge_out)
    for buffer in (act_now, centre_now, out_now, in_now, last_now):
        buffer[...] = jnp.zeros_like(buffer)

    def backward(step, carry):
        @pl.when(step < chunks)
        def arrive():
            for copy in fetch(step, behind):
                copy.wait()

        place = clamped(step - 3)
        sums[...] += mm(hot_t[place], in_now[...])
        ge_out[...] += mm_tn(hidden[span(place)], last_now[...])

        place = clamped(step - 2)
        rows = span(place)
        d_out = out_now[...]
        d_in = unpaired(mm_nt(d_out, back[...]) * slope[pairs_of(place)])
        beyond = far[rows] > 0
        zero = jnp.zeros_like(d_in)
        in_now[:, :width] = jnp.where(beyond, zero, d_in).astype(BF16)
        in_now[:, width:] = jnp.where(beyond, d_in, zero).astype(BF16)
        last_now[...] = unpaired(d_out)

        place = clamped(step - 1)
        along = mm(act_now[...], means[...])
        d_out = centre_now[...] - normed[pairs_of(place)] * along
        out_now[...] = (scale[pairs_of(place)] * d_out).astype(BF16)

        place = clamped(step)
        rows = span(place)
        upstream = paired(cot_part[rows].astype(F32) + mm(hot[rows, count_p:], d_agg))
        centre_now[...] = upstream
        act_now[...] = (upstream * normed[pairs_of(place)]).astype(BF16)
        return carry

    lax.fori_loop(0, chunks + 3, backward, 0)

    recv_sums = (sums[:count_p, :width] + sums[:count_p, width:]).astype(BF16)
    near_sums = sums[count_p : 2 * count_p, :width].astype(BF16)
    far_sums = sums[count_p : 2 * count_p, width:].astype(BF16)
    edge_sums = sums[2 * count_p :, :width] + sums[2 * count_p :, width:]
    packed[:width] = (mm_tn(near_rows[...], near_sums) + mm_tn(far_rows[...], far_sums)).astype(BF16)
    packed[width : 2 * width] = mm_tn(nodes[...], recv_sums).astype(BF16)
    packed[2 * width : 3 * width] = edge_sums.astype(BF16)
    packed[3 * width : 4 * width] = ge_out[...].astype(BF16)
    if packed.shape[0] > 7 * width:
        packed[7 * width :] = jnp.zeros((packed.shape[0] - 7 * width, width), BF16)
    local_grad[...] = (
        agg[...]
        + mm_nt(near_sums, w_edge_in[:width])
        + mm_nt(recv_sums, w_edge_in[width : 2 * width])
    )
    owed = mm_nt(far_sums, w_edge_in[:width]).astype(BF16)
    for slot in range(slots):
        parts[slot, :share] = packed[slot * share : (slot + 1) * share]
        parts[slot, share:] = jnp.zeros((2 * border, width), BF16)
    spot = 0
    for d_strip in (-1, 0, 1):
        strip = my_strip + d_strip
        for d_sub in (-1, 0, 1):
            if d_strip == 0 and d_sub == 0:
                continue
            if d_sub == 0:
                slot, part = 2 * strip + my_y, 0
            elif d_sub == 1:
                slot, part = 2 * strip + 1 - my_y, my_y
            else:
                slot, part = 2 * strip + 1 - my_y, 1 - my_y
            first = pl.multiple_of(share + part * border, 16)
            block = owed[spot * border : (spot + 1) * border]

            @pl.when((strip >= 0) & (strip < strips))
            def put(slot=slot, first=first, block=block):
                parts[slot, pl.ds(first, border), :] = block

            spot += 1
    for step in range(chunks):
        emit(step).wait()
    node_copy.wait()


def plane_sum_kernel(came, out, mine):
    border = mine.shape[0]
    zs = out.shape[0]
    share = out.shape[1] - border
    total = came[0].astype(F32)
    for slot in range(1, came.shape[0]):
        total = total + came[slot].astype(F32)
    share_total = total[:share].astype(BF16)
    mine[...] = total[share : share + border]
    beyond = total[share + border :].astype(BF16)
    for target in range(zs):
        out[target, :share] = share_total
        out[target, share:] = jnp.zeros_like(beyond)
    target = lax.axis_index("z") + 1 - 2 * lax.axis_index("y")

    @pl.when((target >= 0) & (target < zs))
    def put():
        out[target, share:] = beyond


def line_sum_kernel(factor, came, mine, out, rim_grad):
    share = out.shape[1]
    total = came[0].astype(F32)
    for slot in range(1, came.shape[0]):
        total = total + came[slot].astype(F32)
    share_total = (total[:share] * factor).astype(BF16)
    for target in range(out.shape[0]):
        out[target] = share_total
    rim_grad[...] = mine[...] + total[share:]


def finish_kernel(came, rim_grad, local_grad, node_grad, *outs):
    border = rim_grad.shape[0]
    share = came.shape[1]
    node_grad[...] = local_grad[...]
    node_grad[:border] += rim_grad[...]
    start = 0
    for out in outs:
        size = out.shape[0]
        done = 0
        while done < size:
            slot, offset = divmod(start + done, share)
            step = min(size - done, share - offset)
            out[done : done + step] = came[slot, offset : offset + step].astype(F32)
            done += step
        start += size


def shards(
    node_latents,
    edge_latents,
    senders,
    receivers,
    edge_count,
    w_edge_in,
    w_edge_out,
    w_node_in,
    w_node_out,
    node_cotangent,
    edge_cotangent,
):
    count_p, width = node_latents.shape
    count_e = edge_latents.shape[0]
    border = count_p // 8
    strips, zs, ys = (lax.axis_size(axis) for axis in ALL)
    subs = zs * ys
    slots = strips * ys
    my_strip, my_z, my_y = (lax.axis_index(axis).astype(jnp.int32) for axis in ALL)
    my_sub = my_z * ys + my_y
    devices = strips * subs

    (rims,) = call(
        rim_kernel,
        [((devices, border, width), BF16)],
        [node_latents],
        [HBM],
        [
            pltpu.VMEM((border, width), BF16),
            pltpu.VMEM((devices, border, width), BF16),
            SEM,
            SEM,
        ],
        [HBM],
    )
    rims = lax.all_to_all(rims, ALL, 0, 0)

    owner = senders // count_p
    within = senders % count_p
    is_local = owner == my_strip * subs + my_sub
    block = (owner // subs - my_strip + 1) * 3 + (owner % subs - my_sub + 1)
    block = jnp.where(block > 4, block - 1, block)
    send_index = jnp.where(is_local, within, block * border + jnp.minimum(within, border - 1))
    chunk = min(CHUNK, count_e)
    chunks = count_e // chunk
    info = jnp.stack(
        [
            value.reshape(chunks, chunk)
            for value in [send_index, receivers, 1 - is_local.astype(jnp.int32)]
            + [jnp.zeros_like(receivers)] * 5
        ],
        axis=1,
    )

    def by_rows(*shape):
        return pl.BlockSpec(shape, lambda i: (i, 0))

    def by_chunk(*shape):
        return pl.BlockSpec((1, *shape), lambda i: (i, 0, 0))

    def whole(*shape):
        return pl.BlockSpec(shape, lambda i: (0, 0))

    early = pl.pallas_call(
        early_kernel,
        grid=(chunks,),
        out_shape=[
            pltpu.HBM(shape, dtype)
            for shape, dtype in [
                ((count_e, 2 * count_p), BF16),
                ((chunks, 2 * count_p + width, chunk), BF16),
                ((count_e, width), BF16),
                ((count_e, width), F32),
                ((count_e, width), BF16),
            ]
        ],
        in_specs=[
            whole(count_p, width),
            by_rows(chunk, width),
            by_rows(chunk, width),
            by_chunk(8, chunk),
            whole(3 * width, width),
        ],
        out_specs=[
            by_rows(chunk, 2 * count_p),
            by_chunk(2 * count_p + width, chunk),
            by_rows(chunk, width),
            by_rows(chunk, width),
            by_rows(chunk, width),
        ],
        scratch_shapes=[pltpu.VMEM((count_p + width, width), BF16)],
        compiler_params=pltpu.CompilerParams(vmem_limit_bytes=32 * 2**20),
    )(
        in_hbm(node_latents),
        in_hbm(edge_latents),
        in_hbm(edge_cotangent),
        info,
        in_hbm(w_edge_in),
    )

    share = -(-7 * width // (slots * 16)) * 16

    def like(value):
        return pltpu.VMEM(value.shape, value.dtype)

    new_nodes, new_edges, local_grad, parts = call(
        layer_kernel,
        [
            ((count_p, width), BF16),
            ((count_e, width), BF16),
            ((count_p, width), F32),
            ((slots, share + 2 * border, width), BF16),
        ],
        [
            edge_count,
            node_latents,
            rims,
            edge_latents,
            *early,
            w_edge_in,
            w_edge_out,
            w_node_in,
            w_node_out,
            node_cotangent,
        ],
        [SMEM] + [HBM] * 13,
        [
            like(node_latents),
            like(rims),
            like(edge_latents),
            *[like(value) for value in early],
            like(w_edge_in),
            like(w_edge_out),
            like(w_node_in),
            like(w_node_out),
            like(node_cotangent),
            pltpu.VMEM((count_p, width), BF16),
            pltpu.VMEM((count_e, width), BF16),
            pltpu.VMEM((count_p, width), BF16),
            pltpu.VMEM((8 * border, width), BF16),
            pltpu.VMEM((count_p, 2 * width), BF16),
            pltpu.VMEM((2 * width, 2 * width), BF16),
            pltpu.VMEM((2 * width, 2 * width), BF16),
            pltpu.VMEM((2 * width, 2 * width), BF16),
            pltpu.VMEM((count_e, width), BF16),
            pltpu.VMEM((count_e // 2, 2 * width), F32),
            pltpu.VMEM((count_e // 2, 2 * width), F32),
            pltpu.VMEM((count_e // 2, 2 * width), F32),
            pltpu.VMEM((2 * count_p + width, 2 * width), F32),
            pltpu.VMEM((width, width), F32),
            pltpu.VMEM((count_p, width), F32),
            pltpu.VMEM((slots * share, width), BF16),
            pltpu.VMEM((chunk // 2, 2 * width), BF16),
            pltpu.VMEM((chunk // 2, 2 * width), F32),
            pltpu.VMEM((chunk, width), BF16),
            pltpu.VMEM((chunk // 2, 2 * width), BF16),
            pltpu.VMEM((chunk, 2 * width), BF16),
            pltpu.VMEM((chunk, width), BF16),
            SEM((7,)),
            SEM((8, chunks)),
            SEM((chunks,)),
            SEM,
        ],
        [HBM, HBM, VMEM, VMEM],
        limit=48,
    )

    came = lax.all_to_all(parts, PLANE, 0, 0)
    parts, mine = call(
        plane_sum_kernel,
        [((zs, share + border, width), BF16), ((border, width), F32)],
        [came],
        [VMEM],
    )
    came = lax.all_to_all(parts, "z", 0, 0)
    factor = 1.0 / math.sqrt(count_e * strips * subs)
    parts, rim_grad = call(
        functools.partial(line_sum_kernel, factor),
        [((slots, share, width), BF16), ((border, width), F32)],
        [came, mine],
        [VMEM, VMEM],
    )
    came = lax.all_to_all(parts, PLANE, 0, 0)
    node_grad, *grads = call(
        finish_kernel,
        [((rows, width), F32) for rows in (count_p, 3 * width, width, 2 * width, width)],
        [came, rim_grad, local_grad],
        [VMEM, VMEM, VMEM],
    )
    return (new_nodes, new_edges, node_grad, *grads)


def solution(mesh):
    strips, subs = mesh.devices.shape
    grid = Mesh(mesh.devices.reshape(strips, subs // 2, 2), ALL)
    rows = P(ALL, None)
    line = P(ALL)
    return jax.shard_map(
        shards,
        mesh=grid,
        in_specs=(rows, rows, line, line, line, P(), P(), P(), P(), rows, rows),
        out_specs=(rows, rows, rows, P(), P(), P(), P()),
        check_vma=False,
    )
```

```python
import functools
import math

import jax
import jax.numpy as jnp
from jax import lax
from jax.experimental import pallas as pl
from jax.experimental.pallas import tpu as pltpu
from jax.sharding import Mesh
from jax.sharding import PartitionSpec as P

EPS = 1e-05
CHUNK = 1024
SPLIT = 2
PLANE = ("strip", "y")
ALL = ("strip", "z", "y")
F32 = jnp.float32
BF16 = jnp.bfloat16
VMEM = pl.BlockSpec(memory_space=pltpu.VMEM)
SMEM = pl.BlockSpec(memory_space=pltpu.SMEM)
HBM = pl.BlockSpec(memory_space=pltpu.HBM)
SEM = pltpu.SemaphoreType.DMA


def mm(left, right):
    return jnp.dot(left, right, preferred_element_type=F32)


def mm_nt(left, right):
    return lax.dot_general(left, right, (((1,), (1,)), ((), ())), preferred_element_type=F32)


def mm_tn(left, right):
    return lax.dot_general(left, right, (((0,), (0,)), ((), ())), preferred_element_type=F32)


def norm_rows(values):
    centre = values - jnp.mean(values, axis=1, keepdims=True)
    scale = lax.rsqrt(jnp.mean(centre * centre, axis=1, keepdims=True) + EPS)
    return (centre * scale, scale)


def norm_back(normed, scale, upstream):
    first = jnp.mean(upstream, axis=1, keepdims=True)
    second = jnp.mean(upstream * normed, axis=1, keepdims=True)
    return scale * (upstream - first - normed * second)


def silu_and_slope(values):
    sig = 0.5 + 0.5 * jnp.tanh(0.5 * values)
    act = values * sig
    return (act, sig + act * (1.0 - sig))


def found(codes, blocks):
    lane = lax.broadcasted_iota(jnp.int32, codes.shape, 1)
    one, zero = jnp.ones((), BF16), jnp.zeros((), BF16)
    width = codes.shape[1]
    return jnp.concatenate(
        [
            jnp.where(codes == (lane + width * k).astype(F32).astype(BF16), one, zero)
            for k in range(blocks)
        ],
        axis=1,
    )


def found_t(line, size):
    place = lax.broadcasted_iota(jnp.int32, (size, line.shape[1]), 0).astype(F32).astype(BF16)
    one, zero = jnp.ones((), BF16), jnp.zeros((), BF16)
    return jnp.where(place == line.astype(F32).astype(BF16), one, zero)


def in_hbm(value):
    return pltpu.with_memory_space_constraint(value, pltpu.HBM)


def call(kernel, outs, ins, specs, scratch=(), out_specs=None, limit=24):
    out_specs = [VMEM] * len(outs) if out_specs is None else out_specs
    return pl.pallas_call(
        kernel,
        out_shape=[
            pltpu.HBM(shape, dtype) if spec is HBM else jax.ShapeDtypeStruct(shape, dtype)
            for (shape, dtype), spec in zip(outs, out_specs)
        ],
        in_specs=specs,
        out_specs=out_specs,
        scratch_shapes=list(scratch),
        compiler_params=pltpu.CompilerParams(vmem_limit_bytes=limit * 2**20),
    )(*[in_hbm(value) if spec is HBM else value for value, spec in zip(ins, specs)])


def rim_kernel(nodes, out, rim, many, in_sem, out_sem):
    border = out.shape[1]
    copy = pltpu.make_async_copy(nodes.at[pl.ds(0, border)], rim, in_sem)
    copy.start()
    copy.wait()
    for target in range(out.shape[0]):
        many[target] = rim[...]
    copy = pltpu.make_async_copy(many, out, out_sem)
    copy.start()
    copy.wait()


def early_kernel(
    nodes,
    edges,
    edge_cot,
    info,
    w_edge_in,
    send_codes,
    recv_codes,
    edges_t,
    pre_part,
    cot_part,
    tables,
):
    count_p, width = nodes.shape

    @pl.when(pl.program_id(0) == 0)
    def prepare():
        tables[:count_p] = mm(nodes[...], w_edge_in[width : 2 * width]).astype(BF16)
        tables[count_p:] = w_edge_in[2 * width :]

    columns = info[0].T
    edge = edges[...]
    cot = edge_cot[...].astype(F32)
    recv = jnp.broadcast_to(columns[:, 1:2], edge.shape).astype(F32).astype(BF16)
    recv_codes[...] = recv
    send_codes[...] = jnp.broadcast_to(columns[:, 2:3], edge.shape).astype(F32).astype(BF16)
    recv = found(recv, count_p // width)
    pre_part[...] = mm(jnp.concatenate([recv, edge], axis=1), tables[...])
    edges_t[0] = edge.T
    cot_part[...] = (cot - jnp.mean(cot, axis=1, keepdims=True)).astype(BF16)


def layer_kernel(
    edge_count,
    nodes_in,
    rims_in,
    edges_in,
    info_in,
    send_codes_in,
    recv_codes_in,
    edges_t_in,
    pre_part_in,
    cot_part_in,
    w_edge_in_in,
    w_edge_out_in,
    w_node_in_in,
    w_node_out_in,
    node_cot_in,
    new_nodes_out,
    new_edges_out,
    local_grad,
    parts,
    nodes,
    rims,
    edges,
    info,
    send_codes,
    recv_codes,
    edges_t,
    pre_part,
    cot_part,
    w_edge_in,
    w_edge_out,
    w_node_in,
    w_node_out,
    node_cot,
    new_nodes,
    new_edges,
    near_rows,
    far_rows,
    tables,
    centring,
    back,
    means,
    hidden,
    slope,
    normed,
    scale,
    sums,
    ge_out,
    agg,
    packed,
    small_sems,
    sems,
    out_sems,
    last_sem,
):
    count_p, width = nodes.shape
    border = rims.shape[1]
    slots = parts.shape[0]
    strips = slots // 2
    chunks, _, chunk = edges_t.shape
    block = chunk // SPLIT
    half = block // 2
    share = parts.shape[1] - 2 * border
    my_strip, my_y = lax.axis_index("strip"), lax.axis_index("y")
    subs = lax.axis_size("z") * lax.axis_size("y")
    my_sub = lax.axis_index("z") * lax.axis_size("y") + my_y
    live_count = edge_count[0]

    small = [
        pltpu.make_async_copy(source, target, small_sems.at[k])
        for k, (source, target) in enumerate(
            [
                (nodes_in, nodes),
                (rims_in, rims),
                (w_edge_in_in, w_edge_in),
                (w_edge_out_in, w_edge_out),
                (w_node_in_in, w_node_in),
                (w_node_out_in, w_node_out),
                (node_cot_in, node_cot),
            ]
        )
    ]

    def span(step):
        return pl.ds(pl.multiple_of(step * chunk, chunk), chunk)

    def block_rows(step, part):
        return pl.ds(pl.multiple_of(step * chunk + part * block, block), block)

    def block_pairs(step, part):
        return pl.ds(pl.multiple_of((step * SPLIT + part) * half, half), half)

    def fetch(step, which):
        rows = span(step)
        pairs = [
            (send_codes_in.at[rows], send_codes.at[rows]),
            (pre_part_in.at[rows], pre_part.at[rows]),
            (info_in.at[step], info.at[step]),
            (edges_in.at[rows], edges.at[rows]),
            (recv_codes_in.at[rows], recv_codes.at[rows]),
            (cot_part_in.at[rows], cot_part.at[rows]),
            (edges_t_in.at[step], edges_t.at[step]),
        ]
        return [pltpu.make_async_copy(*pairs[k], sems.at[k, step]) for k in which]

    def emit(step):
        rows = span(step)
        return pltpu.make_async_copy(
            new_edges.at[rows], new_edges_out.at[rows], out_sems.at[step]
        )

    def paired(value):
        return jnp.concatenate([value[:half], value[half:]], axis=1)

    def unpaired(value):
        return jnp.concatenate([value[:, :width], value[:, width:]], axis=0)

    def twice(block):
        zero = jnp.zeros_like(block)
        return jnp.concatenate(
            [
                jnp.concatenate([block, zero], axis=1),
                jnp.concatenate([zero, block], axis=1),
            ],
            axis=0,
        )

    ahead, behind = range(4), range(4, 7)
    for copy in small[:4] + fetch(0, ahead) + small[4:]:
        copy.start()
    for step in range(1, chunks):
        for copy in fetch(step, ahead):
            copy.start()
    for step in range(chunks):
        for copy in fetch(step, behind):
            copy.start()
    for copy in small[:4]:
        copy.wait()

    near_rows[...] = nodes[...]
    spot = 0
    for d_strip in (-1, 0, 1):
        strip = jnp.clip(my_strip + d_strip, 0, strips - 1)
        for d_sub in (-1, 0, 1):
            if d_strip == 0 and d_sub == 0:
                continue
            sub = jnp.clip(my_sub + d_sub, 0, subs - 1)
            far_rows[spot * border : (spot + 1) * border] = rims[strip * subs + sub]
            spot += 1
    tables[:, :width] = mm(near_rows[...], w_edge_in[:width]).astype(BF16)
    tables[:, width:] = mm(far_rows[...], w_edge_in[:width]).astype(BF16)
    weight = w_edge_out[...].astype(F32)
    centring[...] = twice(weight - jnp.mean(weight, axis=1, keepdims=True)).astype(BF16)
    back[...] = twice(weight).astype(BF16)
    means[...] = twice(jnp.full((width, width), 1.0 / width, F32)).astype(BF16)

    row = lax.broadcasted_iota(jnp.int32, (half, 2 * width), 0)
    lane = lax.broadcasted_iota(jnp.int32, (half, 2 * width), 1)
    edge_row = jnp.where(lane < width, row, row + half)
    agg[...] = jnp.zeros_like(agg)

    def forward(step, carry):
        for copy in fetch(step, ahead):
            copy.wait()
        recv_t = found_t(info[step][1:2], count_p)
        units = []
        for part in range(SPLIT):
            rows, pairs = block_rows(step, part), block_pairs(step, part)
            codes = send_codes[rows]
            begun = pre_part[rows]
            edge = paired(edges[rows].astype(F32))
            place = jnp.where(codes < 0, -1 - codes, codes)
            picked = mm(found(place, count_p // width), tables[...])
            beyond = codes.astype(F32) < 0.0
            pre = begun + jnp.where(beyond, picked[:, width:], picked[:, :width])
            act, bend = silu_and_slope(paired(pre))
            act = act.astype(BF16)
            centre = mm(act, centring[...])
            spare = mm((centre * centre).astype(BF16), means[...])
            live = edge_row < live_count - step * chunk - part * block
            factor = jnp.where(live, lax.rsqrt(spare + EPS), 0.0)
            unit = centre * factor
            slope[pairs] = bend
            hidden[rows] = unpaired(act)
            scale[pairs] = factor
            normed[pairs] = unit
            new_edges[rows] = unpaired((edge + unit).astype(BF16))
            units.append(unpaired(unit.astype(BF16)))
        agg[...] += mm(recv_t, jnp.concatenate(units, axis=0))
        emit(step).start()
        return carry

    lax.fori_loop(0, chunks, forward, 0)

    for copy in small[4:]:
        copy.wait()
    joined = jnp.concatenate([nodes[...], agg[...].astype(BF16)], axis=1)
    node_pre = mm(joined, w_node_in[...])
    node_act, node_slope = silu_and_slope(node_pre)
    node_act = node_act.astype(BF16)
    node_unit, node_scale = norm_rows(mm(node_act, w_node_out[...]))
    new_nodes[...] = (nodes[...].astype(F32) + node_unit).astype(BF16)
    cot = node_cot[...].astype(F32)
    d_outer = norm_back(node_unit, node_scale, cot).astype(BF16)
    d_pre = (mm_nt(d_outer, w_node_out[...]) * node_slope).astype(BF16)
    d_joined = mm_nt(d_pre, w_node_in[...])
    d_agg = d_joined[:, width:]
    d_agg = (d_agg - jnp.mean(d_agg, axis=1, keepdims=True)).astype(BF16)
    agg[...] = cot + d_joined[:, :width]
    packed[4 * width : 6 * width] = mm_tn(joined, d_pre).astype(BF16)
    packed[6 * width : 7 * width] = mm_tn(node_act, d_outer).astype(BF16)
    node_copy = pltpu.make_async_copy(new_nodes, new_nodes_out, last_sem)
    node_copy.start()

    sums[...] = jnp.zeros_like(sums)
    ge_out[...] = jnp.zeros_like(ge_out)

    def backward(step, carry):
        for copy in fetch(step, behind):
            copy.wait()
        index = info[step]
        turned = jnp.concatenate(
            [found_t(index[1:2], count_p), found_t(index[0:1], count_p), edges_t[step]], axis=0
        )
        acts, outs, ins = [], [], []
        for part in range(SPLIT):
            rows, pairs = block_rows(step, part), block_pairs(step, part)
            cot = cot_part[rows].astype(F32)
            recv = found(recv_codes[rows], count_p // width)
            unit = normed[pairs]
            acts.append(hidden[rows])
            beyond = send_codes[rows] < 0
            upstream = paired(cot + mm(recv, d_agg))
            along = mm((upstream * unit).astype(BF16), means[...])
            d_out = (scale[pairs] * (upstream - unit * along)).astype(BF16)
            outs.append(unpaired(d_out))
            d_in = unpaired((mm_nt(d_out, back[...]) * slope[pairs]).astype(BF16))
            zero = jnp.zeros_like(d_in)
            ins.append(
                jnp.concatenate(
                    [jnp.where(beyond, zero, d_in), jnp.where(beyond, d_in, zero)], axis=1
                )
            )
        ge_out[...] += mm_tn(jnp.concatenate(acts, axis=0), jnp.concatenate(outs, axis=0))
        sums[...] += mm(turned, jnp.concatenate(ins, axis=0))
        return carry

    lax.fori_loop(0, chunks, backward, 0)

    recv_sums = (sums[:count_p, :width] + sums[:count_p, width:]).astype(BF16)
    near_sums = sums[count_p : 2 * count_p, :width].astype(BF16)
    far_sums = sums[count_p : 2 * count_p, width:].astype(BF16)
    edge_sums = sums[2 * count_p :, :width] + sums[2 * count_p :, width:]
    packed[:width] = (mm_tn(near_rows[...], near_sums) + mm_tn(far_rows[...], far_sums)).astype(BF16)
    packed[width : 2 * width] = mm_tn(nodes[...], recv_sums).astype(BF16)
    packed[2 * width : 3 * width] = edge_sums.astype(BF16)
    packed[3 * width : 4 * width] = ge_out[...].astype(BF16)
    if packed.shape[0] > 7 * width:
        packed[7 * width :] = jnp.zeros((packed.shape[0] - 7 * width, width), BF16)
    local_grad[...] = (
        agg[...]
        + mm_nt(near_sums, w_edge_in[:width])
        + mm_nt(recv_sums, w_edge_in[width : 2 * width])
    )
    owed = mm_nt(far_sums, w_edge_in[:width]).astype(BF16)
    for slot in range(slots):
        parts[slot, :share] = packed[slot * share : (slot + 1) * share]
        parts[slot, share:] = jnp.zeros((2 * border, width), BF16)
    spot = 0
    for d_strip in (-1, 0, 1):
        strip = my_strip + d_strip
        for d_sub in (-1, 0, 1):
            if d_strip == 0 and d_sub == 0:
                continue
            if d_sub == 0:
                slot, part = 2 * strip + my_y, 0
            elif d_sub == 1:
                slot, part = 2 * strip + 1 - my_y, my_y
            else:
                slot, part = 2 * strip + 1 - my_y, 1 - my_y
            first = pl.multiple_of(share + part * border, 16)
            block = owed[spot * border : (spot + 1) * border]

            @pl.when((strip >= 0) & (strip < strips))
            def put(slot=slot, first=first, block=block):
                parts[slot, pl.ds(first, border), :] = block

            spot += 1
    for step in range(chunks):
        emit(step).wait()
    node_copy.wait()


def plane_sum_kernel(came, out, mine):
    border = mine.shape[0]
    zs = out.shape[0]
    share = out.shape[1] - border
    total = came[0].astype(F32)
    for slot in range(1, came.shape[0]):
        total = total + came[slot].astype(F32)
    share_total = total[:share].astype(BF16)
    mine[...] = total[share : share + border]
    beyond = total[share + border :].astype(BF16)
    for target in range(zs):
        out[target, :share] = share_total
        out[target, share:] = jnp.zeros_like(beyond)
    target = lax.axis_index("z") + 1 - 2 * lax.axis_index("y")

    @pl.when((target >= 0) & (target < zs))
    def put():
        out[target, share:] = beyond


def line_sum_kernel(factor, came, mine, out, rim_grad):
    share = out.shape[1]
    total = came[0].astype(F32)
    for slot in range(1, came.shape[0]):
        total = total + came[slot].astype(F32)
    share_total = (total[:share] * factor).astype(BF16)
    for target in range(out.shape[0]):
        out[target] = share_total
    rim_grad[...] = mine[...] + total[share:]


def finish_kernel(came, rim_grad, local_grad, node_grad, *outs):
    border = rim_grad.shape[0]
    share = came.shape[1]
    node_grad[...] = local_grad[...]
    node_grad[:border] += rim_grad[...]
    start = 0
    for out in outs:
        size = out.shape[0]
        done = 0
        while done < size:
            slot, offset = divmod(start + done, share)
            step = min(size - done, share - offset)
            out[done : done + step] = came[slot, offset : offset + step].astype(F32)
            done += step
        start += size


def shards(
    node_latents,
    edge_latents,
    senders,
    receivers,
    edge_count,
    w_edge_in,
    w_edge_out,
    w_node_in,
    w_node_out,
    node_cotangent,
    edge_cotangent,
):
    count_p, width = node_latents.shape
    count_e = edge_latents.shape[0]
    border = count_p // 8
    strips, zs, ys = (lax.axis_size(axis) for axis in ALL)
    subs = zs * ys
    slots = strips * ys
    my_strip, my_z, my_y = (lax.axis_index(axis).astype(jnp.int32) for axis in ALL)
    my_sub = my_z * ys + my_y
    devices = strips * subs

    (rims,) = call(
        rim_kernel,
        [((devices, border, width), BF16)],
        [node_latents],
        [HBM],
        [
            pltpu.VMEM((border, width), BF16),
            pltpu.VMEM((devices, border, width), BF16),
            SEM,
            SEM,
        ],
        [HBM],
    )
    rims = lax.all_to_all(rims, ALL, 0, 0)

    owner = senders // count_p
    within = senders % count_p
    is_local = owner == my_strip * subs + my_sub
    block = (owner // subs - my_strip + 1) * 3 + (owner % subs - my_sub + 1)
    block = jnp.where(block > 4, block - 1, block)
    send_index = jnp.where(is_local, within, block * border + jnp.minimum(within, border - 1))
    codes = jnp.where(is_local, send_index, -1 - send_index)
    chunk = min(CHUNK, count_e)
    chunks = count_e // chunk
    info = jnp.stack(
        [
            value.reshape(chunks, chunk)
            for value in [send_index, receivers, codes]
            + [jnp.zeros_like(receivers)] * 5
        ],
        axis=1,
    )

    def by_rows(*shape):
        return pl.BlockSpec(shape, lambda i: (i, 0))

    def by_chunk(*shape):
        return pl.BlockSpec((1, *shape), lambda i: (i, 0, 0))

    def whole(*shape):
        return pl.BlockSpec(shape, lambda i: (0, 0))

    early = pl.pallas_call(
        early_kernel,
        grid=(chunks,),
        out_shape=[
            pltpu.HBM(shape, dtype)
            for shape, dtype in [
                ((count_e, width), BF16),
                ((count_e, width), BF16),
                ((chunks, width, chunk), BF16),
                ((count_e, width), F32),
                ((count_e, width), BF16),
            ]
        ],
        in_specs=[
            whole(count_p, width),
            by_rows(chunk, width),
            by_rows(chunk, width),
            by_chunk(8, chunk),
            whole(3 * width, width),
        ],
        out_specs=[
            by_rows(chunk, width),
            by_rows(chunk, width),
            by_chunk(width, chunk),
            by_rows(chunk, width),
            by_rows(chunk, width),
        ],
        scratch_shapes=[pltpu.VMEM((count_p + width, width), BF16)],
        compiler_params=pltpu.CompilerParams(vmem_limit_bytes=32 * 2**20),
    )(
        in_hbm(node_latents),
        in_hbm(edge_latents),
        in_hbm(edge_cotangent),
        info,
        in_hbm(w_edge_in),
    )

    share = -(-7 * width // (slots * 16)) * 16

    def like(value):
        return pltpu.VMEM(value.shape, value.dtype)

    new_nodes, new_edges, local_grad, parts = call(
        layer_kernel,
        [
            ((count_p, width), BF16),
            ((count_e, width), BF16),
            ((count_p, width), F32),
            ((slots, share + 2 * border, width), BF16),
        ],
        [
            edge_count,
            node_latents,
            rims,
            edge_latents,
            info,
            *early,
            w_edge_in,
            w_edge_out,
            w_node_in,
            w_node_out,
            node_cotangent,
        ],
        [SMEM] + [HBM] * 14,
        [
            like(node_latents),
            like(rims),
            like(edge_latents),
            like(info),
            *[like(value) for value in early],
            like(w_edge_in),
            like(w_edge_out),
            like(w_node_in),
            like(w_node_out),
            like(node_cotangent),
            pltpu.VMEM((count_p, width), BF16),
            pltpu.VMEM((count_e, width), BF16),
            pltpu.VMEM((count_p, width), BF16),
            pltpu.VMEM((8 * border, width), BF16),
            pltpu.VMEM((count_p, 2 * width), BF16),
            pltpu.VMEM((2 * width, 2 * width), BF16),
            pltpu.VMEM((2 * width, 2 * width), BF16),
            pltpu.VMEM((2 * width, 2 * width), BF16),
            pltpu.VMEM((count_e, width), BF16),
            pltpu.VMEM((count_e // 2, 2 * width), F32),
            pltpu.VMEM((count_e // 2, 2 * width), F32),
            pltpu.VMEM((count_e // 2, 2 * width), F32),
            pltpu.VMEM((2 * count_p + width, 2 * width), F32),
            pltpu.VMEM((width, width), F32),
            pltpu.VMEM((count_p, width), F32),
            pltpu.VMEM((slots * share, width), BF16),
            SEM((7,)),
            SEM((7, chunks)),
            SEM((chunks,)),
            SEM,
        ],
        [HBM, HBM, VMEM, VMEM],
        limit=48,
    )

    came = lax.all_to_all(parts, PLANE, 0, 0)
    parts, mine = call(
        plane_sum_kernel,
        [((zs, share + border, width), BF16), ((border, width), F32)],
        [came],
        [VMEM],
    )
    came = lax.all_to_all(parts, "z", 0, 0)
    factor = 1.0 / math.sqrt(count_e * strips * subs)
    parts, rim_grad = call(
        functools.partial(line_sum_kernel, factor),
        [((slots, share, width), BF16), ((border, width), F32)],
        [came, mine],
        [VMEM, VMEM],
    )
    came = lax.all_to_all(parts, PLANE, 0, 0)
    node_grad, *grads = call(
        finish_kernel,
        [((rows, width), F32) for rows in (count_p, 3 * width, width, 2 * width, width)],
        [came, rim_grad, local_grad],
        [VMEM, VMEM, VMEM],
    )
    return (new_nodes, new_edges, node_grad, *grads)


def solution(mesh):
    strips, subs = mesh.devices.shape
    grid = Mesh(mesh.devices.reshape(strips, subs // 2, 2), ALL)
    rows = P(ALL, None)
    line = P(ALL)
    return jax.shard_map(
        shards,
        mesh=grid,
        in_specs=(rows, rows, line, line, line, P(), P(), P(), P(), rows, rows),
        out_specs=(rows, rows, rows, P(), P(), P(), P()),
        check_vma=False,
    )
```

```python
import functools
import math

import jax
import jax.numpy as jnp
from jax import lax
from jax.experimental import pallas as pl
from jax.experimental.pallas import tpu as pltpu
from jax.sharding import Mesh
from jax.sharding import PartitionSpec as P

EPS = 1e-05
CHUNK = 1024
SPLIT = 2
PLANE = ("strip", "y")
ALL = ("strip", "z", "y")
F32 = jnp.float32
BF16 = jnp.bfloat16
VMEM = pl.BlockSpec(memory_space=pltpu.VMEM)
SMEM = pl.BlockSpec(memory_space=pltpu.SMEM)
HBM = pl.BlockSpec(memory_space=pltpu.HBM)
SEM = pltpu.SemaphoreType.DMA


def mm(left, right):
    return jnp.dot(left, right, preferred_element_type=F32)


def mm_nt(left, right):
    return lax.dot_general(left, right, (((1,), (1,)), ((), ())), preferred_element_type=F32)


def mm_tn(left, right):
    return lax.dot_general(left, right, (((0,), (0,)), ((), ())), preferred_element_type=F32)


def norm_rows(values):
    centre = values - jnp.mean(values, axis=1, keepdims=True)
    scale = lax.rsqrt(jnp.mean(centre * centre, axis=1, keepdims=True) + EPS)
    return (centre * scale, scale)


def norm_back(normed, scale, upstream):
    first = jnp.mean(upstream, axis=1, keepdims=True)
    second = jnp.mean(upstream * normed, axis=1, keepdims=True)
    return scale * (upstream - first - normed * second)


def silu_and_slope(values):
    sig = 0.5 + 0.5 * jnp.tanh(0.5 * values)
    act = values * sig
    return (act, sig + act * (1.0 - sig))


def found(codes, blocks):
    lane = lax.broadcasted_iota(jnp.int32, codes.shape, 1)
    one, zero = jnp.ones((), BF16), jnp.zeros((), BF16)
    width = codes.shape[1]
    return jnp.concatenate(
        [
            jnp.where(codes == (lane + width * k).astype(F32).astype(BF16), one, zero)
            for k in range(blocks)
        ],
        axis=1,
    )


def found_t(line, size):
    place = lax.broadcasted_iota(jnp.int32, (size, line.shape[1]), 0).astype(F32).astype(BF16)
    one, zero = jnp.ones((), BF16), jnp.zeros((), BF16)
    return jnp.where(place == line.astype(F32).astype(BF16), one, zero)


def in_hbm(value):
    return pltpu.with_memory_space_constraint(value, pltpu.HBM)


def call(kernel, outs, ins, specs, scratch=(), out_specs=None, limit=24):
    out_specs = [VMEM] * len(outs) if out_specs is None else out_specs
    return pl.pallas_call(
        kernel,
        out_shape=[
            pltpu.HBM(shape, dtype) if spec is HBM else jax.ShapeDtypeStruct(shape, dtype)
            for (shape, dtype), spec in zip(outs, out_specs)
        ],
        in_specs=specs,
        out_specs=out_specs,
        scratch_shapes=list(scratch),
        compiler_params=pltpu.CompilerParams(vmem_limit_bytes=limit * 2**20),
    )(*[in_hbm(value) if spec is HBM else value for value, spec in zip(ins, specs)])


def rim_kernel(nodes, out, rim, many, in_sem, out_sem):
    border = out.shape[1]
    copy = pltpu.make_async_copy(nodes.at[pl.ds(0, border)], rim, in_sem)
    copy.start()
    copy.wait()
    for target in range(out.shape[0]):
        many[target] = rim[...]
    copy = pltpu.make_async_copy(many, out, out_sem)
    copy.start()
    copy.wait()


def early_kernel(
    nodes,
    edges,
    edge_cot,
    info,
    w_edge_in,
    send_codes,
    recv_codes,
    edges_t,
    pre_part,
    cot_part,
    tables,
):
    count_p, width = nodes.shape

    @pl.when(pl.program_id(0) == 0)
    def prepare():
        tables[:count_p] = mm(nodes[...], w_edge_in[width : 2 * width]).astype(BF16)
        tables[count_p:] = w_edge_in[2 * width :]

    columns = info[0].T
    edge = edges[...]
    cot = edge_cot[...].astype(F32)
    recv = jnp.broadcast_to(columns[:, 1:2], edge.shape).astype(F32).astype(BF16)
    recv_codes[...] = recv
    send_codes[...] = jnp.broadcast_to(columns[:, 2:3], edge.shape).astype(F32).astype(BF16)
    recv = found(recv, count_p // width)
    pre_part[...] = mm(jnp.concatenate([recv, edge], axis=1), tables[...])
    edges_t[0] = edge.T
    cot_part[...] = (cot - jnp.mean(cot, axis=1, keepdims=True)).astype(BF16)


def layer_kernel(
    edge_count,
    nodes_in,
    rims,
    edges_in,
    info_in,
    send_codes_in,
    recv_codes_in,
    edges_t_in,
    pre_part_in,
    cot_part_in,
    w_edge_in_in,
    w_edge_out_in,
    w_node_in_in,
    w_node_out_in,
    node_cot_in,
    new_nodes_out,
    new_edges_out,
    local_grad,
    parts,
    nodes,
    edges,
    info,
    send_codes,
    recv_codes,
    edges_t,
    pre_part,
    cot_part,
    w_edge_in,
    w_edge_out,
    w_node_in,
    w_node_out,
    node_cot,
    new_nodes,
    new_edges,
    near_rows,
    far_rows,
    tables,
    centring,
    back,
    means,
    hidden,
    slope,
    normed,
    scale,
    sums,
    ge_out,
    agg,
    packed,
    kept,
    small_sems,
    sems,
    out_sems,
    last_sem,
):
    count_p, width = nodes.shape
    border = rims.shape[1]
    slots = parts.shape[0]
    strips = slots // 2
    chunks, _, chunk = edges_t.shape
    block = chunk // SPLIT
    half = block // 2
    share = parts.shape[1] - 2 * border
    my_strip, my_y = lax.axis_index("strip"), lax.axis_index("y")
    subs = lax.axis_size("z") * lax.axis_size("y")
    my_sub = lax.axis_index("z") * lax.axis_size("y") + my_y
    live_count = edge_count[0]

    small = [
        pltpu.make_async_copy(source, target, small_sems.at[k])
        for k, (source, target) in enumerate(
            [
                (nodes_in, nodes),
                (w_edge_in_in, w_edge_in),
                (w_edge_out_in, w_edge_out),
                (w_node_in_in, w_node_in),
                (w_node_out_in, w_node_out),
                (node_cot_in, node_cot),
            ]
        )
    ]

    def span(step):
        return pl.ds(pl.multiple_of(step * chunk, chunk), chunk)

    def block_rows(step, part):
        return pl.ds(pl.multiple_of(step * chunk + part * block, block), block)

    def block_pairs(step, part):
        return pl.ds(pl.multiple_of((step * SPLIT + part) * half, half), half)

    def fetch(step, which):
        rows = span(step)
        pairs = [
            (send_codes_in.at[rows], send_codes.at[rows]),
            (pre_part_in.at[rows], pre_part.at[rows]),
            (info_in.at[step], info.at[step]),
            (edges_in.at[rows], edges.at[rows]),
            (recv_codes_in.at[rows], recv_codes.at[rows]),
            (cot_part_in.at[rows], cot_part.at[rows]),
            (edges_t_in.at[step], edges_t.at[step]),
        ]
        return [pltpu.make_async_copy(*pairs[k], sems.at[k, step]) for k in which]

    def emit(step):
        rows = span(step)
        return pltpu.make_async_copy(
            new_edges.at[rows], new_edges_out.at[rows], out_sems.at[step]
        )

    def paired(value):
        return jnp.concatenate([value[:half], value[half:]], axis=1)

    def unpaired(value):
        return jnp.concatenate([value[:, :width], value[:, width:]], axis=0)

    def twice(block):
        zero = jnp.zeros_like(block)
        return jnp.concatenate(
            [
                jnp.concatenate([block, zero], axis=1),
                jnp.concatenate([zero, block], axis=1),
            ],
            axis=0,
        )

    ahead, behind = range(4), range(4, 7)
    for copy in small[:3] + fetch(0, ahead) + small[3:]:
        copy.start()
    for step in range(1, chunks):
        for copy in fetch(step, ahead):
            copy.start()
    for step in range(chunks):
        for copy in fetch(step, behind):
            copy.start()
    for copy in small[:3]:
        copy.wait()

    near_rows[...] = nodes[...]
    spot = 0
    for d_strip in (-1, 0, 1):
        strip = jnp.clip(my_strip + d_strip, 0, strips - 1)
        for d_sub in (-1, 0, 1):
            if d_strip == 0 and d_sub == 0:
                continue
            sub = jnp.clip(my_sub + d_sub, 0, subs - 1)
            far_rows[spot * border : (spot + 1) * border] = rims[strip * subs + sub]
            spot += 1
    tables[:, :width] = mm(near_rows[...], w_edge_in[:width]).astype(BF16)
    tables[:, width:] = mm(far_rows[...], w_edge_in[:width]).astype(BF16)
    weight = w_edge_out[...].astype(F32)
    centring[...] = twice(weight - jnp.mean(weight, axis=1, keepdims=True)).astype(BF16)
    back[...] = twice(weight).astype(BF16)
    means[...] = twice(jnp.full((width, width), 1.0 / width, F32)).astype(BF16)

    row = lax.broadcasted_iota(jnp.int32, (half, 2 * width), 0)
    lane = lax.broadcasted_iota(jnp.int32, (half, 2 * width), 1)
    edge_row = jnp.where(lane < width, row, row + half)
    agg[...] = jnp.zeros_like(agg)

    def forward(step, carry):
        for copy in fetch(step, ahead):
            copy.wait()
        recv_t = found_t(info[step][1:2], count_p)
        units = []
        for part in range(SPLIT):
            rows, pairs = block_rows(step, part), block_pairs(step, part)
            codes = send_codes[rows]
            begun = pre_part[rows]
            edge = paired(edges[rows].astype(F32))
            place = jnp.where(codes < 0, -1 - codes, codes)
            picked = mm(found(place, count_p // width), tables[...])
            beyond = codes.astype(F32) < 0.0
            pre = begun + jnp.where(beyond, picked[:, width:], picked[:, :width])
            act, bend = silu_and_slope(paired(pre))
            act = act.astype(BF16)
            centre = mm(act, centring[...])
            spare = mm((centre * centre).astype(BF16), means[...])
            live = edge_row < live_count - step * chunk - part * block
            factor = jnp.where(live, lax.rsqrt(spare + EPS), 0.0)
            unit = centre * factor
            slope[pairs] = bend
            hidden[rows] = unpaired(act)
            scale[pairs] = factor
            normed[pairs] = unit
            new_edges[rows] = unpaired((edge + unit).astype(BF16))
            units.append(unpaired(unit.astype(BF16)))
        agg[...] += mm(recv_t, jnp.concatenate(units, axis=0))
        emit(step).start()
        return carry

    lax.fori_loop(0, chunks, forward, 0)

    for copy in small[3:]:
        copy.wait()
    joined = jnp.concatenate([nodes[...], agg[...].astype(BF16)], axis=1)
    node_pre = mm(joined, w_node_in[...])
    node_act, node_slope = silu_and_slope(node_pre)
    node_act = node_act.astype(BF16)
    node_unit, node_scale = norm_rows(mm(node_act, w_node_out[...]))
    new_nodes[...] = (nodes[...].astype(F32) + node_unit).astype(BF16)
    cot = node_cot[...].astype(F32)
    d_outer = norm_back(node_unit, node_scale, cot).astype(BF16)
    d_pre = (mm_nt(d_outer, w_node_out[...]) * node_slope).astype(BF16)
    d_joined = mm_nt(d_pre, w_node_in[...])
    d_agg = d_joined[:, width:]
    d_agg = (d_agg - jnp.mean(d_agg, axis=1, keepdims=True)).astype(BF16)
    agg[...] = cot + d_joined[:, :width]
    kept[:, : 2 * width] = joined
    kept[:, 2 * width : 3 * width] = node_act
    kept[:, 3 * width : 4 * width] = d_outer
    kept[:, 4 * width :] = d_pre
    node_copy = pltpu.make_async_copy(new_nodes, new_nodes_out, last_sem)
    node_copy.start()

    sums[...] = jnp.zeros_like(sums)
    ge_out[...] = jnp.zeros_like(ge_out)

    def backward(step, carry):
        for copy in fetch(step, behind):
            copy.wait()
        index = info[step]
        turned = jnp.concatenate(
            [found_t(index[1:2], count_p), found_t(index[0:1], count_p), edges_t[step]], axis=0
        )
        acts, outs, ins = [], [], []
        for part in range(SPLIT):
            rows, pairs = block_rows(step, part), block_pairs(step, part)
            cot = cot_part[rows].astype(F32)
            recv = found(recv_codes[rows], count_p // width)
            unit = normed[pairs]
            acts.append(hidden[rows])
            beyond = send_codes[rows] < 0
            upstream = paired(cot + mm(recv, d_agg))
            along = mm((upstream * unit).astype(BF16), means[...])
            d_out = (scale[pairs] * (upstream - unit * along)).astype(BF16)
            outs.append(unpaired(d_out))
            d_in = unpaired((mm_nt(d_out, back[...]) * slope[pairs]).astype(BF16))
            zero = jnp.zeros_like(d_in)
            ins.append(
                jnp.concatenate(
                    [jnp.where(beyond, zero, d_in), jnp.where(beyond, d_in, zero)], axis=1
                )
            )
        ge_out[...] += mm_tn(jnp.concatenate(acts, axis=0), jnp.concatenate(outs, axis=0))
        sums[...] += mm(turned, jnp.concatenate(ins, axis=0))
        return carry

    lax.fori_loop(0, chunks, backward, 0)

    recv_sums = (sums[:count_p, :width] + sums[:count_p, width:]).astype(BF16)
    near_sums = sums[count_p : 2 * count_p, :width].astype(BF16)
    far_sums = sums[count_p : 2 * count_p, width:].astype(BF16)
    edge_sums = sums[2 * count_p :, :width] + sums[2 * count_p :, width:]
    packed[:width] = (mm_tn(near_rows[...], near_sums) + mm_tn(far_rows[...], far_sums)).astype(BF16)
    packed[width : 2 * width] = mm_tn(nodes[...], recv_sums).astype(BF16)
    packed[4 * width : 6 * width] = mm_tn(kept[:, : 2 * width], kept[:, 4 * width :]).astype(BF16)
    packed[6 * width : 7 * width] = mm_tn(
        kept[:, 2 * width : 3 * width], kept[:, 3 * width : 4 * width]
    ).astype(BF16)
    packed[2 * width : 3 * width] = edge_sums.astype(BF16)
    packed[3 * width : 4 * width] = ge_out[...].astype(BF16)
    if packed.shape[0] > 7 * width:
        packed[7 * width :] = jnp.zeros((packed.shape[0] - 7 * width, width), BF16)
    local_grad[...] = (
        agg[...]
        + mm_nt(near_sums, w_edge_in[:width])
        + mm_nt(recv_sums, w_edge_in[width : 2 * width])
    )
    owed = mm_nt(far_sums, w_edge_in[:width]).astype(BF16)
    for slot in range(slots):
        parts[slot, :share] = packed[slot * share : (slot + 1) * share]
        parts[slot, share:] = jnp.zeros((2 * border, width), BF16)
    spot = 0
    for d_strip in (-1, 0, 1):
        strip = my_strip + d_strip
        for d_sub in (-1, 0, 1):
            if d_strip == 0 and d_sub == 0:
                continue
            if d_sub == 0:
                slot, part = 2 * strip + my_y, 0
            elif d_sub == 1:
                slot, part = 2 * strip + 1 - my_y, my_y
            else:
                slot, part = 2 * strip + 1 - my_y, 1 - my_y
            first = pl.multiple_of(share + part * border, 16)
            block = owed[spot * border : (spot + 1) * border]

            @pl.when((strip >= 0) & (strip < strips))
            def put(slot=slot, first=first, block=block):
                parts[slot, pl.ds(first, border), :] = block

            spot += 1
    for step in range(chunks):
        emit(step).wait()
    node_copy.wait()


def plane_sum_kernel(came, message, mine):
    border = mine.shape[0]
    share = message.shape[0] - border
    total = came[0].astype(F32)
    for slot in range(1, came.shape[0]):
        total = total + came[slot].astype(F32)
    mine[...] = total[share : share + border]
    message[:share] = total[:share].astype(BF16)
    message[share:] = total[share + border :].astype(BF16)


def joined_line(bit, own, came, mine):
    share = came.shape[0] - mine.shape[0]
    total = own[:share].astype(F32) + came[:share].astype(F32)
    passing = came[share:].astype(F32)
    mine_bit = lax.rem(lax.div(lax.axis_index("z"), 2**bit), 2)
    here = jnp.where(mine_bit != lax.axis_index("y"), 1.0, 0.0)
    return total, mine[...] + here * passing, (1.0 - here) * passing


def line_step_kernel(bit, own, came, mine, message, next_mine):
    share = came.shape[0] - mine.shape[0]
    total, arrived, passing = joined_line(bit, own, came, mine)
    next_mine[...] = arrived
    message[:share] = total.astype(BF16)
    message[share:] = passing.astype(BF16)


def line_last_kernel(bit, factor, own, came, mine, out, rim_grad):
    total, rim_grad[...], _ = joined_line(bit, own, came, mine)
    total = (total * factor).astype(BF16)
    for target in range(out.shape[0]):
        out[target] = total


def finish_kernel(came, rim_grad, local_grad, node_grad, *outs):
    border = rim_grad.shape[0]
    share = came.shape[1]
    node_grad[...] = local_grad[...]
    node_grad[:border] += rim_grad[...]
    start = 0
    for out in outs:
        size = out.shape[0]
        done = 0
        while done < size:
            slot, offset = divmod(start + done, share)
            step = min(size - done, share - offset)
            out[done : done + step] = came[slot, offset : offset + step].astype(F32)
            done += step
        start += size


def shards(
    node_latents,
    edge_latents,
    senders,
    receivers,
    edge_count,
    w_edge_in,
    w_edge_out,
    w_node_in,
    w_node_out,
    node_cotangent,
    edge_cotangent,
):
    count_p, width = node_latents.shape
    count_e = edge_latents.shape[0]
    border = count_p // 8
    strips, zs, ys = (lax.axis_size(axis) for axis in ALL)
    subs = zs * ys
    slots = strips * ys
    my_strip, my_z, my_y = (lax.axis_index(axis).astype(jnp.int32) for axis in ALL)
    my_sub = my_z * ys + my_y
    devices = strips * subs

    (rims,) = call(
        rim_kernel,
        [((devices, border, width), BF16)],
        [node_latents],
        [HBM],
        [
            pltpu.VMEM((border, width), BF16),
            pltpu.VMEM((devices, border, width), BF16),
            SEM,
            SEM,
        ],
        [HBM],
    )
    rims = lax.all_to_all(rims, ALL, 0, 0)

    owner = senders // count_p
    within = senders % count_p
    is_local = owner == my_strip * subs + my_sub
    block = (owner // subs - my_strip + 1) * 3 + (owner % subs - my_sub + 1)
    block = jnp.where(block > 4, block - 1, block)
    send_index = jnp.where(is_local, within, block * border + jnp.minimum(within, border - 1))
    codes = jnp.where(is_local, send_index, -1 - send_index)
    chunk = min(CHUNK, count_e)
    chunks = count_e // chunk
    info = jnp.stack(
        [
            value.reshape(chunks, chunk)
            for value in [send_index, receivers, codes]
            + [jnp.zeros_like(receivers)] * 5
        ],
        axis=1,
    )

    def by_rows(*shape):
        return pl.BlockSpec(shape, lambda i: (i, 0))

    def by_chunk(*shape):
        return pl.BlockSpec((1, *shape), lambda i: (i, 0, 0))

    def whole(*shape):
        return pl.BlockSpec(shape, lambda i: (0, 0))

    early = pl.pallas_call(
        early_kernel,
        grid=(chunks,),
        out_shape=[
            pltpu.HBM(shape, dtype)
            for shape, dtype in [
                ((count_e, width), BF16),
                ((count_e, width), BF16),
                ((chunks, width, chunk), BF16),
                ((count_e, width), F32),
                ((count_e, width), BF16),
            ]
        ],
        in_specs=[
            whole(count_p, width),
            by_rows(chunk, width),
            by_rows(chunk, width),
            by_chunk(8, chunk),
            whole(3 * width, width),
        ],
        out_specs=[
            by_rows(chunk, width),
            by_rows(chunk, width),
            by_chunk(width, chunk),
            by_rows(chunk, width),
            by_rows(chunk, width),
        ],
        scratch_shapes=[pltpu.VMEM((count_p + width, width), BF16)],
        compiler_params=pltpu.CompilerParams(vmem_limit_bytes=32 * 2**20),
    )(
        in_hbm(node_latents),
        in_hbm(edge_latents),
        in_hbm(edge_cotangent),
        info,
        in_hbm(w_edge_in),
    )

    share = -(-7 * width // (slots * 16)) * 16

    def like(value):
        return pltpu.VMEM(value.shape, value.dtype)

    new_nodes, new_edges, local_grad, parts = call(
        layer_kernel,
        [
            ((count_p, width), BF16),
            ((count_e, width), BF16),
            ((count_p, width), F32),
            ((slots, share + 2 * border, width), BF16),
        ],
        [
            edge_count,
            node_latents,
            rims,
            edge_latents,
            info,
            *early,
            w_edge_in,
            w_edge_out,
            w_node_in,
            w_node_out,
            node_cotangent,
        ],
        [SMEM, HBM, VMEM] + [HBM] * 12,
        [
            like(node_latents),
            like(edge_latents),
            like(info),
            *[like(value) for value in early],
            like(w_edge_in),
            like(w_edge_out),
            like(w_node_in),
            like(w_node_out),
            like(node_cotangent),
            pltpu.VMEM((count_p, width), BF16),
            pltpu.VMEM((count_e, width), BF16),
            pltpu.VMEM((count_p, width), BF16),
            pltpu.VMEM((8 * border, width), BF16),
            pltpu.VMEM((count_p, 2 * width), BF16),
            pltpu.VMEM((2 * width, 2 * width), BF16),
            pltpu.VMEM((2 * width, 2 * width), BF16),
            pltpu.VMEM((2 * width, 2 * width), BF16),
            pltpu.VMEM((count_e, width), BF16),
            pltpu.VMEM((count_e // 2, 2 * width), F32),
            pltpu.VMEM((count_e // 2, 2 * width), F32),
            pltpu.VMEM((count_e // 2, 2 * width), F32),
            pltpu.VMEM((2 * count_p + width, 2 * width), F32),
            pltpu.VMEM((width, width), F32),
            pltpu.VMEM((count_p, width), F32),
            pltpu.VMEM((slots * share, width), BF16),
            pltpu.VMEM((count_p, 5 * width), BF16),
            SEM((6,)),
            SEM((7, chunks)),
            SEM((chunks,)),
            SEM,
        ],
        [HBM, HBM, VMEM, VMEM],
        limit=48,
    )

    came = lax.all_to_all(parts, PLANE, 0, 0)
    state = [((share + border, width), BF16), ((border, width), F32)]
    message, mine = call(plane_sum_kernel, state, [came], [VMEM])
    factor = 1.0 / math.sqrt(count_e * strips * subs)
    bits = zs.bit_length() - 1
    for bit in range(bits):
        came = lax.ppermute(message, "z", [(z, z ^ (1 << bit)) for z in range(zs)])
        if bit < bits - 1:
            message, mine = call(
                functools.partial(line_step_kernel, bit), state, [message, came, mine], [VMEM] * 3
            )
    parts, rim_grad = call(
        functools.partial(line_last_kernel, bits - 1, factor),
        [((slots, share, width), BF16), ((border, width), F32)],
        [message, came, mine],
        [VMEM] * 3,
    )
    came = lax.all_to_all(parts, PLANE, 0, 0)
    node_grad, *grads = call(
        finish_kernel,
        [((rows, width), F32) for rows in (count_p, 3 * width, width, 2 * width, width)],
        [came, rim_grad, local_grad],
        [VMEM, VMEM, VMEM],
    )
    return (new_nodes, new_edges, node_grad, *grads)


def solution(mesh):
    strips, subs = mesh.devices.shape
    grid = Mesh(mesh.devices.reshape(strips, subs // 2, 2), ALL)
    rows = P(ALL, None)
    line = P(ALL)
    return jax.shard_map(
        shards,
        mesh=grid,
        in_specs=(rows, rows, line, line, line, P(), P(), P(), P(), rows, rows),
        out_specs=(rows, rows, rows, P(), P(), P(), P()),
        check_vma=False,
    )
```

```python
import functools
import math

import jax
import jax.numpy as jnp
from jax import lax
from jax.experimental import pallas as pl
from jax.experimental.pallas import tpu as pltpu
from jax.sharding import Mesh
from jax.sharding import PartitionSpec as P

EPS = 1e-05
CHUNK = 1024
SPLIT = 2
PLANE = ("strip", "y")
ALL = ("strip", "z", "y")
F32 = jnp.float32
BF16 = jnp.bfloat16
VMEM = pl.BlockSpec(memory_space=pltpu.VMEM)
SMEM = pl.BlockSpec(memory_space=pltpu.SMEM)
HBM = pl.BlockSpec(memory_space=pltpu.HBM)
SEM = pltpu.SemaphoreType.DMA


def mm(left, right):
    return jnp.dot(left, right, preferred_element_type=F32)


def mm_nt(left, right):
    return lax.dot_general(left, right, (((1,), (1,)), ((), ())), preferred_element_type=F32)


def mm_tn(left, right):
    return lax.dot_general(left, right, (((0,), (0,)), ((), ())), preferred_element_type=F32)


def norm_rows(values):
    centre = values - jnp.mean(values, axis=1, keepdims=True)
    scale = lax.rsqrt(jnp.mean(centre * centre, axis=1, keepdims=True) + EPS)
    return (centre * scale, scale)


def norm_back(normed, scale, upstream):
    first = jnp.mean(upstream, axis=1, keepdims=True)
    second = jnp.mean(upstream * normed, axis=1, keepdims=True)
    return scale * (upstream - first - normed * second)


def silu_and_slope(values):
    sig = 0.5 + 0.5 * jnp.tanh(0.5 * values)
    act = values * sig
    return (act, sig + act * (1.0 - sig))


def found(codes, blocks):
    lane = lax.broadcasted_iota(jnp.int32, codes.shape, 1)
    one, zero = jnp.ones((), BF16), jnp.zeros((), BF16)
    width = codes.shape[1]
    return jnp.concatenate(
        [
            jnp.where(codes == (lane + width * k).astype(F32).astype(BF16), one, zero)
            for k in range(blocks)
        ],
        axis=1,
    )


def found_t(line, size):
    place = lax.broadcasted_iota(jnp.int32, (size, line.shape[1]), 0).astype(F32).astype(BF16)
    one, zero = jnp.ones((), BF16), jnp.zeros((), BF16)
    return jnp.where(place == line.astype(F32).astype(BF16), one, zero)


def in_hbm(value):
    return pltpu.with_memory_space_constraint(value, pltpu.HBM)


def call(kernel, outs, ins, specs, scratch=(), out_specs=None, limit=24):
    out_specs = [VMEM] * len(outs) if out_specs is None else out_specs
    return pl.pallas_call(
        kernel,
        out_shape=[
            pltpu.HBM(shape, dtype) if spec is HBM else jax.ShapeDtypeStruct(shape, dtype)
            for (shape, dtype), spec in zip(outs, out_specs)
        ],
        in_specs=specs,
        out_specs=out_specs,
        scratch_shapes=list(scratch),
        compiler_params=pltpu.CompilerParams(vmem_limit_bytes=limit * 2**20),
    )(*[in_hbm(value) if spec is HBM else value for value, spec in zip(ins, specs)])


def column_kernel(nodes, even, odd, out):
    border = even.shape[0]
    out[:border] = nodes[:border]
    out[border : 2 * border] = even[...]
    out[2 * border :] = odd[...]


def swapped(value, axes):
    count = lax.axis_size(axes)
    even = [(k, k ^ 1) for k in range(count)]
    odd = [(k, min(max(((k + 1) ^ 1) - 1, 0), count - 1)) for k in range(count)]
    return lax.ppermute(value, axes, even), lax.ppermute(value, axes, odd)


def early_kernel(
    nodes,
    edges,
    edge_cot,
    info,
    w_edge_in,
    send_codes,
    recv_codes,
    edges_t,
    pre_part,
    cot_part,
    tables,
):
    count_p, width = nodes.shape

    @pl.when(pl.program_id(0) == 0)
    def prepare():
        tables[:count_p] = mm(nodes[...], w_edge_in[width : 2 * width]).astype(BF16)
        tables[count_p:] = w_edge_in[2 * width :]

    columns = info[0].T
    edge = edges[...]
    cot = edge_cot[...].astype(F32)
    recv = jnp.broadcast_to(columns[:, 1:2], edge.shape).astype(F32).astype(BF16)
    recv_codes[...] = recv
    send_codes[...] = jnp.broadcast_to(columns[:, 2:3], edge.shape).astype(F32).astype(BF16)
    recv = found(recv, count_p // width)
    pre_part[...] = mm(jnp.concatenate([recv, edge], axis=1), tables[...])
    edges_t[0] = edge.T
    cot_part[...] = (cot - jnp.mean(cot, axis=1, keepdims=True)).astype(BF16)


def layer_kernel(
    edge_count,
    nodes_in,
    own_column,
    even_column,
    odd_column,
    edges_in,
    info_in,
    send_codes_in,
    recv_codes_in,
    edges_t_in,
    pre_part_in,
    cot_part_in,
    w_edge_in_in,
    w_edge_out_in,
    w_node_in_in,
    w_node_out_in,
    node_cot_in,
    new_nodes_out,
    new_edges_out,
    local_grad,
    parts,
    nodes,
    edges,
    info,
    send_codes,
    recv_codes,
    edges_t,
    pre_part,
    cot_part,
    w_edge_in,
    w_edge_out,
    w_node_in,
    w_node_out,
    node_cot,
    new_nodes,
    new_edges,
    near_rows,
    far_rows,
    tables,
    centring,
    back,
    means,
    hidden,
    slope,
    normed,
    scale,
    sums,
    ge_out,
    agg,
    packed,
    kept,
    columns,
    small_sems,
    sems,
    out_sems,
    last_sem,
):
    count_p, width = nodes.shape
    border = own_column.shape[0] // 3
    slots = parts.shape[0]
    strips = slots // 2
    chunks, _, chunk = edges_t.shape
    block = chunk // SPLIT
    half = block // 2
    share = parts.shape[1] - 2 * border
    my_strip, my_y = lax.axis_index("strip"), lax.axis_index("y")
    live_count = edge_count[0]

    small = [
        pltpu.make_async_copy(source, target, small_sems.at[k])
        for k, (source, target) in enumerate(
            [
                (nodes_in, nodes),
                (w_edge_in_in, w_edge_in),
                (w_edge_out_in, w_edge_out),
                (w_node_in_in, w_node_in),
                (w_node_out_in, w_node_out),
                (node_cot_in, node_cot),
            ]
        )
    ]

    def span(step):
        return pl.ds(pl.multiple_of(step * chunk, chunk), chunk)

    def block_rows(step, part):
        return pl.ds(pl.multiple_of(step * chunk + part * block, block), block)

    def block_pairs(step, part):
        return pl.ds(pl.multiple_of((step * SPLIT + part) * half, half), half)

    def fetch(step, which):
        rows = span(step)
        pairs = [
            (send_codes_in.at[rows], send_codes.at[rows]),
            (pre_part_in.at[rows], pre_part.at[rows]),
            (info_in.at[step], info.at[step]),
            (edges_in.at[rows], edges.at[rows]),
            (recv_codes_in.at[rows], recv_codes.at[rows]),
            (cot_part_in.at[rows], cot_part.at[rows]),
            (edges_t_in.at[step], edges_t.at[step]),
        ]
        return [pltpu.make_async_copy(*pairs[k], sems.at[k, step]) for k in which]

    def emit(step):
        rows = span(step)
        return pltpu.make_async_copy(
            new_edges.at[rows], new_edges_out.at[rows], out_sems.at[step]
        )

    def paired(value):
        return jnp.concatenate([value[:half], value[half:]], axis=1)

    def unpaired(value):
        return jnp.concatenate([value[:, :width], value[:, width:]], axis=0)

    def twice(block):
        zero = jnp.zeros_like(block)
        return jnp.concatenate(
            [
                jnp.concatenate([block, zero], axis=1),
                jnp.concatenate([zero, block], axis=1),
            ],
            axis=0,
        )

    ahead, behind = range(4), range(4, 7)
    for copy in small[:3] + fetch(0, ahead) + small[3:]:
        copy.start()
    for step in range(1, chunks):
        for copy in fetch(step, ahead):
            copy.start()
    for step in range(chunks):
        for copy in fetch(step, behind):
            copy.start()
    for copy in small[:3]:
        copy.wait()

    near_rows[...] = nodes[...]
    for k, column in enumerate((own_column, even_column, odd_column)):
        for part in range(3):
            columns[3 * k + part] = column[part * border : (part + 1) * border]

    def partner(mine, step):
        if step == 0:
            return 0
        is_odd = lax.rem(mine, 2)
        return 1 + is_odd if step > 0 else 2 - is_odd

    spot = 0
    for d_strip in (-1, 0, 1):
        column = partner(my_strip, d_strip)
        for d_sub in (-1, 0, 1):
            if d_strip == 0 and d_sub == 0:
                continue
            rows = slice(spot * border, (spot + 1) * border)
            far_rows[rows] = columns[3 * column + partner(my_y, d_sub)]
            spot += 1
    tables[:, :width] = mm(near_rows[...], w_edge_in[:width]).astype(BF16)
    tables[:, width:] = mm(far_rows[...], w_edge_in[:width]).astype(BF16)
    weight = w_edge_out[...].astype(F32)
    centring[...] = twice(weight - jnp.mean(weight, axis=1, keepdims=True)).astype(BF16)
    back[...] = twice(weight).astype(BF16)
    means[...] = twice(jnp.full((width, width), 1.0 / width, F32)).astype(BF16)

    row = lax.broadcasted_iota(jnp.int32, (half, 2 * width), 0)
    lane = lax.broadcasted_iota(jnp.int32, (half, 2 * width), 1)
    edge_row = jnp.where(lane < width, row, row + half)
    agg[...] = jnp.zeros_like(agg)

    def forward(step, carry):
        for copy in fetch(step, ahead):
            copy.wait()
        recv_t = found_t(info[step][1:2], count_p)
        units = []
        for part in range(SPLIT):
            rows, pairs = block_rows(step, part), block_pairs(step, part)
            codes = send_codes[rows]
            begun = pre_part[rows]
            edge = paired(edges[rows].astype(F32))
            place = jnp.where(codes < 0, -1 - codes, codes)
            picked = mm(found(place, count_p // width), tables[...])
            beyond = codes.astype(F32) < 0.0
            pre = begun + jnp.where(beyond, picked[:, width:], picked[:, :width])
            act, bend = silu_and_slope(paired(pre))
            act = act.astype(BF16)
            centre = mm(act, centring[...])
            spare = mm((centre * centre).astype(BF16), means[...])
            live = edge_row < live_count - step * chunk - part * block
            factor = jnp.where(live, lax.rsqrt(spare + EPS), 0.0)
            unit = centre * factor
            slope[pairs] = bend
            hidden[rows] = unpaired(act)
            scale[pairs] = factor
            normed[pairs] = unit
            new_edges[rows] = unpaired((edge + unit).astype(BF16))
            units.append(unpaired(unit.astype(BF16)))
        agg[...] += mm(recv_t, jnp.concatenate(units, axis=0))
        emit(step).start()
        return carry

    lax.fori_loop(0, chunks, forward, 0)

    for copy in small[3:]:
        copy.wait()
    joined = jnp.concatenate([nodes[...], agg[...].astype(BF16)], axis=1)
    node_pre = mm(joined, w_node_in[...])
    node_act, node_slope = silu_and_slope(node_pre)
    node_act = node_act.astype(BF16)
    node_unit, node_scale = norm_rows(mm(node_act, w_node_out[...]))
    new_nodes[...] = (nodes[...].astype(F32) + node_unit).astype(BF16)
    cot = node_cot[...].astype(F32)
    d_outer = norm_back(node_unit, node_scale, cot).astype(BF16)
    d_pre = (mm_nt(d_outer, w_node_out[...]) * node_slope).astype(BF16)
    d_joined = mm_nt(d_pre, w_node_in[...])
    d_agg = d_joined[:, width:]
    d_agg = (d_agg - jnp.mean(d_agg, axis=1, keepdims=True)).astype(BF16)
    agg[...] = cot + d_joined[:, :width]
    kept[:, : 2 * width] = joined
    kept[:, 2 * width : 3 * width] = node_act
    kept[:, 3 * width : 4 * width] = d_outer
    kept[:, 4 * width :] = d_pre
    node_copy = pltpu.make_async_copy(new_nodes, new_nodes_out, last_sem)
    node_copy.start()

    sums[...] = jnp.zeros_like(sums)
    ge_out[...] = jnp.zeros_like(ge_out)

    def backward(step, carry):
        for copy in fetch(step, behind):
            copy.wait()
        index = info[step]
        turned = jnp.concatenate(
            [found_t(index[1:2], count_p), found_t(index[0:1], count_p), edges_t[step]], axis=0
        )
        acts, outs, ins = [], [], []
        for part in range(SPLIT):
            rows, pairs = block_rows(step, part), block_pairs(step, part)
            cot = cot_part[rows].astype(F32)
            recv = found(recv_codes[rows], count_p // width)
            unit = normed[pairs]
            acts.append(hidden[rows])
            beyond = send_codes[rows] < 0
            upstream = paired(cot + mm(recv, d_agg))
            along = mm((upstream * unit).astype(BF16), means[...])
            d_out = (scale[pairs] * (upstream - unit * along)).astype(BF16)
            outs.append(unpaired(d_out))
            d_in = unpaired((mm_nt(d_out, back[...]) * slope[pairs]).astype(BF16))
            zero = jnp.zeros_like(d_in)
            ins.append(
                jnp.concatenate(
                    [jnp.where(beyond, zero, d_in), jnp.where(beyond, d_in, zero)], axis=1
                )
            )
        ge_out[...] += mm_tn(jnp.concatenate(acts, axis=0), jnp.concatenate(outs, axis=0))
        sums[...] += mm(turned, jnp.concatenate(ins, axis=0))
        return carry

    lax.fori_loop(0, chunks, backward, 0)

    recv_sums = (sums[:count_p, :width] + sums[:count_p, width:]).astype(BF16)
    near_sums = sums[count_p : 2 * count_p, :width].astype(BF16)
    far_sums = sums[count_p : 2 * count_p, width:].astype(BF16)
    edge_sums = sums[2 * count_p :, :width] + sums[2 * count_p :, width:]
    packed[:width] = (mm_tn(near_rows[...], near_sums) + mm_tn(far_rows[...], far_sums)).astype(BF16)
    packed[width : 2 * width] = mm_tn(nodes[...], recv_sums).astype(BF16)
    packed[4 * width : 6 * width] = mm_tn(kept[:, : 2 * width], kept[:, 4 * width :]).astype(BF16)
    packed[6 * width : 7 * width] = mm_tn(
        kept[:, 2 * width : 3 * width], kept[:, 3 * width : 4 * width]
    ).astype(BF16)
    packed[2 * width : 3 * width] = edge_sums.astype(BF16)
    packed[3 * width : 4 * width] = ge_out[...].astype(BF16)
    if packed.shape[0] > 7 * width:
        packed[7 * width :] = jnp.zeros((packed.shape[0] - 7 * width, width), BF16)
    local_grad[...] = (
        agg[...]
        + mm_nt(near_sums, w_edge_in[:width])
        + mm_nt(recv_sums, w_edge_in[width : 2 * width])
    )
    owed = mm_nt(far_sums, w_edge_in[:width]).astype(BF16)
    for slot in range(slots):
        parts[slot, :share] = packed[slot * share : (slot + 1) * share]
        parts[slot, share:] = jnp.zeros((2 * border, width), BF16)
    spot = 0
    for d_strip in (-1, 0, 1):
        strip = my_strip + d_strip
        for d_sub in (-1, 0, 1):
            if d_strip == 0 and d_sub == 0:
                continue
            if d_sub == 0:
                slot, part = 2 * strip + my_y, 0
            elif d_sub == 1:
                slot, part = 2 * strip + 1 - my_y, my_y
            else:
                slot, part = 2 * strip + 1 - my_y, 1 - my_y
            first = pl.multiple_of(share + part * border, 16)
            block = owed[spot * border : (spot + 1) * border]

            @pl.when((strip >= 0) & (strip < strips))
            def put(slot=slot, first=first, block=block):
                parts[slot, pl.ds(first, border), :] = block

            spot += 1
    for step in range(chunks):
        emit(step).wait()
    node_copy.wait()


def plane_sum_kernel(came, message, mine):
    border = mine.shape[0]
    share = message.shape[0] - border
    total = came[0].astype(F32)
    for slot in range(1, came.shape[0]):
        total = total + came[slot].astype(F32)
    mine[...] = total[share : share + border]
    message[:share] = total[:share].astype(BF16)
    message[share:] = total[share + border :].astype(BF16)


def line_sum_kernel(factor, mine, *refs):
    messages, (out, rim_grad, held) = refs[:-3], refs[-3:]
    border = mine.shape[0]
    share = out.shape[1]
    for k, message in enumerate(messages):
        held[k] = message[...].astype(F32)
    my_z, my_y = lax.axis_index("z"), lax.axis_index("y")
    total = held[lax.bitwise_xor(my_z, 0), :share]
    for z in range(1, len(messages)):
        total = total + held[lax.bitwise_xor(my_z, z), :share]
    total = (total * factor).astype(BF16)
    for target in range(out.shape[0]):
        out[target] = total
    source = my_z - 1 + 2 * my_y
    inside = (source >= 0) & (source < len(messages))
    passed = held[lax.bitwise_xor(my_z, jnp.clip(source, 0, len(messages) - 1)), share:]
    rim_grad[...] = mine[...] + jnp.where(inside, passed, 0.0)


def finish_kernel(came, rim_grad, local_grad, node_grad, *outs):
    border = rim_grad.shape[0]
    share = came.shape[1]
    node_grad[...] = local_grad[...]
    node_grad[:border] += rim_grad[...]
    start = 0
    for out in outs:
        size = out.shape[0]
        done = 0
        while done < size:
            slot, offset = divmod(start + done, share)
            step = min(size - done, share - offset)
            out[done : done + step] = came[slot, offset : offset + step].astype(F32)
            done += step
        start += size


def shards(
    node_latents,
    edge_latents,
    senders,
    receivers,
    edge_count,
    w_edge_in,
    w_edge_out,
    w_node_in,
    w_node_out,
    node_cotangent,
    edge_cotangent,
):
    count_p, width = node_latents.shape
    count_e = edge_latents.shape[0]
    border = count_p // 8
    strips, zs, ys = (lax.axis_size(axis) for axis in ALL)
    subs = zs * ys
    slots = strips * ys
    my_strip, my_z, my_y = (lax.axis_index(axis).astype(jnp.int32) for axis in ALL)
    my_sub = my_z * ys + my_y

    even, odd = swapped(node_latents[:border], ("z", "y"))
    (own_column,) = call(
        column_kernel, [((3 * border, width), BF16)], [node_latents[:border], even, odd], [VMEM] * 3
    )
    even_column, odd_column = swapped(own_column, "strip")

    owner = senders // count_p
    within = senders % count_p
    is_local = owner == my_strip * subs + my_sub
    block = (owner // subs - my_strip + 1) * 3 + (owner % subs - my_sub + 1)
    block = jnp.where(block > 4, block - 1, block)
    send_index = jnp.where(is_local, within, block * border + jnp.minimum(within, border - 1))
    codes = jnp.where(is_local, send_index, -1 - send_index)
    chunk = min(CHUNK, count_e)
    chunks = count_e // chunk
    info = jnp.stack(
        [
            value.reshape(chunks, chunk)
            for value in [send_index, receivers, codes]
            + [jnp.zeros_like(receivers)] * 5
        ],
        axis=1,
    )

    def by_rows(*shape):
        return pl.BlockSpec(shape, lambda i: (i, 0))

    def by_chunk(*shape):
        return pl.BlockSpec((1, *shape), lambda i: (i, 0, 0))

    def whole(*shape):
        return pl.BlockSpec(shape, lambda i: (0, 0))

    info, own_column = lax.optimization_barrier((info, own_column))
    early = pl.pallas_call(
        early_kernel,
        grid=(chunks,),
        out_shape=[
            pltpu.HBM(shape, dtype)
            for shape, dtype in [
                ((count_e, width), BF16),
                ((count_e, width), BF16),
                ((chunks, width, chunk), BF16),
                ((count_e, width), F32),
                ((count_e, width), BF16),
            ]
        ],
        in_specs=[
            whole(count_p, width),
            by_rows(chunk, width),
            by_rows(chunk, width),
            by_chunk(8, chunk),
            whole(3 * width, width),
        ],
        out_specs=[
            by_rows(chunk, width),
            by_rows(chunk, width),
            by_chunk(width, chunk),
            by_rows(chunk, width),
            by_rows(chunk, width),
        ],
        scratch_shapes=[pltpu.VMEM((count_p + width, width), BF16)],
        compiler_params=pltpu.CompilerParams(vmem_limit_bytes=32 * 2**20),
    )(
        in_hbm(node_latents),
        in_hbm(edge_latents),
        in_hbm(edge_cotangent),
        info,
        in_hbm(w_edge_in),
    )

    share = -(-7 * width // (slots * 16)) * 16

    def like(value):
        return pltpu.VMEM(value.shape, value.dtype)

    new_nodes, new_edges, local_grad, parts = call(
        layer_kernel,
        [
            ((count_p, width), BF16),
            ((count_e, width), BF16),
            ((count_p, width), F32),
            ((slots, share + 2 * border, width), BF16),
        ],
        [
            edge_count,
            node_latents,
            own_column,
            even_column,
            odd_column,
            edge_latents,
            info,
            *early,
            w_edge_in,
            w_edge_out,
            w_node_in,
            w_node_out,
            node_cotangent,
        ],
        [SMEM, HBM] + [VMEM] * 3 + [HBM] * 12,
        [
            like(node_latents),
            like(edge_latents),
            like(info),
            *[like(value) for value in early],
            like(w_edge_in),
            like(w_edge_out),
            like(w_node_in),
            like(w_node_out),
            like(node_cotangent),
            pltpu.VMEM((count_p, width), BF16),
            pltpu.VMEM((count_e, width), BF16),
            pltpu.VMEM((count_p, width), BF16),
            pltpu.VMEM((8 * border, width), BF16),
            pltpu.VMEM((count_p, 2 * width), BF16),
            pltpu.VMEM((2 * width, 2 * width), BF16),
            pltpu.VMEM((2 * width, 2 * width), BF16),
            pltpu.VMEM((2 * width, 2 * width), BF16),
            pltpu.VMEM((count_e, width), BF16),
            pltpu.VMEM((count_e // 2, 2 * width), F32),
            pltpu.VMEM((count_e // 2, 2 * width), F32),
            pltpu.VMEM((count_e // 2, 2 * width), F32),
            pltpu.VMEM((2 * count_p + width, 2 * width), F32),
            pltpu.VMEM((width, width), F32),
            pltpu.VMEM((count_p, width), F32),
            pltpu.VMEM((slots * share, width), BF16),
            pltpu.VMEM((count_p, 5 * width), BF16),
            pltpu.VMEM((9, border, width), BF16),
            SEM((6,)),
            SEM((7, chunks)),
            SEM((chunks,)),
            SEM,
        ],
        [HBM, HBM, VMEM, VMEM],
        limit=48,
    )

    came = lax.all_to_all(parts, PLANE, 0, 0)
    state = [((share + border, width), BF16), ((border, width), F32)]
    message, mine = call(plane_sum_kernel, state, [came], [VMEM])
    factor = 1.0 / math.sqrt(count_e * strips * subs)
    messages = [message] + [
        lax.ppermute(message, "z", [(z, z ^ k) for z in range(zs)]) for k in range(1, zs)
    ]
    parts, rim_grad = call(
        functools.partial(line_sum_kernel, factor),
        [((slots, share, width), BF16), ((border, width), F32)],
        [mine, *messages],
        [VMEM] * (1 + zs),
        [pltpu.VMEM((zs, share + border, width), F32)],
    )
    came = lax.all_to_all(parts, PLANE, 0, 0)
    node_grad, *grads = call(
        finish_kernel,
        [((rows, width), F32) for rows in (count_p, 3 * width, width, 2 * width, width)],
        [came, rim_grad, local_grad],
        [VMEM, VMEM, VMEM],
    )
    return (new_nodes, new_edges, node_grad, *grads)


def solution(mesh):
    strips, subs = mesh.devices.shape
    grid = Mesh(mesh.devices.reshape(strips, subs // 2, 2), ALL)
    rows = P(ALL, None)
    line = P(ALL)
    return jax.shard_map(
        shards,
        mesh=grid,
        in_specs=(rows, rows, line, line, line, P(), P(), P(), P(), rows, rows),
        out_specs=(rows, rows, rows, P(), P(), P(), P()),
        check_vma=False,
    )
```

```python
import functools
import math

import jax
import jax.numpy as jnp
from jax import lax
from jax.experimental import pallas as pl
from jax.experimental.pallas import tpu as pltpu
from jax.sharding import Mesh
from jax.sharding import PartitionSpec as P

EPS = 1e-05
CHUNK = 1024
SPLIT = 2
PLANE = ("strip", "y")
ALL = ("strip", "z", "y")
F32 = jnp.float32
BF16 = jnp.bfloat16
VMEM = pl.BlockSpec(memory_space=pltpu.VMEM)
SMEM = pl.BlockSpec(memory_space=pltpu.SMEM)
HBM = pl.BlockSpec(memory_space=pltpu.HBM)
SEM = pltpu.SemaphoreType.DMA


def mm(left, right):
    return jnp.dot(left, right, preferred_element_type=F32)


def mm_nt(left, right):
    return lax.dot_general(left, right, (((1,), (1,)), ((), ())), preferred_element_type=F32)


def mm_tn(left, right):
    return lax.dot_general(left, right, (((0,), (0,)), ((), ())), preferred_element_type=F32)


def norm_rows(values):
    centre = values - jnp.mean(values, axis=1, keepdims=True)
    scale = lax.rsqrt(jnp.mean(centre * centre, axis=1, keepdims=True) + EPS)
    return (centre * scale, scale)


def norm_back(normed, scale, upstream):
    first = jnp.mean(upstream, axis=1, keepdims=True)
    second = jnp.mean(upstream * normed, axis=1, keepdims=True)
    return scale * (upstream - first - normed * second)


def silu_and_slope(values):
    sig = 0.5 + 0.5 * jnp.tanh(0.5 * values)
    act = values * sig
    return (act, sig + act * (1.0 - sig))


def found(codes, blocks):
    lane = lax.broadcasted_iota(jnp.int32, codes.shape, 1)
    one, zero = jnp.ones((), BF16), jnp.zeros((), BF16)
    width = codes.shape[1]
    return jnp.concatenate(
        [
            jnp.where(codes == (lane + width * k).astype(F32).astype(BF16), one, zero)
            for k in range(blocks)
        ],
        axis=1,
    )


def found_t(line, size):
    place = lax.broadcasted_iota(jnp.int32, (size, line.shape[1]), 0).astype(F32).astype(BF16)
    one, zero = jnp.ones((), BF16), jnp.zeros((), BF16)
    return jnp.where(place == line.astype(F32).astype(BF16), one, zero)


def in_hbm(value):
    return pltpu.with_memory_space_constraint(value, pltpu.HBM)


def call(kernel, outs, ins, specs, scratch=(), out_specs=None, limit=24):
    out_specs = [VMEM] * len(outs) if out_specs is None else out_specs
    return pl.pallas_call(
        kernel,
        out_shape=[
            pltpu.HBM(shape, dtype) if spec is HBM else jax.ShapeDtypeStruct(shape, dtype)
            for (shape, dtype), spec in zip(outs, out_specs)
        ],
        in_specs=specs,
        out_specs=out_specs,
        scratch_shapes=list(scratch),
        compiler_params=pltpu.CompilerParams(vmem_limit_bytes=limit * 2**20),
    )(*[in_hbm(value) if spec is HBM else value for value, spec in zip(ins, specs)])


def column_kernel(nodes, even, odd, out):
    border = even.shape[0]
    out[:border] = nodes[:border]
    out[border : 2 * border] = even[...]
    out[2 * border :] = odd[...]


def swapped(value, axes):
    count = lax.axis_size(axes)
    even = [(k, k ^ 1) for k in range(count)]
    odd = [(k, min(max(((k + 1) ^ 1) - 1, 0), count - 1)) for k in range(count)]
    return lax.ppermute(value, axes, even), lax.ppermute(value, axes, odd)


def early_kernel(
    nodes_in,
    edges_in,
    edge_cot_in,
    senders_in,
    receivers_in,
    w_edge_in_in,
    edges,
    send_codes,
    recv_codes,
    edges_t,
    pre_part,
    cot_part,
    info,
    tables,
    nodes,
    edge_cot,
    senders,
    receivers,
    w_edge_in,
    small_sems,
    sems,
):
    count_p, width = nodes_in.shape
    chunks, _, chunk = info.shape
    border = count_p // 8
    my_strip = lax.axis_index("strip")
    subs = lax.axis_size("z") * lax.axis_size("y")
    my_sub = lax.axis_index("z") * lax.axis_size("y") + lax.axis_index("y")
    place_bits, sub_bits = count_p.bit_length() - 1, subs.bit_length() - 1

    def fetch(step):
        rows = pl.ds(pl.multiple_of(step * chunk, chunk), chunk)
        return [
            pltpu.make_async_copy(edges_in.at[rows], edges.at[rows], sems.at[0, step]),
            pltpu.make_async_copy(edge_cot_in.at[rows], edge_cot.at[rows], sems.at[1, step]),
        ]

    small = [
        pltpu.make_async_copy(source, target, small_sems.at[k])
        for k, (source, target) in enumerate(
            [
                (nodes_in, nodes),
                (w_edge_in_in, w_edge_in),
                (senders_in, senders),
                (receivers_in, receivers),
            ]
        )
    ]
    for copy in small:
        copy.start()
    for step in range(chunks):
        for copy in fetch(step):
            copy.start()
    for copy in small:
        copy.wait()
    tables[:count_p] = mm(nodes[...], w_edge_in[width : 2 * width]).astype(BF16)
    tables[count_p:] = w_edge_in[2 * width :]
    line = lax.broadcasted_iota(jnp.int32, (8, chunk), 0)

    def one(step, carry):
        rows = pl.ds(pl.multiple_of(step * chunk, chunk), chunk)
        sender = jnp.broadcast_to(senders[step], (8, chunk))
        receiver = jnp.broadcast_to(receivers[step], (8, chunk))
        owner = lax.shift_right_logical(sender, place_bits)
        within = lax.bitwise_and(sender, count_p - 1)
        d_strip = lax.shift_right_logical(owner, sub_bits) - my_strip
        d_sub = lax.bitwise_and(owner, subs - 1) - my_sub
        spot = 3 * d_strip + d_sub + 4
        spot = jnp.where(spot > 4, spot - 1, spot)
        near = (d_strip == 0) & (d_sub == 0)
        spot = jnp.where(near, within, spot * border + jnp.minimum(within, border - 1))
        index = jnp.where(line == 0, spot, receiver)
        index = jnp.where(line == 2, jnp.where(near, spot, -1 - spot), index)
        info[step] = index
        columns = index.T
        for copy in fetch(step):
            copy.wait()
        edge = edges[rows]
        cot = edge_cot[rows].astype(F32)
        recv = jnp.broadcast_to(columns[:, 1:2], edge.shape).astype(F32).astype(BF16)
        recv_codes[rows] = recv
        send_codes[rows] = jnp.broadcast_to(columns[:, 2:3], edge.shape).astype(F32).astype(BF16)
        recv = found(recv, count_p // width)
        pre_part[rows] = mm(jnp.concatenate([recv, edge], axis=1), tables[...])
        edges_t[step] = edge.T
        cot_part[rows] = (cot - jnp.mean(cot, axis=1, keepdims=True)).astype(BF16)
        return carry

    lax.fori_loop(0, chunks, one, 0)


def layer_kernel(
    edge_count,
    nodes,
    own_column,
    even_column,
    odd_column,
    edges,
    send_codes,
    recv_codes,
    edges_t,
    pre_part,
    cot_part,
    info,
    w_edge_in,
    w_edge_out,
    w_node_in,
    w_node_out,
    node_cot,
    new_nodes_out,
    new_edges_out,
    local_grad,
    parts,
    new_nodes,
    new_edges,
    near_rows,
    far_rows,
    tables,
    centring,
    back,
    means,
    hidden,
    slope,
    normed,
    scale,
    sums,
    ge_out,
    agg,
    packed,
    kept,
    columns,
    out_sems,
    last_sem,
):
    count_p, width = nodes.shape
    border = own_column.shape[0] // 3
    slots = parts.shape[0]
    strips = slots // 2
    chunks, _, chunk = edges_t.shape
    block = chunk // SPLIT
    half = block // 2
    share = parts.shape[1] - 2 * border
    my_strip, my_y = lax.axis_index("strip"), lax.axis_index("y")
    live_count = edge_count[0]

    def span(step):
        return pl.ds(pl.multiple_of(step * chunk, chunk), chunk)

    def block_rows(step, part):
        return pl.ds(pl.multiple_of(step * chunk + part * block, block), block)

    def block_pairs(step, part):
        return pl.ds(pl.multiple_of((step * SPLIT + part) * half, half), half)

    def emit(step):
        rows = span(step)
        return pltpu.make_async_copy(
            new_edges.at[rows], new_edges_out.at[rows], out_sems.at[step]
        )

    def paired(value):
        return jnp.concatenate([value[:half], value[half:]], axis=1)

    def unpaired(value):
        return jnp.concatenate([value[:, :width], value[:, width:]], axis=0)

    def twice(block):
        zero = jnp.zeros_like(block)
        return jnp.concatenate(
            [
                jnp.concatenate([block, zero], axis=1),
                jnp.concatenate([zero, block], axis=1),
            ],
            axis=0,
        )

    near_rows[...] = nodes[...]
    for k, column in enumerate((own_column, even_column, odd_column)):
        for part in range(3):
            columns[3 * k + part] = column[part * border : (part + 1) * border]

    def partner(mine, step):
        if step == 0:
            return 0
        is_odd = lax.rem(mine, 2)
        return 1 + is_odd if step > 0 else 2 - is_odd

    spot = 0
    for d_strip in (-1, 0, 1):
        column = partner(my_strip, d_strip)
        for d_sub in (-1, 0, 1):
            if d_strip == 0 and d_sub == 0:
                continue
            rows = slice(spot * border, (spot + 1) * border)
            far_rows[rows] = columns[3 * column + partner(my_y, d_sub)]
            spot += 1
    tables[:, :width] = mm(near_rows[...], w_edge_in[:width]).astype(BF16)
    tables[:, width:] = mm(far_rows[...], w_edge_in[:width]).astype(BF16)
    weight = w_edge_out[...].astype(F32)
    centring[...] = twice(weight - jnp.mean(weight, axis=1, keepdims=True)).astype(BF16)
    back[...] = twice(weight).astype(BF16)
    means[...] = twice(jnp.full((width, width), 1.0 / width, F32)).astype(BF16)

    row = lax.broadcasted_iota(jnp.int32, (half, 2 * width), 0)
    lane = lax.broadcasted_iota(jnp.int32, (half, 2 * width), 1)
    edge_row = jnp.where(lane < width, row, row + half)
    agg[...] = jnp.zeros_like(agg)

    def forward(step, carry):
        recv_t = found_t(info[step][1:2], count_p)
        units = []
        for part in range(SPLIT):
            rows, pairs = block_rows(step, part), block_pairs(step, part)
            codes = send_codes[rows]
            begun = pre_part[rows]
            edge = paired(edges[rows].astype(F32))
            place = jnp.where(codes < 0, -1 - codes, codes)
            picked = mm(found(place, count_p // width), tables[...])
            beyond = codes.astype(F32) < 0.0
            pre = begun + jnp.where(beyond, picked[:, width:], picked[:, :width])
            act, bend = silu_and_slope(paired(pre))
            act = act.astype(BF16)
            centre = mm(act, centring[...])
            spare = mm((centre * centre).astype(BF16), means[...])
            live = edge_row < live_count - step * chunk - part * block
            factor = jnp.where(live, lax.rsqrt(spare + EPS), 0.0)
            unit = centre * factor
            slope[pairs] = bend
            hidden[rows] = unpaired(act)
            scale[pairs] = factor
            normed[pairs] = unit
            new_edges[rows] = unpaired((edge + unit).astype(BF16))
            units.append(unpaired(unit.astype(BF16)))
        agg[...] += mm(recv_t, jnp.concatenate(units, axis=0))
        emit(step).start()
        return carry

    lax.fori_loop(0, chunks, forward, 0)

    joined = jnp.concatenate([nodes[...], agg[...].astype(BF16)], axis=1)
    node_pre = mm(joined, w_node_in[...])
    node_act, node_slope = silu_and_slope(node_pre)
    node_act = node_act.astype(BF16)
    node_unit, node_scale = norm_rows(mm(node_act, w_node_out[...]))
    new_nodes[...] = (nodes[...].astype(F32) + node_unit).astype(BF16)
    cot = node_cot[...].astype(F32)
    d_outer = norm_back(node_unit, node_scale, cot).astype(BF16)
    d_pre = (mm_nt(d_outer, w_node_out[...]) * node_slope).astype(BF16)
    d_joined = mm_nt(d_pre, w_node_in[...])
    d_agg = d_joined[:, width:]
    d_agg = (d_agg - jnp.mean(d_agg, axis=1, keepdims=True)).astype(BF16)
    agg[...] = cot + d_joined[:, :width]
    kept[:, : 2 * width] = joined
    kept[:, 2 * width : 3 * width] = node_act
    kept[:, 3 * width : 4 * width] = d_outer
    kept[:, 4 * width :] = d_pre
    node_copy = pltpu.make_async_copy(new_nodes, new_nodes_out, last_sem)
    node_copy.start()

    sums[...] = jnp.zeros_like(sums)
    ge_out[...] = jnp.zeros_like(ge_out)

    def backward(step, carry):
        index = info[step]
        turned = jnp.concatenate(
            [found_t(index[1:2], count_p), found_t(index[0:1], count_p), edges_t[step]], axis=0
        )
        acts, outs, ins = [], [], []
        for part in range(SPLIT):
            rows, pairs = block_rows(step, part), block_pairs(step, part)
            cot = cot_part[rows].astype(F32)
            recv = found(recv_codes[rows], count_p // width)
            unit = normed[pairs]
            acts.append(hidden[rows])
            beyond = send_codes[rows] < 0
            upstream = paired(cot + mm(recv, d_agg))
            along = mm((upstream * unit).astype(BF16), means[...])
            d_out = (scale[pairs] * (upstream - unit * along)).astype(BF16)
            outs.append(unpaired(d_out))
            d_in = unpaired((mm_nt(d_out, back[...]) * slope[pairs]).astype(BF16))
            zero = jnp.zeros_like(d_in)
            ins.append(
                jnp.concatenate(
                    [jnp.where(beyond, zero, d_in), jnp.where(beyond, d_in, zero)], axis=1
                )
            )
        ge_out[...] += mm_tn(jnp.concatenate(acts, axis=0), jnp.concatenate(outs, axis=0))
        sums[...] += mm(turned, jnp.concatenate(ins, axis=0))
        return carry

    lax.fori_loop(0, chunks, backward, 0)

    recv_sums = (sums[:count_p, :width] + sums[:count_p, width:]).astype(BF16)
    near_sums = sums[count_p : 2 * count_p, :width].astype(BF16)
    far_sums = sums[count_p : 2 * count_p, width:].astype(BF16)
    edge_sums = sums[2 * count_p :, :width] + sums[2 * count_p :, width:]
    packed[:width] = (mm_tn(near_rows[...], near_sums) + mm_tn(far_rows[...], far_sums)).astype(BF16)
    packed[width : 2 * width] = mm_tn(nodes[...], recv_sums).astype(BF16)
    packed[4 * width : 6 * width] = mm_tn(kept[:, : 2 * width], kept[:, 4 * width :]).astype(BF16)
    packed[6 * width : 7 * width] = mm_tn(
        kept[:, 2 * width : 3 * width], kept[:, 3 * width : 4 * width]
    ).astype(BF16)
    packed[2 * width : 3 * width] = edge_sums.astype(BF16)
    packed[3 * width : 4 * width] = ge_out[...].astype(BF16)
    if packed.shape[0] > 7 * width:
        packed[7 * width :] = jnp.zeros((packed.shape[0] - 7 * width, width), BF16)
    local_grad[...] = (
        agg[...]
        + mm_nt(near_sums, w_edge_in[:width])
        + mm_nt(recv_sums, w_edge_in[width : 2 * width])
    )
    owed = mm_nt(far_sums, w_edge_in[:width]).astype(BF16)
    for slot in range(slots):
        parts[slot, :share] = packed[slot * share : (slot + 1) * share]
        parts[slot, share:] = jnp.zeros((2 * border, width), BF16)
    spot = 0
    for d_strip in (-1, 0, 1):
        strip = my_strip + d_strip
        for d_sub in (-1, 0, 1):
            if d_strip == 0 and d_sub == 0:
                continue
            if d_sub == 0:
                slot, part = 2 * strip + my_y, 0
            elif d_sub == 1:
                slot, part = 2 * strip + 1 - my_y, my_y
            else:
                slot, part = 2 * strip + 1 - my_y, 1 - my_y
            first = pl.multiple_of(share + part * border, 16)
            block = owed[spot * border : (spot + 1) * border]

            @pl.when((strip >= 0) & (strip < strips))
            def put(slot=slot, first=first, block=block):
                parts[slot, pl.ds(first, border), :] = block

            spot += 1
    for step in range(chunks):
        emit(step).wait()
    node_copy.wait()


def plane_sum_kernel(came, message, mine):
    border = mine.shape[0]
    share = message.shape[0] - border
    total = came[0].astype(F32)
    for slot in range(1, came.shape[0]):
        total = total + came[slot].astype(F32)
    mine[...] = total[share : share + border]
    message[:share] = total[:share].astype(BF16)
    message[share:] = total[share + border :].astype(BF16)


def line_sum_kernel(factor, mine, *refs):
    messages, (out, rim_grad, held) = refs[:-3], refs[-3:]
    border = mine.shape[0]
    share = out.shape[1]
    for k, message in enumerate(messages):
        held[k] = message[...].astype(F32)
    my_z, my_y = lax.axis_index("z"), lax.axis_index("y")
    total = held[lax.bitwise_xor(my_z, 0), :share]
    for z in range(1, len(messages)):
        total = total + held[lax.bitwise_xor(my_z, z), :share]
    total = (total * factor).astype(BF16)
    for target in range(out.shape[0]):
        out[target] = total
    source = my_z - 1 + 2 * my_y
    inside = (source >= 0) & (source < len(messages))
    passed = held[lax.bitwise_xor(my_z, jnp.clip(source, 0, len(messages) - 1)), share:]
    rim_grad[...] = mine[...] + jnp.where(inside, passed, 0.0)


def finish_kernel(came, rim_grad, local_grad, node_grad, *outs):
    border = rim_grad.shape[0]
    share = came.shape[1]
    node_grad[...] = local_grad[...]
    node_grad[:border] += rim_grad[...]
    start = 0
    for out in outs:
        size = out.shape[0]
        done = 0
        while done < size:
            slot, offset = divmod(start + done, share)
            step = min(size - done, share - offset)
            out[done : done + step] = came[slot, offset : offset + step].astype(F32)
            done += step
        start += size


def shards(
    node_latents,
    edge_latents,
    senders,
    receivers,
    edge_count,
    w_edge_in,
    w_edge_out,
    w_node_in,
    w_node_out,
    node_cotangent,
    edge_cotangent,
):
    count_p, width = node_latents.shape
    count_e = edge_latents.shape[0]
    border = count_p // 8
    strips, zs, ys = (lax.axis_size(axis) for axis in ALL)
    subs = zs * ys
    slots = strips * ys
    even, odd = swapped(node_latents[:border], ("z", "y"))
    (own_column,) = call(
        column_kernel, [((3 * border, width), BF16)], [node_latents[:border], even, odd], [VMEM] * 3
    )
    even_column, odd_column = swapped(own_column, "strip")

    chunk = min(CHUNK, count_e)
    chunks = count_e // chunk
    early = call(
        early_kernel,
        [
            ((count_e, width), BF16),
            ((count_e, width), BF16),
            ((count_e, width), BF16),
            ((chunks, width, chunk), BF16),
            ((count_e, width), F32),
            ((count_e, width), BF16),
            ((chunks, 8, chunk), jnp.int32),
        ],
        [
            node_latents,
            edge_latents,
            edge_cotangent,
            senders.reshape(chunks, 1, chunk),
            receivers.reshape(chunks, 1, chunk),
            w_edge_in,
        ],
        [HBM] * 6,
        [
            pltpu.VMEM((count_p + width, width), BF16),
            pltpu.VMEM((count_p, width), BF16),
            pltpu.VMEM((count_e, width), BF16),
            pltpu.VMEM((chunks, 1, chunk), jnp.int32),
            pltpu.VMEM((chunks, 1, chunk), jnp.int32),
            pltpu.VMEM((3 * width, width), BF16),
            SEM((4,)),
            SEM((2, chunks)),
        ],
    )

    share = -(-7 * width // (slots * 16)) * 16

    new_nodes, new_edges, local_grad, parts = call(
        layer_kernel,
        [
            ((count_p, width), BF16),
            ((count_e, width), BF16),
            ((count_p, width), F32),
            ((slots, share + 2 * border, width), BF16),
        ],
        [
            edge_count,
            node_latents,
            own_column,
            even_column,
            odd_column,
            *early,
            w_edge_in,
            w_edge_out,
            w_node_in,
            w_node_out,
            node_cotangent,
        ],
        [SMEM] + [VMEM] * 16,
        [
            pltpu.VMEM((count_p, width), BF16),
            pltpu.VMEM((count_e, width), BF16),
            pltpu.VMEM((count_p, width), BF16),
            pltpu.VMEM((8 * border, width), BF16),
            pltpu.VMEM((count_p, 2 * width), BF16),
            pltpu.VMEM((2 * width, 2 * width), BF16),
            pltpu.VMEM((2 * width, 2 * width), BF16),
            pltpu.VMEM((2 * width, 2 * width), BF16),
            pltpu.VMEM((count_e, width), BF16),
            pltpu.VMEM((count_e // 2, 2 * width), F32),
            pltpu.VMEM((count_e // 2, 2 * width), F32),
            pltpu.VMEM((count_e // 2, 2 * width), F32),
            pltpu.VMEM((2 * count_p + width, 2 * width), F32),
            pltpu.VMEM((width, width), F32),
            pltpu.VMEM((count_p, width), F32),
            pltpu.VMEM((slots * share, width), BF16),
            pltpu.VMEM((count_p, 5 * width), BF16),
            pltpu.VMEM((9, border, width), BF16),
            SEM((chunks,)),
            SEM,
        ],
        [HBM, HBM, VMEM, VMEM],
        limit=24,
    )

    came = lax.all_to_all(parts, PLANE, 0, 0)
    state = [((share + border, width), BF16), ((border, width), F32)]
    message, mine = call(plane_sum_kernel, state, [came], [VMEM])
    factor = 1.0 / math.sqrt(count_e * strips * subs)
    messages = [message] + [
        lax.ppermute(message, "z", [(z, z ^ k) for z in range(zs)]) for k in range(1, zs)
    ]
    parts, rim_grad = call(
        functools.partial(line_sum_kernel, factor),
        [((slots, share, width), BF16), ((border, width), F32)],
        [mine, *messages],
        [VMEM] * (1 + zs),
        [pltpu.VMEM((zs, share + border, width), F32)],
    )
    came = lax.all_to_all(parts, PLANE, 0, 0)
    node_grad, *grads = call(
        finish_kernel,
        [((rows, width), F32) for rows in (count_p, 3 * width, width, 2 * width, width)],
        [came, rim_grad, local_grad],
        [VMEM, VMEM, VMEM],
    )
    return (new_nodes, new_edges, node_grad, *grads)


def solution(mesh):
    strips, subs = mesh.devices.shape
    grid = Mesh(mesh.devices.reshape(strips, subs // 2, 2), ALL)
    rows = P(ALL, None)
    line = P(ALL)
    return jax.shard_map(
        shards,
        mesh=grid,
        in_specs=(rows, rows, line, line, line, P(), P(), P(), P(), rows, rows),
        out_specs=(rows, rows, rows, P(), P(), P(), P()),
        check_vma=False,
    )
```

```python
import functools
import math

import jax
import jax.numpy as jnp
from jax import lax
from jax.experimental import pallas as pl
from jax.experimental.pallas import tpu as pltpu
from jax.sharding import Mesh
from jax.sharding import PartitionSpec as P

EPS = 1e-05
CHUNK = 1024
SPLIT = 2
UNROLL = 4
PLANE = ("strip", "y")
ALL = ("strip", "z", "y")
F32 = jnp.float32
BF16 = jnp.bfloat16
VMEM = pl.BlockSpec(memory_space=pltpu.VMEM)
SMEM = pl.BlockSpec(memory_space=pltpu.SMEM)
HBM = pl.BlockSpec(memory_space=pltpu.HBM)
SEM = pltpu.SemaphoreType.DMA


def mm(left, right):
    return jnp.dot(left, right, preferred_element_type=F32)


def mm_nt(left, right):
    return lax.dot_general(left, right, (((1,), (1,)), ((), ())), preferred_element_type=F32)


def mm_tn(left, right):
    return lax.dot_general(left, right, (((0,), (0,)), ((), ())), preferred_element_type=F32)


def norm_rows(values):
    centre = values - jnp.mean(values, axis=1, keepdims=True)
    scale = lax.rsqrt(jnp.mean(centre * centre, axis=1, keepdims=True) + EPS)
    return (centre * scale, scale)


def norm_back(normed, scale, upstream):
    first = jnp.mean(upstream, axis=1, keepdims=True)
    second = jnp.mean(upstream * normed, axis=1, keepdims=True)
    return scale * (upstream - first - normed * second)


def silu_and_slope(values):
    sig = 0.5 + 0.5 * jnp.tanh(0.5 * values)
    act = values * sig
    return (act, sig + act * (1.0 - sig))


def found(codes, blocks):
    lane = lax.broadcasted_iota(jnp.int32, codes.shape, 1)
    one, zero = jnp.ones((), BF16), jnp.zeros((), BF16)
    width = codes.shape[1]
    return jnp.concatenate(
        [
            jnp.where(codes == (lane + width * k).astype(F32).astype(BF16), one, zero)
            for k in range(blocks)
        ],
        axis=1,
    )


def found_t(line, size):
    place = lax.broadcasted_iota(jnp.int32, (size, line.shape[1]), 0).astype(F32).astype(BF16)
    one, zero = jnp.ones((), BF16), jnp.zeros((), BF16)
    return jnp.where(place == line.astype(F32).astype(BF16), one, zero)


def in_hbm(value):
    return pltpu.with_memory_space_constraint(value, pltpu.HBM)


def call(kernel, outs, ins, specs, scratch=(), out_specs=None, limit=24):
    out_specs = [VMEM] * len(outs) if out_specs is None else out_specs
    return pl.pallas_call(
        kernel,
        out_shape=[
            pltpu.HBM(shape, dtype) if spec is HBM else jax.ShapeDtypeStruct(shape, dtype)
            for (shape, dtype), spec in zip(outs, out_specs)
        ],
        in_specs=specs,
        out_specs=out_specs,
        scratch_shapes=list(scratch),
        compiler_params=pltpu.CompilerParams(vmem_limit_bytes=limit * 2**20),
    )(*[in_hbm(value) if spec is HBM else value for value, spec in zip(ins, specs)])


def column_kernel(edge_count, nodes, odd, even, out):
    border = even.shape[0]
    out[:border] = nodes[:border]
    out[border : 2 * border] = even[...]
    out[2 * border :] = odd[...]


def swapped(value, axes):
    count = lax.axis_size(axes)
    even = [(k, k ^ 1) for k in range(count)]
    odd = [(k, min(max(((k + 1) ^ 1) - 1, 0), count - 1)) for k in range(count)]
    from_odd = lax.ppermute(value, axes, odd)
    from_even = lax.ppermute(value, axes, even)
    return from_even, from_odd


def early_kernel(
    nodes_in,
    edges_in,
    edge_cot_in,
    senders_in,
    receivers_in,
    w_edge_in_in,
    edges,
    send_codes,
    recv_codes,
    edges_t,
    pre_part,
    cot_part,
    info,
    tables,
    nodes,
    edge_cot,
    senders,
    receivers,
    w_edge_in,
    small_sems,
    sems,
):
    count_p, width = nodes_in.shape
    chunks, _, chunk = info.shape
    border = count_p // 8
    my_strip = lax.axis_index("strip")
    subs = lax.axis_size("z") * lax.axis_size("y")
    my_sub = lax.axis_index("z") * lax.axis_size("y") + lax.axis_index("y")
    place_bits, sub_bits = count_p.bit_length() - 1, subs.bit_length() - 1

    def fetch(step):
        rows = pl.ds(pl.multiple_of(step * chunk, chunk), chunk)
        return [
            pltpu.make_async_copy(edges_in.at[rows], edges.at[rows], sems.at[0, step]),
            pltpu.make_async_copy(edge_cot_in.at[rows], edge_cot.at[rows], sems.at[1, step]),
        ]

    small = [
        pltpu.make_async_copy(source, target, small_sems.at[k])
        for k, (source, target) in enumerate(
            [
                (nodes_in, nodes),
                (w_edge_in_in, w_edge_in),
                (senders_in, senders),
                (receivers_in, receivers),
            ]
        )
    ]
    for copy in small:
        copy.start()
    for step in range(chunks):
        for copy in fetch(step):
            copy.start()
    for copy in small:
        copy.wait()
    tables[:count_p] = mm(nodes[...], w_edge_in[width : 2 * width]).astype(BF16)
    tables[count_p:] = w_edge_in[2 * width :]
    line = lax.broadcasted_iota(jnp.int32, (8, chunk), 0)

    def one(step, carry):
        rows = pl.ds(pl.multiple_of(step * chunk, chunk), chunk)
        sender = jnp.broadcast_to(senders[step], (8, chunk))
        receiver = jnp.broadcast_to(receivers[step], (8, chunk))
        owner = lax.shift_right_logical(sender, place_bits)
        within = lax.bitwise_and(sender, count_p - 1)
        d_strip = lax.shift_right_logical(owner, sub_bits) - my_strip
        d_sub = lax.bitwise_and(owner, subs - 1) - my_sub
        spot = 3 * d_strip + d_sub + 4
        spot = jnp.where(spot > 4, spot - 1, spot)
        near = (d_strip == 0) & (d_sub == 0)
        spot = jnp.where(near, within, spot * border + jnp.minimum(within, border - 1))
        index = jnp.where(line == 0, spot, receiver)
        index = jnp.where(line == 2, jnp.where(near, spot, -1 - spot), index)
        info[step] = index
        columns = index.T
        for copy in fetch(step):
            copy.wait()
        edge = edges[rows]
        cot = edge_cot[rows].astype(F32)
        recv = jnp.broadcast_to(columns[:, 1:2], edge.shape).astype(F32).astype(BF16)
        recv_codes[rows] = recv
        send_codes[rows] = jnp.broadcast_to(columns[:, 2:3], edge.shape).astype(F32).astype(BF16)
        recv = found(recv, count_p // width)
        pre_part[rows] = mm(jnp.concatenate([recv, edge], axis=1), tables[...])
        edges_t[step] = edge.T
        cot_part[rows] = (cot - jnp.mean(cot, axis=1, keepdims=True)).astype(BF16)
        return carry

    lax.fori_loop(0, chunks, one, 0)


def layer_kernel(
    edge_count,
    nodes,
    own_column,
    odd_column,
    even_column,
    edges,
    send_codes,
    recv_codes,
    edges_t,
    pre_part,
    cot_part,
    info,
    w_edge_in,
    w_edge_out,
    w_node_in,
    w_node_out,
    node_cot,
    new_nodes_out,
    new_edges_out,
    local_grad,
    parts,
    new_nodes,
    new_edges,
    near_rows,
    far_rows,
    tables,
    centring,
    back,
    means,
    hidden,
    slope,
    normed,
    scale,
    sums,
    ge_out,
    agg,
    packed,
    kept,
    columns,
    out_sems,
    last_sem,
):
    count_p, width = nodes.shape
    border = own_column.shape[0] // 3
    slots = parts.shape[0]
    strips = slots // 2
    chunks, _, chunk = edges_t.shape
    block = chunk // SPLIT
    half = block // 2
    share = parts.shape[1] - 2 * border
    my_strip, my_y = lax.axis_index("strip"), lax.axis_index("y")
    live_count = edge_count[0]

    def span(step):
        return pl.ds(pl.multiple_of(step * chunk, chunk), chunk)

    def block_rows(step, part):
        return pl.ds(pl.multiple_of(step * chunk + part * block, block), block)

    def block_pairs(step, part):
        return pl.ds(pl.multiple_of((step * SPLIT + part) * half, half), half)

    def emit(step):
        rows = span(step)
        return pltpu.make_async_copy(
            new_edges.at[rows], new_edges_out.at[rows], out_sems.at[step]
        )

    def paired(value):
        return jnp.concatenate([value[:half], value[half:]], axis=1)

    def unpaired(value):
        return jnp.concatenate([value[:, :width], value[:, width:]], axis=0)

    def twice(block):
        zero = jnp.zeros_like(block)
        return jnp.concatenate(
            [
                jnp.concatenate([block, zero], axis=1),
                jnp.concatenate([zero, block], axis=1),
            ],
            axis=0,
        )

    near_rows[...] = nodes[...]
    for k, column in enumerate((own_column, even_column, odd_column)):
        for part in range(3):
            columns[3 * k + part] = column[part * border : (part + 1) * border]

    def partner(mine, step):
        if step == 0:
            return 0
        is_odd = lax.rem(mine, 2)
        return 1 + is_odd if step > 0 else 2 - is_odd

    spot = 0
    for d_strip in (-1, 0, 1):
        column = partner(my_strip, d_strip)
        for d_sub in (-1, 0, 1):
            if d_strip == 0 and d_sub == 0:
                continue
            rows = slice(spot * border, (spot + 1) * border)
            far_rows[rows] = columns[3 * column + partner(my_y, d_sub)]
            spot += 1
    tables[:, :width] = mm(near_rows[...], w_edge_in[:width]).astype(BF16)
    tables[:, width:] = mm(far_rows[...], w_edge_in[:width]).astype(BF16)
    weight = w_edge_out[...].astype(F32)
    centring[...] = twice(weight - jnp.mean(weight, axis=1, keepdims=True)).astype(BF16)
    back[...] = twice(weight).astype(BF16)
    means[...] = twice(jnp.full((width, width), 1.0 / width, F32)).astype(BF16)

    row = lax.broadcasted_iota(jnp.int32, (half, 2 * width), 0)
    lane = lax.broadcasted_iota(jnp.int32, (half, 2 * width), 1)
    edge_row = jnp.where(lane < width, row, row + half)
    agg[...] = jnp.zeros_like(agg)

    def forward(step, carry):
        recv_t = found_t(info[step][1:2], count_p)
        units = []
        for part in range(SPLIT):
            rows, pairs = block_rows(step, part), block_pairs(step, part)
            codes = send_codes[rows]
            begun = pre_part[rows]
            edge = paired(edges[rows].astype(F32))
            place = jnp.where(codes < 0, -1 - codes, codes)
            picked = mm(found(place, count_p // width), tables[...])
            beyond = codes.astype(F32) < 0.0
            pre = begun + jnp.where(beyond, picked[:, width:], picked[:, :width])
            act, bend = silu_and_slope(paired(pre))
            act = act.astype(BF16)
            centre = mm(act, centring[...])
            spare = mm((centre * centre).astype(BF16), means[...])
            live = edge_row < live_count - step * chunk - part * block
            factor = jnp.where(live, lax.rsqrt(spare + EPS), 0.0)
            unit = centre * factor
            slope[pairs] = bend
            hidden[rows] = unpaired(act)
            scale[pairs] = factor
            normed[pairs] = unit
            new_edges[rows] = unpaired((edge + unit).astype(BF16))
            units.append(unpaired(unit.astype(BF16)))
        agg[...] += mm(recv_t, jnp.concatenate(units, axis=0))
        emit(step).start()
        return carry

    lax.fori_loop(0, chunks, forward, 0, unroll=UNROLL)

    joined = jnp.concatenate([nodes[...], agg[...].astype(BF16)], axis=1)
    node_pre = mm(joined, w_node_in[...])
    node_act, node_slope = silu_and_slope(node_pre)
    node_act = node_act.astype(BF16)
    node_unit, node_scale = norm_rows(mm(node_act, w_node_out[...]))
    new_nodes[...] = (nodes[...].astype(F32) + node_unit).astype(BF16)
    cot = node_cot[...].astype(F32)
    d_outer = norm_back(node_unit, node_scale, cot).astype(BF16)
    d_pre = (mm_nt(d_outer, w_node_out[...]) * node_slope).astype(BF16)
    d_joined = mm_nt(d_pre, w_node_in[...])
    d_agg = d_joined[:, width:]
    d_agg = (d_agg - jnp.mean(d_agg, axis=1, keepdims=True)).astype(BF16)
    agg[...] = cot + d_joined[:, :width]
    kept[:, : 2 * width] = joined
    kept[:, 2 * width : 3 * width] = node_act
    kept[:, 3 * width : 4 * width] = d_outer
    kept[:, 4 * width :] = d_pre
    node_copy = pltpu.make_async_copy(new_nodes, new_nodes_out, last_sem)
    node_copy.start()

    sums[...] = jnp.zeros_like(sums)
    ge_out[...] = jnp.zeros_like(ge_out)

    def backward(step, carry):
        index = info[step]
        turned = jnp.concatenate(
            [found_t(index[1:2], count_p), found_t(index[0:1], count_p), edges_t[step]], axis=0
        )
        acts, outs, ins = [], [], []
        for part in range(SPLIT):
            rows, pairs = block_rows(step, part), block_pairs(step, part)
            cot = cot_part[rows].astype(F32)
            recv = found(recv_codes[rows], count_p // width)
            unit = normed[pairs]
            acts.append(hidden[rows])
            beyond = send_codes[rows] < 0
            upstream = paired(cot + mm(recv, d_agg))
            along = mm((upstream * unit).astype(BF16), means[...])
            d_out = (scale[pairs] * (upstream - unit * along)).astype(BF16)
            outs.append(unpaired(d_out))
            d_in = unpaired((mm_nt(d_out, back[...]) * slope[pairs]).astype(BF16))
            zero = jnp.zeros_like(d_in)
            ins.append(
                jnp.concatenate(
                    [jnp.where(beyond, zero, d_in), jnp.where(beyond, d_in, zero)], axis=1
                )
            )
        ge_out[...] += mm_tn(jnp.concatenate(acts, axis=0), jnp.concatenate(outs, axis=0))
        sums[...] += mm(turned, jnp.concatenate(ins, axis=0))
        return carry

    lax.fori_loop(0, chunks, backward, 0, unroll=UNROLL)

    recv_sums = (sums[:count_p, :width] + sums[:count_p, width:]).astype(BF16)
    near_sums = sums[count_p : 2 * count_p, :width].astype(BF16)
    far_sums = sums[count_p : 2 * count_p, width:].astype(BF16)
    edge_sums = sums[2 * count_p :, :width] + sums[2 * count_p :, width:]
    packed[:width] = (mm_tn(near_rows[...], near_sums) + mm_tn(far_rows[...], far_sums)).astype(BF16)
    packed[width : 2 * width] = mm_tn(nodes[...], recv_sums).astype(BF16)
    packed[4 * width : 6 * width] = mm_tn(kept[:, : 2 * width], kept[:, 4 * width :]).astype(BF16)
    packed[6 * width : 7 * width] = mm_tn(
        kept[:, 2 * width : 3 * width], kept[:, 3 * width : 4 * width]
    ).astype(BF16)
    packed[2 * width : 3 * width] = edge_sums.astype(BF16)
    packed[3 * width : 4 * width] = ge_out[...].astype(BF16)
    if packed.shape[0] > 7 * width:
        packed[7 * width :] = jnp.zeros((packed.shape[0] - 7 * width, width), BF16)
    local_grad[...] = (
        agg[...]
        + mm_nt(near_sums, w_edge_in[:width])
        + mm_nt(recv_sums, w_edge_in[width : 2 * width])
    )
    owed = mm_nt(far_sums, w_edge_in[:width]).astype(BF16)
    for slot in range(slots):
        parts[slot, :share] = packed[slot * share : (slot + 1) * share]
        parts[slot, share:] = jnp.zeros((2 * border, width), BF16)
    spot = 0
    for d_strip in (-1, 0, 1):
        strip = my_strip + d_strip
        for d_sub in (-1, 0, 1):
            if d_strip == 0 and d_sub == 0:
                continue
            if d_sub == 0:
                slot, part = 2 * strip + my_y, 0
            elif d_sub == 1:
                slot, part = 2 * strip + 1 - my_y, my_y
            else:
                slot, part = 2 * strip + 1 - my_y, 1 - my_y
            first = pl.multiple_of(share + part * border, 16)
            block = owed[spot * border : (spot + 1) * border]

            @pl.when((strip >= 0) & (strip < strips))
            def put(slot=slot, first=first, block=block):
                parts[slot, pl.ds(first, border), :] = block

            spot += 1
    for step in range(chunks):
        emit(step).wait()
    node_copy.wait()


def plane_sum_kernel(came, message, mine):
    border = mine.shape[0]
    share = message.shape[0] - border
    total = came[0].astype(F32)
    for slot in range(1, came.shape[0]):
        total = total + came[slot].astype(F32)
    mine[...] = total[share : share + border]
    message[:share] = total[:share].astype(BF16)
    message[share:] = total[share + border :].astype(BF16)


def line_sum_kernel(factor, mine, *refs):
    messages, (out, rim_grad, held) = refs[:-3], refs[-3:]
    border = mine.shape[0]
    share = out.shape[1]
    for k, message in enumerate(messages):
        held[k] = message[...].astype(F32)
    my_z, my_y = lax.axis_index("z"), lax.axis_index("y")
    total = held[lax.bitwise_xor(my_z, 0), :share]
    for z in range(1, len(messages)):
        total = total + held[lax.bitwise_xor(my_z, z), :share]
    total = (total * factor).astype(BF16)
    for target in range(out.shape[0]):
        out[target] = total
    source = my_z - 1 + 2 * my_y
    inside = (source >= 0) & (source < len(messages))
    passed = held[lax.bitwise_xor(my_z, jnp.clip(source, 0, len(messages) - 1)), share:]
    rim_grad[...] = mine[...] + jnp.where(inside, passed, 0.0)


def finish_kernel(came, rim_grad, local_grad, node_grad, *outs):
    border = rim_grad.shape[0]
    share = came.shape[1]
    node_grad[...] = local_grad[...]
    node_grad[:border] += rim_grad[...]
    start = 0
    for out in outs:
        size = out.shape[0]
        done = 0
        while done < size:
            slot, offset = divmod(start + done, share)
            step = min(size - done, share - offset)
            out[done : done + step] = came[slot, offset : offset + step].astype(F32)
            done += step
        start += size


def shards(
    node_latents,
    edge_latents,
    senders,
    receivers,
    edge_count,
    w_edge_in,
    w_edge_out,
    w_node_in,
    w_node_out,
    node_cotangent,
    edge_cotangent,
):
    count_p, width = node_latents.shape
    count_e = edge_latents.shape[0]
    border = count_p // 8
    strips, zs, ys = (lax.axis_size(axis) for axis in ALL)
    subs = zs * ys
    slots = strips * ys
    even, odd = swapped(node_latents[:border], ("z", "y"))
    (own_column,) = call(
        column_kernel,
        [((3 * border, width), BF16)],
        [edge_count, node_latents[:border], odd, even],
        [SMEM] + [VMEM] * 3,
    )
    even_column, odd_column = swapped(own_column, "strip")

    chunk = min(CHUNK, count_e)
    chunks = count_e // chunk
    early = call(
        early_kernel,
        [
            ((count_e, width), BF16),
            ((count_e, width), BF16),
            ((count_e, width), BF16),
            ((chunks, width, chunk), BF16),
            ((count_e, width), F32),
            ((count_e, width), BF16),
            ((chunks, 8, chunk), jnp.int32),
        ],
        [
            node_latents,
            edge_latents,
            edge_cotangent,
            senders.reshape(chunks, 1, chunk),
            receivers.reshape(chunks, 1, chunk),
            w_edge_in,
        ],
        [HBM] * 6,
        [
            pltpu.VMEM((count_p + width, width), BF16),
            pltpu.VMEM((count_p, width), BF16),
            pltpu.VMEM((count_e, width), BF16),
            pltpu.VMEM((chunks, 1, chunk), jnp.int32),
            pltpu.VMEM((chunks, 1, chunk), jnp.int32),
            pltpu.VMEM((3 * width, width), BF16),
            SEM((4,)),
            SEM((2, chunks)),
        ],
    )

    share = -(-7 * width // (slots * 16)) * 16

    new_nodes, new_edges, local_grad, parts = call(
        layer_kernel,
        [
            ((count_p, width), BF16),
            ((count_e, width), BF16),
            ((count_p, width), F32),
            ((slots, share + 2 * border, width), BF16),
        ],
        [
            edge_count,
            node_latents,
            own_column,
            odd_column,
            even_column,
            *early,
            w_edge_in,
            w_edge_out,
            w_node_in,
            w_node_out,
            node_cotangent,
        ],
        [SMEM] + [VMEM] * 16,
        [
            pltpu.VMEM((count_p, width), BF16),
            pltpu.VMEM((count_e, width), BF16),
            pltpu.VMEM((count_p, width), BF16),
            pltpu.VMEM((8 * border, width), BF16),
            pltpu.VMEM((count_p, 2 * width), BF16),
            pltpu.VMEM((2 * width, 2 * width), BF16),
            pltpu.VMEM((2 * width, 2 * width), BF16),
            pltpu.VMEM((2 * width, 2 * width), BF16),
            pltpu.VMEM((count_e, width), BF16),
            pltpu.VMEM((count_e // 2, 2 * width), F32),
            pltpu.VMEM((count_e // 2, 2 * width), F32),
            pltpu.VMEM((count_e // 2, 2 * width), F32),
            pltpu.VMEM((2 * count_p + width, 2 * width), F32),
            pltpu.VMEM((width, width), F32),
            pltpu.VMEM((count_p, width), F32),
            pltpu.VMEM((slots * share, width), BF16),
            pltpu.VMEM((count_p, 5 * width), BF16),
            pltpu.VMEM((9, border, width), BF16),
            SEM((chunks,)),
            SEM,
        ],
        [HBM, HBM, VMEM, VMEM],
        limit=24,
    )

    came = lax.all_to_all(parts, PLANE, 0, 0)
    state = [((share + border, width), BF16), ((border, width), F32)]
    message, mine = call(plane_sum_kernel, state, [came], [VMEM])
    factor = 1.0 / math.sqrt(count_e * strips * subs)
    messages = [message] + [
        lax.ppermute(message, "z", [(z, z ^ k) for z in range(zs)]) for k in range(1, zs)
    ]
    parts, rim_grad = call(
        functools.partial(line_sum_kernel, factor),
        [((slots, share, width), BF16), ((border, width), F32)],
        [mine, *messages],
        [VMEM] * (1 + zs),
        [pltpu.VMEM((zs, share + border, width), F32)],
    )
    came = lax.all_to_all(parts, PLANE, 0, 0)
    node_grad, *grads = call(
        finish_kernel,
        [((rows, width), F32) for rows in (count_p, 3 * width, width, 2 * width, width)],
        [came, rim_grad, local_grad],
        [VMEM, VMEM, VMEM],
    )
    return (new_nodes, new_edges, node_grad, *grads)


def solution(mesh):
    strips, subs = mesh.devices.shape
    grid = Mesh(mesh.devices.reshape(strips, subs // 2, 2), ALL)
    rows = P(ALL, None)
    line = P(ALL)
    return jax.shard_map(
        shards,
        mesh=grid,
        in_specs=(rows, rows, line, line, line, P(), P(), P(), P(), rows, rows),
        out_specs=(rows, rows, rows, P(), P(), P(), P()),
        check_vma=False,
    )
```

```python
import functools
import math

import jax
import jax.numpy as jnp
from jax import lax
from jax.experimental import pallas as pl
from jax.experimental.pallas import tpu as pltpu
from jax.sharding import Mesh
from jax.sharding import PartitionSpec as P

EPS = 1e-05
CHUNK = 1024
SPLIT = 2
UNROLL = 4
PLANE = ("strip", "y")
ALL = ("strip", "z", "y")
F32 = jnp.float32
BF16 = jnp.bfloat16
VMEM = pl.BlockSpec(memory_space=pltpu.VMEM)
SMEM = pl.BlockSpec(memory_space=pltpu.SMEM)
HBM = pl.BlockSpec(memory_space=pltpu.HBM)
SEM = pltpu.SemaphoreType.DMA


def mm(left, right):
    return jnp.dot(left, right, preferred_element_type=F32)


def mm_nt(left, right):
    return lax.dot_general(left, right, (((1,), (1,)), ((), ())), preferred_element_type=F32)


def mm_tn(left, right):
    return lax.dot_general(left, right, (((0,), (0,)), ((), ())), preferred_element_type=F32)


def silu_and_slope(values):
    sig = 0.5 + 0.5 * jnp.tanh(0.5 * values)
    act = values * sig
    return (act, sig + act * (1.0 - sig))


def found(codes, blocks):
    lane = lax.broadcasted_iota(jnp.int32, codes.shape, 1)
    one, zero = jnp.ones((), BF16), jnp.zeros((), BF16)
    width = codes.shape[1]
    return jnp.concatenate(
        [
            jnp.where(codes == (lane + width * k).astype(F32).astype(BF16), one, zero)
            for k in range(blocks)
        ],
        axis=1,
    )


def found_t(line, size):
    place = lax.broadcasted_iota(jnp.int32, (size, line.shape[1]), 0).astype(F32).astype(BF16)
    one, zero = jnp.ones((), BF16), jnp.zeros((), BF16)
    return jnp.where(place == line.astype(F32).astype(BF16), one, zero)


def in_hbm(value):
    return pltpu.with_memory_space_constraint(value, pltpu.HBM)


def call(kernel, outs, ins, specs, scratch=(), out_specs=None, limit=24):
    out_specs = [VMEM] * len(outs) if out_specs is None else out_specs
    return pl.pallas_call(
        kernel,
        out_shape=[
            pltpu.HBM(shape, dtype) if spec is HBM else jax.ShapeDtypeStruct(shape, dtype)
            for (shape, dtype), spec in zip(outs, out_specs)
        ],
        in_specs=specs,
        out_specs=out_specs,
        scratch_shapes=list(scratch),
        compiler_params=pltpu.CompilerParams(vmem_limit_bytes=limit * 2**20),
    )(*[in_hbm(value) if spec is HBM else value for value, spec in zip(ins, specs)])


def column_kernel(edge_count, nodes, odd, even, out):
    border = even.shape[0]
    out[:border] = nodes[:border]
    out[border : 2 * border] = even[...]
    out[2 * border :] = odd[...]


def swapped(value, axes):
    count = lax.axis_size(axes)
    even = [(k, k ^ 1) for k in range(count)]
    odd = [(k, min(max(((k + 1) ^ 1) - 1, 0), count - 1)) for k in range(count)]
    from_odd = lax.ppermute(value, axes, odd)
    from_even = lax.ppermute(value, axes, even)
    return from_even, from_odd


def early_kernel(
    nodes_in,
    edges_in,
    edge_cot_in,
    senders_in,
    receivers_in,
    w_edge_in_in,
    edges,
    send_codes,
    recv_codes,
    edges_t,
    pre_part,
    cot_part,
    info,
    tables,
    nodes,
    edge_cot,
    senders,
    receivers,
    w_edge_in,
    small_sems,
    sems,
):
    count_p, width = nodes_in.shape
    chunks, _, chunk = info.shape
    border = count_p // 8
    my_strip = lax.axis_index("strip")
    subs = lax.axis_size("z") * lax.axis_size("y")
    my_sub = lax.axis_index("z") * lax.axis_size("y") + lax.axis_index("y")
    place_bits, sub_bits = count_p.bit_length() - 1, subs.bit_length() - 1

    def fetch(step):
        rows = pl.ds(pl.multiple_of(step * chunk, chunk), chunk)
        return [
            pltpu.make_async_copy(edges_in.at[rows], edges.at[rows], sems.at[0, step]),
            pltpu.make_async_copy(edge_cot_in.at[rows], edge_cot.at[rows], sems.at[1, step]),
        ]

    small = [
        pltpu.make_async_copy(source, target, small_sems.at[k])
        for k, (source, target) in enumerate(
            [
                (nodes_in, nodes),
                (w_edge_in_in, w_edge_in),
                (senders_in, senders),
                (receivers_in, receivers),
            ]
        )
    ]
    for copy in small:
        copy.start()
    for step in range(chunks):
        for copy in fetch(step):
            copy.start()
    for copy in small:
        copy.wait()
    tables[:count_p] = mm(nodes[...], w_edge_in[width : 2 * width]).astype(BF16)
    tables[count_p:] = w_edge_in[2 * width :]
    line = lax.broadcasted_iota(jnp.int32, (8, chunk), 0)

    def one(step, carry):
        rows = pl.ds(pl.multiple_of(step * chunk, chunk), chunk)
        sender = jnp.broadcast_to(senders[step], (8, chunk))
        receiver = jnp.broadcast_to(receivers[step], (8, chunk))
        owner = lax.shift_right_logical(sender, place_bits)
        within = lax.bitwise_and(sender, count_p - 1)
        d_strip = lax.shift_right_logical(owner, sub_bits) - my_strip
        d_sub = lax.bitwise_and(owner, subs - 1) - my_sub
        spot = 3 * d_strip + d_sub + 4
        spot = jnp.where(spot > 4, spot - 1, spot)
        near = (d_strip == 0) & (d_sub == 0)
        spot = jnp.where(near, within, spot * border + jnp.minimum(within, border - 1))
        index = jnp.where(line == 0, spot, receiver)
        index = jnp.where(line == 2, jnp.where(near, spot, -1 - spot), index)
        info[step] = index
        columns = index.T
        for copy in fetch(step):
            copy.wait()
        edge = edges[rows]
        cot = edge_cot[rows].astype(F32)
        recv = jnp.broadcast_to(columns[:, 1:2], edge.shape).astype(F32).astype(BF16)
        recv_codes[rows] = recv
        send_codes[rows] = jnp.broadcast_to(columns[:, 2:3], edge.shape).astype(F32).astype(BF16)
        recv = found(recv, count_p // width)
        pre_part[rows] = mm(jnp.concatenate([recv, edge], axis=1), tables[...])
        edges_t[step] = edge.T
        cot_part[rows] = (cot - jnp.mean(cot, axis=1, keepdims=True)).astype(BF16)
        return carry

    lax.fori_loop(0, chunks, one, 0, unroll=UNROLL)


def layer_kernel(
    edge_count,
    nodes,
    own_column,
    odd_column,
    even_column,
    edges,
    send_codes,
    recv_codes,
    edges_t,
    pre_part,
    cot_part,
    info,
    w_edge_in,
    w_edge_out,
    w_node_in,
    w_node_out,
    node_cot,
    new_nodes_out,
    new_edges_out,
    local_grad,
    parts,
    new_nodes,
    new_edges,
    near_rows,
    far_rows,
    tables,
    centring,
    back,
    means,
    hidden,
    slope,
    normed,
    scale,
    sums,
    ge_out,
    agg,
    packed,
    kept,
    columns,
    node_centring,
    agg_centring,
    node_cot_c,
    out_sems,
    last_sem,
):
    count_p, width = nodes.shape
    border = own_column.shape[0] // 3
    slots = parts.shape[0]
    strips = slots // 2
    chunks, _, chunk = edges_t.shape
    block = chunk // SPLIT
    half = block // 2
    share = parts.shape[1] - 2 * border
    my_strip, my_y = lax.axis_index("strip"), lax.axis_index("y")
    live_count = edge_count[0]

    def span(step):
        return pl.ds(pl.multiple_of(step * chunk, chunk), chunk)

    def block_rows(step, part):
        return pl.ds(pl.multiple_of(step * chunk + part * block, block), block)

    def block_pairs(step, part):
        return pl.ds(pl.multiple_of((step * SPLIT + part) * half, half), half)

    def emit(step):
        rows = span(step)
        return pltpu.make_async_copy(
            new_edges.at[rows], new_edges_out.at[rows], out_sems.at[step]
        )

    def paired(value):
        return jnp.concatenate([value[:half], value[half:]], axis=1)

    def unpaired(value):
        return jnp.concatenate([value[:, :width], value[:, width:]], axis=0)

    def twice(block):
        zero = jnp.zeros_like(block)
        return jnp.concatenate(
            [
                jnp.concatenate([block, zero], axis=1),
                jnp.concatenate([zero, block], axis=1),
            ],
            axis=0,
        )

    near_rows[...] = nodes[...]
    for k, column in enumerate((own_column, even_column, odd_column)):
        for part in range(3):
            columns[3 * k + part] = column[part * border : (part + 1) * border]

    def partner(mine, step):
        if step == 0:
            return 0
        is_odd = lax.rem(mine, 2)
        return 1 + is_odd if step > 0 else 2 - is_odd

    spot = 0
    for d_strip in (-1, 0, 1):
        column = partner(my_strip, d_strip)
        for d_sub in (-1, 0, 1):
            if d_strip == 0 and d_sub == 0:
                continue
            rows = slice(spot * border, (spot + 1) * border)
            far_rows[rows] = columns[3 * column + partner(my_y, d_sub)]
            spot += 1
    tables[:, :width] = mm(near_rows[...], w_edge_in[:width]).astype(BF16)
    tables[:, width:] = mm(far_rows[...], w_edge_in[:width]).astype(BF16)
    weight = w_edge_out[...].astype(F32)
    centring[...] = twice(weight - jnp.mean(weight, axis=1, keepdims=True)).astype(BF16)
    back[...] = twice(weight).astype(BF16)
    weight = w_node_out[...].astype(F32)
    node_centring[...] = (weight - jnp.mean(weight, axis=1, keepdims=True)).astype(BF16)
    weight = w_node_in[width:].astype(F32)
    agg_centring[...] = (weight - jnp.mean(weight, axis=0, keepdims=True)).astype(BF16)
    cot = node_cot[...].astype(F32)
    node_cot_c[...] = cot - jnp.mean(cot, axis=1, keepdims=True)
    means[...] = twice(jnp.full((width, width), 1.0 / width, F32)).astype(BF16)

    row = lax.broadcasted_iota(jnp.int32, (half, 2 * width), 0)
    lane = lax.broadcasted_iota(jnp.int32, (half, 2 * width), 1)
    edge_row = jnp.where(lane < width, row, row + half)
    agg[...] = jnp.zeros_like(agg)

    def forward(step, carry):
        recv_t = found_t(info[step][1:2], count_p)
        units = []
        for part in range(SPLIT):
            rows, pairs = block_rows(step, part), block_pairs(step, part)
            codes = send_codes[rows]
            begun = pre_part[rows]
            edge = paired(edges[rows].astype(F32))
            place = jnp.where(codes < 0, -1 - codes, codes)
            picked = mm(found(place, count_p // width), tables[...])
            beyond = codes.astype(F32) < 0.0
            pre = begun + jnp.where(beyond, picked[:, width:], picked[:, :width])
            act, bend = silu_and_slope(paired(pre))
            act = act.astype(BF16)
            centre = mm(act, centring[...])
            spare = mm((centre * centre).astype(BF16), means[...])
            live = edge_row < live_count - step * chunk - part * block
            factor = jnp.where(live, lax.rsqrt(spare + EPS), 0.0)
            unit = centre * factor
            slope[pairs] = bend
            hidden[rows] = unpaired(act)
            scale[pairs] = factor
            normed[pairs] = unit
            new_edges[rows] = unpaired((edge + unit).astype(BF16))
            units.append(unpaired(unit.astype(BF16)))
        agg[...] += mm(recv_t, jnp.concatenate(units, axis=0))
        emit(step).start()
        return carry

    lax.fori_loop(0, chunks, forward, 0, unroll=UNROLL)

    joined = jnp.concatenate([nodes[...], agg[...].astype(BF16)], axis=1)
    node_pre = mm(joined, w_node_in[...])
    node_act, node_slope = silu_and_slope(node_pre)
    node_act = node_act.astype(BF16)
    centre = mm(node_act, node_centring[...])
    spare = jnp.mean(centre * centre, axis=1, keepdims=True)
    along = jnp.mean(node_cot_c[...] * centre, axis=1, keepdims=True)
    node_scale = lax.rsqrt(spare + EPS)
    node_unit = centre * node_scale
    d_outer = node_scale * (node_cot_c[...] - node_unit * (along * node_scale))
    d_outer = d_outer.astype(BF16)
    d_pre = (mm_nt(d_outer, w_node_out[...]) * node_slope).astype(BF16)
    d_agg = mm_nt(d_pre, agg_centring[...]).astype(BF16)
    new_nodes[...] = (nodes[...].astype(F32) + node_unit).astype(BF16)
    agg[...] = node_cot[...].astype(F32) + mm_nt(d_pre, w_node_in[:width])
    kept[:, : 2 * width] = joined
    kept[:, 2 * width : 3 * width] = node_act
    kept[:, 3 * width : 4 * width] = d_outer
    kept[:, 4 * width :] = d_pre
    node_copy = pltpu.make_async_copy(new_nodes, new_nodes_out, last_sem)
    node_copy.start()

    sums[...] = jnp.zeros_like(sums)
    ge_out[...] = jnp.zeros_like(ge_out)

    def backward(step, carry):
        index = info[step]
        turned = jnp.concatenate(
            [found_t(index[1:2], count_p), found_t(index[0:1], count_p), edges_t[step]], axis=0
        )
        acts, outs, ins = [], [], []
        for part in range(SPLIT):
            rows, pairs = block_rows(step, part), block_pairs(step, part)
            cot = cot_part[rows].astype(F32)
            recv = found(recv_codes[rows], count_p // width)
            unit = normed[pairs]
            acts.append(hidden[rows])
            beyond = send_codes[rows] < 0
            upstream = paired(cot + mm(recv, d_agg))
            along = mm((upstream * unit).astype(BF16), means[...])
            d_out = (scale[pairs] * (upstream - unit * along)).astype(BF16)
            outs.append(unpaired(d_out))
            d_in = unpaired((mm_nt(d_out, back[...]) * slope[pairs]).astype(BF16))
            zero = jnp.zeros_like(d_in)
            ins.append(
                jnp.concatenate(
                    [jnp.where(beyond, zero, d_in), jnp.where(beyond, d_in, zero)], axis=1
                )
            )
        ge_out[...] += mm_tn(jnp.concatenate(acts, axis=0), jnp.concatenate(outs, axis=0))
        sums[...] += mm(turned, jnp.concatenate(ins, axis=0))
        return carry

    lax.fori_loop(0, chunks, backward, 0, unroll=UNROLL)

    recv_sums = (sums[:count_p, :width] + sums[:count_p, width:]).astype(BF16)
    near_sums = sums[count_p : 2 * count_p, :width].astype(BF16)
    far_sums = sums[count_p : 2 * count_p, width:].astype(BF16)
    edge_sums = sums[2 * count_p :, :width] + sums[2 * count_p :, width:]
    packed[:width] = (mm_tn(near_rows[...], near_sums) + mm_tn(far_rows[...], far_sums)).astype(BF16)
    packed[width : 2 * width] = mm_tn(nodes[...], recv_sums).astype(BF16)
    packed[4 * width : 6 * width] = mm_tn(kept[:, : 2 * width], kept[:, 4 * width :]).astype(BF16)
    packed[6 * width : 7 * width] = mm_tn(
        kept[:, 2 * width : 3 * width], kept[:, 3 * width : 4 * width]
    ).astype(BF16)
    packed[2 * width : 3 * width] = edge_sums.astype(BF16)
    packed[3 * width : 4 * width] = ge_out[...].astype(BF16)
    if packed.shape[0] > 7 * width:
        packed[7 * width :] = jnp.zeros((packed.shape[0] - 7 * width, width), BF16)
    local_grad[...] = (
        agg[...]
        + mm_nt(near_sums, w_edge_in[:width])
        + mm_nt(recv_sums, w_edge_in[width : 2 * width])
    )
    owed = mm_nt(far_sums, w_edge_in[:width]).astype(BF16)
    for slot in range(slots):
        parts[slot, :share] = packed[slot * share : (slot + 1) * share]
        parts[slot, share:] = jnp.zeros((2 * border, width), BF16)
    spot = 0
    for d_strip in (-1, 0, 1):
        strip = my_strip + d_strip
        for d_sub in (-1, 0, 1):
            if d_strip == 0 and d_sub == 0:
                continue
            if d_sub == 0:
                slot, part = 2 * strip + my_y, 0
            elif d_sub == 1:
                slot, part = 2 * strip + 1 - my_y, my_y
            else:
                slot, part = 2 * strip + 1 - my_y, 1 - my_y
            first = pl.multiple_of(share + part * border, 16)
            block = owed[spot * border : (spot + 1) * border]

            @pl.when((strip >= 0) & (strip < strips))
            def put(slot=slot, first=first, block=block):
                parts[slot, pl.ds(first, border), :] = block

            spot += 1
    for step in range(chunks):
        emit(step).wait()
    node_copy.wait()


def plane_sum_kernel(came, message, mine):
    border = mine.shape[0]
    share = message.shape[0] - border
    total = came[0].astype(F32)
    for slot in range(1, came.shape[0]):
        total = total + came[slot].astype(F32)
    mine[...] = total[share : share + border]
    message[:share] = total[:share].astype(BF16)
    message[share:] = total[share + border :].astype(BF16)


def line_sum_kernel(factor, mine, *refs):
    messages, (out, rim_grad, held) = refs[:-3], refs[-3:]
    border = mine.shape[0]
    share = out.shape[1]
    for k, message in enumerate(messages):
        held[k] = message[...].astype(F32)
    my_z, my_y = lax.axis_index("z"), lax.axis_index("y")
    total = held[lax.bitwise_xor(my_z, 0), :share]
    for z in range(1, len(messages)):
        total = total + held[lax.bitwise_xor(my_z, z), :share]
    total = (total * factor).astype(BF16)
    for target in range(out.shape[0]):
        out[target] = total
    source = my_z - 1 + 2 * my_y
    inside = (source >= 0) & (source < len(messages))
    passed = held[lax.bitwise_xor(my_z, jnp.clip(source, 0, len(messages) - 1)), share:]
    rim_grad[...] = mine[...] + jnp.where(inside, passed, 0.0)


def finish_kernel(came, rim_grad, local_grad, node_grad, *outs):
    border = rim_grad.shape[0]
    share = came.shape[1]
    node_grad[...] = local_grad[...]
    node_grad[:border] += rim_grad[...]
    start = 0
    for out in outs:
        size = out.shape[0]
        done = 0
        while done < size:
            slot, offset = divmod(start + done, share)
            step = min(size - done, share - offset)
            out[done : done + step] = came[slot, offset : offset + step].astype(F32)
            done += step
        start += size


def shards(
    node_latents,
    edge_latents,
    senders,
    receivers,
    edge_count,
    w_edge_in,
    w_edge_out,
    w_node_in,
    w_node_out,
    node_cotangent,
    edge_cotangent,
):
    count_p, width = node_latents.shape
    count_e = edge_latents.shape[0]
    border = count_p // 8
    strips, zs, ys = (lax.axis_size(axis) for axis in ALL)
    subs = zs * ys
    slots = strips * ys
    even, odd = swapped(node_latents[:border], ("z", "y"))
    chunk = min(CHUNK, count_e)
    chunks = count_e // chunk
    early = call(
        early_kernel,
        [
            ((count_e, width), BF16),
            ((count_e, width), BF16),
            ((count_e, width), BF16),
            ((chunks, width, chunk), BF16),
            ((count_e, width), F32),
            ((count_e, width), BF16),
            ((chunks, 8, chunk), jnp.int32),
        ],
        [
            node_latents,
            edge_latents,
            edge_cotangent,
            senders.reshape(chunks, 1, chunk),
            receivers.reshape(chunks, 1, chunk),
            w_edge_in,
        ],
        [HBM] * 6,
        [
            pltpu.VMEM((count_p + width, width), BF16),
            pltpu.VMEM((count_p, width), BF16),
            pltpu.VMEM((count_e, width), BF16),
            pltpu.VMEM((chunks, 1, chunk), jnp.int32),
            pltpu.VMEM((chunks, 1, chunk), jnp.int32),
            pltpu.VMEM((3 * width, width), BF16),
            SEM((4,)),
            SEM((2, chunks)),
        ],
    )

    *early, even, odd = lax.optimization_barrier((*early, even, odd))
    (own_column,) = call(
        column_kernel,
        [((3 * border, width), BF16)],
        [edge_count, node_latents[:border], odd, even],
        [SMEM] + [VMEM] * 3,
    )
    even_column, odd_column = swapped(own_column, "strip")

    share = -(-7 * width // (slots * 16)) * 16

    new_nodes, new_edges, local_grad, parts = call(
        layer_kernel,
        [
            ((count_p, width), BF16),
            ((count_e, width), BF16),
            ((count_p, width), F32),
            ((slots, share + 2 * border, width), BF16),
        ],
        [
            edge_count,
            node_latents,
            own_column,
            odd_column,
            even_column,
            *early,
            w_edge_in,
            w_edge_out,
            w_node_in,
            w_node_out,
            node_cotangent,
        ],
        [SMEM] + [VMEM] * 16,
        [
            pltpu.VMEM((count_p, width), BF16),
            pltpu.VMEM((count_e, width), BF16),
            pltpu.VMEM((count_p, width), BF16),
            pltpu.VMEM((8 * border, width), BF16),
            pltpu.VMEM((count_p, 2 * width), BF16),
            pltpu.VMEM((2 * width, 2 * width), BF16),
            pltpu.VMEM((2 * width, 2 * width), BF16),
            pltpu.VMEM((2 * width, 2 * width), BF16),
            pltpu.VMEM((count_e, width), BF16),
            pltpu.VMEM((count_e // 2, 2 * width), F32),
            pltpu.VMEM((count_e // 2, 2 * width), F32),
            pltpu.VMEM((count_e // 2, 2 * width), F32),
            pltpu.VMEM((2 * count_p + width, 2 * width), F32),
            pltpu.VMEM((width, width), F32),
            pltpu.VMEM((count_p, width), F32),
            pltpu.VMEM((slots * share, width), BF16),
            pltpu.VMEM((count_p, 5 * width), BF16),
            pltpu.VMEM((9, border, width), BF16),
            pltpu.VMEM((width, width), BF16),
            pltpu.VMEM((width, width), BF16),
            pltpu.VMEM((count_p, width), F32),
            SEM((chunks,)),
            SEM,
        ],
        [HBM, HBM, VMEM, VMEM],
        limit=24,
    )

    came = lax.all_to_all(parts, PLANE, 0, 0)
    state = [((share + border, width), BF16), ((border, width), F32)]
    message, mine = call(plane_sum_kernel, state, [came], [VMEM])
    factor = 1.0 / math.sqrt(count_e * strips * subs)
    messages = [message] + [
        lax.ppermute(message, "z", [(z, z ^ k) for z in range(zs)]) for k in range(1, zs)
    ]
    parts, rim_grad = call(
        functools.partial(line_sum_kernel, factor),
        [((slots, share, width), BF16), ((border, width), F32)],
        [mine, *messages],
        [VMEM] * (1 + zs),
        [pltpu.VMEM((zs, share + border, width), F32)],
    )
    came = lax.all_to_all(parts, PLANE, 0, 0)
    node_grad, *grads = call(
        finish_kernel,
        [((rows, width), F32) for rows in (count_p, 3 * width, width, 2 * width, width)],
        [came, rim_grad, local_grad],
        [VMEM, VMEM, VMEM],
    )
    return (new_nodes, new_edges, node_grad, *grads)


def solution(mesh):
    strips, subs = mesh.devices.shape
    grid = Mesh(mesh.devices.reshape(strips, subs // 2, 2), ALL)
    rows = P(ALL, None)
    line = P(ALL)
    return jax.shard_map(
        shards,
        mesh=grid,
        in_specs=(rows, rows, line, line, line, P(), P(), P(), P(), rows, rows),
        out_specs=(rows, rows, rows, P(), P(), P(), P()),
        check_vma=False,
    )
```

```python
import functools
import math

import jax
import jax.numpy as jnp
from jax import lax
from jax.experimental import pallas as pl
from jax.experimental.pallas import tpu as pltpu
from jax.sharding import Mesh
from jax.sharding import PartitionSpec as P

EPS = 1e-05
CHUNK = 1024
SPLIT = 2
UNROLL = 4
PLANE = ("strip", "y")
ALL = ("strip", "z", "y")
F32 = jnp.float32
BF16 = jnp.bfloat16
VMEM = pl.BlockSpec(memory_space=pltpu.VMEM)
SMEM = pl.BlockSpec(memory_space=pltpu.SMEM)
HBM = pl.BlockSpec(memory_space=pltpu.HBM)
SEM = pltpu.SemaphoreType.DMA


def mm(left, right):
    return jnp.dot(left, right, preferred_element_type=F32)


def mm_nt(left, right):
    return lax.dot_general(left, right, (((1,), (1,)), ((), ())), preferred_element_type=F32)


def mm_tn(left, right):
    return lax.dot_general(left, right, (((0,), (0,)), ((), ())), preferred_element_type=F32)


def silu_and_slope(values):
    sig = 0.5 + 0.5 * jnp.tanh(0.5 * values)
    act = values * sig
    return (act, sig + act * (1.0 - sig))


def found(codes, blocks):
    lane = lax.broadcasted_iota(jnp.int32, codes.shape, 1)
    one, zero = jnp.ones((), BF16), jnp.zeros((), BF16)
    width = codes.shape[1]
    return jnp.concatenate(
        [
            jnp.where(codes == (lane + width * k).astype(F32).astype(BF16), one, zero)
            for k in range(blocks)
        ],
        axis=1,
    )


def found_t(line, size):
    place = lax.broadcasted_iota(jnp.int32, (size, line.shape[1]), 0).astype(F32).astype(BF16)
    one, zero = jnp.ones((), BF16), jnp.zeros((), BF16)
    return jnp.where(place == line.astype(F32).astype(BF16), one, zero)


def in_hbm(value):
    return pltpu.with_memory_space_constraint(value, pltpu.HBM)


def call(kernel, outs, ins, specs, scratch=(), out_specs=None, limit=24):
    out_specs = [VMEM] * len(outs) if out_specs is None else out_specs
    return pl.pallas_call(
        kernel,
        out_shape=[
            pltpu.HBM(shape, dtype) if spec is HBM else jax.ShapeDtypeStruct(shape, dtype)
            for (shape, dtype), spec in zip(outs, out_specs)
        ],
        in_specs=specs,
        out_specs=out_specs,
        scratch_shapes=list(scratch),
        compiler_params=pltpu.CompilerParams(vmem_limit_bytes=limit * 2**20),
    )(*[in_hbm(value) if spec is HBM else value for value, spec in zip(ins, specs)])


def column_kernel(nodes, odd, even, out):
    border = out.shape[0] // 3
    out[:border] = nodes[:border]
    out[border : 2 * border] = even[:border]
    out[2 * border :] = odd[:border]


def swapped(value, axes):
    count = lax.axis_size(axes)
    even = [(k, k ^ 1) for k in range(count)]
    odd = [(k, min(max(((k + 1) ^ 1) - 1, 0), count - 1)) for k in range(count)]
    from_odd = lax.ppermute(value, axes, odd)
    from_even = lax.ppermute(value, axes, even)
    return from_even, from_odd


def early_kernel(
    nodes_in,
    edges_in,
    edge_cot_in,
    senders_in,
    receivers_in,
    w_edge_in_in,
    edges,
    send_codes,
    recv_codes,
    edges_t,
    pre_part,
    cot_part,
    info,
    tables,
    nodes,
    edge_cot,
    senders,
    receivers,
    w_edge_in,
    small_sems,
    sems,
):
    count_p, width = nodes_in.shape
    chunks, _, chunk = info.shape
    border = count_p // 8
    my_strip = lax.axis_index("strip")
    subs = lax.axis_size("z") * lax.axis_size("y")
    my_sub = lax.axis_index("z") * lax.axis_size("y") + lax.axis_index("y")
    place_bits, sub_bits = count_p.bit_length() - 1, subs.bit_length() - 1

    def fetch(step):
        rows = pl.ds(pl.multiple_of(step * chunk, chunk), chunk)
        return [
            pltpu.make_async_copy(edges_in.at[rows], edges.at[rows], sems.at[0, step]),
            pltpu.make_async_copy(edge_cot_in.at[rows], edge_cot.at[rows], sems.at[1, step]),
        ]

    small = [
        pltpu.make_async_copy(source, target, small_sems.at[k])
        for k, (source, target) in enumerate(
            [
                (nodes_in, nodes),
                (w_edge_in_in, w_edge_in),
                (senders_in, senders),
                (receivers_in, receivers),
            ]
        )
    ]
    for copy in small:
        copy.start()
    for step in range(chunks):
        for copy in fetch(step):
            copy.start()
    for copy in small:
        copy.wait()
    tables[:count_p] = mm(nodes[...], w_edge_in[width : 2 * width]).astype(BF16)
    tables[count_p:] = w_edge_in[2 * width :]
    line = lax.broadcasted_iota(jnp.int32, (8, chunk), 0)

    def one(step, carry):
        rows = pl.ds(pl.multiple_of(step * chunk, chunk), chunk)
        sender = jnp.broadcast_to(senders[step], (8, chunk))
        receiver = jnp.broadcast_to(receivers[step], (8, chunk))
        owner = lax.shift_right_logical(sender, place_bits)
        within = lax.bitwise_and(sender, count_p - 1)
        d_strip = lax.shift_right_logical(owner, sub_bits) - my_strip
        d_sub = lax.bitwise_and(owner, subs - 1) - my_sub
        spot = 3 * d_strip + d_sub + 4
        spot = jnp.where(spot > 4, spot - 1, spot)
        near = (d_strip == 0) & (d_sub == 0)
        spot = jnp.where(near, within, spot * border + jnp.minimum(within, border - 1))
        index = jnp.where(line == 0, spot, receiver)
        index = jnp.where(line == 2, jnp.where(near, spot, -1 - spot), index)
        info[step] = index
        columns = index.T
        for copy in fetch(step):
            copy.wait()
        edge = edges[rows]
        cot = edge_cot[rows].astype(F32)
        recv = jnp.broadcast_to(columns[:, 1:2], edge.shape).astype(F32).astype(BF16)
        recv_codes[rows] = recv
        send_codes[rows] = jnp.broadcast_to(columns[:, 2:3], edge.shape).astype(F32).astype(BF16)
        recv = found(recv, count_p // width)
        pre_part[rows] = mm(jnp.concatenate([recv, edge], axis=1), tables[...])
        edges_t[step] = edge.T
        cot_part[rows] = (cot - jnp.mean(cot, axis=1, keepdims=True)).astype(BF16)
        return carry

    lax.fori_loop(0, chunks, one, 0, unroll=UNROLL)


def prepare_kernel(
    column,
    nodes,
    w_edge_in,
    w_edge_out,
    w_node_in,
    w_node_out,
    node_cot,
    near_table,
    centring,
    back,
    means,
    node_centring,
    agg_centring,
    node_cot_c,
):
    width = nodes.shape[1]

    def twice(block):
        zero = jnp.zeros_like(block)
        return jnp.concatenate(
            [
                jnp.concatenate([block, zero], axis=1),
                jnp.concatenate([zero, block], axis=1),
            ],
            axis=0,
        )

    near_table[...] = mm(nodes[...], w_edge_in[:width]).astype(BF16)
    weight = w_edge_out[...].astype(F32)
    centring[...] = twice(weight - jnp.mean(weight, axis=1, keepdims=True)).astype(BF16)
    back[...] = twice(weight).astype(BF16)
    weight = w_node_out[...].astype(F32)
    node_centring[...] = (weight - jnp.mean(weight, axis=1, keepdims=True)).astype(BF16)
    weight = w_node_in[width:].astype(F32)
    agg_centring[...] = (weight - jnp.mean(weight, axis=0, keepdims=True)).astype(BF16)
    cot = node_cot[...].astype(F32)
    node_cot_c[...] = cot - jnp.mean(cot, axis=1, keepdims=True)
    means[...] = twice(jnp.full((width, width), 1.0 / width, F32)).astype(BF16)


def layer_kernel(
    edge_count,
    nodes,
    own_column,
    odd_column,
    even_column,
    edges,
    send_codes,
    recv_codes,
    edges_t,
    pre_part,
    cot_part,
    info,
    w_edge_in,
    w_edge_out,
    w_node_in,
    w_node_out,
    node_cot,
    near_table,
    centring,
    back,
    means,
    node_centring,
    agg_centring,
    node_cot_c,
    new_nodes_out,
    new_edges_out,
    local_grad,
    parts,
    new_nodes,
    new_edges,
    far_rows,
    tables,
    hidden,
    slope,
    normed,
    scale,
    sums,
    ge_out,
    agg,
    packed,
    kept,
    columns,
    out_sems,
    last_sem,
):
    count_p, width = nodes.shape
    border = own_column.shape[0] // 3
    slots = parts.shape[0]
    strips = slots // 2
    chunks, _, chunk = edges_t.shape
    block = chunk // SPLIT
    half = block // 2
    share = parts.shape[1] - 2 * border
    my_strip, my_y = lax.axis_index("strip"), lax.axis_index("y")
    live_count = edge_count[0]

    def span(step):
        return pl.ds(pl.multiple_of(step * chunk, chunk), chunk)

    def block_rows(step, part):
        return pl.ds(pl.multiple_of(step * chunk + part * block, block), block)

    def block_pairs(step, part):
        return pl.ds(pl.multiple_of((step * SPLIT + part) * half, half), half)

    def emit(step):
        rows = span(step)
        return pltpu.make_async_copy(
            new_edges.at[rows], new_edges_out.at[rows], out_sems.at[step]
        )

    def paired(value):
        return jnp.concatenate([value[:half], value[half:]], axis=1)

    def unpaired(value):
        return jnp.concatenate([value[:, :width], value[:, width:]], axis=0)

    for k, column in enumerate((own_column, even_column, odd_column)):
        for part in range(3):
            columns[3 * k + part] = column[part * border : (part + 1) * border]

    def partner(mine, step):
        if step == 0:
            return 0
        is_odd = lax.rem(mine, 2)
        return 1 + is_odd if step > 0 else 2 - is_odd

    spot = 0
    for d_strip in (-1, 0, 1):
        column = partner(my_strip, d_strip)
        for d_sub in (-1, 0, 1):
            if d_strip == 0 and d_sub == 0:
                continue
            rows = slice(spot * border, (spot + 1) * border)
            far_rows[rows] = columns[3 * column + partner(my_y, d_sub)]
            spot += 1
    tables[:, :width] = near_table[...]
    tables[:, width:] = mm(far_rows[...], w_edge_in[:width]).astype(BF16)
    row = lax.broadcasted_iota(jnp.int32, (half, 2 * width), 0)
    lane = lax.broadcasted_iota(jnp.int32, (half, 2 * width), 1)
    edge_row = jnp.where(lane < width, row, row + half)
    agg[...] = jnp.zeros_like(agg)

    def forward(step, carry):
        recv_t = found_t(info[step][1:2], count_p)
        units = []
        for part in range(SPLIT):
            rows, pairs = block_rows(step, part), block_pairs(step, part)
            codes = send_codes[rows]
            begun = pre_part[rows]
            edge = paired(edges[rows].astype(F32))
            place = jnp.where(codes < 0, -1 - codes, codes)
            picked = mm(found(place, count_p // width), tables[...])
            beyond = codes.astype(F32) < 0.0
            pre = begun + jnp.where(beyond, picked[:, width:], picked[:, :width])
            act, bend = silu_and_slope(paired(pre))
            act = act.astype(BF16)
            centre = mm(act, centring[...])
            spare = mm((centre * centre).astype(BF16), means[...])
            live = edge_row < live_count - step * chunk - part * block
            factor = jnp.where(live, lax.rsqrt(spare + EPS), 0.0)
            unit = centre * factor
            slope[pairs] = bend
            hidden[rows] = unpaired(act)
            scale[pairs] = factor
            normed[pairs] = unit
            new_edges[rows] = unpaired((edge + unit).astype(BF16))
            units.append(unpaired(unit.astype(BF16)))
        agg[...] += mm(recv_t, jnp.concatenate(units, axis=0))
        emit(step).start()
        return carry

    lax.fori_loop(0, chunks, forward, 0, unroll=UNROLL)

    joined = jnp.concatenate([nodes[...], agg[...].astype(BF16)], axis=1)
    node_pre = mm(joined, w_node_in[...])
    node_act, node_slope = silu_and_slope(node_pre)
    node_act = node_act.astype(BF16)
    centre = mm(node_act, node_centring[...])
    spare = jnp.mean(centre * centre, axis=1, keepdims=True)
    along = jnp.mean(node_cot_c[...] * centre, axis=1, keepdims=True)
    node_scale = lax.rsqrt(spare + EPS)
    node_unit = centre * node_scale
    d_outer = node_scale * (node_cot_c[...] - node_unit * (along * node_scale))
    d_outer = d_outer.astype(BF16)
    d_pre = (mm_nt(d_outer, w_node_out[...]) * node_slope).astype(BF16)
    d_agg = mm_nt(d_pre, agg_centring[...]).astype(BF16)
    new_nodes[...] = (nodes[...].astype(F32) + node_unit).astype(BF16)
    agg[...] = node_cot[...].astype(F32) + mm_nt(d_pre, w_node_in[:width])
    kept[:, : 2 * width] = joined
    kept[:, 2 * width : 3 * width] = node_act
    kept[:, 3 * width : 4 * width] = d_outer
    kept[:, 4 * width :] = d_pre
    node_copy = pltpu.make_async_copy(new_nodes, new_nodes_out, last_sem)
    node_copy.start()

    sums[...] = jnp.zeros_like(sums)
    ge_out[...] = jnp.zeros_like(ge_out)

    def backward(step, carry):
        index = info[step]
        turned = jnp.concatenate(
            [found_t(index[1:2], count_p), found_t(index[0:1], count_p), edges_t[step]], axis=0
        )
        acts, outs, ins = [], [], []
        for part in range(SPLIT):
            rows, pairs = block_rows(step, part), block_pairs(step, part)
            cot = cot_part[rows].astype(F32)
            recv = found(recv_codes[rows], count_p // width)
            unit = normed[pairs]
            acts.append(hidden[rows])
            beyond = send_codes[rows] < 0
            upstream = paired(cot + mm(recv, d_agg))
            along = mm((upstream * unit).astype(BF16), means[...])
            d_out = (scale[pairs] * (upstream - unit * along)).astype(BF16)
            outs.append(unpaired(d_out))
            d_in = unpaired((mm_nt(d_out, back[...]) * slope[pairs]).astype(BF16))
            zero = jnp.zeros_like(d_in)
            ins.append(
                jnp.concatenate(
                    [jnp.where(beyond, zero, d_in), jnp.where(beyond, d_in, zero)], axis=1
                )
            )
        ge_out[...] += mm_tn(jnp.concatenate(acts, axis=0), jnp.concatenate(outs, axis=0))
        sums[...] += mm(turned, jnp.concatenate(ins, axis=0))
        return carry

    lax.fori_loop(0, chunks, backward, 0, unroll=UNROLL)

    recv_sums = (sums[:count_p, :width] + sums[:count_p, width:]).astype(BF16)
    near_sums = sums[count_p : 2 * count_p, :width].astype(BF16)
    far_sums = sums[count_p : 2 * count_p, width:].astype(BF16)
    edge_sums = sums[2 * count_p :, :width] + sums[2 * count_p :, width:]
    packed[:width] = (mm_tn(nodes[...], near_sums) + mm_tn(far_rows[...], far_sums)).astype(BF16)
    packed[width : 2 * width] = mm_tn(nodes[...], recv_sums).astype(BF16)
    packed[4 * width : 6 * width] = mm_tn(kept[:, : 2 * width], kept[:, 4 * width :]).astype(BF16)
    packed[6 * width : 7 * width] = mm_tn(
        kept[:, 2 * width : 3 * width], kept[:, 3 * width : 4 * width]
    ).astype(BF16)
    packed[2 * width : 3 * width] = edge_sums.astype(BF16)
    packed[3 * width : 4 * width] = ge_out[...].astype(BF16)
    if packed.shape[0] > 7 * width:
        packed[7 * width :] = jnp.zeros((packed.shape[0] - 7 * width, width), BF16)
    local_grad[...] = (
        agg[...]
        + mm_nt(near_sums, w_edge_in[:width])
        + mm_nt(recv_sums, w_edge_in[width : 2 * width])
    )
    owed = mm_nt(far_sums, w_edge_in[:width]).astype(BF16)
    for slot in range(slots):
        parts[slot, :share] = packed[slot * share : (slot + 1) * share]
        parts[slot, share:] = jnp.zeros((2 * border, width), BF16)
    spot = 0
    for d_strip in (-1, 0, 1):
        strip = my_strip + d_strip
        for d_sub in (-1, 0, 1):
            if d_strip == 0 and d_sub == 0:
                continue
            if d_sub == 0:
                slot, part = 2 * strip + my_y, 0
            elif d_sub == 1:
                slot, part = 2 * strip + 1 - my_y, my_y
            else:
                slot, part = 2 * strip + 1 - my_y, 1 - my_y
            first = pl.multiple_of(share + part * border, 16)
            block = owed[spot * border : (spot + 1) * border]

            @pl.when((strip >= 0) & (strip < strips))
            def put(slot=slot, first=first, block=block):
                parts[slot, pl.ds(first, border), :] = block

            spot += 1
    for step in range(chunks):
        emit(step).wait()
    node_copy.wait()


def plane_sum_kernel(came, message, mine):
    border = mine.shape[0]
    share = message.shape[0] - border
    total = came[0].astype(F32)
    for slot in range(1, came.shape[0]):
        total = total + came[slot].astype(F32)
    mine[...] = total[share : share + border]
    message[:share] = total[:share].astype(BF16)
    message[share:] = total[share + border :].astype(BF16)


def line_sum_kernel(factor, mine, *refs):
    messages, (out, rim_grad, held) = refs[:-3], refs[-3:]
    border = mine.shape[0]
    share = out.shape[1]
    for k, message in enumerate(messages):
        held[k] = message[...].astype(F32)
    my_z, my_y = lax.axis_index("z"), lax.axis_index("y")
    total = held[lax.bitwise_xor(my_z, 0), :share]
    for z in range(1, len(messages)):
        total = total + held[lax.bitwise_xor(my_z, z), :share]
    total = (total * factor).astype(BF16)
    for target in range(out.shape[0]):
        out[target] = total
    source = my_z - 1 + 2 * my_y
    inside = (source >= 0) & (source < len(messages))
    passed = held[lax.bitwise_xor(my_z, jnp.clip(source, 0, len(messages) - 1)), share:]
    rim_grad[...] = mine[...] + jnp.where(inside, passed, 0.0)


def finish_kernel(came, rim_grad, local_grad, node_grad, *outs):
    border = rim_grad.shape[0]
    share = came.shape[1]
    node_grad[...] = local_grad[...]
    node_grad[:border] += rim_grad[...]
    start = 0
    for out in outs:
        size = out.shape[0]
        done = 0
        while done < size:
            slot, offset = divmod(start + done, share)
            step = min(size - done, share - offset)
            out[done : done + step] = came[slot, offset : offset + step].astype(F32)
            done += step
        start += size


def shards(
    node_latents,
    edge_latents,
    senders,
    receivers,
    edge_count,
    w_edge_in,
    w_edge_out,
    w_node_in,
    w_node_out,
    node_cotangent,
    edge_cotangent,
):
    count_p, width = node_latents.shape
    count_e = edge_latents.shape[0]
    border = count_p // 8
    strips, zs, ys = (lax.axis_size(axis) for axis in ALL)
    subs = zs * ys
    slots = strips * ys
    even, odd = swapped(node_latents, ("z", "y"))
    chunk = min(CHUNK, count_e)
    chunks = count_e // chunk
    early = call(
        early_kernel,
        [
            ((count_e, width), BF16),
            ((count_e, width), BF16),
            ((count_e, width), BF16),
            ((chunks, width, chunk), BF16),
            ((count_e, width), F32),
            ((count_e, width), BF16),
            ((chunks, 8, chunk), jnp.int32),
        ],
        [
            node_latents,
            edge_latents,
            edge_cotangent,
            senders.reshape(chunks, 1, chunk),
            receivers.reshape(chunks, 1, chunk),
            w_edge_in,
        ],
        [HBM] * 6,
        [
            pltpu.VMEM((count_p + width, width), BF16),
            pltpu.VMEM((count_p, width), BF16),
            pltpu.VMEM((count_e, width), BF16),
            pltpu.VMEM((chunks, 1, chunk), jnp.int32),
            pltpu.VMEM((chunks, 1, chunk), jnp.int32),
            pltpu.VMEM((3 * width, width), BF16),
            SEM((4,)),
            SEM((2, chunks)),
        ],
    )

    *early, odd, even = lax.optimization_barrier((*early, odd, even))
    (own_column,) = call(
        column_kernel,
        [((3 * border, width), BF16)],
        [node_latents, odd, even],
        [VMEM] * 3,
    )
    even_column, odd_column = swapped(own_column, "strip")

    share = -(-7 * width // (slots * 16)) * 16

    prepared = call(
        prepare_kernel,
        [
            ((count_p, width), BF16),
            ((2 * width, 2 * width), BF16),
            ((2 * width, 2 * width), BF16),
            ((2 * width, 2 * width), BF16),
            ((width, width), BF16),
            ((width, width), BF16),
            ((count_p, width), F32),
        ],
        [
            own_column,
            node_latents,
            w_edge_in,
            w_edge_out,
            w_node_in,
            w_node_out,
            node_cotangent,
        ],
        [VMEM] * 7,
    )
    new_nodes, new_edges, local_grad, parts = call(
        layer_kernel,
        [
            ((count_p, width), BF16),
            ((count_e, width), BF16),
            ((count_p, width), F32),
            ((slots, share + 2 * border, width), BF16),
        ],
        [
            edge_count,
            node_latents,
            own_column,
            odd_column,
            even_column,
            *early,
            w_edge_in,
            w_edge_out,
            w_node_in,
            w_node_out,
            node_cotangent,
            *prepared,
        ],
        [SMEM] + [VMEM] * 23,
        [
            pltpu.VMEM((count_p, width), BF16),
            pltpu.VMEM((count_e, width), BF16),
            pltpu.VMEM((8 * border, width), BF16),
            pltpu.VMEM((count_p, 2 * width), BF16),
            pltpu.VMEM((count_e, width), BF16),
            pltpu.VMEM((count_e // 2, 2 * width), F32),
            pltpu.VMEM((count_e // 2, 2 * width), F32),
            pltpu.VMEM((count_e // 2, 2 * width), F32),
            pltpu.VMEM((2 * count_p + width, 2 * width), F32),
            pltpu.VMEM((width, width), F32),
            pltpu.VMEM((count_p, width), F32),
            pltpu.VMEM((slots * share, width), BF16),
            pltpu.VMEM((count_p, 5 * width), BF16),
            pltpu.VMEM((9, border, width), BF16),
            SEM((chunks,)),
            SEM,
        ],
        [HBM, HBM, VMEM, VMEM],
        limit=24,
    )

    came = lax.all_to_all(parts, PLANE, 0, 0)
    state = [((share + border, width), BF16), ((border, width), F32)]
    message, mine = call(plane_sum_kernel, state, [came], [VMEM])
    factor = 1.0 / math.sqrt(count_e * strips * subs)
    messages = [message] + [
        lax.ppermute(message, "z", [(z, z ^ k) for z in range(zs)]) for k in range(1, zs)
    ]
    parts, rim_grad = call(
        functools.partial(line_sum_kernel, factor),
        [((slots, share, width), BF16), ((border, width), F32)],
        [mine, *messages],
        [VMEM] * (1 + zs),
        [pltpu.VMEM((zs, share + border, width), F32)],
    )
    came = lax.all_to_all(parts, PLANE, 0, 0)
    node_grad, *grads = call(
        finish_kernel,
        [((rows, width), F32) for rows in (count_p, 3 * width, width, 2 * width, width)],
        [came, rim_grad, local_grad],
        [VMEM, VMEM, VMEM],
    )
    return (new_nodes, new_edges, node_grad, *grads)


def solution(mesh):
    strips, subs = mesh.devices.shape
    grid = Mesh(mesh.devices.reshape(strips, subs // 2, 2), ALL)
    rows = P(ALL, None)
    line = P(ALL)
    return jax.shard_map(
        shards,
        mesh=grid,
        in_specs=(rows, rows, line, line, line, P(), P(), P(), P(), rows, rows),
        out_specs=(rows, rows, rows, P(), P(), P(), P()),
        check_vma=False,
    )
```

```python
import functools
import math

import jax
import jax.numpy as jnp
from jax import lax
from jax.experimental import pallas as pl
from jax.experimental.pallas import tpu as pltpu
from jax.sharding import Mesh
from jax.sharding import PartitionSpec as P

EPS = 1e-05
CHUNK = 1024
SPLIT = 4
UNROLL = 4
PLANE = ("strip", "y")
ALL = ("strip", "z", "y")
F32 = jnp.float32
BF16 = jnp.bfloat16
VMEM = pl.BlockSpec(memory_space=pltpu.VMEM)
SMEM = pl.BlockSpec(memory_space=pltpu.SMEM)
HBM = pl.BlockSpec(memory_space=pltpu.HBM)
SEM = pltpu.SemaphoreType.DMA


def mm(left, right):
    return jnp.dot(left, right, preferred_element_type=F32)


def mm_nt(left, right):
    return lax.dot_general(left, right, (((1,), (1,)), ((), ())), preferred_element_type=F32)


def mm_tn(left, right):
    return lax.dot_general(left, right, (((0,), (0,)), ((), ())), preferred_element_type=F32)


def silu_and_slope(values):
    sig = 0.5 + 0.5 * jnp.tanh(0.5 * values)
    act = values * sig
    return (act, sig + act * (1.0 - sig))


def found(codes, blocks):
    lane = lax.broadcasted_iota(jnp.int32, codes.shape, 1)
    one, zero = jnp.ones((), BF16), jnp.zeros((), BF16)
    width = codes.shape[1]
    return jnp.concatenate(
        [
            jnp.where(codes == (lane + width * k).astype(F32).astype(BF16), one, zero)
            for k in range(blocks)
        ],
        axis=1,
    )


def found_t(line, size):
    place = lax.broadcasted_iota(jnp.int32, (size, line.shape[1]), 0).astype(F32).astype(BF16)
    one, zero = jnp.ones((), BF16), jnp.zeros((), BF16)
    return jnp.where(place == line.astype(F32).astype(BF16), one, zero)


def in_hbm(value):
    return pltpu.with_memory_space_constraint(value, pltpu.HBM)


def call(kernel, outs, ins, specs, scratch=(), out_specs=None, limit=24):
    out_specs = [VMEM] * len(outs) if out_specs is None else out_specs
    return pl.pallas_call(
        kernel,
        out_shape=[
            pltpu.HBM(shape, dtype) if spec is HBM else jax.ShapeDtypeStruct(shape, dtype)
            for (shape, dtype), spec in zip(outs, out_specs)
        ],
        in_specs=specs,
        out_specs=out_specs,
        scratch_shapes=list(scratch),
        compiler_params=pltpu.CompilerParams(vmem_limit_bytes=limit * 2**20),
    )(*[in_hbm(value) if spec is HBM else value for value, spec in zip(ins, specs)])


def column_kernel(nodes, odd, even, out):
    border = out.shape[0] // 3
    out[:border] = nodes[:border]
    out[border : 2 * border] = even[:border]
    out[2 * border :] = odd[:border]


def swapped(value, axes):
    count = lax.axis_size(axes)
    even = [(k, k ^ 1) for k in range(count)]
    odd = [(k, min(max(((k + 1) ^ 1) - 1, 0), count - 1)) for k in range(count)]
    from_odd = lax.ppermute(value, axes, odd)
    from_even = lax.ppermute(value, axes, even)
    return from_even, from_odd


def early_kernel(
    nodes_in,
    edges_in,
    edge_cot_in,
    senders_in,
    receivers_in,
    w_edge_in_in,
    edges,
    send_codes,
    recv_codes,
    edges_t,
    pre_part,
    cot_part,
    info,
    tables,
    nodes,
    edge_cot,
    senders,
    receivers,
    w_edge_in,
    small_sems,
    sems,
):
    count_p, width = nodes_in.shape
    chunks, _, chunk = info.shape
    border = count_p // 8
    my_strip = lax.axis_index("strip")
    subs = lax.axis_size("z") * lax.axis_size("y")
    my_sub = lax.axis_index("z") * lax.axis_size("y") + lax.axis_index("y")
    place_bits, sub_bits = count_p.bit_length() - 1, subs.bit_length() - 1

    def fetch(step):
        rows = pl.ds(pl.multiple_of(step * chunk, chunk), chunk)
        return [
            pltpu.make_async_copy(edges_in.at[rows], edges.at[rows], sems.at[0, step]),
            pltpu.make_async_copy(edge_cot_in.at[rows], edge_cot.at[rows], sems.at[1, step]),
        ]

    small = [
        pltpu.make_async_copy(source, target, small_sems.at[k])
        for k, (source, target) in enumerate(
            [
                (nodes_in, nodes),
                (w_edge_in_in, w_edge_in),
                (senders_in, senders),
                (receivers_in, receivers),
            ]
        )
    ]
    for copy in small:
        copy.start()
    for step in range(chunks):
        for copy in fetch(step):
            copy.start()
    for copy in small:
        copy.wait()
    tables[:count_p] = mm(nodes[...], w_edge_in[width : 2 * width]).astype(BF16)
    tables[count_p:] = w_edge_in[2 * width :]
    line = lax.broadcasted_iota(jnp.int32, (8, chunk), 0)

    def one(step, carry):
        rows = pl.ds(pl.multiple_of(step * chunk, chunk), chunk)
        sender = jnp.broadcast_to(senders[step], (8, chunk))
        receiver = jnp.broadcast_to(receivers[step], (8, chunk))
        owner = lax.shift_right_logical(sender, place_bits)
        within = lax.bitwise_and(sender, count_p - 1)
        d_strip = lax.shift_right_logical(owner, sub_bits) - my_strip
        d_sub = lax.bitwise_and(owner, subs - 1) - my_sub
        spot = 3 * d_strip + d_sub + 4
        spot = jnp.where(spot > 4, spot - 1, spot)
        near = (d_strip == 0) & (d_sub == 0)
        spot = jnp.where(near, within, spot * border + jnp.minimum(within, border - 1))
        index = jnp.where(line == 0, spot, receiver)
        index = jnp.where(line == 2, jnp.where(near, spot, -1 - spot), index)
        info[step] = index
        columns = index.T
        for copy in fetch(step):
            copy.wait()
        edge = edges[rows]
        cot = edge_cot[rows].astype(F32)
        recv = jnp.broadcast_to(columns[:, 1:2], edge.shape).astype(F32).astype(BF16)
        recv_codes[rows] = recv
        send_codes[rows] = jnp.broadcast_to(columns[:, 2:3], edge.shape).astype(F32).astype(BF16)
        recv = found(recv, count_p // width)
        pre_part[rows] = mm(jnp.concatenate([recv, edge], axis=1), tables[...])
        edges_t[step] = edge.T
        cot_part[rows] = (cot - jnp.mean(cot, axis=1, keepdims=True)).astype(BF16)
        return carry

    lax.fori_loop(0, chunks, one, 0, unroll=UNROLL)


def prepare_kernel(
    column,
    nodes,
    w_edge_in,
    w_edge_out,
    w_node_in,
    w_node_out,
    node_cot,
    near_table,
    centring,
    back,
    means,
    node_centring,
    agg_centring,
    node_cot_c,
):
    width = nodes.shape[1]

    def twice(block):
        zero = jnp.zeros_like(block)
        return jnp.concatenate(
            [
                jnp.concatenate([block, zero], axis=1),
                jnp.concatenate([zero, block], axis=1),
            ],
            axis=0,
        )

    near_table[...] = mm(nodes[...], w_edge_in[:width]).astype(BF16)
    weight = w_edge_out[...].astype(F32)
    centring[...] = twice(weight - jnp.mean(weight, axis=1, keepdims=True)).astype(BF16)
    back[...] = twice(weight).astype(BF16)
    weight = w_node_out[...].astype(F32)
    node_centring[...] = (weight - jnp.mean(weight, axis=1, keepdims=True)).astype(BF16)
    weight = w_node_in[width:].astype(F32)
    agg_centring[...] = (weight - jnp.mean(weight, axis=0, keepdims=True)).astype(BF16)
    cot = node_cot[...].astype(F32)
    node_cot_c[...] = cot - jnp.mean(cot, axis=1, keepdims=True)
    means[...] = twice(jnp.full((width, width), 1.0 / width, F32)).astype(BF16)


def layer_kernel(
    edge_count,
    nodes,
    own_column,
    even_column,
    odd_column,
    edges,
    send_codes,
    recv_codes,
    edges_t,
    pre_part,
    cot_part,
    info,
    w_edge_in,
    w_edge_out,
    w_node_in,
    w_node_out,
    node_cot,
    near_table,
    centring,
    back,
    means,
    node_centring,
    agg_centring,
    node_cot_c,
    new_nodes_out,
    new_edges_out,
    local_grad,
    parts,
    new_nodes,
    new_edges,
    far_rows,
    tables,
    hidden,
    slope,
    normed,
    scale,
    sums,
    ge_out,
    agg,
    packed,
    kept,
    columns,
    out_sems,
    last_sem,
):
    count_p, width = nodes.shape
    border = own_column.shape[0] // 3
    slots = parts.shape[0]
    strips = slots // 2
    chunks, _, chunk = edges_t.shape
    block = chunk // SPLIT
    half = block // 2
    share = parts.shape[1] - 2 * border
    my_strip, my_y = lax.axis_index("strip"), lax.axis_index("y")
    live_count = edge_count[0]

    def span(step):
        return pl.ds(pl.multiple_of(step * chunk, chunk), chunk)

    def block_rows(step, part):
        return pl.ds(pl.multiple_of(step * chunk + part * block, block), block)

    def block_pairs(step, part):
        return pl.ds(pl.multiple_of((step * SPLIT + part) * half, half), half)

    def emit(step):
        rows = span(step)
        return pltpu.make_async_copy(
            new_edges.at[rows], new_edges_out.at[rows], out_sems.at[step]
        )

    def paired(value):
        return jnp.concatenate([value[:half], value[half:]], axis=1)

    def unpaired(value):
        return jnp.concatenate([value[:, :width], value[:, width:]], axis=0)

    for k, column in enumerate((own_column, even_column, odd_column)):
        for part in range(3):
            columns[3 * k + part] = column[part * border : (part + 1) * border]

    def partner(mine, step):
        if step == 0:
            return 0
        is_odd = lax.rem(mine, 2)
        return 1 + is_odd if step > 0 else 2 - is_odd

    spot = 0
    for d_strip in (-1, 0, 1):
        column = partner(my_strip, d_strip)
        for d_sub in (-1, 0, 1):
            if d_strip == 0 and d_sub == 0:
                continue
            rows = slice(spot * border, (spot + 1) * border)
            far_rows[rows] = columns[3 * column + partner(my_y, d_sub)]
            spot += 1
    tables[:, :width] = near_table[...]
    tables[:, width:] = mm(far_rows[...], w_edge_in[:width]).astype(BF16)
    row = lax.broadcasted_iota(jnp.int32, (half, 2 * width), 0)
    lane = lax.broadcasted_iota(jnp.int32, (half, 2 * width), 1)
    edge_row = jnp.where(lane < width, row, row + half)
    agg[...] = jnp.zeros_like(agg)

    def forward(step, carry):
        recv_t = found_t(info[step][1:2], count_p)
        units = []
        for part in range(SPLIT):
            rows, pairs = block_rows(step, part), block_pairs(step, part)
            codes = send_codes[rows]
            begun = pre_part[rows]
            edge = paired(edges[rows].astype(F32))
            place = jnp.where(codes < 0, -1 - codes, codes)
            picked = mm(found(place, count_p // width), tables[...])
            beyond = codes.astype(F32) < 0.0
            pre = begun + jnp.where(beyond, picked[:, width:], picked[:, :width])
            act, bend = silu_and_slope(paired(pre))
            act = act.astype(BF16)
            centre = mm(act, centring[...])
            spare = mm((centre * centre).astype(BF16), means[...])
            live = edge_row < live_count - step * chunk - part * block
            factor = jnp.where(live, lax.rsqrt(spare + EPS), 0.0)
            unit = centre * factor
            slope[pairs] = bend
            hidden[rows] = unpaired(act)
            scale[pairs] = factor
            normed[pairs] = unit
            new_edges[rows] = unpaired((edge + unit).astype(BF16))
            units.append(unpaired(unit.astype(BF16)))
        agg[...] += mm(recv_t, jnp.concatenate(units, axis=0))
        emit(step).start()
        return carry

    lax.fori_loop(0, chunks, forward, 0, unroll=UNROLL)

    joined = jnp.concatenate([nodes[...], agg[...].astype(BF16)], axis=1)
    node_pre = mm(joined, w_node_in[...])
    node_act, node_slope = silu_and_slope(node_pre)
    node_act = node_act.astype(BF16)
    centre = mm(node_act, node_centring[...])
    spare = jnp.mean(centre * centre, axis=1, keepdims=True)
    along = jnp.mean(node_cot_c[...] * centre, axis=1, keepdims=True)
    node_scale = lax.rsqrt(spare + EPS)
    node_unit = centre * node_scale
    d_outer = node_scale * (node_cot_c[...] - node_unit * (along * node_scale))
    d_outer = d_outer.astype(BF16)
    d_pre = (mm_nt(d_outer, w_node_out[...]) * node_slope).astype(BF16)
    d_agg = mm_nt(d_pre, agg_centring[...]).astype(BF16)
    new_nodes[...] = (nodes[...].astype(F32) + node_unit).astype(BF16)
    agg[...] = node_cot[...].astype(F32) + mm_nt(d_pre, w_node_in[:width])
    kept[:, : 2 * width] = joined
    kept[:, 2 * width : 3 * width] = node_act
    kept[:, 3 * width : 4 * width] = d_outer
    kept[:, 4 * width :] = d_pre
    node_copy = pltpu.make_async_copy(new_nodes, new_nodes_out, last_sem)
    node_copy.start()

    sums[...] = jnp.zeros_like(sums)
    ge_out[...] = jnp.zeros_like(ge_out)

    def backward(step, carry):
        index = info[step]
        turned = jnp.concatenate(
            [found_t(index[1:2], count_p), found_t(index[0:1], count_p), edges_t[step]], axis=0
        )
        acts, outs, ins = [], [], []
        for part in range(SPLIT):
            rows, pairs = block_rows(step, part), block_pairs(step, part)
            cot = cot_part[rows].astype(F32)
            recv = found(recv_codes[rows], count_p // width)
            unit = normed[pairs]
            acts.append(hidden[rows])
            beyond = send_codes[rows] < 0
            upstream = paired(cot + mm(recv, d_agg))
            along = mm((upstream * unit).astype(BF16), means[...])
            d_out = (scale[pairs] * (upstream - unit * along)).astype(BF16)
            outs.append(unpaired(d_out))
            d_in = unpaired((mm_nt(d_out, back[...]) * slope[pairs]).astype(BF16))
            zero = jnp.zeros_like(d_in)
            ins.append(
                jnp.concatenate(
                    [jnp.where(beyond, zero, d_in), jnp.where(beyond, d_in, zero)], axis=1
                )
            )
        ge_out[...] += mm_tn(jnp.concatenate(acts, axis=0), jnp.concatenate(outs, axis=0))
        sums[...] += mm(turned, jnp.concatenate(ins, axis=0))
        return carry

    lax.fori_loop(0, chunks, backward, 0, unroll=UNROLL)

    recv_sums = (sums[:count_p, :width] + sums[:count_p, width:]).astype(BF16)
    near_sums = sums[count_p : 2 * count_p, :width].astype(BF16)
    far_sums = sums[count_p : 2 * count_p, width:].astype(BF16)
    edge_sums = sums[2 * count_p :, :width] + sums[2 * count_p :, width:]
    packed[:width] = (mm_tn(nodes[...], near_sums) + mm_tn(far_rows[...], far_sums)).astype(BF16)
    packed[width : 2 * width] = mm_tn(nodes[...], recv_sums).astype(BF16)
    packed[4 * width : 6 * width] = mm_tn(kept[:, : 2 * width], kept[:, 4 * width :]).astype(BF16)
    packed[6 * width : 7 * width] = mm_tn(
        kept[:, 2 * width : 3 * width], kept[:, 3 * width : 4 * width]
    ).astype(BF16)
    packed[2 * width : 3 * width] = edge_sums.astype(BF16)
    packed[3 * width : 4 * width] = ge_out[...].astype(BF16)
    if packed.shape[0] > 7 * width:
        packed[7 * width :] = jnp.zeros((packed.shape[0] - 7 * width, width), BF16)
    local_grad[...] = (
        agg[...]
        + mm_nt(near_sums, w_edge_in[:width])
        + mm_nt(recv_sums, w_edge_in[width : 2 * width])
    )
    owed = mm_nt(far_sums, w_edge_in[:width]).astype(BF16)
    for slot in range(slots):
        parts[slot, :share] = packed[slot * share : (slot + 1) * share]
        parts[slot, share:] = jnp.zeros((2 * border, width), BF16)
    spot = 0
    for d_strip in (-1, 0, 1):
        strip = my_strip + d_strip
        for d_sub in (-1, 0, 1):
            if d_strip == 0 and d_sub == 0:
                continue
            if d_sub == 0:
                slot, part = 2 * strip + my_y, 0
            elif d_sub == 1:
                slot, part = 2 * strip + 1 - my_y, my_y
            else:
                slot, part = 2 * strip + 1 - my_y, 1 - my_y
            first = pl.multiple_of(share + part * border, 16)
            block = owed[spot * border : (spot + 1) * border]

            @pl.when((strip >= 0) & (strip < strips))
            def put(slot=slot, first=first, block=block):
                parts[slot, pl.ds(first, border), :] = block

            spot += 1
    for step in range(chunks):
        emit(step).wait()
    node_copy.wait()


def plane_sum_kernel(came, message, mine):
    border = mine.shape[0]
    share = message.shape[0] - border
    total = came[0].astype(F32)
    for slot in range(1, came.shape[0]):
        total = total + came[slot].astype(F32)
    mine[...] = total[share : share + border]
    message[:share] = total[:share].astype(BF16)
    message[share:] = total[share + border :].astype(BF16)


def line_sum_kernel(factor, mine, *refs):
    messages, (out, rim_grad, held) = refs[:-3], refs[-3:]
    border = mine.shape[0]
    share = out.shape[1]
    for k, message in enumerate(messages):
        held[k] = message[...].astype(F32)
    my_z, my_y = lax.axis_index("z"), lax.axis_index("y")
    total = held[lax.bitwise_xor(my_z, 0), :share]
    for z in range(1, len(messages)):
        total = total + held[lax.bitwise_xor(my_z, z), :share]
    total = (total * factor).astype(BF16)
    for target in range(out.shape[0]):
        out[target] = total
    source = my_z - 1 + 2 * my_y
    inside = (source >= 0) & (source < len(messages))
    passed = held[lax.bitwise_xor(my_z, jnp.clip(source, 0, len(messages) - 1)), share:]
    rim_grad[...] = mine[...] + jnp.where(inside, passed, 0.0)


def finish_kernel(came, rim_grad, local_grad, node_grad, *outs):
    border = rim_grad.shape[0]
    share = came.shape[1]
    node_grad[...] = local_grad[...]
    node_grad[:border] += rim_grad[...]
    start = 0
    for out in outs:
        size = out.shape[0]
        done = 0
        while done < size:
            slot, offset = divmod(start + done, share)
            step = min(size - done, share - offset)
            out[done : done + step] = came[slot, offset : offset + step].astype(F32)
            done += step
        start += size


def shards(
    node_latents,
    edge_latents,
    senders,
    receivers,
    edge_count,
    w_edge_in,
    w_edge_out,
    w_node_in,
    w_node_out,
    node_cotangent,
    edge_cotangent,
):
    count_p, width = node_latents.shape
    count_e = edge_latents.shape[0]
    border = count_p // 8
    strips, zs, ys = (lax.axis_size(axis) for axis in ALL)
    subs = zs * ys
    slots = strips * ys
    even, odd = swapped(node_latents, ("z", "y"))
    chunk = min(CHUNK, count_e)
    chunks = count_e // chunk
    early = call(
        early_kernel,
        [
            ((count_e, width), BF16),
            ((count_e, width), BF16),
            ((count_e, width), BF16),
            ((chunks, width, chunk), BF16),
            ((count_e, width), F32),
            ((count_e, width), BF16),
            ((chunks, 8, chunk), jnp.int32),
        ],
        [
            node_latents,
            edge_latents,
            edge_cotangent,
            senders.reshape(chunks, 1, chunk),
            receivers.reshape(chunks, 1, chunk),
            w_edge_in,
        ],
        [HBM] * 6,
        [
            pltpu.VMEM((count_p + width, width), BF16),
            pltpu.VMEM((count_p, width), BF16),
            pltpu.VMEM((count_e, width), BF16),
            pltpu.VMEM((chunks, 1, chunk), jnp.int32),
            pltpu.VMEM((chunks, 1, chunk), jnp.int32),
            pltpu.VMEM((3 * width, width), BF16),
            SEM((4,)),
            SEM((2, chunks)),
        ],
    )

    *early, odd, even = lax.optimization_barrier((*early, odd, even))
    (own_column,) = call(
        column_kernel,
        [((3 * border, width), BF16)],
        [node_latents, odd, even],
        [VMEM] * 3,
    )
    even_column, odd_column = swapped(own_column, "strip")

    share = -(-7 * width // (slots * 16)) * 16

    prepared = call(
        prepare_kernel,
        [
            ((count_p, width), BF16),
            ((2 * width, 2 * width), BF16),
            ((2 * width, 2 * width), BF16),
            ((2 * width, 2 * width), BF16),
            ((width, width), BF16),
            ((width, width), BF16),
            ((count_p, width), F32),
        ],
        [
            own_column,
            node_latents,
            w_edge_in,
            w_edge_out,
            w_node_in,
            w_node_out,
            node_cotangent,
        ],
        [VMEM] * 7,
    )
    new_nodes, new_edges, local_grad, parts = call(
        layer_kernel,
        [
            ((count_p, width), BF16),
            ((count_e, width), BF16),
            ((count_p, width), F32),
            ((slots, share + 2 * border, width), BF16),
        ],
        [
            edge_count,
            node_latents,
            own_column,
            even_column,
            odd_column,
            *early,
            w_edge_in,
            w_edge_out,
            w_node_in,
            w_node_out,
            node_cotangent,
            *prepared,
        ],
        [SMEM] + [VMEM] * 23,
        [
            pltpu.VMEM((count_p, width), BF16),
            pltpu.VMEM((count_e, width), BF16),
            pltpu.VMEM((8 * border, width), BF16),
            pltpu.VMEM((count_p, 2 * width), BF16),
            pltpu.VMEM((count_e, width), BF16),
            pltpu.VMEM((count_e // 2, 2 * width), F32),
            pltpu.VMEM((count_e // 2, 2 * width), F32),
            pltpu.VMEM((count_e // 2, 2 * width), F32),
            pltpu.VMEM((2 * count_p + width, 2 * width), F32),
            pltpu.VMEM((width, width), F32),
            pltpu.VMEM((count_p, width), F32),
            pltpu.VMEM((slots * share, width), BF16),
            pltpu.VMEM((count_p, 5 * width), BF16),
            pltpu.VMEM((9, border, width), BF16),
            SEM((chunks,)),
            SEM,
        ],
        [HBM, HBM, VMEM, VMEM],
        limit=24,
    )

    came = lax.all_to_all(parts, PLANE, 0, 0)
    state = [((share + border, width), BF16), ((border, width), F32)]
    message, mine = call(plane_sum_kernel, state, [came], [VMEM])
    factor = 1.0 / math.sqrt(count_e * strips * subs)
    messages = [message] + [
        lax.ppermute(message, "z", [(z, z ^ k) for z in range(zs)]) for k in range(1, zs)
    ]
    parts, rim_grad = call(
        functools.partial(line_sum_kernel, factor),
        [((slots, share, width), BF16), ((border, width), F32)],
        [mine, *messages],
        [VMEM] * (1 + zs),
        [pltpu.VMEM((zs, share + border, width), F32)],
    )
    came = lax.all_to_all(parts, PLANE, 0, 0)
    node_grad, *grads = call(
        finish_kernel,
        [((rows, width), F32) for rows in (count_p, 3 * width, width, 2 * width, width)],
        [came, rim_grad, local_grad],
        [VMEM, VMEM, VMEM],
    )
    return (new_nodes, new_edges, node_grad, *grads)


def solution(mesh):
    strips, subs = mesh.devices.shape
    grid = Mesh(mesh.devices.reshape(strips, subs // 2, 2), ALL)
    rows = P(ALL, None)
    line = P(ALL)
    return jax.shard_map(
        shards,
        mesh=grid,
        in_specs=(rows, rows, line, line, line, P(), P(), P(), P(), rows, rows),
        out_specs=(rows, rows, rows, P(), P(), P(), P()),
        check_vma=False,
    )
```

```python
import functools
import math

import jax
import jax.numpy as jnp
from jax import lax
from jax.experimental import pallas as pl
from jax.experimental.pallas import tpu as pltpu
from jax.sharding import Mesh
from jax.sharding import PartitionSpec as P

EPS = 1e-05
CHUNK = 1024
SPLIT = 1
UNROLL = 4
PLANE = ("strip", "y")
ALL = ("strip", "z", "y")
F32 = jnp.float32
BF16 = jnp.bfloat16
VMEM = pl.BlockSpec(memory_space=pltpu.VMEM)
SMEM = pl.BlockSpec(memory_space=pltpu.SMEM)
HBM = pl.BlockSpec(memory_space=pltpu.HBM)
SEM = pltpu.SemaphoreType.DMA


def mm(left, right):
    return jnp.dot(left, right, preferred_element_type=F32)


def mm_nt(left, right):
    return lax.dot_general(left, right, (((1,), (1,)), ((), ())), preferred_element_type=F32)


def mm_tn(left, right):
    return lax.dot_general(left, right, (((0,), (0,)), ((), ())), preferred_element_type=F32)


def silu_and_slope(values):
    sig = 0.5 + 0.5 * jnp.tanh(0.5 * values)
    act = values * sig
    return (act, sig + act * (1.0 - sig))


def found(codes, blocks):
    lane = lax.broadcasted_iota(jnp.int32, codes.shape, 1)
    one, zero = jnp.ones((), BF16), jnp.zeros((), BF16)
    width = codes.shape[1]
    return jnp.concatenate(
        [
            jnp.where(codes == (lane + width * k).astype(F32).astype(BF16), one, zero)
            for k in range(blocks)
        ],
        axis=1,
    )


def found_t(line, size):
    place = lax.broadcasted_iota(jnp.int32, (size, line.shape[1]), 0).astype(F32).astype(BF16)
    one, zero = jnp.ones((), BF16), jnp.zeros((), BF16)
    return jnp.where(place == line.astype(F32).astype(BF16), one, zero)


def in_hbm(value):
    return pltpu.with_memory_space_constraint(value, pltpu.HBM)


def call(kernel, outs, ins, specs, scratch=(), out_specs=None, limit=24):
    out_specs = [VMEM] * len(outs) if out_specs is None else out_specs
    return pl.pallas_call(
        kernel,
        out_shape=[
            pltpu.HBM(shape, dtype) if spec is HBM else jax.ShapeDtypeStruct(shape, dtype)
            for (shape, dtype), spec in zip(outs, out_specs)
        ],
        in_specs=specs,
        out_specs=out_specs,
        scratch_shapes=list(scratch),
        compiler_params=pltpu.CompilerParams(vmem_limit_bytes=limit * 2**20),
    )(*[in_hbm(value) if spec is HBM else value for value, spec in zip(ins, specs)])


def column_kernel(nodes, odd, even, out):
    border = out.shape[0] // 3
    out[:border] = nodes[:border]
    out[border : 2 * border] = even[:border]
    out[2 * border :] = odd[:border]


def swapped(value, axes):
    count = lax.axis_size(axes)
    even = [(k, k ^ 1) for k in range(count)]
    odd = [(k, min(max(((k + 1) ^ 1) - 1, 0), count - 1)) for k in range(count)]
    from_odd = lax.ppermute(value, axes, odd)
    from_even = lax.ppermute(value, axes, even)
    return from_even, from_odd


def early_kernel(
    nodes_in,
    edges_in,
    edge_cot_in,
    senders_in,
    receivers_in,
    w_edge_in_in,
    edges,
    send_codes,
    recv_codes,
    edges_t,
    pre_part,
    cot_part,
    info,
    tables,
    nodes,
    edge_cot,
    senders,
    receivers,
    w_edge_in,
    small_sems,
    sems,
):
    count_p, width = nodes_in.shape
    chunks, _, chunk = info.shape
    border = count_p // 8
    my_strip = lax.axis_index("strip")
    subs = lax.axis_size("z") * lax.axis_size("y")
    my_sub = lax.axis_index("z") * lax.axis_size("y") + lax.axis_index("y")
    place_bits, sub_bits = count_p.bit_length() - 1, subs.bit_length() - 1

    def fetch(step):
        rows = pl.ds(pl.multiple_of(step * chunk, chunk), chunk)
        return [
            pltpu.make_async_copy(edges_in.at[rows], edges.at[rows], sems.at[0, step]),
            pltpu.make_async_copy(edge_cot_in.at[rows], edge_cot.at[rows], sems.at[1, step]),
        ]

    small = [
        pltpu.make_async_copy(source, target, small_sems.at[k])
        for k, (source, target) in enumerate(
            [
                (nodes_in, nodes),
                (w_edge_in_in, w_edge_in),
                (senders_in, senders),
                (receivers_in, receivers),
            ]
        )
    ]
    for copy in small:
        copy.start()
    for step in range(chunks):
        for copy in fetch(step):
            copy.start()
    for copy in small:
        copy.wait()
    tables[:count_p] = mm(nodes[...], w_edge_in[width : 2 * width]).astype(BF16)
    tables[count_p:] = w_edge_in[2 * width :]
    line = lax.broadcasted_iota(jnp.int32, (8, chunk), 0)

    def one(step, carry):
        rows = pl.ds(pl.multiple_of(step * chunk, chunk), chunk)
        sender = jnp.broadcast_to(senders[step], (8, chunk))
        receiver = jnp.broadcast_to(receivers[step], (8, chunk))
        owner = lax.shift_right_logical(sender, place_bits)
        within = lax.bitwise_and(sender, count_p - 1)
        d_strip = lax.shift_right_logical(owner, sub_bits) - my_strip
        d_sub = lax.bitwise_and(owner, subs - 1) - my_sub
        spot = 3 * d_strip + d_sub + 4
        spot = jnp.where(spot > 4, spot - 1, spot)
        near = (d_strip == 0) & (d_sub == 0)
        spot = jnp.where(near, within, spot * border + jnp.minimum(within, border - 1))
        index = jnp.where(line == 0, spot, receiver)
        index = jnp.where(line == 2, jnp.where(near, spot, -1 - spot), index)
        info[step] = index
        columns = index.T
        for copy in fetch(step):
            copy.wait()
        edge = edges[rows]
        cot = edge_cot[rows].astype(F32)
        recv = jnp.broadcast_to(columns[:, 1:2], edge.shape).astype(F32).astype(BF16)
        recv_codes[rows] = recv
        send_codes[rows] = jnp.broadcast_to(columns[:, 2:3], edge.shape).astype(F32).astype(BF16)
        recv = found(recv, count_p // width)
        pre_part[rows] = mm(jnp.concatenate([recv, edge], axis=1), tables[...])
        edges_t[step] = edge.T
        cot_part[rows] = (cot - jnp.mean(cot, axis=1, keepdims=True)).astype(BF16)
        return carry

    lax.fori_loop(0, chunks, one, 0, unroll=UNROLL)


def prepare_kernel(
    column,
    nodes,
    w_edge_in,
    w_edge_out,
    w_node_in,
    w_node_out,
    node_cot,
    near_table,
    centring,
    back,
    means,
    node_centring,
    agg_centring,
    node_cot_c,
):
    width = nodes.shape[1]

    def twice(block):
        zero = jnp.zeros_like(block)
        return jnp.concatenate(
            [
                jnp.concatenate([block, zero], axis=1),
                jnp.concatenate([zero, block], axis=1),
            ],
            axis=0,
        )

    near_table[...] = mm(nodes[...], w_edge_in[:width]).astype(BF16)
    weight = w_edge_out[...].astype(F32)
    centring[...] = twice(weight - jnp.mean(weight, axis=1, keepdims=True)).astype(BF16)
    back[...] = twice(weight).astype(BF16)
    weight = w_node_out[...].astype(F32)
    node_centring[...] = (weight - jnp.mean(weight, axis=1, keepdims=True)).astype(BF16)
    weight = w_node_in[width:].astype(F32)
    agg_centring[...] = (weight - jnp.mean(weight, axis=0, keepdims=True)).astype(BF16)
    cot = node_cot[...].astype(F32)
    node_cot_c[...] = cot - jnp.mean(cot, axis=1, keepdims=True)
    means[...] = twice(jnp.full((width, width), 1.0 / width, F32)).astype(BF16)


def layer_kernel(
    edge_count,
    nodes,
    own_column,
    even_column,
    odd_column,
    edges,
    send_codes,
    recv_codes,
    edges_t,
    pre_part,
    cot_part,
    info,
    w_edge_in,
    w_edge_out,
    w_node_in,
    w_node_out,
    node_cot,
    near_table,
    centring,
    back,
    means,
    node_centring,
    agg_centring,
    node_cot_c,
    new_nodes_out,
    new_edges_out,
    local_grad,
    parts,
    new_nodes,
    new_edges,
    far_rows,
    tables,
    hidden,
    slope,
    normed,
    scale,
    sums,
    ge_out,
    agg,
    packed,
    kept,
    columns,
    out_sems,
    last_sem,
):
    count_p, width = nodes.shape
    border = own_column.shape[0] // 3
    slots = parts.shape[0]
    strips = slots // 2
    chunks, _, chunk = edges_t.shape
    block = chunk // SPLIT
    half = block // 2
    share = parts.shape[1] - 2 * border
    my_strip, my_y = lax.axis_index("strip"), lax.axis_index("y")
    live_count = edge_count[0]

    def span(step):
        return pl.ds(pl.multiple_of(step * chunk, chunk), chunk)

    def block_rows(step, part):
        return pl.ds(pl.multiple_of(step * chunk + part * block, block), block)

    def block_pairs(step, part):
        return pl.ds(pl.multiple_of((step * SPLIT + part) * half, half), half)

    def emit(step):
        rows = span(step)
        return pltpu.make_async_copy(
            new_edges.at[rows], new_edges_out.at[rows], out_sems.at[step]
        )

    def paired(value):
        return jnp.concatenate([value[:half], value[half:]], axis=1)

    def unpaired(value):
        return jnp.concatenate([value[:, :width], value[:, width:]], axis=0)

    for k, column in enumerate((own_column, even_column, odd_column)):
        for part in range(3):
            columns[3 * k + part] = column[part * border : (part + 1) * border]

    def partner(mine, step):
        if step == 0:
            return 0
        is_odd = lax.rem(mine, 2)
        return 1 + is_odd if step > 0 else 2 - is_odd

    spot = 0
    for d_strip in (-1, 0, 1):
        column = partner(my_strip, d_strip)
        for d_sub in (-1, 0, 1):
            if d_strip == 0 and d_sub == 0:
                continue
            rows = slice(spot * border, (spot + 1) * border)
            far_rows[rows] = columns[3 * column + partner(my_y, d_sub)]
            spot += 1
    tables[:, :width] = near_table[...]
    tables[:, width:] = mm(far_rows[...], w_edge_in[:width]).astype(BF16)
    row = lax.broadcasted_iota(jnp.int32, (half, 2 * width), 0)
    lane = lax.broadcasted_iota(jnp.int32, (half, 2 * width), 1)
    edge_row = jnp.where(lane < width, row, row + half)
    agg[...] = jnp.zeros_like(agg)

    def forward(step, carry):
        recv_t = found_t(info[step][1:2], count_p)
        units = []
        for part in range(SPLIT):
            rows, pairs = block_rows(step, part), block_pairs(step, part)
            codes = send_codes[rows]
            begun = pre_part[rows]
            edge = paired(edges[rows].astype(F32))
            place = jnp.where(codes < 0, -1 - codes, codes)
            picked = mm(found(place, count_p // width), tables[...])
            beyond = codes.astype(F32) < 0.0
            pre = begun + jnp.where(beyond, picked[:, width:], picked[:, :width])
            act, bend = silu_and_slope(paired(pre))
            act = act.astype(BF16)
            centre = mm(act, centring[...])
            spare = mm((centre * centre).astype(BF16), means[...])
            live = edge_row < live_count - step * chunk - part * block
            factor = jnp.where(live, lax.rsqrt(spare + EPS), 0.0)
            unit = centre * factor
            slope[pairs] = bend
            hidden[rows] = unpaired(act)
            scale[pairs] = factor
            normed[pairs] = unit
            new_edges[rows] = unpaired((edge + unit).astype(BF16))
            units.append(unpaired(unit.astype(BF16)))
        agg[...] += mm(recv_t, jnp.concatenate(units, axis=0))
        emit(step).start()
        return carry

    lax.fori_loop(0, chunks, forward, 0, unroll=UNROLL)

    joined = jnp.concatenate([nodes[...], agg[...].astype(BF16)], axis=1)
    node_pre = mm(joined, w_node_in[...])
    node_act, node_slope = silu_and_slope(node_pre)
    node_act = node_act.astype(BF16)
    centre = mm(node_act, node_centring[...])
    spare = jnp.mean(centre * centre, axis=1, keepdims=True)
    along = jnp.mean(node_cot_c[...] * centre, axis=1, keepdims=True)
    node_scale = lax.rsqrt(spare + EPS)
    node_unit = centre * node_scale
    d_outer = node_scale * (node_cot_c[...] - node_unit * (along * node_scale))
    d_outer = d_outer.astype(BF16)
    d_pre = (mm_nt(d_outer, w_node_out[...]) * node_slope).astype(BF16)
    d_agg = mm_nt(d_pre, agg_centring[...]).astype(BF16)
    new_nodes[...] = (nodes[...].astype(F32) + node_unit).astype(BF16)
    agg[...] = node_cot[...].astype(F32) + mm_nt(d_pre, w_node_in[:width])
    kept[:, : 2 * width] = joined
    kept[:, 2 * width : 3 * width] = node_act
    kept[:, 3 * width : 4 * width] = d_outer
    kept[:, 4 * width :] = d_pre
    node_copy = pltpu.make_async_copy(new_nodes, new_nodes_out, last_sem)
    node_copy.start()

    sums[...] = jnp.zeros_like(sums)
    ge_out[...] = jnp.zeros_like(ge_out)

    def backward(step, carry):
        index = info[step]
        turned = jnp.concatenate(
            [found_t(index[1:2], count_p), found_t(index[0:1], count_p), edges_t[step]], axis=0
        )
        acts, outs, ins = [], [], []
        for part in range(SPLIT):
            rows, pairs = block_rows(step, part), block_pairs(step, part)
            cot = cot_part[rows].astype(F32)
            recv = found(recv_codes[rows], count_p // width)
            unit = normed[pairs]
            acts.append(hidden[rows])
            beyond = send_codes[rows] < 0
            upstream = paired(cot + mm(recv, d_agg))
            along = mm((upstream * unit).astype(BF16), means[...])
            d_out = (scale[pairs] * (upstream - unit * along)).astype(BF16)
            outs.append(unpaired(d_out))
            d_in = unpaired((mm_nt(d_out, back[...]) * slope[pairs]).astype(BF16))
            zero = jnp.zeros_like(d_in)
            ins.append(
                jnp.concatenate(
                    [jnp.where(beyond, zero, d_in), jnp.where(beyond, d_in, zero)], axis=1
                )
            )
        ge_out[...] += mm_tn(jnp.concatenate(acts, axis=0), jnp.concatenate(outs, axis=0))
        sums[...] += mm(turned, jnp.concatenate(ins, axis=0))
        return carry

    lax.fori_loop(0, chunks, backward, 0, unroll=UNROLL)

    recv_sums = (sums[:count_p, :width] + sums[:count_p, width:]).astype(BF16)
    near_sums = sums[count_p : 2 * count_p, :width].astype(BF16)
    far_sums = sums[count_p : 2 * count_p, width:].astype(BF16)
    edge_sums = sums[2 * count_p :, :width] + sums[2 * count_p :, width:]
    packed[:width] = (mm_tn(nodes[...], near_sums) + mm_tn(far_rows[...], far_sums)).astype(BF16)
    packed[width : 2 * width] = mm_tn(nodes[...], recv_sums).astype(BF16)
    packed[4 * width : 6 * width] = mm_tn(kept[:, : 2 * width], kept[:, 4 * width :]).astype(BF16)
    packed[6 * width : 7 * width] = mm_tn(
        kept[:, 2 * width : 3 * width], kept[:, 3 * width : 4 * width]
    ).astype(BF16)
    packed[2 * width : 3 * width] = edge_sums.astype(BF16)
    packed[3 * width : 4 * width] = ge_out[...].astype(BF16)
    if packed.shape[0] > 7 * width:
        packed[7 * width :] = jnp.zeros((packed.shape[0] - 7 * width, width), BF16)
    local_grad[...] = (
        agg[...]
        + mm_nt(near_sums, w_edge_in[:width])
        + mm_nt(recv_sums, w_edge_in[width : 2 * width])
    )
    owed = mm_nt(far_sums, w_edge_in[:width]).astype(BF16)
    for slot in range(slots):
        parts[slot, :share] = packed[slot * share : (slot + 1) * share]
        parts[slot, share:] = jnp.zeros((2 * border, width), BF16)
    spot = 0
    for d_strip in (-1, 0, 1):
        strip = my_strip + d_strip
        for d_sub in (-1, 0, 1):
            if d_strip == 0 and d_sub == 0:
                continue
            if d_sub == 0:
                slot, part = 2 * strip + my_y, 0
            elif d_sub == 1:
                slot, part = 2 * strip + 1 - my_y, my_y
            else:
                slot, part = 2 * strip + 1 - my_y, 1 - my_y
            first = pl.multiple_of(share + part * border, 16)
            block = owed[spot * border : (spot + 1) * border]

            @pl.when((strip >= 0) & (strip < strips))
            def put(slot=slot, first=first, block=block):
                parts[slot, pl.ds(first, border), :] = block

            spot += 1
    for step in range(chunks):
        emit(step).wait()
    node_copy.wait()


def plane_sum_kernel(came, message, mine):
    border = mine.shape[0]
    share = message.shape[0] - border
    total = came[0].astype(F32)
    for slot in range(1, came.shape[0]):
        total = total + came[slot].astype(F32)
    mine[...] = total[share : share + border]
    message[:share] = total[:share].astype(BF16)
    message[share:] = total[share + border :].astype(BF16)


def line_sum_kernel(factor, mine, *refs):
    messages, (out, rim_grad, held) = refs[:-3], refs[-3:]
    border = mine.shape[0]
    share = out.shape[1]
    for k, message in enumerate(messages):
        held[k] = message[...].astype(F32)
    my_z, my_y = lax.axis_index("z"), lax.axis_index("y")
    total = held[lax.bitwise_xor(my_z, 0), :share]
    for z in range(1, len(messages)):
        total = total + held[lax.bitwise_xor(my_z, z), :share]
    total = (total * factor).astype(BF16)
    for target in range(out.shape[0]):
        out[target] = total
    source = my_z - 1 + 2 * my_y
    inside = (source >= 0) & (source < len(messages))
    passed = held[lax.bitwise_xor(my_z, jnp.clip(source, 0, len(messages) - 1)), share:]
    rim_grad[...] = mine[...] + jnp.where(inside, passed, 0.0)


def finish_kernel(came, rim_grad, local_grad, node_grad, *outs):
    border = rim_grad.shape[0]
    share = came.shape[1]
    node_grad[...] = local_grad[...]
    node_grad[:border] += rim_grad[...]
    start = 0
    for out in outs:
        size = out.shape[0]
        done = 0
        while done < size:
            slot, offset = divmod(start + done, share)
            step = min(size - done, share - offset)
            out[done : done + step] = came[slot, offset : offset + step].astype(F32)
            done += step
        start += size


def shards(
    node_latents,
    edge_latents,
    senders,
    receivers,
    edge_count,
    w_edge_in,
    w_edge_out,
    w_node_in,
    w_node_out,
    node_cotangent,
    edge_cotangent,
):
    count_p, width = node_latents.shape
    count_e = edge_latents.shape[0]
    border = count_p // 8
    strips, zs, ys = (lax.axis_size(axis) for axis in ALL)
    subs = zs * ys
    slots = strips * ys
    even, odd = swapped(node_latents, ("z", "y"))
    chunk = min(CHUNK, count_e)
    chunks = count_e // chunk
    early = call(
        early_kernel,
        [
            ((count_e, width), BF16),
            ((count_e, width), BF16),
            ((count_e, width), BF16),
            ((chunks, width, chunk), BF16),
            ((count_e, width), F32),
            ((count_e, width), BF16),
            ((chunks, 8, chunk), jnp.int32),
        ],
        [
            node_latents,
            edge_latents,
            edge_cotangent,
            senders.reshape(chunks, 1, chunk),
            receivers.reshape(chunks, 1, chunk),
            w_edge_in,
        ],
        [HBM] * 6,
        [
            pltpu.VMEM((count_p + width, width), BF16),
            pltpu.VMEM((count_p, width), BF16),
            pltpu.VMEM((count_e, width), BF16),
            pltpu.VMEM((chunks, 1, chunk), jnp.int32),
            pltpu.VMEM((chunks, 1, chunk), jnp.int32),
            pltpu.VMEM((3 * width, width), BF16),
            SEM((4,)),
            SEM((2, chunks)),
        ],
    )

    *early, odd, even = lax.optimization_barrier((*early, odd, even))
    (own_column,) = call(
        column_kernel,
        [((3 * border, width), BF16)],
        [node_latents, odd, even],
        [VMEM] * 3,
    )
    even_column, odd_column = swapped(own_column, "strip")

    share = -(-7 * width // (slots * 16)) * 16

    prepared = call(
        prepare_kernel,
        [
            ((count_p, width), BF16),
            ((2 * width, 2 * width), BF16),
            ((2 * width, 2 * width), BF16),
            ((2 * width, 2 * width), BF16),
            ((width, width), BF16),
            ((width, width), BF16),
            ((count_p, width), F32),
        ],
        [
            own_column,
            node_latents,
            w_edge_in,
            w_edge_out,
            w_node_in,
            w_node_out,
            node_cotangent,
        ],
        [VMEM] * 7,
    )
    new_nodes, new_edges, local_grad, parts = call(
        layer_kernel,
        [
            ((count_p, width), BF16),
            ((count_e, width), BF16),
            ((count_p, width), F32),
            ((slots, share + 2 * border, width), BF16),
        ],
        [
            edge_count,
            node_latents,
            own_column,
            even_column,
            odd_column,
            *early,
            w_edge_in,
            w_edge_out,
            w_node_in,
            w_node_out,
            node_cotangent,
            *prepared,
        ],
        [SMEM] + [VMEM] * 23,
        [
            pltpu.VMEM((count_p, width), BF16),
            pltpu.VMEM((count_e, width), BF16),
            pltpu.VMEM((8 * border, width), BF16),
            pltpu.VMEM((count_p, 2 * width), BF16),
            pltpu.VMEM((count_e, width), BF16),
            pltpu.VMEM((count_e // 2, 2 * width), F32),
            pltpu.VMEM((count_e // 2, 2 * width), F32),
            pltpu.VMEM((count_e // 2, 2 * width), F32),
            pltpu.VMEM((2 * count_p + width, 2 * width), F32),
            pltpu.VMEM((width, width), F32),
            pltpu.VMEM((count_p, width), F32),
            pltpu.VMEM((slots * share, width), BF16),
            pltpu.VMEM((count_p, 5 * width), BF16),
            pltpu.VMEM((9, border, width), BF16),
            SEM((chunks,)),
            SEM,
        ],
        [HBM, HBM, VMEM, VMEM],
        limit=24,
    )

    came = lax.all_to_all(parts, PLANE, 0, 0)
    state = [((share + border, width), BF16), ((border, width), F32)]
    message, mine = call(plane_sum_kernel, state, [came], [VMEM])
    factor = 1.0 / math.sqrt(count_e * strips * subs)
    messages = [message] + [
        lax.ppermute(message, "z", [(z, z ^ k) for z in range(zs)]) for k in range(1, zs)
    ]
    parts, rim_grad = call(
        functools.partial(line_sum_kernel, factor),
        [((slots, share, width), BF16), ((border, width), F32)],
        [mine, *messages],
        [VMEM] * (1 + zs),
        [pltpu.VMEM((zs, share + border, width), F32)],
    )
    came = lax.all_to_all(parts, PLANE, 0, 0)
    node_grad, *grads = call(
        finish_kernel,
        [((rows, width), F32) for rows in (count_p, 3 * width, width, 2 * width, width)],
        [came, rim_grad, local_grad],
        [VMEM, VMEM, VMEM],
    )
    return (new_nodes, new_edges, node_grad, *grads)


def solution(mesh):
    strips, subs = mesh.devices.shape
    grid = Mesh(mesh.devices.reshape(strips, subs // 2, 2), ALL)
    rows = P(ALL, None)
    line = P(ALL)
    return jax.shard_map(
        shards,
        mesh=grid,
        in_specs=(rows, rows, line, line, line, P(), P(), P(), P(), rows, rows),
        out_specs=(rows, rows, rows, P(), P(), P(), P()),
        check_vma=False,
    )
```

```python
import functools
import math

import jax
import jax.numpy as jnp
from jax import lax
from jax.experimental import pallas as pl
from jax.experimental.pallas import tpu as pltpu
from jax.sharding import Mesh
from jax.sharding import PartitionSpec as P

EPS = 1e-05
CHUNK = 2048
SPLIT = 1
UNROLL = 2
PLANE = ("strip", "y")
ALL = ("strip", "z", "y")
F32 = jnp.float32
BF16 = jnp.bfloat16
VMEM = pl.BlockSpec(memory_space=pltpu.VMEM)
SMEM = pl.BlockSpec(memory_space=pltpu.SMEM)
HBM = pl.BlockSpec(memory_space=pltpu.HBM)
SEM = pltpu.SemaphoreType.DMA


def mm(left, right):
    return jnp.dot(left, right, preferred_element_type=F32)


def mm_nt(left, right):
    return lax.dot_general(left, right, (((1,), (1,)), ((), ())), preferred_element_type=F32)


def mm_tn(left, right):
    return lax.dot_general(left, right, (((0,), (0,)), ((), ())), preferred_element_type=F32)


def silu_and_slope(values):
    sig = 0.5 + 0.5 * jnp.tanh(0.5 * values)
    act = values * sig
    return (act, sig + act * (1.0 - sig))


def found(codes, blocks):
    lane = lax.broadcasted_iota(jnp.int32, codes.shape, 1)
    one, zero = jnp.ones((), BF16), jnp.zeros((), BF16)
    width = codes.shape[1]
    return jnp.concatenate(
        [
            jnp.where(codes == (lane + width * k).astype(F32).astype(BF16), one, zero)
            for k in range(blocks)
        ],
        axis=1,
    )


def found_t(line, size):
    place = lax.broadcasted_iota(jnp.int32, (size, line.shape[1]), 0).astype(F32).astype(BF16)
    one, zero = jnp.ones((), BF16), jnp.zeros((), BF16)
    return jnp.where(place == line.astype(F32).astype(BF16), one, zero)


def in_hbm(value):
    return pltpu.with_memory_space_constraint(value, pltpu.HBM)


def call(kernel, outs, ins, specs, scratch=(), out_specs=None, limit=24):
    out_specs = [VMEM] * len(outs) if out_specs is None else out_specs
    return pl.pallas_call(
        kernel,
        out_shape=[
            pltpu.HBM(shape, dtype) if spec is HBM else jax.ShapeDtypeStruct(shape, dtype)
            for (shape, dtype), spec in zip(outs, out_specs)
        ],
        in_specs=specs,
        out_specs=out_specs,
        scratch_shapes=list(scratch),
        compiler_params=pltpu.CompilerParams(vmem_limit_bytes=limit * 2**20),
    )(*[in_hbm(value) if spec is HBM else value for value, spec in zip(ins, specs)])


def column_kernel(nodes, odd, even, out):
    border = out.shape[0] // 3
    out[:border] = nodes[:border]
    out[border : 2 * border] = even[:border]
    out[2 * border :] = odd[:border]


def swapped(value, axes):
    count = lax.axis_size(axes)
    even = [(k, k ^ 1) for k in range(count)]
    odd = [(k, min(max(((k + 1) ^ 1) - 1, 0), count - 1)) for k in range(count)]
    from_odd = lax.ppermute(value, axes, odd)
    from_even = lax.ppermute(value, axes, even)
    return from_even, from_odd


def early_kernel(
    nodes_in,
    edges_in,
    edge_cot_in,
    senders_in,
    receivers_in,
    w_edge_in_in,
    edges,
    send_codes,
    recv_codes,
    edges_t,
    pre_part,
    cot_part,
    info,
    tables,
    nodes,
    edge_cot,
    senders,
    receivers,
    w_edge_in,
    small_sems,
    sems,
):
    count_p, width = nodes_in.shape
    chunks, _, chunk = info.shape
    border = count_p // 8
    my_strip = lax.axis_index("strip")
    subs = lax.axis_size("z") * lax.axis_size("y")
    my_sub = lax.axis_index("z") * lax.axis_size("y") + lax.axis_index("y")
    place_bits, sub_bits = count_p.bit_length() - 1, subs.bit_length() - 1

    def fetch(step):
        rows = pl.ds(pl.multiple_of(step * chunk, chunk), chunk)
        return [
            pltpu.make_async_copy(edges_in.at[rows], edges.at[rows], sems.at[0, step]),
            pltpu.make_async_copy(edge_cot_in.at[rows], edge_cot.at[rows], sems.at[1, step]),
        ]

    small = [
        pltpu.make_async_copy(source, target, small_sems.at[k])
        for k, (source, target) in enumerate(
            [
                (nodes_in, nodes),
                (w_edge_in_in, w_edge_in),
                (senders_in, senders),
                (receivers_in, receivers),
            ]
        )
    ]
    for copy in small:
        copy.start()
    for step in range(chunks):
        for copy in fetch(step):
            copy.start()
    for copy in small:
        copy.wait()
    tables[:count_p] = mm(nodes[...], w_edge_in[width : 2 * width]).astype(BF16)
    tables[count_p:] = w_edge_in[2 * width :]
    line = lax.broadcasted_iota(jnp.int32, (8, chunk), 0)

    def one(step, carry):
        rows = pl.ds(pl.multiple_of(step * chunk, chunk), chunk)
        sender = jnp.broadcast_to(senders[step], (8, chunk))
        receiver = jnp.broadcast_to(receivers[step], (8, chunk))
        owner = lax.shift_right_logical(sender, place_bits)
        within = lax.bitwise_and(sender, count_p - 1)
        d_strip = lax.shift_right_logical(owner, sub_bits) - my_strip
        d_sub = lax.bitwise_and(owner, subs - 1) - my_sub
        spot = 3 * d_strip + d_sub + 4
        spot = jnp.where(spot > 4, spot - 1, spot)
        near = (d_strip == 0) & (d_sub == 0)
        spot = jnp.where(near, within, spot * border + jnp.minimum(within, border - 1))
        index = jnp.where(line == 0, spot, receiver)
        index = jnp.where(line == 2, jnp.where(near, spot, -1 - spot), index)
        info[step] = index
        columns = index.T
        for copy in fetch(step):
            copy.wait()
        edge = edges[rows]
        cot = edge_cot[rows].astype(F32)
        recv = jnp.broadcast_to(columns[:, 1:2], edge.shape).astype(F32).astype(BF16)
        recv_codes[rows] = recv
        send_codes[rows] = jnp.broadcast_to(columns[:, 2:3], edge.shape).astype(F32).astype(BF16)
        recv = found(recv, count_p // width)
        pre_part[rows] = mm(jnp.concatenate([recv, edge], axis=1), tables[...])
        edges_t[step] = edge.T
        cot_part[rows] = (cot - jnp.mean(cot, axis=1, keepdims=True)).astype(BF16)
        return carry

    lax.fori_loop(0, chunks, one, 0, unroll=UNROLL)


def prepare_kernel(
    column,
    nodes,
    w_edge_in,
    w_edge_out,
    w_node_in,
    w_node_out,
    node_cot,
    near_table,
    centring,
    back,
    means,
    node_centring,
    agg_centring,
    node_cot_c,
):
    width = nodes.shape[1]

    def twice(block):
        zero = jnp.zeros_like(block)
        return jnp.concatenate(
            [
                jnp.concatenate([block, zero], axis=1),
                jnp.concatenate([zero, block], axis=1),
            ],
            axis=0,
        )

    near_table[...] = mm(nodes[...], w_edge_in[:width]).astype(BF16)
    weight = w_edge_out[...].astype(F32)
    centring[...] = twice(weight - jnp.mean(weight, axis=1, keepdims=True)).astype(BF16)
    back[...] = twice(weight).astype(BF16)
    weight = w_node_out[...].astype(F32)
    node_centring[...] = (weight - jnp.mean(weight, axis=1, keepdims=True)).astype(BF16)
    weight = w_node_in[width:].astype(F32)
    agg_centring[...] = (weight - jnp.mean(weight, axis=0, keepdims=True)).astype(BF16)
    cot = node_cot[...].astype(F32)
    node_cot_c[...] = cot - jnp.mean(cot, axis=1, keepdims=True)
    means[...] = twice(jnp.full((width, width), 1.0 / width, F32)).astype(BF16)


def layer_kernel(
    edge_count,
    nodes,
    own_column,
    even_column,
    odd_column,
    edges,
    send_codes,
    recv_codes,
    edges_t,
    pre_part,
    cot_part,
    info,
    w_edge_in,
    w_edge_out,
    w_node_in,
    w_node_out,
    node_cot,
    near_table,
    centring,
    back,
    means,
    node_centring,
    agg_centring,
    node_cot_c,
    new_nodes_out,
    new_edges_out,
    local_grad,
    parts,
    new_nodes,
    new_edges,
    far_rows,
    tables,
    hidden,
    slope,
    normed,
    scale,
    sums,
    ge_out,
    agg,
    packed,
    kept,
    columns,
    out_sems,
    last_sem,
):
    count_p, width = nodes.shape
    border = own_column.shape[0] // 3
    slots = parts.shape[0]
    strips = slots // 2
    chunks, _, chunk = edges_t.shape
    block = chunk // SPLIT
    half = block // 2
    share = parts.shape[1] - 2 * border
    my_strip, my_y = lax.axis_index("strip"), lax.axis_index("y")
    live_count = edge_count[0]

    def span(step):
        return pl.ds(pl.multiple_of(step * chunk, chunk), chunk)

    def block_rows(step, part):
        return pl.ds(pl.multiple_of(step * chunk + part * block, block), block)

    def block_pairs(step, part):
        return pl.ds(pl.multiple_of((step * SPLIT + part) * half, half), half)

    def emit(step):
        rows = span(step)
        return pltpu.make_async_copy(
            new_edges.at[rows], new_edges_out.at[rows], out_sems.at[step]
        )

    def paired(value):
        return jnp.concatenate([value[:half], value[half:]], axis=1)

    def unpaired(value):
        return jnp.concatenate([value[:, :width], value[:, width:]], axis=0)

    for k, column in enumerate((own_column, even_column, odd_column)):
        for part in range(3):
            columns[3 * k + part] = column[part * border : (part + 1) * border]

    def partner(mine, step):
        if step == 0:
            return 0
        is_odd = lax.rem(mine, 2)
        return 1 + is_odd if step > 0 else 2 - is_odd

    spot = 0
    for d_strip in (-1, 0, 1):
        column = partner(my_strip, d_strip)
        for d_sub in (-1, 0, 1):
            if d_strip == 0 and d_sub == 0:
                continue
            rows = slice(spot * border, (spot + 1) * border)
            far_rows[rows] = columns[3 * column + partner(my_y, d_sub)]
            spot += 1
    tables[:, :width] = near_table[...]
    tables[:, width:] = mm(far_rows[...], w_edge_in[:width]).astype(BF16)
    row = lax.broadcasted_iota(jnp.int32, (half, 2 * width), 0)
    lane = lax.broadcasted_iota(jnp.int32, (half, 2 * width), 1)
    edge_row = jnp.where(lane < width, row, row + half)
    agg[...] = jnp.zeros_like(agg)

    def forward(step, carry):
        recv_t = found_t(info[step][1:2], count_p)
        units = []
        for part in range(SPLIT):
            rows, pairs = block_rows(step, part), block_pairs(step, part)
            codes = send_codes[rows]
            begun = pre_part[rows]
            edge = paired(edges[rows].astype(F32))
            place = jnp.where(codes < 0, -1 - codes, codes)
            picked = mm(found(place, count_p // width), tables[...])
            beyond = codes.astype(F32) < 0.0
            pre = begun + jnp.where(beyond, picked[:, width:], picked[:, :width])
            act, bend = silu_and_slope(paired(pre))
            act = act.astype(BF16)
            centre = mm(act, centring[...])
            spare = mm((centre * centre).astype(BF16), means[...])
            live = edge_row < live_count - step * chunk - part * block
            factor = jnp.where(live, lax.rsqrt(spare + EPS), 0.0)
            unit = centre * factor
            slope[pairs] = bend
            hidden[rows] = unpaired(act)
            scale[pairs] = factor
            normed[pairs] = unit
            new_edges[rows] = unpaired((edge + unit).astype(BF16))
            units.append(unpaired(unit.astype(BF16)))
        agg[...] += mm(recv_t, jnp.concatenate(units, axis=0))
        emit(step).start()
        return carry

    lax.fori_loop(0, chunks, forward, 0, unroll=UNROLL)

    joined = jnp.concatenate([nodes[...], agg[...].astype(BF16)], axis=1)
    node_pre = mm(joined, w_node_in[...])
    node_act, node_slope = silu_and_slope(node_pre)
    node_act = node_act.astype(BF16)
    centre = mm(node_act, node_centring[...])
    spare = jnp.mean(centre * centre, axis=1, keepdims=True)
    along = jnp.mean(node_cot_c[...] * centre, axis=1, keepdims=True)
    node_scale = lax.rsqrt(spare + EPS)
    node_unit = centre * node_scale
    d_outer = node_scale * (node_cot_c[...] - node_unit * (along * node_scale))
    d_outer = d_outer.astype(BF16)
    d_pre = (mm_nt(d_outer, w_node_out[...]) * node_slope).astype(BF16)
    d_agg = mm_nt(d_pre, agg_centring[...]).astype(BF16)
    new_nodes[...] = (nodes[...].astype(F32) + node_unit).astype(BF16)
    agg[...] = node_cot[...].astype(F32) + mm_nt(d_pre, w_node_in[:width])
    kept[:, : 2 * width] = joined
    kept[:, 2 * width : 3 * width] = node_act
    kept[:, 3 * width : 4 * width] = d_outer
    kept[:, 4 * width :] = d_pre
    node_copy = pltpu.make_async_copy(new_nodes, new_nodes_out, last_sem)
    node_copy.start()

    sums[...] = jnp.zeros_like(sums)
    ge_out[...] = jnp.zeros_like(ge_out)

    def backward(step, carry):
        index = info[step]
        turned = jnp.concatenate(
            [found_t(index[1:2], count_p), found_t(index[0:1], count_p), edges_t[step]], axis=0
        )
        acts, outs, ins = [], [], []
        for part in range(SPLIT):
            rows, pairs = block_rows(step, part), block_pairs(step, part)
            cot = cot_part[rows].astype(F32)
            recv = found(recv_codes[rows], count_p // width)
            unit = normed[pairs]
            acts.append(hidden[rows])
            beyond = send_codes[rows] < 0
            upstream = paired(cot + mm(recv, d_agg))
            along = mm((upstream * unit).astype(BF16), means[...])
            d_out = (scale[pairs] * (upstream - unit * along)).astype(BF16)
            outs.append(unpaired(d_out))
            d_in = unpaired((mm_nt(d_out, back[...]) * slope[pairs]).astype(BF16))
            zero = jnp.zeros_like(d_in)
            ins.append(
                jnp.concatenate(
                    [jnp.where(beyond, zero, d_in), jnp.where(beyond, d_in, zero)], axis=1
                )
            )
        ge_out[...] += mm_tn(jnp.concatenate(acts, axis=0), jnp.concatenate(outs, axis=0))
        sums[...] += mm(turned, jnp.concatenate(ins, axis=0))
        return carry

    lax.fori_loop(0, chunks, backward, 0, unroll=UNROLL)

    recv_sums = (sums[:count_p, :width] + sums[:count_p, width:]).astype(BF16)
    near_sums = sums[count_p : 2 * count_p, :width].astype(BF16)
    far_sums = sums[count_p : 2 * count_p, width:].astype(BF16)
    edge_sums = sums[2 * count_p :, :width] + sums[2 * count_p :, width:]
    packed[:width] = (mm_tn(nodes[...], near_sums) + mm_tn(far_rows[...], far_sums)).astype(BF16)
    packed[width : 2 * width] = mm_tn(nodes[...], recv_sums).astype(BF16)
    packed[4 * width : 6 * width] = mm_tn(kept[:, : 2 * width], kept[:, 4 * width :]).astype(BF16)
    packed[6 * width : 7 * width] = mm_tn(
        kept[:, 2 * width : 3 * width], kept[:, 3 * width : 4 * width]
    ).astype(BF16)
    packed[2 * width : 3 * width] = edge_sums.astype(BF16)
    packed[3 * width : 4 * width] = ge_out[...].astype(BF16)
    if packed.shape[0] > 7 * width:
        packed[7 * width :] = jnp.zeros((packed.shape[0] - 7 * width, width), BF16)
    local_grad[...] = (
        agg[...]
        + mm_nt(near_sums, w_edge_in[:width])
        + mm_nt(recv_sums, w_edge_in[width : 2 * width])
    )
    owed = mm_nt(far_sums, w_edge_in[:width]).astype(BF16)
    for slot in range(slots):
        parts[slot, :share] = packed[slot * share : (slot + 1) * share]
        parts[slot, share:] = jnp.zeros((2 * border, width), BF16)
    spot = 0
    for d_strip in (-1, 0, 1):
        strip = my_strip + d_strip
        for d_sub in (-1, 0, 1):
            if d_strip == 0 and d_sub == 0:
                continue
            if d_sub == 0:
                slot, part = 2 * strip + my_y, 0
            elif d_sub == 1:
                slot, part = 2 * strip + 1 - my_y, my_y
            else:
                slot, part = 2 * strip + 1 - my_y, 1 - my_y
            first = pl.multiple_of(share + part * border, 16)
            block = owed[spot * border : (spot + 1) * border]

            @pl.when((strip >= 0) & (strip < strips))
            def put(slot=slot, first=first, block=block):
                parts[slot, pl.ds(first, border), :] = block

            spot += 1
    for step in range(chunks):
        emit(step).wait()
    node_copy.wait()


def plane_sum_kernel(came, message, mine):
    border = mine.shape[0]
    share = message.shape[0] - border
    total = came[0].astype(F32)
    for slot in range(1, came.shape[0]):
        total = total + came[slot].astype(F32)
    mine[...] = total[share : share + border]
    message[:share] = total[:share].astype(BF16)
    message[share:] = total[share + border :].astype(BF16)


def line_sum_kernel(factor, mine, *refs):
    messages, (out, rim_grad, held) = refs[:-3], refs[-3:]
    border = mine.shape[0]
    share = out.shape[1]
    for k, message in enumerate(messages):
        held[k] = message[...].astype(F32)
    my_z, my_y = lax.axis_index("z"), lax.axis_index("y")
    total = held[lax.bitwise_xor(my_z, 0), :share]
    for z in range(1, len(messages)):
        total = total + held[lax.bitwise_xor(my_z, z), :share]
    total = (total * factor).astype(BF16)
    for target in range(out.shape[0]):
        out[target] = total
    source = my_z - 1 + 2 * my_y
    inside = (source >= 0) & (source < len(messages))
    passed = held[lax.bitwise_xor(my_z, jnp.clip(source, 0, len(messages) - 1)), share:]
    rim_grad[...] = mine[...] + jnp.where(inside, passed, 0.0)


def finish_kernel(came, rim_grad, local_grad, node_grad, *outs):
    border = rim_grad.shape[0]
    share = came.shape[1]
    node_grad[...] = local_grad[...]
    node_grad[:border] += rim_grad[...]
    start = 0
    for out in outs:
        size = out.shape[0]
        done = 0
        while done < size:
            slot, offset = divmod(start + done, share)
            step = min(size - done, share - offset)
            out[done : done + step] = came[slot, offset : offset + step].astype(F32)
            done += step
        start += size


def shards(
    node_latents,
    edge_latents,
    senders,
    receivers,
    edge_count,
    w_edge_in,
    w_edge_out,
    w_node_in,
    w_node_out,
    node_cotangent,
    edge_cotangent,
):
    count_p, width = node_latents.shape
    count_e = edge_latents.shape[0]
    border = count_p // 8
    strips, zs, ys = (lax.axis_size(axis) for axis in ALL)
    subs = zs * ys
    slots = strips * ys
    even, odd = swapped(node_latents, ("z", "y"))
    chunk = min(CHUNK, count_e)
    chunks = count_e // chunk
    early = call(
        early_kernel,
        [
            ((count_e, width), BF16),
            ((count_e, width), BF16),
            ((count_e, width), BF16),
            ((chunks, width, chunk), BF16),
            ((count_e, width), F32),
            ((count_e, width), BF16),
            ((chunks, 8, chunk), jnp.int32),
        ],
        [
            node_latents,
            edge_latents,
            edge_cotangent,
            senders.reshape(chunks, 1, chunk),
            receivers.reshape(chunks, 1, chunk),
            w_edge_in,
        ],
        [HBM] * 6,
        [
            pltpu.VMEM((count_p + width, width), BF16),
            pltpu.VMEM((count_p, width), BF16),
            pltpu.VMEM((count_e, width), BF16),
            pltpu.VMEM((chunks, 1, chunk), jnp.int32),
            pltpu.VMEM((chunks, 1, chunk), jnp.int32),
            pltpu.VMEM((3 * width, width), BF16),
            SEM((4,)),
            SEM((2, chunks)),
        ],
    )

    *early, odd, even = lax.optimization_barrier((*early, odd, even))
    (own_column,) = call(
        column_kernel,
        [((3 * border, width), BF16)],
        [node_latents, odd, even],
        [VMEM] * 3,
    )
    even_column, odd_column = swapped(own_column, "strip")

    share = -(-7 * width // (slots * 16)) * 16

    prepared = call(
        prepare_kernel,
        [
            ((count_p, width), BF16),
            ((2 * width, 2 * width), BF16),
            ((2 * width, 2 * width), BF16),
            ((2 * width, 2 * width), BF16),
            ((width, width), BF16),
            ((width, width), BF16),
            ((count_p, width), F32),
        ],
        [
            own_column,
            node_latents,
            w_edge_in,
            w_edge_out,
            w_node_in,
            w_node_out,
            node_cotangent,
        ],
        [VMEM] * 7,
    )
    new_nodes, new_edges, local_grad, parts = call(
        layer_kernel,
        [
            ((count_p, width), BF16),
            ((count_e, width), BF16),
            ((count_p, width), F32),
            ((slots, share + 2 * border, width), BF16),
        ],
        [
            edge_count,
            node_latents,
            own_column,
            even_column,
            odd_column,
            *early,
            w_edge_in,
            w_edge_out,
            w_node_in,
            w_node_out,
            node_cotangent,
            *prepared,
        ],
        [SMEM] + [VMEM] * 23,
        [
            pltpu.VMEM((count_p, width), BF16),
            pltpu.VMEM((count_e, width), BF16),
            pltpu.VMEM((8 * border, width), BF16),
            pltpu.VMEM((count_p, 2 * width), BF16),
            pltpu.VMEM((count_e, width), BF16),
            pltpu.VMEM((count_e // 2, 2 * width), F32),
            pltpu.VMEM((count_e // 2, 2 * width), F32),
            pltpu.VMEM((count_e // 2, 2 * width), F32),
            pltpu.VMEM((2 * count_p + width, 2 * width), F32),
            pltpu.VMEM((width, width), F32),
            pltpu.VMEM((count_p, width), F32),
            pltpu.VMEM((slots * share, width), BF16),
            pltpu.VMEM((count_p, 5 * width), BF16),
            pltpu.VMEM((9, border, width), BF16),
            SEM((chunks,)),
            SEM,
        ],
        [HBM, HBM, VMEM, VMEM],
        limit=24,
    )

    came = lax.all_to_all(parts, PLANE, 0, 0)
    state = [((share + border, width), BF16), ((border, width), F32)]
    message, mine = call(plane_sum_kernel, state, [came], [VMEM])
    factor = 1.0 / math.sqrt(count_e * strips * subs)
    messages = [message] + [
        lax.ppermute(message, "z", [(z, z ^ k) for z in range(zs)]) for k in range(1, zs)
    ]
    parts, rim_grad = call(
        functools.partial(line_sum_kernel, factor),
        [((slots, share, width), BF16), ((border, width), F32)],
        [mine, *messages],
        [VMEM] * (1 + zs),
        [pltpu.VMEM((zs, share + border, width), F32)],
    )
    came = lax.all_to_all(parts, PLANE, 0, 0)
    node_grad, *grads = call(
        finish_kernel,
        [((rows, width), F32) for rows in (count_p, 3 * width, width, 2 * width, width)],
        [came, rim_grad, local_grad],
        [VMEM, VMEM, VMEM],
    )
    return (new_nodes, new_edges, node_grad, *grads)


def solution(mesh):
    strips, subs = mesh.devices.shape
    grid = Mesh(mesh.devices.reshape(strips, subs // 2, 2), ALL)
    rows = P(ALL, None)
    line = P(ALL)
    return jax.shard_map(
        shards,
        mesh=grid,
        in_specs=(rows, rows, line, line, line, P(), P(), P(), P(), rows, rows),
        out_specs=(rows, rows, rows, P(), P(), P(), P()),
        check_vma=False,
    )
```

```python
import functools
import math

import jax
import jax.numpy as jnp
from jax import lax
from jax.experimental import pallas as pl
from jax.experimental.pallas import tpu as pltpu
from jax.sharding import Mesh
from jax.sharding import PartitionSpec as P

EPS = 1e-05
CHUNK = 1024
SPLIT = 1
UNROLL = 4
PLANE = ("strip", "y")
ALL = ("strip", "z", "y")
F32 = jnp.float32
BF16 = jnp.bfloat16
VMEM = pl.BlockSpec(memory_space=pltpu.VMEM)
SMEM = pl.BlockSpec(memory_space=pltpu.SMEM)
HBM = pl.BlockSpec(memory_space=pltpu.HBM)
SEM = pltpu.SemaphoreType.DMA


def mm(left, right):
    return jnp.dot(left, right, preferred_element_type=F32)


def mm_nt(left, right):
    return lax.dot_general(left, right, (((1,), (1,)), ((), ())), preferred_element_type=F32)


def mm_tn(left, right):
    return lax.dot_general(left, right, (((0,), (0,)), ((), ())), preferred_element_type=F32)


def silu_and_slope(values):
    sig = 0.5 + 0.5 * jnp.tanh(0.5 * values)
    act = values * sig
    return (act, sig + act * (1.0 - sig))


def found(codes, blocks):
    lane = lax.broadcasted_iota(jnp.int32, codes.shape, 1)
    one, zero = jnp.ones((), BF16), jnp.zeros((), BF16)
    width = codes.shape[1]
    return jnp.concatenate(
        [
            jnp.where(codes == (lane + width * k).astype(F32).astype(BF16), one, zero)
            for k in range(blocks)
        ],
        axis=1,
    )


def found_t(line, size):
    place = lax.broadcasted_iota(jnp.int32, (size, line.shape[1]), 0).astype(F32).astype(BF16)
    one, zero = jnp.ones((), BF16), jnp.zeros((), BF16)
    return jnp.where(place == line.astype(F32).astype(BF16), one, zero)


def in_hbm(value):
    return pltpu.with_memory_space_constraint(value, pltpu.HBM)


def call(kernel, outs, ins, specs, scratch=(), out_specs=None, limit=24):
    out_specs = [VMEM] * len(outs) if out_specs is None else out_specs
    return pl.pallas_call(
        kernel,
        out_shape=[
            pltpu.HBM(shape, dtype) if spec is HBM else jax.ShapeDtypeStruct(shape, dtype)
            for (shape, dtype), spec in zip(outs, out_specs)
        ],
        in_specs=specs,
        out_specs=out_specs,
        scratch_shapes=list(scratch),
        compiler_params=pltpu.CompilerParams(vmem_limit_bytes=limit * 2**20),
    )(*[in_hbm(value) if spec is HBM else value for value, spec in zip(ins, specs)])


def column_kernel(nodes, odd, even, out):
    border = out.shape[0] // 3
    out[:border] = nodes[:border]
    out[border : 2 * border] = even[:border]
    out[2 * border :] = odd[:border]


def swapped(value, axes):
    count = lax.axis_size(axes)
    even = [(k, k ^ 1) for k in range(count)]
    odd = [(k, min(max(((k + 1) ^ 1) - 1, 0), count - 1)) for k in range(count)]
    from_odd = lax.ppermute(value, axes, odd)
    from_even = lax.ppermute(value, axes, even)
    return from_even, from_odd


def early_kernel(
    nodes_in,
    edges_in,
    edge_cot_in,
    senders_in,
    receivers_in,
    w_edge_in_in,
    edges,
    send_codes,
    recv_codes,
    edges_t,
    pre_part,
    cot_part,
    info,
    tables,
    nodes,
    edge_cot,
    senders,
    receivers,
    w_edge_in,
    small_sems,
    sems,
):
    count_p, width = nodes_in.shape
    chunks, _, chunk = info.shape
    border = count_p // 8
    my_strip = lax.axis_index("strip")
    subs = lax.axis_size("z") * lax.axis_size("y")
    my_sub = lax.axis_index("z") * lax.axis_size("y") + lax.axis_index("y")
    place_bits, sub_bits = count_p.bit_length() - 1, subs.bit_length() - 1

    def fetch(step):
        rows = pl.ds(pl.multiple_of(step * chunk, chunk), chunk)
        return [
            pltpu.make_async_copy(edges_in.at[rows], edges.at[rows], sems.at[0, step]),
            pltpu.make_async_copy(edge_cot_in.at[rows], edge_cot.at[rows], sems.at[1, step]),
        ]

    small = [
        pltpu.make_async_copy(source, target, small_sems.at[k])
        for k, (source, target) in enumerate(
            [
                (nodes_in, nodes),
                (w_edge_in_in, w_edge_in),
                (senders_in, senders),
                (receivers_in, receivers),
            ]
        )
    ]
    for copy in small:
        copy.start()
    for step in range(chunks):
        for copy in fetch(step):
            copy.start()
    for copy in small:
        copy.wait()
    tables[:count_p] = mm(nodes[...], w_edge_in[width : 2 * width]).astype(BF16)
    tables[count_p:] = w_edge_in[2 * width :]
    line = lax.broadcasted_iota(jnp.int32, (8, chunk), 0)

    def one(step):
        rows = slice(step * chunk, (step + 1) * chunk)
        sender = jnp.broadcast_to(senders[step], (8, chunk))
        receiver = jnp.broadcast_to(receivers[step], (8, chunk))
        owner = lax.shift_right_logical(sender, place_bits)
        within = lax.bitwise_and(sender, count_p - 1)
        d_strip = lax.shift_right_logical(owner, sub_bits) - my_strip
        d_sub = lax.bitwise_and(owner, subs - 1) - my_sub
        spot = 3 * d_strip + d_sub + 4
        spot = jnp.where(spot > 4, spot - 1, spot)
        near = (d_strip == 0) & (d_sub == 0)
        spot = jnp.where(near, within, spot * border + jnp.minimum(within, border - 1))
        index = jnp.where(line == 0, spot, receiver)
        index = jnp.where(line == 2, jnp.where(near, spot, -1 - spot), index)
        info[step] = index
        columns = index.T
        edge = edges[rows]
        cot = edge_cot[rows].astype(F32)
        recv = jnp.broadcast_to(columns[:, 1:2], edge.shape).astype(F32).astype(BF16)
        recv_codes[rows] = recv
        send_codes[rows] = jnp.broadcast_to(columns[:, 2:3], edge.shape).astype(F32).astype(BF16)
        recv = found(recv, count_p // width)
        edges_t[step] = edge.T
        cot_part[rows] = (cot - jnp.mean(cot, axis=1, keepdims=True)).astype(BF16)
        return jnp.concatenate([recv, edge], axis=1)

    group = 2 if chunks % 2 == 0 else 1
    for first in range(0, chunks, group):
        steps = range(first, first + group)
        for step in steps:
            for copy in fetch(step):
                copy.wait()
        left = jnp.concatenate([one(step) for step in steps], axis=0)
        pre_part[first * chunk : (first + group) * chunk] = mm(left, tables[...])


def prepare_kernel(
    column,
    nodes,
    w_edge_in,
    w_edge_out,
    w_node_in,
    w_node_out,
    node_cot,
    near_table,
    centring,
    back,
    means,
    node_centring,
    agg_centring,
    node_cot_c,
):
    width = nodes.shape[1]

    def twice(block):
        zero = jnp.zeros_like(block)
        return jnp.concatenate(
            [
                jnp.concatenate([block, zero], axis=1),
                jnp.concatenate([zero, block], axis=1),
            ],
            axis=0,
        )

    near_table[...] = mm(nodes[...], w_edge_in[:width]).astype(BF16)
    weight = w_edge_out[...].astype(F32)
    centring[...] = twice(weight - jnp.mean(weight, axis=1, keepdims=True)).astype(BF16)
    back[...] = twice(weight).astype(BF16)
    weight = w_node_out[...].astype(F32)
    node_centring[...] = (weight - jnp.mean(weight, axis=1, keepdims=True)).astype(BF16)
    weight = w_node_in[width:].astype(F32)
    agg_centring[...] = (weight - jnp.mean(weight, axis=0, keepdims=True)).astype(BF16)
    cot = node_cot[...].astype(F32)
    node_cot_c[...] = cot - jnp.mean(cot, axis=1, keepdims=True)
    means[...] = twice(jnp.full((width, width), 1.0 / width, F32)).astype(BF16)


def layer_kernel(
    edge_count,
    nodes,
    own_column,
    even_column,
    odd_column,
    edges,
    send_codes,
    recv_codes,
    edges_t,
    pre_part,
    cot_part,
    info,
    w_edge_in,
    w_edge_out,
    w_node_in,
    w_node_out,
    node_cot,
    near_table,
    centring,
    back,
    means,
    node_centring,
    agg_centring,
    node_cot_c,
    new_nodes_out,
    new_edges_out,
    local_grad,
    parts,
    new_nodes,
    new_edges,
    far_rows,
    tables,
    hidden,
    slope,
    normed,
    scale,
    sums,
    ge_out,
    agg,
    packed,
    kept,
    columns,
    out_sems,
    last_sem,
):
    count_p, width = nodes.shape
    border = own_column.shape[0] // 3
    slots = parts.shape[0]
    strips = slots // 2
    chunks, _, chunk = edges_t.shape
    block = chunk // SPLIT
    half = block // 2
    share = parts.shape[1] - 2 * border
    my_strip, my_y = lax.axis_index("strip"), lax.axis_index("y")
    live_count = edge_count[0]

    def span(step):
        return pl.ds(pl.multiple_of(step * chunk, chunk), chunk)

    def block_rows(step, part):
        return pl.ds(pl.multiple_of(step * chunk + part * block, block), block)

    def block_pairs(step, part):
        return pl.ds(pl.multiple_of((step * SPLIT + part) * half, half), half)

    def emit(step):
        rows = span(step)
        return pltpu.make_async_copy(
            new_edges.at[rows], new_edges_out.at[rows], out_sems.at[step]
        )

    def paired(value):
        return jnp.concatenate([value[:half], value[half:]], axis=1)

    def unpaired(value):
        return jnp.concatenate([value[:, :width], value[:, width:]], axis=0)

    for k, column in enumerate((own_column, even_column, odd_column)):
        for part in range(3):
            columns[3 * k + part] = column[part * border : (part + 1) * border]

    def partner(mine, step):
        if step == 0:
            return 0
        is_odd = lax.rem(mine, 2)
        return 1 + is_odd if step > 0 else 2 - is_odd

    spot = 0
    for d_strip in (-1, 0, 1):
        column = partner(my_strip, d_strip)
        for d_sub in (-1, 0, 1):
            if d_strip == 0 and d_sub == 0:
                continue
            rows = slice(spot * border, (spot + 1) * border)
            far_rows[rows] = columns[3 * column + partner(my_y, d_sub)]
            spot += 1
    tables[:, :width] = near_table[...]
    tables[:, width:] = mm(far_rows[...], w_edge_in[:width]).astype(BF16)
    row = lax.broadcasted_iota(jnp.int32, (half, 2 * width), 0)
    lane = lax.broadcasted_iota(jnp.int32, (half, 2 * width), 1)
    edge_row = jnp.where(lane < width, row, row + half)
    agg[...] = jnp.zeros_like(agg)

    def forward(step, carry):
        recv_t = found_t(info[step][1:2], count_p)
        units = []
        for part in range(SPLIT):
            rows, pairs = block_rows(step, part), block_pairs(step, part)
            codes = send_codes[rows]
            begun = pre_part[rows]
            edge = paired(edges[rows].astype(F32))
            place = jnp.where(codes < 0, -1 - codes, codes)
            picked = mm(found(place, count_p // width), tables[...])
            beyond = codes.astype(F32) < 0.0
            pre = begun + jnp.where(beyond, picked[:, width:], picked[:, :width])
            act, bend = silu_and_slope(paired(pre))
            act = act.astype(BF16)
            centre = mm(act, centring[...])
            spare = mm((centre * centre).astype(BF16), means[...])
            live = edge_row < live_count - step * chunk - part * block
            factor = jnp.where(live, lax.rsqrt(spare + EPS), 0.0)
            unit = centre * factor
            slope[pairs] = bend
            hidden[rows] = unpaired(act)
            scale[pairs] = factor
            normed[pairs] = unit
            new_edges[rows] = unpaired((edge + unit).astype(BF16))
            units.append(unpaired(unit.astype(BF16)))
        agg[...] += mm(recv_t, jnp.concatenate(units, axis=0))
        emit(step).start()
        return carry

    lax.fori_loop(0, chunks, forward, 0, unroll=UNROLL)

    joined = jnp.concatenate([nodes[...], agg[...].astype(BF16)], axis=1)
    node_pre = mm(joined, w_node_in[...])
    node_act, node_slope = silu_and_slope(node_pre)
    node_act = node_act.astype(BF16)
    centre = mm(node_act, node_centring[...])
    spare = jnp.mean(centre * centre, axis=1, keepdims=True)
    along = jnp.mean(node_cot_c[...] * centre, axis=1, keepdims=True)
    node_scale = lax.rsqrt(spare + EPS)
    node_unit = centre * node_scale
    d_outer = node_scale * (node_cot_c[...] - node_unit * (along * node_scale))
    d_outer = d_outer.astype(BF16)
    d_pre = (mm_nt(d_outer, w_node_out[...]) * node_slope).astype(BF16)
    d_agg = mm_nt(d_pre, agg_centring[...]).astype(BF16)
    new_nodes[...] = (nodes[...].astype(F32) + node_unit).astype(BF16)
    agg[...] = node_cot[...].astype(F32) + mm_nt(d_pre, w_node_in[:width])
    kept[:, : 2 * width] = joined
    kept[:, 2 * width : 3 * width] = node_act
    kept[:, 3 * width : 4 * width] = d_outer
    kept[:, 4 * width :] = d_pre
    node_copy = pltpu.make_async_copy(new_nodes, new_nodes_out, last_sem)
    node_copy.start()

    sums[...] = jnp.zeros_like(sums)
    ge_out[...] = jnp.zeros_like(ge_out)

    def backward(step, carry):
        index = info[step]
        turned = jnp.concatenate(
            [found_t(index[1:2], count_p), found_t(index[0:1], count_p), edges_t[step]], axis=0
        )
        acts, outs, ins = [], [], []
        for part in range(SPLIT):
            rows, pairs = block_rows(step, part), block_pairs(step, part)
            cot = cot_part[rows].astype(F32)
            recv = found(recv_codes[rows], count_p // width)
            unit = normed[pairs]
            acts.append(hidden[rows])
            beyond = send_codes[rows] < 0
            upstream = paired(cot + mm(recv, d_agg))
            along = mm((upstream * unit).astype(BF16), means[...])
            d_out = (scale[pairs] * (upstream - unit * along)).astype(BF16)
            outs.append(unpaired(d_out))
            d_in = unpaired((mm_nt(d_out, back[...]) * slope[pairs]).astype(BF16))
            zero = jnp.zeros_like(d_in)
            ins.append(
                jnp.concatenate(
                    [jnp.where(beyond, zero, d_in), jnp.where(beyond, d_in, zero)], axis=1
                )
            )
        ge_out[...] += mm_tn(jnp.concatenate(acts, axis=0), jnp.concatenate(outs, axis=0))
        sums[...] += mm(turned, jnp.concatenate(ins, axis=0))
        return carry

    lax.fori_loop(0, chunks, backward, 0, unroll=UNROLL)

    recv_sums = (sums[:count_p, :width] + sums[:count_p, width:]).astype(BF16)
    near_sums = sums[count_p : 2 * count_p, :width].astype(BF16)
    far_sums = sums[count_p : 2 * count_p, width:].astype(BF16)
    edge_sums = sums[2 * count_p :, :width] + sums[2 * count_p :, width:]
    packed[:width] = (mm_tn(nodes[...], near_sums) + mm_tn(far_rows[...], far_sums)).astype(BF16)
    packed[width : 2 * width] = mm_tn(nodes[...], recv_sums).astype(BF16)
    packed[4 * width : 6 * width] = mm_tn(kept[:, : 2 * width], kept[:, 4 * width :]).astype(BF16)
    packed[6 * width : 7 * width] = mm_tn(
        kept[:, 2 * width : 3 * width], kept[:, 3 * width : 4 * width]
    ).astype(BF16)
    packed[2 * width : 3 * width] = edge_sums.astype(BF16)
    packed[3 * width : 4 * width] = ge_out[...].astype(BF16)
    if packed.shape[0] > 7 * width:
        packed[7 * width :] = jnp.zeros((packed.shape[0] - 7 * width, width), BF16)
    local_grad[...] = (
        agg[...]
        + mm_nt(near_sums, w_edge_in[:width])
        + mm_nt(recv_sums, w_edge_in[width : 2 * width])
    )
    owed = mm_nt(far_sums, w_edge_in[:width]).astype(BF16)
    for slot in range(slots):
        parts[slot, :share] = packed[slot * share : (slot + 1) * share]
        parts[slot, share:] = jnp.zeros((2 * border, width), BF16)
    spot = 0
    for d_strip in (-1, 0, 1):
        strip = my_strip + d_strip
        for d_sub in (-1, 0, 1):
            if d_strip == 0 and d_sub == 0:
                continue
            if d_sub == 0:
                slot, part = 2 * strip + my_y, 0
            elif d_sub == 1:
                slot, part = 2 * strip + 1 - my_y, my_y
            else:
                slot, part = 2 * strip + 1 - my_y, 1 - my_y
            first = pl.multiple_of(share + part * border, 16)
            block = owed[spot * border : (spot + 1) * border]

            @pl.when((strip >= 0) & (strip < strips))
            def put(slot=slot, first=first, block=block):
                parts[slot, pl.ds(first, border), :] = block

            spot += 1
    for step in range(chunks):
        emit(step).wait()
    node_copy.wait()


def plane_sum_kernel(came, message, mine):
    border = mine.shape[0]
    share = message.shape[0] - border
    total = came[0].astype(F32)
    for slot in range(1, came.shape[0]):
        total = total + came[slot].astype(F32)
    mine[...] = total[share : share + border]
    message[:share] = total[:share].astype(BF16)
    message[share:] = total[share + border :].astype(BF16)


def line_sum_kernel(factor, mine, first, *refs):
    messages, (out, rim_grad, held) = (first, *refs[-4::-1]), refs[-3:]
    border = mine.shape[0]
    share = out.shape[1]
    for k, message in enumerate(messages):
        held[k] = message[...].astype(F32)
    my_z, my_y = lax.axis_index("z"), lax.axis_index("y")
    total = held[lax.bitwise_xor(my_z, 0), :share]
    for z in range(1, len(messages)):
        total = total + held[lax.bitwise_xor(my_z, z), :share]
    total = (total * factor).astype(BF16)
    for target in range(out.shape[0]):
        out[target] = total
    source = my_z - 1 + 2 * my_y
    inside = (source >= 0) & (source < len(messages))
    passed = held[lax.bitwise_xor(my_z, jnp.clip(source, 0, len(messages) - 1)), share:]
    rim_grad[...] = mine[...] + jnp.where(inside, passed, 0.0)


def finish_kernel(came, rim_grad, local_grad, node_grad, *outs):
    border = rim_grad.shape[0]
    share = came.shape[1]
    node_grad[...] = local_grad[...]
    node_grad[:border] += rim_grad[...]
    start = 0
    for out in outs:
        size = out.shape[0]
        done = 0
        while done < size:
            slot, offset = divmod(start + done, share)
            step = min(size - done, share - offset)
            out[done : done + step] = came[slot, offset : offset + step].astype(F32)
            done += step
        start += size


def shards(
    node_latents,
    edge_latents,
    senders,
    receivers,
    edge_count,
    w_edge_in,
    w_edge_out,
    w_node_in,
    w_node_out,
    node_cotangent,
    edge_cotangent,
):
    count_p, width = node_latents.shape
    count_e = edge_latents.shape[0]
    border = count_p // 8
    strips, zs, ys = (lax.axis_size(axis) for axis in ALL)
    subs = zs * ys
    slots = strips * ys
    even, odd = swapped(node_latents, ("z", "y"))
    chunk = min(CHUNK, count_e)
    chunks = count_e // chunk
    early = call(
        early_kernel,
        [
            ((count_e, width), BF16),
            ((count_e, width), BF16),
            ((count_e, width), BF16),
            ((chunks, width, chunk), BF16),
            ((count_e, width), F32),
            ((count_e, width), BF16),
            ((chunks, 8, chunk), jnp.int32),
        ],
        [
            node_latents,
            edge_latents,
            edge_cotangent,
            senders.reshape(chunks, 1, chunk),
            receivers.reshape(chunks, 1, chunk),
            w_edge_in,
        ],
        [HBM] * 6,
        [
            pltpu.VMEM((count_p + width, width), BF16),
            pltpu.VMEM((count_p, width), BF16),
            pltpu.VMEM((count_e, width), BF16),
            pltpu.VMEM((chunks, 1, chunk), jnp.int32),
            pltpu.VMEM((chunks, 1, chunk), jnp.int32),
            pltpu.VMEM((3 * width, width), BF16),
            SEM((4,)),
            SEM((2, chunks)),
        ],
    )

    *early, odd, even = lax.optimization_barrier((*early, odd, even))
    (own_column,) = call(
        column_kernel,
        [((3 * border, width), BF16)],
        [node_latents, odd, even],
        [VMEM] * 3,
    )
    even_column, odd_column = swapped(own_column, "strip")

    share = -(-7 * width // (slots * 16)) * 16

    prepared = call(
        prepare_kernel,
        [
            ((count_p, width), BF16),
            ((2 * width, 2 * width), BF16),
            ((2 * width, 2 * width), BF16),
            ((2 * width, 2 * width), BF16),
            ((width, width), BF16),
            ((width, width), BF16),
            ((count_p, width), F32),
        ],
        [
            own_column,
            node_latents,
            w_edge_in,
            w_edge_out,
            w_node_in,
            w_node_out,
            node_cotangent,
        ],
        [VMEM] * 7,
    )
    new_nodes, new_edges, local_grad, parts = call(
        layer_kernel,
        [
            ((count_p, width), BF16),
            ((count_e, width), BF16),
            ((count_p, width), F32),
            ((slots, share + 2 * border, width), BF16),
        ],
        [
            edge_count,
            node_latents,
            own_column,
            even_column,
            odd_column,
            *early,
            w_edge_in,
            w_edge_out,
            w_node_in,
            w_node_out,
            node_cotangent,
            *prepared,
        ],
        [SMEM] + [VMEM] * 23,
        [
            pltpu.VMEM((count_p, width), BF16),
            pltpu.VMEM((count_e, width), BF16),
            pltpu.VMEM((8 * border, width), BF16),
            pltpu.VMEM((count_p, 2 * width), BF16),
            pltpu.VMEM((count_e, width), BF16),
            pltpu.VMEM((count_e // 2, 2 * width), F32),
            pltpu.VMEM((count_e // 2, 2 * width), F32),
            pltpu.VMEM((count_e // 2, 2 * width), F32),
            pltpu.VMEM((2 * count_p + width, 2 * width), F32),
            pltpu.VMEM((width, width), F32),
            pltpu.VMEM((count_p, width), F32),
            pltpu.VMEM((slots * share, width), BF16),
            pltpu.VMEM((count_p, 5 * width), BF16),
            pltpu.VMEM((9, border, width), BF16),
            SEM((chunks,)),
            SEM,
        ],
        [HBM, HBM, VMEM, VMEM],
        limit=24,
    )

    came = lax.all_to_all(parts, PLANE, 0, 0)
    state = [((share + border, width), BF16), ((border, width), F32)]
    message, mine = call(plane_sum_kernel, state, [came], [VMEM])
    factor = 1.0 / math.sqrt(count_e * strips * subs)
    messages = [message] + [
        lax.ppermute(message, "z", [(z, z ^ k) for z in range(zs)]) for k in range(1, zs)
    ]
    parts, rim_grad = call(
        functools.partial(line_sum_kernel, factor),
        [((slots, share, width), BF16), ((border, width), F32)],
        [mine, messages[0], *messages[:0:-1]],
        [VMEM] * (1 + zs),
        [pltpu.VMEM((zs, share + border, width), F32)],
    )
    came = lax.all_to_all(parts, PLANE, 0, 0)
    node_grad, *grads = call(
        finish_kernel,
        [((rows, width), F32) for rows in (count_p, 3 * width, width, 2 * width, width)],
        [came, rim_grad, local_grad],
        [VMEM, VMEM, VMEM],
    )
    return (new_nodes, new_edges, node_grad, *grads)


def solution(mesh):
    strips, subs = mesh.devices.shape
    grid = Mesh(mesh.devices.reshape(strips, subs // 2, 2), ALL)
    rows = P(ALL, None)
    line = P(ALL)
    return jax.shard_map(
        shards,
        mesh=grid,
        in_specs=(rows, rows, line, line, line, P(), P(), P(), P(), rows, rows),
        out_specs=(rows, rows, rows, P(), P(), P(), P()),
        check_vma=False,
    )
```

```python
import functools
import math

import jax
import jax.numpy as jnp
from jax import lax
from jax.experimental import pallas as pl
from jax.experimental.pallas import tpu as pltpu
from jax.sharding import Mesh
from jax.sharding import PartitionSpec as P

EPS = 1e-05
CHUNK = 1024
SPLIT = 1
UNROLL = 4
PLANE = ("strip", "y")
ALL = ("strip", "z", "y")
F32 = jnp.float32
BF16 = jnp.bfloat16
VMEM = pl.BlockSpec(memory_space=pltpu.VMEM)
SMEM = pl.BlockSpec(memory_space=pltpu.SMEM)
HBM = pl.BlockSpec(memory_space=pltpu.HBM)
SEM = pltpu.SemaphoreType.DMA


def mm(left, right):
    return jnp.dot(left, right, preferred_element_type=F32)


def mm_nt(left, right):
    return lax.dot_general(left, right, (((1,), (1,)), ((), ())), preferred_element_type=F32)


def mm_tn(left, right):
    return lax.dot_general(left, right, (((0,), (0,)), ((), ())), preferred_element_type=F32)


def silu_and_slope(values):
    sig = 0.5 + 0.5 * jnp.tanh(0.5 * values)
    act = values * sig
    return (act, sig + act * (1.0 - sig))


def found(codes, blocks):
    lane = lax.broadcasted_iota(jnp.int32, codes.shape, 1)
    one, zero = jnp.ones((), BF16), jnp.zeros((), BF16)
    width = codes.shape[1]
    return jnp.concatenate(
        [
            jnp.where(codes == (lane + width * k).astype(F32).astype(BF16), one, zero)
            for k in range(blocks)
        ],
        axis=1,
    )


def found_t(line, size):
    place = lax.broadcasted_iota(jnp.int32, (size, line.shape[1]), 0).astype(F32).astype(BF16)
    one, zero = jnp.ones((), BF16), jnp.zeros((), BF16)
    return jnp.where(place == line.astype(F32).astype(BF16), one, zero)


def in_hbm(value):
    return pltpu.with_memory_space_constraint(value, pltpu.HBM)


def call(kernel, outs, ins, specs, scratch=(), out_specs=None, limit=24):
    out_specs = [VMEM] * len(outs) if out_specs is None else out_specs
    return pl.pallas_call(
        kernel,
        out_shape=[
            pltpu.HBM(shape, dtype) if spec is HBM else jax.ShapeDtypeStruct(shape, dtype)
            for (shape, dtype), spec in zip(outs, out_specs)
        ],
        in_specs=specs,
        out_specs=out_specs,
        scratch_shapes=list(scratch),
        compiler_params=pltpu.CompilerParams(vmem_limit_bytes=limit * 2**20),
    )(*[in_hbm(value) if spec is HBM else value for value, spec in zip(ins, specs)])


def column_kernel(nodes, odd, even, out):
    border = out.shape[0] // 3
    out[:border] = nodes[:border]
    out[border : 2 * border] = even[:border]
    out[2 * border :] = odd[:border]


def swapped(value, axes):
    count = lax.axis_size(axes)
    even = [(k, k ^ 1) for k in range(count)]
    odd = [(k, min(max(((k + 1) ^ 1) - 1, 0), count - 1)) for k in range(count)]
    from_odd = lax.ppermute(value, axes, odd)
    from_even = lax.ppermute(value, axes, even)
    return from_even, from_odd


def early_kernel(
    nodes_in,
    edges_in,
    edge_cot_in,
    senders_in,
    receivers_in,
    w_edge_in_in,
    edges,
    send_codes,
    recv_codes,
    edges_t,
    pre_part,
    cot_part,
    info,
    tables,
    nodes,
    edge_cot,
    senders,
    receivers,
    w_edge_in,
    small_sems,
    sems,
):
    count_p, width = nodes_in.shape
    pieces, _, piece = info.shape
    chunks, _, chunk = senders_in.shape
    group = chunk // piece
    border = count_p // 8
    my_strip = lax.axis_index("strip")
    subs = lax.axis_size("z") * lax.axis_size("y")
    my_sub = lax.axis_index("z") * lax.axis_size("y") + lax.axis_index("y")
    place_bits, sub_bits = count_p.bit_length() - 1, subs.bit_length() - 1

    def fetch(step):
        rows = pl.ds(pl.multiple_of(step * chunk, chunk), chunk)
        return [
            pltpu.make_async_copy(edges_in.at[rows], edges.at[rows], sems.at[0, step]),
            pltpu.make_async_copy(edge_cot_in.at[rows], edge_cot.at[rows], sems.at[1, step]),
        ]

    small = [
        pltpu.make_async_copy(source, target, small_sems.at[k])
        for k, (source, target) in enumerate(
            [
                (nodes_in, nodes),
                (w_edge_in_in, w_edge_in),
                (senders_in, senders),
                (receivers_in, receivers),
            ]
        )
    ]
    for copy in small:
        copy.start()
    for step in range(chunks):
        for copy in fetch(step):
            copy.start()
    for copy in small:
        copy.wait()
    tables[:count_p] = mm(nodes[...], w_edge_in[width : 2 * width]).astype(BF16)
    tables[count_p:] = w_edge_in[2 * width :]
    line = lax.broadcasted_iota(jnp.int32, (8, chunk), 0)

    def one(step, carry):
        rows = pl.ds(pl.multiple_of(step * chunk, chunk), chunk)
        sender = jnp.broadcast_to(senders[step], (8, chunk))
        receiver = jnp.broadcast_to(receivers[step], (8, chunk))
        owner = lax.shift_right_logical(sender, place_bits)
        within = lax.bitwise_and(sender, count_p - 1)
        d_strip = lax.shift_right_logical(owner, sub_bits) - my_strip
        d_sub = lax.bitwise_and(owner, subs - 1) - my_sub
        spot = 3 * d_strip + d_sub + 4
        spot = jnp.where(spot > 4, spot - 1, spot)
        near = (d_strip == 0) & (d_sub == 0)
        spot = jnp.where(near, within, spot * border + jnp.minimum(within, border - 1))
        index = jnp.where(line == 0, spot, receiver)
        index = jnp.where(line == 2, jnp.where(near, spot, -1 - spot), index)
        for part in range(group):
            info[step * group + part] = index[:, part * piece : (part + 1) * piece]
        columns = index.T
        for copy in fetch(step):
            copy.wait()
        edge = edges[rows]
        cot = edge_cot[rows].astype(F32)
        recv = jnp.broadcast_to(columns[:, 1:2], edge.shape).astype(F32).astype(BF16)
        recv_codes[rows] = recv
        send_codes[rows] = jnp.broadcast_to(columns[:, 2:3], edge.shape).astype(F32).astype(BF16)
        recv = found(recv, count_p // width)
        pre_part[rows] = mm(jnp.concatenate([recv, edge], axis=1), tables[...])
        for part in range(group):
            edges_t[step * group + part] = edge[part * piece : (part + 1) * piece].T
        cot_part[rows] = (cot - jnp.mean(cot, axis=1, keepdims=True)).astype(BF16)
        return carry

    lax.fori_loop(0, chunks, one, 0, unroll=chunks)


def prepare_kernel(
    column,
    nodes,
    w_edge_in,
    w_edge_out,
    w_node_in,
    w_node_out,
    node_cot,
    near_table,
    centring,
    back,
    means,
    node_centring,
    agg_centring,
    node_cot_c,
):
    width = nodes.shape[1]

    def twice(block):
        zero = jnp.zeros_like(block)
        return jnp.concatenate(
            [
                jnp.concatenate([block, zero], axis=1),
                jnp.concatenate([zero, block], axis=1),
            ],
            axis=0,
        )

    near_table[...] = mm(nodes[...], w_edge_in[:width]).astype(BF16)
    weight = w_edge_out[...].astype(F32)
    centring[...] = twice(weight - jnp.mean(weight, axis=1, keepdims=True)).astype(BF16)
    back[...] = twice(weight).astype(BF16)
    weight = w_node_out[...].astype(F32)
    node_centring[...] = (weight - jnp.mean(weight, axis=1, keepdims=True)).astype(BF16)
    weight = w_node_in[width:].astype(F32)
    agg_centring[...] = (weight - jnp.mean(weight, axis=0, keepdims=True)).astype(BF16)
    cot = node_cot[...].astype(F32)
    node_cot_c[...] = cot - jnp.mean(cot, axis=1, keepdims=True)
    means[...] = twice(jnp.full((width, width), 1.0 / width, F32)).astype(BF16)


def layer_kernel(
    edge_count,
    nodes,
    own_column,
    even_column,
    odd_column,
    edges,
    send_codes,
    recv_codes,
    edges_t,
    pre_part,
    cot_part,
    info,
    w_edge_in,
    w_edge_out,
    w_node_in,
    w_node_out,
    node_cot,
    near_table,
    centring,
    back,
    means,
    node_centring,
    agg_centring,
    node_cot_c,
    new_nodes_out,
    new_edges_out,
    local_grad,
    parts,
    new_nodes,
    new_edges,
    far_rows,
    tables,
    hidden,
    slope,
    normed,
    scale,
    sums,
    ge_out,
    agg,
    packed,
    kept,
    columns,
    out_sems,
    last_sem,
):
    count_p, width = nodes.shape
    border = own_column.shape[0] // 3
    slots = parts.shape[0]
    strips = slots // 2
    chunks, _, chunk = edges_t.shape
    block = chunk // SPLIT
    half = block // 2
    share = parts.shape[1] - 2 * border
    my_strip, my_y = lax.axis_index("strip"), lax.axis_index("y")
    live_count = edge_count[0]

    def span(step):
        return pl.ds(pl.multiple_of(step * chunk, chunk), chunk)

    def block_rows(step, part):
        return pl.ds(pl.multiple_of(step * chunk + part * block, block), block)

    def block_pairs(step, part):
        return pl.ds(pl.multiple_of((step * SPLIT + part) * half, half), half)

    def emit(step):
        rows = span(step)
        return pltpu.make_async_copy(
            new_edges.at[rows], new_edges_out.at[rows], out_sems.at[step]
        )

    def paired(value):
        return jnp.concatenate([value[:half], value[half:]], axis=1)

    def unpaired(value):
        return jnp.concatenate([value[:, :width], value[:, width:]], axis=0)

    for k, column in enumerate((own_column, even_column, odd_column)):
        for part in range(3):
            columns[3 * k + part] = column[part * border : (part + 1) * border]

    def partner(mine, step):
        if step == 0:
            return 0
        is_odd = lax.rem(mine, 2)
        return 1 + is_odd if step > 0 else 2 - is_odd

    spot = 0
    for d_strip in (-1, 0, 1):
        column = partner(my_strip, d_strip)
        for d_sub in (-1, 0, 1):
            if d_strip == 0 and d_sub == 0:
                continue
            rows = slice(spot * border, (spot + 1) * border)
            far_rows[rows] = columns[3 * column + partner(my_y, d_sub)]
            spot += 1
    tables[:, :width] = near_table[...]
    tables[:, width:] = mm(far_rows[...], w_edge_in[:width]).astype(BF16)
    row = lax.broadcasted_iota(jnp.int32, (half, 2 * width), 0)
    lane = lax.broadcasted_iota(jnp.int32, (half, 2 * width), 1)
    edge_row = jnp.where(lane < width, row, row + half)
    agg[...] = jnp.zeros_like(agg)

    def forward(step, carry):
        recv_t = found_t(info[step][1:2], count_p)
        units = []
        for part in range(SPLIT):
            rows, pairs = block_rows(step, part), block_pairs(step, part)
            codes = send_codes[rows]
            begun = pre_part[rows]
            edge = paired(edges[rows].astype(F32))
            place = jnp.where(codes < 0, -1 - codes, codes)
            picked = mm(found(place, count_p // width), tables[...])
            beyond = codes.astype(F32) < 0.0
            pre = begun + jnp.where(beyond, picked[:, width:], picked[:, :width])
            act, bend = silu_and_slope(paired(pre))
            act = act.astype(BF16)
            centre = mm(act, centring[...])
            spare = mm((centre * centre).astype(BF16), means[...])
            live = edge_row < live_count - step * chunk - part * block
            factor = jnp.where(live, lax.rsqrt(spare + EPS), 0.0)
            unit = centre * factor
            slope[pairs] = bend
            hidden[rows] = unpaired(act)
            scale[pairs] = factor
            normed[pairs] = unit
            new_edges[rows] = unpaired((edge + unit).astype(BF16))
            units.append(unpaired(unit.astype(BF16)))
        agg[...] += mm(recv_t, jnp.concatenate(units, axis=0))
        emit(step).start()
        return carry

    lax.fori_loop(0, chunks, forward, 0, unroll=UNROLL)

    joined = jnp.concatenate([nodes[...], agg[...].astype(BF16)], axis=1)
    node_pre = mm(joined, w_node_in[...])
    node_act, node_slope = silu_and_slope(node_pre)
    node_act = node_act.astype(BF16)
    centre = mm(node_act, node_centring[...])
    spare = jnp.mean(centre * centre, axis=1, keepdims=True)
    along = jnp.mean(node_cot_c[...] * centre, axis=1, keepdims=True)
    node_scale = lax.rsqrt(spare + EPS)
    node_unit = centre * node_scale
    d_outer = node_scale * (node_cot_c[...] - node_unit * (along * node_scale))
    d_outer = d_outer.astype(BF16)
    d_pre = (mm_nt(d_outer, w_node_out[...]) * node_slope).astype(BF16)
    d_agg = mm_nt(d_pre, agg_centring[...]).astype(BF16)
    new_nodes[...] = (nodes[...].astype(F32) + node_unit).astype(BF16)
    agg[...] = node_cot[...].astype(F32) + mm_nt(d_pre, w_node_in[:width])
    kept[:, : 2 * width] = joined
    kept[:, 2 * width : 3 * width] = node_act
    kept[:, 3 * width : 4 * width] = d_outer
    kept[:, 4 * width :] = d_pre
    node_copy = pltpu.make_async_copy(new_nodes, new_nodes_out, last_sem)
    node_copy.start()

    sums[...] = jnp.zeros_like(sums)
    ge_out[...] = jnp.zeros_like(ge_out)

    def backward(step, carry):
        index = info[step]
        turned = jnp.concatenate(
            [found_t(index[1:2], count_p), found_t(index[0:1], count_p), edges_t[step]], axis=0
        )
        acts, outs, ins = [], [], []
        for part in range(SPLIT):
            rows, pairs = block_rows(step, part), block_pairs(step, part)
            cot = cot_part[rows].astype(F32)
            recv = found(recv_codes[rows], count_p // width)
            unit = normed[pairs]
            acts.append(hidden[rows])
            beyond = send_codes[rows] < 0
            upstream = paired(cot + mm(recv, d_agg))
            along = mm((upstream * unit).astype(BF16), means[...])
            d_out = (scale[pairs] * (upstream - unit * along)).astype(BF16)
            outs.append(unpaired(d_out))
            d_in = unpaired((mm_nt(d_out, back[...]) * slope[pairs]).astype(BF16))
            zero = jnp.zeros_like(d_in)
            ins.append(
                jnp.concatenate(
                    [jnp.where(beyond, zero, d_in), jnp.where(beyond, d_in, zero)], axis=1
                )
            )
        ge_out[...] += mm_tn(jnp.concatenate(acts, axis=0), jnp.concatenate(outs, axis=0))
        sums[...] += mm(turned, jnp.concatenate(ins, axis=0))
        return carry

    lax.fori_loop(0, chunks, backward, 0, unroll=UNROLL)

    recv_sums = (sums[:count_p, :width] + sums[:count_p, width:]).astype(BF16)
    near_sums = sums[count_p : 2 * count_p, :width].astype(BF16)
    far_sums = sums[count_p : 2 * count_p, width:].astype(BF16)
    edge_sums = sums[2 * count_p :, :width] + sums[2 * count_p :, width:]
    packed[:width] = (mm_tn(nodes[...], near_sums) + mm_tn(far_rows[...], far_sums)).astype(BF16)
    packed[width : 2 * width] = mm_tn(nodes[...], recv_sums).astype(BF16)
    packed[4 * width : 6 * width] = mm_tn(kept[:, : 2 * width], kept[:, 4 * width :]).astype(BF16)
    packed[6 * width : 7 * width] = mm_tn(
        kept[:, 2 * width : 3 * width], kept[:, 3 * width : 4 * width]
    ).astype(BF16)
    packed[2 * width : 3 * width] = edge_sums.astype(BF16)
    packed[3 * width : 4 * width] = ge_out[...].astype(BF16)
    if packed.shape[0] > 7 * width:
        packed[7 * width :] = jnp.zeros((packed.shape[0] - 7 * width, width), BF16)
    local_grad[...] = (
        agg[...]
        + mm_nt(near_sums, w_edge_in[:width])
        + mm_nt(recv_sums, w_edge_in[width : 2 * width])
    )
    owed = mm_nt(far_sums, w_edge_in[:width]).astype(BF16)
    for slot in range(slots):
        parts[slot, :share] = packed[slot * share : (slot + 1) * share]
        parts[slot, share:] = jnp.zeros((2 * border, width), BF16)
    spot = 0
    for d_strip in (-1, 0, 1):
        strip = my_strip + d_strip
        for d_sub in (-1, 0, 1):
            if d_strip == 0 and d_sub == 0:
                continue
            if d_sub == 0:
                slot, part = 2 * strip + my_y, 0
            elif d_sub == 1:
                slot, part = 2 * strip + 1 - my_y, my_y
            else:
                slot, part = 2 * strip + 1 - my_y, 1 - my_y
            first = pl.multiple_of(share + part * border, 16)
            block = owed[spot * border : (spot + 1) * border]

            @pl.when((strip >= 0) & (strip < strips))
            def put(slot=slot, first=first, block=block):
                parts[slot, pl.ds(first, border), :] = block

            spot += 1
    for step in range(chunks):
        emit(step).wait()
    node_copy.wait()


def plane_sum_kernel(came, message, mine):
    border = mine.shape[0]
    share = message.shape[0] - border
    total = came[0].astype(F32)
    for slot in range(1, came.shape[0]):
        total = total + came[slot].astype(F32)
    mine[...] = total[share : share + border]
    message[:share] = total[:share].astype(BF16)
    message[share:] = total[share + border :].astype(BF16)


def line_sum_kernel(factor, mine, *refs):
    messages, (out, rim_grad, held) = refs[:-3], refs[-3:]
    border = mine.shape[0]
    share = out.shape[1]
    for k, message in enumerate(messages):
        held[k] = message[...].astype(F32)
    my_z, my_y = lax.axis_index("z"), lax.axis_index("y")
    total = held[lax.bitwise_xor(my_z, 0), :share]
    for z in range(1, len(messages)):
        total = total + held[lax.bitwise_xor(my_z, z), :share]
    total = (total * factor).astype(BF16)
    for target in range(out.shape[0]):
        out[target] = total
    source = my_z - 1 + 2 * my_y
    inside = (source >= 0) & (source < len(messages))
    passed = held[lax.bitwise_xor(my_z, jnp.clip(source, 0, len(messages) - 1)), share:]
    rim_grad[...] = mine[...] + jnp.where(inside, passed, 0.0)


def finish_kernel(came, rim_grad, local_grad, node_grad, *outs):
    border = rim_grad.shape[0]
    share = came.shape[1]
    node_grad[...] = local_grad[...]
    node_grad[:border] += rim_grad[...]
    start = 0
    for out in outs:
        size = out.shape[0]
        done = 0
        while done < size:
            slot, offset = divmod(start + done, share)
            step = min(size - done, share - offset)
            out[done : done + step] = came[slot, offset : offset + step].astype(F32)
            done += step
        start += size


def shards(
    node_latents,
    edge_latents,
    senders,
    receivers,
    edge_count,
    w_edge_in,
    w_edge_out,
    w_node_in,
    w_node_out,
    node_cotangent,
    edge_cotangent,
):
    count_p, width = node_latents.shape
    count_e = edge_latents.shape[0]
    border = count_p // 8
    strips, zs, ys = (lax.axis_size(axis) for axis in ALL)
    subs = zs * ys
    slots = strips * ys
    even, odd = swapped(node_latents, ("z", "y"))
    chunk = min(CHUNK, count_e)
    chunks = count_e // chunk
    steps = chunks // 2 if chunks % 2 == 0 else chunks
    early = call(
        early_kernel,
        [
            ((count_e, width), BF16),
            ((count_e, width), BF16),
            ((count_e, width), BF16),
            ((chunks, width, chunk), BF16),
            ((count_e, width), F32),
            ((count_e, width), BF16),
            ((chunks, 8, chunk), jnp.int32),
        ],
        [
            node_latents,
            edge_latents,
            edge_cotangent,
            senders.reshape(steps, 1, count_e // steps),
            receivers.reshape(steps, 1, count_e // steps),
            w_edge_in,
        ],
        [HBM] * 6,
        [
            pltpu.VMEM((count_p + width, width), BF16),
            pltpu.VMEM((count_p, width), BF16),
            pltpu.VMEM((count_e, width), BF16),
            pltpu.VMEM((steps, 1, count_e // steps), jnp.int32),
            pltpu.VMEM((steps, 1, count_e // steps), jnp.int32),
            pltpu.VMEM((3 * width, width), BF16),
            SEM((4,)),
            SEM((2, steps)),
        ],
    )

    *early, odd, even = lax.optimization_barrier((*early, odd, even))
    (own_column,) = call(
        column_kernel,
        [((3 * border, width), BF16)],
        [node_latents, odd, even],
        [VMEM] * 3,
    )
    even_column, odd_column = swapped(own_column, "strip")

    share = -(-7 * width // (slots * 16)) * 16

    prepared = call(
        prepare_kernel,
        [
            ((count_p, width), BF16),
            ((2 * width, 2 * width), BF16),
            ((2 * width, 2 * width), BF16),
            ((2 * width, 2 * width), BF16),
            ((width, width), BF16),
            ((width, width), BF16),
            ((count_p, width), F32),
        ],
        [
            own_column,
            node_latents,
            w_edge_in,
            w_edge_out,
            w_node_in,
            w_node_out,
            node_cotangent,
        ],
        [VMEM] * 7,
    )
    new_nodes, new_edges, local_grad, parts = call(
        layer_kernel,
        [
            ((count_p, width), BF16),
            ((count_e, width), BF16),
            ((count_p, width), F32),
            ((slots, share + 2 * border, width), BF16),
        ],
        [
            edge_count,
            node_latents,
            own_column,
            even_column,
            odd_column,
            *early,
            w_edge_in,
            w_edge_out,
            w_node_in,
            w_node_out,
            node_cotangent,
            *prepared,
        ],
        [SMEM] + [VMEM] * 23,
        [
            pltpu.VMEM((count_p, width), BF16),
            pltpu.VMEM((count_e, width), BF16),
            pltpu.VMEM((8 * border, width), BF16),
            pltpu.VMEM((count_p, 2 * width), BF16),
            pltpu.VMEM((count_e, width), BF16),
            pltpu.VMEM((count_e // 2, 2 * width), F32),
            pltpu.VMEM((count_e // 2, 2 * width), F32),
            pltpu.VMEM((count_e // 2, 2 * width), F32),
            pltpu.VMEM((2 * count_p + width, 2 * width), F32),
            pltpu.VMEM((width, width), F32),
            pltpu.VMEM((count_p, width), F32),
            pltpu.VMEM((slots * share, width), BF16),
            pltpu.VMEM((count_p, 5 * width), BF16),
            pltpu.VMEM((9, border, width), BF16),
            SEM((chunks,)),
            SEM,
        ],
        [HBM, HBM, VMEM, VMEM],
        limit=24,
    )

    came = lax.all_to_all(parts, PLANE, 0, 0)
    state = [((share + border, width), BF16), ((border, width), F32)]
    message, mine = call(plane_sum_kernel, state, [came], [VMEM])
    factor = 1.0 / math.sqrt(count_e * strips * subs)
    messages = [message] + [
        lax.ppermute(message, "z", [(z, z ^ k) for z in range(zs)]) for k in range(1, zs)
    ]
    parts, rim_grad = call(
        functools.partial(line_sum_kernel, factor),
        [((slots, share, width), BF16), ((border, width), F32)],
        [mine, *messages],
        [VMEM] * (1 + zs),
        [pltpu.VMEM((zs, share + border, width), F32)],
    )
    came = lax.all_to_all(parts, PLANE, 0, 0)
    node_grad, *grads = call(
        finish_kernel,
        [((rows, width), F32) for rows in (count_p, 3 * width, width, 2 * width, width)],
        [came, rim_grad, local_grad],
        [VMEM, VMEM, VMEM],
    )
    return (new_nodes, new_edges, node_grad, *grads)


def solution(mesh):
    strips, subs = mesh.devices.shape
    grid = Mesh(mesh.devices.reshape(strips, subs // 2, 2), ALL)
    rows = P(ALL, None)
    line = P(ALL)
    return jax.shard_map(
        shards,
        mesh=grid,
        in_specs=(rows, rows, line, line, line, P(), P(), P(), P(), rows, rows),
        out_specs=(rows, rows, rows, P(), P(), P(), P()),
        check_vma=False,
    )
```
